32 devices in a mesh: view: 4 (over x, core), tile: 8 (over z, y).
Axes of the slice: x: 2, y: 2, z: 4, core: 2. Of those that a mesh axis runs over, the one named last changes fastest.
Arguments:
- acquired: float32 [4, 128, 128, 256], P('view', 'tile'), may hold values from 0.2 to 5
- estimate: float32 [128, 128, 256], P('tile'), may hold values from 0.5 to 2
- offsets: int32 [4, 3], P('view'), may hold values from -16 to 16, as said below
- view_mask: int32 [4, 128, 128], P('view', 'tile'), may hold values 0 or 1
- kern_x: float32 [4, 31], P('view'), may hold values from 0 to 1, as said below
- kern_y: float32 [4, 31], P('view'), may hold values from 0 to 1, as said below
- kern_z: float32 [4, 61], P('view'), may hold values from 0 to 1, as said below
Outputs:
- refined: float32 [128, 128, 256], P('tile')
The draws below stay inside these ranges and needn't reach their ends.
Inputs may be any that keep to these rules, and one draw needn't show every extreme that they name: `offsets`: every entry is an integer offset; some view's first offset is 16 and another's is -16. `kern_x`: each row is positive and sums to one. `kern_y`: each row is positive and sums to one. `kern_z`: each row is positive and sums to one.
All inputs are finite; a program needn't handle non-finite values. No bound on the sum of `view_mask` on one device may be relied on, other than what follows from the above.
Results may differ from the reference program's by a relative error of at most 0.0001.
Values sent between devices are 32-bit elements; how exact they have to be, the bound alone decides.
No kernel may reach another device: no remote copies, remote signals or barrier semaphores. Data moves between devices by JAX's collectives and lax.ppermute only.
A program may use at most 64 MiB of HBM per device.

```python
import math
import jax
import jax.numpy as jnp
from jax import lax

KX = 31
KY = 31
KZ = 61
TX = 16
Y = 128
Z = 256
ITERS = 2
VIEWS = 4
X = 128


def kernel_rows(key, taps):
    width_key, rough_key = jax.random.split(jax.random.fold_in(key, 17))
    sigma = jnp.exp(jax.random.uniform(width_key, (VIEWS, 1), jnp.float32, jnp.log(taps / 8.0), jnp.log(taps / 3.0)))
    centre = (taps - 1) / 2.0
    place = jnp.arange(taps, dtype=jnp.float32)[None, :] - centre
    profile = jnp.exp(-0.5 * (place / sigma) ** 2) + 0.02
    rough = jax.random.uniform(rough_key, (VIEWS, taps), jnp.float32, 0.5, 1.5)
    rows = profile * rough
    return rows / jnp.sum(rows, axis=1, keepdims=True)


def draw_kern_x(key, part):
    return kernel_rows(key, KX)


def draw_kern_y(key, part):
    return kernel_rows(jax.random.fold_in(key, 3), KY)


def draw_kern_z(key, part):
    return kernel_rows(jax.random.fold_in(key, 5), KZ)


def draw_offsets(key, part):
    value_key, pick_key = jax.random.split(jax.random.fold_in(key, 29))
    values = jax.random.randint(value_key, (VIEWS, 3), -TX, TX + 1, jnp.int32)
    first = jax.random.randint(pick_key, (), 0, VIEWS, jnp.int32)
    values = values.at[first, 0].set(TX)
    values = values.at[(first + 1) % VIEWS, 0].set(-TX)
    return values


def place_ends(result, own_key, low, high):
    extent = result.shape
    spot = [jax.random.randint(jax.random.fold_in(own_key, axis), (), 0, extent[axis]) for axis in range(len(extent))]
    result = result.at[tuple(spot)].set(low)
    longest = extent.index(max(extent))
    spot[longest] = (spot[longest] + 1) % extent[longest]
    return result.at[tuple(spot)].set(high)


def block_scale(own_key, dims, cuts, smallest, top_value):
    level = 1.0
    for dim, shards_of in cuts:
        draws = jax.random.uniform(jax.random.fold_in(jax.random.fold_in(own_key, 6), dim), (shards_of,), jnp.float32, smallest / len(cuts), top_value / len(cuts))
        level = level * jnp.repeat(jnp.exp(draws), dims[dim] // shards_of).reshape((-1,) + (1,) * (len(dims) - 1 - dim))
    return level


def setup_inputs(seed: int = 0) -> dict:
    key_of = jax.random.split(jax.random.key(seed), 8)
    acquired = jnp.clip(jnp.exp(math.log(5.0) - 3.218876 * jax.random.uniform(key_of[0], (VIEWS, X, Y, Z), jnp.float32) ** block_scale(key_of[0], (VIEWS, X, Y, Z), ((0, 4), (1, 8)), -0.2, 0.2)), 0.2, 5.0)
    estimate = jnp.clip(jnp.exp(math.log(2.0) - 1.3862944 * jax.random.uniform(key_of[1], (X, Y, Z), jnp.float32) ** block_scale(key_of[1], (X, Y, Z), ((0, 8),), -0.2, 0.2)), 0.5, 2.0)
    offsets = draw_offsets(jax.random.fold_in(key_of[7], 71), 0)
    view_mask = place_ends((jax.random.randint(key_of[3], (VIEWS, X, Y), 0, 4) < 3).astype(jnp.int32), jax.random.fold_in(key_of[3], 1), 0, 1)
    kern_x = draw_kern_x(jax.random.fold_in(key_of[7], 71), 0)
    kern_y = draw_kern_y(jax.random.fold_in(key_of[7], 71), 0)
    kern_z = draw_kern_z(jax.random.fold_in(key_of[7], 71), 0)
    return {"acquired": acquired, "estimate": estimate, "offsets": offsets, "view_mask": view_mask, "kern_x": kern_x, "kern_y": kern_y, "kern_z": kern_z}


def band_matrix(kern, rows, cols, offset):
    rows_idx = lax.broadcasted_iota(jnp.int32, (rows, cols), 0)
    cols_idx = lax.broadcasted_iota(jnp.int32, (rows, cols), 1)
    delta = cols_idx - rows_idx + offset
    total = jnp.zeros((rows, cols), kern.dtype)
    for tap in range(kern.shape[0]):
        total = total + jnp.where(delta == tap, kern[tap], jnp.zeros((), kern.dtype))
    return total


def apply_blur(field, kx, ky, kz, adjoint):
    my = band_matrix(ky, field.shape[1], field.shape[1], ky.shape[0] // 2)
    mz = band_matrix(kz, field.shape[2], field.shape[2], kz.shape[0] // 2)
    if adjoint:
        my = my.T
        mz = mz.T
        kx = kx[::-1]
    field = jnp.einsum("xyz,wz->xyw", field, mz, precision=lax.Precision.HIGHEST)
    field = jnp.einsum("xyz,wy->xwz", field, my, precision=lax.Precision.HIGHEST)
    radius = kx.shape[0] // 2
    padded = jnp.pad(field, ((radius, radius), (0, 0), (0, 0)))
    total = jnp.zeros_like(field)
    for tap in range(kx.shape[0]):
        total = total + kx[tap] * padded[tap:tap + field.shape[0]]
    return total


def reference(acquired, estimate, offsets, view_mask, kern_x, kern_y, kern_z):
    current = estimate
    images = []
    covers = []
    for view in range(VIEWS):
        padded = jnp.pad(acquired[view], ((TX, TX), (TX, TX), (TX, TX)))
        shift_x = offsets[view, 0].astype(jnp.int32)
        shift_y = offsets[view, 1].astype(jnp.int32)
        shift_z = offsets[view, 2].astype(jnp.int32)
        image = lax.dynamic_slice(padded, (TX + shift_x, TX + shift_y, TX + shift_z), (X, Y, Z))
        inside_x = (jnp.arange(X, dtype=jnp.int32) + shift_x >= 0) & (jnp.arange(X, dtype=jnp.int32) + shift_x < X)
        inside_y = (jnp.arange(Y, dtype=jnp.int32) + shift_y >= 0) & (jnp.arange(Y, dtype=jnp.int32) + shift_y < Y)
        inside_z = (jnp.arange(Z, dtype=jnp.int32) + shift_z >= 0) & (jnp.arange(Z, dtype=jnp.int32) + shift_z < Z)
        plane = (view_mask[view] != 0) & inside_x[:, None] & inside_y[None, :]
        images.append(image)
        covers.append(plane[:, :, None] & inside_z[None, None, :])
    for step in range(ITERS):
        log_total = jnp.zeros_like(current)
        for view in range(VIEWS):
            blurred = apply_blur(current, kern_x[view], kern_y[view], kern_z[view], False)
            ratio = jnp.where(covers[view], images[view] / blurred, jnp.ones((), jnp.float32))
            factor = apply_blur(ratio, kern_x[view], kern_y[view], kern_z[view], True)
            log_total = log_total + jnp.log(factor)
        current = current * jnp.exp(log_total)
    return current
```

```python
import functools

import jax
import jax.numpy as jnp
from jax import lax
from jax.experimental import pallas as pl
from jax.experimental.pallas import tpu as pltpu
from jax.sharding import PartitionSpec as P

ITERS = 2
AXES = ("view", "tile")
F32 = jnp.float32
BF16 = jnp.bfloat16
VMEM = pl.BlockSpec(memory_space=pltpu.VMEM)
SMEM = pl.BlockSpec(memory_space=pltpu.SMEM)
PARAMS = pltpu.CompilerParams(vmem_limit_bytes=48 * 1024 * 1024)


def moves(move):
    views, tiles = lax.axis_size("view"), lax.axis_size("tile")
    pairs = []
    for view in range(views):
        for tile in range(tiles):
            target = move(view // 2, view % 2, tile // 2, tile % 2)
            if target is not None:
                g, c, q, r = target
                pairs.append((view * tiles + tile, (2 * g + c) * tiles + 2 * q + r))
    return pairs


def send(array, move):
    return lax.ppermute(array, AXES, moves(move))


def to_next(g, c, q, r):
    s = 2 * q + c + 1
    return (g, s % 2, s // 2, r) if s < lax.axis_size("tile") else None


def to_previous(g, c, q, r):
    s = 2 * q + c - 1
    return (g, s % 2, s // 2, r) if s >= 0 else None


def to_row_partner(g, c, q, r):
    return (g, c, q, 1 - r)


def to_core_partner(g, c, q, r):
    return (g, 1 - c, q, r)


def split(x):
    high = x.astype(BF16)
    return high, (x - high.astype(F32)).astype(BF16)


def dot(a, b):
    return jnp.dot(a, b, preferred_element_type=F32)


def tables_kernel(half_ref, taps_ref, y_ref, zhi_ref, zlo_ref, *, rows, halo, radius_y, radius_z):
    lanes = taps_ref.shape[1]
    width = rows + halo
    half = half_ref[0]
    lane = lax.broadcasted_iota(jnp.int32, (rows, lanes), 1)
    for index in range(4):
        base = pltpu.roll(taps_ref[index:index + 1, :], lanes - radius_y, 1)
        band = pltpu.roll(jnp.broadcast_to(base, (rows, lanes)), 0, 1, stride=1, stride_axis=0)
        beyond = jnp.where(half == 1, pltpu.roll(band, width, 1), band)
        band = jnp.where(lane < rows, band, jnp.where(lane < width, beyond, jnp.zeros_like(band)))
        high, low = split(band)
        high, low = high.astype(F32), low.astype(F32)
        row = high + pltpu.roll(high, width, 1) + pltpu.roll(low, 2 * width, 1)
        y_ref[index] = row.astype(BF16)
    lane = lax.broadcasted_iota(jnp.int32, (lanes, lanes), 1)
    row = lax.broadcasted_iota(jnp.int32, (lanes, lanes), 0)
    near = jnp.abs(lane - row) <= radius_z
    for index in range(4):
        base = pltpu.roll(taps_ref[4 + index:5 + index, :], lanes - radius_z, 1)
        band = pltpu.roll(jnp.broadcast_to(base, (lanes, lanes)), 0, 1, stride=1, stride_axis=0)
        high, low = split(jnp.where(near, band, jnp.zeros_like(band)))
        zhi_ref[index] = high
        zlo_ref[index] = low


def make_tables(half, taps, rows, halo, radius_y, radius_z):
    lanes = taps.shape[1]
    kernel = functools.partial(tables_kernel, rows=rows, halo=halo, radius_y=radius_y, radius_z=radius_z)
    return pl.pallas_call(
        kernel,
        out_shape=(
            jax.ShapeDtypeStruct((4, rows, lanes), BF16),
            jax.ShapeDtypeStruct((4, lanes, lanes), BF16),
            jax.ShapeDtypeStruct((4, lanes, lanes), BF16),
        ),
        in_specs=[SMEM, VMEM],
        out_specs=(VMEM, VMEM, VMEM),
        compiler_params=PARAMS,
        name="band_matrices",
    )(half, taps)


def shift_kernel(scal_ref, acq_ref, mask_ref, first_ref, second_ref):
    planes, cells_y, cells_z = acq_ref.shape
    rows = cells_y // 2
    shift_y, shift_z, core = scal_ref[0], scal_ref[1], scal_ref[2]
    row = lax.broadcasted_iota(jnp.int32, (cells_y, cells_z), 0) + shift_y
    col = lax.broadcasted_iota(jnp.int32, (cells_y, cells_z), 1) + shift_z
    inside = (row >= 0) & (row < cells_y) & (col >= 0) & (col < cells_z)
    turn_y = lax.rem(cells_y - shift_y, cells_y)
    turn_z = lax.rem(cells_z - shift_z, cells_z)

    def body(p, carry):
        x = acq_ref[p]
        x = pltpu.roll(x, turn_z, 1)
        x = pltpu.roll(x, turn_y, 0)
        x = jnp.where(inside, x, jnp.zeros_like(x))
        low, high = x[:rows], x[rows:]
        first_ref[p] = jnp.where(core == 0, low, high)
        second_ref[p] = jnp.where(core == 0, high, low)
        return carry

    lax.fori_loop(0, planes, body, 0)
    mask = mask_ref[...].astype(F32)
    turned = pltpu.roll(mask, rows, 1)
    first_ref[planes] = jnp.zeros((rows, cells_z), F32)
    second_ref[planes] = jnp.zeros((rows, cells_z), F32)
    first_ref[planes, :planes, :cells_y] = jnp.where(core == 0, mask, turned)
    second_ref[planes, :planes, :cells_y] = jnp.where(core == 0, turned, mask)


def shift_and_cut(scal, acquired, mask):
    planes, cells_y, cells_z = acquired.shape
    shape = jax.ShapeDtypeStruct((planes + 1, cells_y // 2, cells_z), F32)
    return pl.pallas_call(
        shift_kernel,
        out_shape=(shape, shape),
        in_specs=[SMEM, VMEM, VMEM],
        out_specs=(VMEM, VMEM),
        compiler_params=PARAMS,
        name="shift_recorded",
    )(scal, acquired, mask)


def image_kernel(shift_ref, place_ref, *refs, extent_x, cells_y):
    blocks, out_ref = (refs[:3], refs[3:6]), refs[6]
    _, planes, rows, cells_z = out_ref.shape
    slab, half = place_ref[0], place_ref[1]
    eye = lax.broadcasted_iota(jnp.int32, (rows, rows), 0) == lax.broadcasted_iota(jnp.int32, (rows, rows), 1)
    eye = eye.astype(F32).astype(BF16)
    for order, (low_ref, own_ref, high_ref) in enumerate(blocks):
        view = half if order == 0 else 1 - half
        shift_x, shift_y, shift_z = (shift_ref[view, i] for i in range(3))
        mask = own_ref[planes, :planes, :rows].astype(BF16)
        columns = lax.dot_general(eye, mask, (((1,), (1,)), ((), ())), preferred_element_type=F32)
        row = lax.broadcasted_iota(jnp.int32, (rows, cells_z), 0) + shift_y + half * rows
        col = lax.broadcasted_iota(jnp.int32, (rows, cells_z), 1) + shift_z
        inside = (row >= 0) & (row < cells_y) & (col >= 0) & (col < cells_z)
        for p in range(planes):
            source = p + shift_x
            x = slab * planes + source
            own = own_ref[jnp.clip(source, 0, planes - 1)]
            low = low_ref[jnp.clip(source + planes, 0, planes - 1)]
            high = high_ref[jnp.clip(source - planes, 0, planes - 1)]
            value = jnp.where(source < 0, low, jnp.where(source < planes, own, high))
            weight = jnp.broadcast_to(columns[:, p:p + 1], (rows, cells_z))
            covered = inside & (weight > 0.5) & (x >= 0) & (x < extent_x)
            out_ref[view, p] = jnp.where(covered, value, jnp.full_like(value, -1.0))


def make_images(shifts, place, first, second, extent_x, cells_y):
    return pl.pallas_call(
        functools.partial(image_kernel, extent_x=extent_x, cells_y=cells_y),
        out_shape=jax.ShapeDtypeStruct((2,) + first[0].shape, F32),
        in_specs=[SMEM, SMEM] + [VMEM] * 6,
        out_specs=VMEM,
        compiler_params=PARAMS,
        name="images",
    )(shifts, place, *first, *second)


def spread_x(kx_ref, view, refs, store, rows, lanes, adjoint):
    low_ref, own_ref, high_ref = refs
    radius, planes = low_ref.shape[0], own_ref.shape[0]
    count = 2 * radius + 1
    parts = [(low_ref, i) for i in range(radius)] + [(own_ref, i) for i in range(planes)]
    parts += [(high_ref, i) for i in range(radius)]
    taps = [kx_ref[view, count - 1 - a if adjoint else a] for a in range(count)]

    def body(step, carry):
        row = pl.multiple_of(step * 8, 8)
        for column in range(0, lanes, 128):
            total = [None] * planes
            for i, (ref, index) in enumerate(parts):
                x = ref[index, pl.ds(row, 8), column:column + 128]
                for o in range(max(0, i - count + 1), min(planes - 1, i) + 1):
                    term = taps[i - o] * x
                    total[o] = term if total[o] is None else total[o] + term
            for o in range(planes):
                store(o, row, column, total[o])
        return carry

    lax.fori_loop(0, rows // 8, body, 0)


def spread_yz(fetch, y_ref, zhi_ref, zlo_ref, view, planes, width, lanes, store):
    band = y_ref[view]
    rest = band.shape[1] - 3 * width
    group = 4
    for start in range(0, planes, group):
        spread = []
        for p in range(start, min(start + group, planes)):
            high, low = split(fetch(p))
            parts = [high, low, high]
            if rest:
                parts.append(jnp.zeros((rest, lanes), BF16))
            spread.append(dot(band, jnp.concatenate(parts, axis=0)))
        high, low = split(jnp.concatenate(spread, axis=0))
        out = dot(high, zhi_ref[view]) + (dot(low, zhi_ref[view]) + dot(high, zlo_ref[view]))
        rows = band.shape[0]
        for index in range(len(spread)):
            store(start + index, out[index * rows:(index + 1) * rows])


def ratio_kernel(kx_ref, low_ref, own_ref, high_ref, image_ref, y_ref, zhi_ref, zlo_ref, ratio_ref, edge_ref, wide_ref, *, view):
    planes, rows, lanes = ratio_ref.shape
    width = own_ref.shape[1]
    halo = width - rows

    def store(o, row, column, value):
        wide_ref[o, pl.ds(row, 8), column:column + 128] = value

    spread_x(kx_ref, view, (low_ref, own_ref, high_ref), store, width, lanes, False)

    def finish(p, blurred):
        image = image_ref[0, p]
        ratio = jnp.where(image >= 0, image / blurred, jnp.ones_like(image))
        ratio_ref[p] = ratio
        edge_ref[0, p] = ratio[:halo]
        edge_ref[1, p] = ratio[rows - halo:]

    spread_yz(lambda p: wide_ref[p], y_ref, zhi_ref, zlo_ref, view, planes, width, lanes, finish)


def make_ratio(kx, low, own, high, images, tables, view):
    _, planes, rows, lanes = images.shape
    width = own.shape[1]
    return pl.pallas_call(
        functools.partial(ratio_kernel, view=view),
        out_shape=(
            jax.ShapeDtypeStruct(images.shape[1:], F32),
            jax.ShapeDtypeStruct((2, planes, width - rows, lanes), F32),
        ),
        grid=(1,),
        in_specs=[SMEM] + [VMEM] * 3 + [pl.BlockSpec((1, planes, rows, lanes), lambda i: (view, 0, 0, 0))] + [VMEM] * 3,
        out_specs=(VMEM, VMEM),
        scratch_shapes=[pltpu.VMEM((planes, width, lanes), F32)],
        compiler_params=PARAMS,
        name="ratio",
    )(kx, low, own, high, images, *tables)


def spread_kernel(ratio_ref, halo_ref, y_ref, zhi_ref, zlo_ref, out_ref, lower_ref, upper_ref, *, view):
    planes, rows, lanes = out_ref.shape
    width = rows + halo_ref.shape[1]
    radius = lower_ref.shape[0]

    def store(p, value):
        out_ref[p] = value
        if p < radius:
            lower_ref[p] = value
        if p >= planes - radius:
            upper_ref[p - planes + radius] = value

    spread_yz(
        lambda p: jnp.concatenate([ratio_ref[p], halo_ref[p]], axis=0),
        y_ref, zhi_ref, zlo_ref, 2 + view, planes, width, lanes, store,
    )


def make_spread(ratio, halo, tables, view, radius):
    planes, rows, lanes = ratio.shape
    edge = jax.ShapeDtypeStruct((radius, rows, lanes), F32)
    return pl.pallas_call(
        functools.partial(spread_kernel, view=view),
        out_shape=(jax.ShapeDtypeStruct(ratio.shape, F32), edge, edge),
        in_specs=[VMEM] * 5,
        out_specs=(VMEM, VMEM, VMEM),
        compiler_params=PARAMS,
        name="adjoint_yz",
    )(ratio, halo, *tables)


def factor_kernel(kx_ref, low0, own0, high0, low1, own1, high1, out_ref):
    planes, rows, lanes = out_ref.shape

    def first(o, row, column, value):
        out_ref[o, pl.ds(row, 8), column:column + 128] = jnp.log(value)

    def second(o, row, column, value):
        place = (o, pl.ds(row, 8), slice(column, column + 128))
        out_ref[place] = out_ref[place] + jnp.log(value)

    spread_x(kx_ref, 0, (low0, own0, high0), first, rows, lanes, True)
    spread_x(kx_ref, 1, (low1, own1, high1), second, rows, lanes, True)


def make_factor(kx, view0, view1):
    return pl.pallas_call(
        factor_kernel,
        out_shape=jax.ShapeDtypeStruct(view0[1].shape, F32),
        in_specs=[SMEM] + [VMEM] * 6,
        out_specs=VMEM,
        compiler_params=PARAMS,
        name="log_factor",
    )(kx, *view0, *view1)


def shards(acquired, estimate, offsets, view_mask, kern_x, kern_y, kern_z):
    planes, cells_y, cells_z = estimate.shape
    views, slabs = lax.axis_size("view"), lax.axis_size("tile")
    groups = views // 2
    rows = cells_y // 2
    taps_x, taps_y, taps_z = kern_x.shape[1], kern_y.shape[1], kern_z.shape[1]
    radius = taps_x // 2
    halo = -(-(taps_y // 2) // 16) * 16
    core = lax.rem(lax.axis_index("view"), 2)
    half = lax.rem(lax.axis_index("tile"), 2)
    slab = lax.axis_index("tile") - half + core
    straight = core == half

    mine = jnp.concatenate([kern_x[0], kern_y[0], kern_z[0], offsets[0].astype(F32)])
    other = send(mine, to_core_partner)
    both = jnp.where(core == 0, jnp.stack([mine, other]), jnp.stack([other, mine]))
    kx = both[:, :taps_x]
    ky = both[:, taps_x:taps_x + taps_y]
    kz = both[:, taps_x + taps_y:taps_x + taps_y + taps_z]
    shifts = both[:, taps_x + taps_y + taps_z:].astype(jnp.int32)
    pad_y = ((0, 0), (0, cells_z - taps_y))
    pad_z = ((0, 0), (0, cells_z - taps_z))
    taps = jnp.concatenate(
        [jnp.pad(ky, pad_y), jnp.pad(ky[:, ::-1], pad_y), jnp.pad(kz[:, ::-1], pad_z), jnp.pad(kz, pad_z)]
    )
    tables = make_tables(half.reshape(1), taps, rows, halo, taps_y // 2, taps_z // 2)

    def widen(array, side):
        own = lax.dynamic_slice_in_dim(array, side * rows, rows, 1)
        edge = lax.dynamic_slice_in_dim(array, rows - side * halo, halo, 1)
        return jnp.concatenate([own, edge], axis=1)

    crossing = send(widen(estimate, 1 - half), lambda g, c, q, r: (g, c, q, 1 - r) if c == r else None)
    current = jnp.where(straight, widen(estimate, half), crossing)

    scal = jnp.stack([offsets[0, 1], offsets[0, 2], core])
    first, second = shift_and_cut(scal, acquired[0], view_mask[0])
    first = send(first, lambda g, c, q, r: (g, r, q, c))
    second = send(second, lambda g, c, q, r: (g, r, q, 1 - c))
    first, second = (
        (send(block[:planes], to_next), block, send(block[:planes], to_previous)) for block in (first, second)
    )
    place = jnp.stack([slab, half])
    images = make_images(shifts, place, first, second, planes * slabs, cells_y)

    for step in range(ITERS):
        low = send(current[planes - radius:], to_next)
        high = send(current[:radius], to_previous)
        sides = []
        for view in range(2):
            ratio, edges = make_ratio(kx, low, current, high, images, tables, view)
            edge = lax.dynamic_index_in_dim(edges, 1 - half, 0, keepdims=False)
            beyond = send(edge, to_row_partner)
            spread, lower, upper = make_spread(ratio, beyond, tables, view, radius)
            sides.append((send(upper, to_next), spread, send(lower, to_previous)))
        total = make_factor(kx, *sides)
        summed = total
        for turn in range(1, groups):
            summed = summed + send(total, lambda g, c, q, r: ((g + turn) % groups, c, q, r))
        own = current[:, :rows] * jnp.exp(summed)
        if step < ITERS - 1:
            edge = lax.dynamic_slice_in_dim(own, (rows - halo) * (1 - half), halo, 1)
            current = jnp.concatenate([own, send(edge, to_row_partner)], axis=1)

    crossed = send(own, lambda g, c, q, r: (g, c, q, 1 - r) if c != r else None)
    low_rows = jnp.where(half == 0, own, crossed)
    high_rows = jnp.where(half == 0, crossed, own)
    whole = jnp.concatenate([low_rows, high_rows], axis=1)
    copied = send(whole, lambda g, c, q, r: (g, 1 - c, q, r) if c == r else None)
    return jnp.where(straight, whole, copied)


def solution(mesh):
    in_specs = (
        P("view", "tile", None, None),
        P("tile", None, None),
        P("view", None),
        P("view", "tile", None),
        P("view", None),
        P("view", None),
        P("view", None),
    )
    out_specs = P("tile", None, None)
    return jax.shard_map(shards, mesh=mesh, in_specs=in_specs, out_specs=out_specs, check_vma=False)
```

```python
import functools

import jax
import jax.numpy as jnp
from jax import lax
from jax.experimental import pallas as pl
from jax.experimental.pallas import tpu as pltpu
from jax.sharding import PartitionSpec as P

ITERS = 2
AXES = ("view", "tile")
F32 = jnp.float32
BF16 = jnp.bfloat16
VMEM = pl.BlockSpec(memory_space=pltpu.VMEM)
SMEM = pl.BlockSpec(memory_space=pltpu.SMEM)
PARAMS = pltpu.CompilerParams(vmem_limit_bytes=48 * 1024 * 1024)
GROUP = 16


def moves(move):
    views, tiles = lax.axis_size("view"), lax.axis_size("tile")
    pairs = []
    for view in range(views):
        for tile in range(tiles):
            target = move(view // 2, view % 2, tile // 2, tile % 2)
            if target is not None:
                g, c, q, r = target
                pairs.append((view * tiles + tile, (2 * g + c) * tiles + 2 * q + r))
    return pairs


def send(array, move):
    return lax.ppermute(array, AXES, moves(move))


def to_next(g, c, q, r):
    s = 2 * q + c + 1
    return (g, s % 2, s // 2, r) if s < lax.axis_size("tile") else None


def to_previous(g, c, q, r):
    s = 2 * q + c - 1
    return (g, s % 2, s // 2, r) if s >= 0 else None


def to_row_partner(g, c, q, r):
    return (g, c, q, 1 - r)


def to_core_partner(g, c, q, r):
    return (g, 1 - c, q, r)


def split(x):
    high = x.astype(BF16)
    return high, (x - high.astype(F32)).astype(BF16)


def dot(a, b):
    return jnp.dot(a, b, preferred_element_type=F32)


def iota(shape, dim):
    return lax.broadcasted_iota(jnp.int32, shape, dim)


def group_row(half, group, cells_y):
    return group * GROUP + half * (cells_y - GROUP - 2 * group * GROUP)


def global_row(half, local, cells_y):
    group = local // GROUP
    return group_row(half, group, cells_y) + (local - group * GROUP)


def pad_to(value, unit):
    return -(-value // unit) * unit


def call(kernel, out_shape, in_specs, name, scratch=()):
    return pl.pallas_call(
        kernel,
        out_shape=out_shape,
        in_specs=in_specs,
        out_specs=jax.tree.map(lambda _: VMEM, out_shape),
        scratch_shapes=list(scratch),
        compiler_params=PARAMS,
        name=name,
    )


def tables_kernel(
    half_ref, ky_ref, tz_ref, tx_ref, yf_ref, ya_ref, zhi_ref, zlo_ref, xhi_ref, xlo_ref, *, sizes, cells_y, radius_z
):
    taps = ky_ref.shape[1]
    radius = taps // 2
    half = half_ref[0]
    own, near, wide = sizes
    for index in range(4):
        adjoint = index >= 2
        out_ref, rows, width = (ya_ref, own, near) if adjoint else (yf_ref, near, wide)
        lanes = out_ref.shape[2]
        row = global_row(half, iota((rows, lanes), 0), cells_y)
        lane = iota((rows, lanes), 1)
        col = global_row(half, lane, cells_y)
        delta = (row - col if adjoint else col - row) + radius
        delta = jnp.where(lane < width, delta, -1)
        band = jnp.zeros((rows, lanes), F32)
        for a in range(taps):
            band = jnp.where(delta == a, ky_ref[index % 2, a], band)
        high, low = split(band)
        high, low = high.astype(F32), low.astype(F32)
        out_ref[index % 2] = (high + pltpu.roll(high, width, 1) + pltpu.roll(low, 2 * width, 1)).astype(BF16)

    lanes = tz_ref.shape[1]
    near_z = jnp.abs(iota((lanes, lanes), 1) - iota((lanes, lanes), 0)) <= radius_z
    for index in range(4):
        base = pltpu.roll(tz_ref[index:index + 1, :], lanes - radius_z, 1)
        band = pltpu.roll(jnp.broadcast_to(base, (lanes, lanes)), 0, 1, stride=1, stride_axis=0)
        zhi_ref[index], zlo_ref[index] = split(jnp.where(near_z, band, jnp.zeros_like(band)))

    rows, lanes = xhi_ref.shape[1] // 2, tx_ref.shape[1]
    for index in range(4):
        base = jnp.broadcast_to(tx_ref[index:index + 1, :], (rows, lanes))
        band = pltpu.roll(base, 0, 1, stride=1, stride_axis=0)[:, :xhi_ref.shape[2]]
        place = (index // 2, slice(index % 2 * rows, index % 2 * rows + rows))
        xhi_ref[place], xlo_ref[place] = split(band)


def make_tables(half, kx, ky, kz, planes, cells_y, cells_z, sizes):
    own, near, wide = sizes
    taps_x, taps_z = kx.shape[1], kz.shape[1]
    depth = 8 * pad_to(planes + taps_x - 1, 16)
    lanes = max(512, 1 << (depth - 1).bit_length())
    zero = jnp.zeros((), F32)
    tx = jnp.concatenate([kx, kx[:, ::-1]])
    tx = lax.pad(tx, zero, ((0, 0, 0), (0, lanes - 8 * taps_x + 7, 7)))
    tz = jnp.concatenate([kz[:, ::-1], kz])
    tz = lax.pad(tz, zero, ((0, 0, 0), (0, cells_z - taps_z, 0)))
    kernel = functools.partial(tables_kernel, sizes=sizes, cells_y=cells_y, radius_z=taps_z // 2)
    shape = jax.ShapeDtypeStruct
    out_shape = (
        shape((2, near, pad_to(3 * wide, 128)), BF16),
        shape((2, own, pad_to(3 * near, 128)), BF16),
        shape((4, cells_z, cells_z), BF16),
        shape((4, cells_z, cells_z), BF16),
        shape((2, 2 * 8 * planes, depth), BF16),
        shape((2, 2 * 8 * planes, depth), BF16),
    )
    return call(kernel, out_shape, [SMEM, SMEM, VMEM, VMEM], "band_matrices")(half.reshape(1), ky, tz, tx)


def window_kernel(half_ref, estimate_ref, own_ref, other_ref):
    cells_y = estimate_ref.shape[1]
    half = half_ref[0]
    for side, out_ref in ((half, own_ref), (1 - half, other_ref)):
        for group in range(out_ref.shape[1] // GROUP):
            start = pl.multiple_of(group_row(side, group, cells_y), GROUP)
            out_ref[:, group * GROUP:(group + 1) * GROUP, :] = estimate_ref[:, pl.ds(start, GROUP), :]


def make_windows(half, estimate, wide):
    planes, _, cells_z = estimate.shape
    shape = jax.ShapeDtypeStruct((planes, wide, cells_z), F32)
    return call(window_kernel, (shape, shape), [SMEM, VMEM], "estimate_windows")(half.reshape(1), estimate)


def shift_kernel(scal_ref, acq_ref, mask_ref, first_ref, second_ref, turned_ref):
    planes, cells_y, cells_z = acq_ref.shape
    near = first_ref.shape[1]
    shift_y, shift_z, core = scal_ref[0], scal_ref[1], scal_ref[2]
    row = iota((cells_y, cells_z), 0) + shift_y
    col = iota((cells_y, cells_z), 1) + shift_z
    inside = (row >= 0) & (row < cells_y) & (col >= 0) & (col < cells_z)
    turn_y = lax.rem(cells_y - shift_y, cells_y)
    turn_z = lax.rem(cells_z - shift_z, cells_z)

    def body(p, carry):
        x = pltpu.roll(pltpu.roll(acq_ref[p], turn_z, 1), turn_y, 0)
        turned_ref[...] = jnp.where(inside, x, jnp.zeros_like(x))
        for side, out_ref in ((core, first_ref), (1 - core, second_ref)):
            for group in range(near // GROUP):
                start = pl.multiple_of(group_row(side, group, cells_y), GROUP)
                out_ref[p, group * GROUP:(group + 1) * GROUP, :] = turned_ref[pl.ds(start, GROUP), :]
        return carry

    lax.fori_loop(0, planes, body, 0)
    mask = mask_ref[...].astype(F32)
    for out_ref in (first_ref, second_ref):
        out_ref[planes] = jnp.zeros((near, cells_z), F32)
        out_ref[planes, :planes, :cells_y] = mask


def shift_and_cut(scal, acquired, mask, near):
    planes, cells_y, cells_z = acquired.shape
    shape = jax.ShapeDtypeStruct((planes + 1, near, cells_z), F32)
    scratch = [pltpu.VMEM((cells_y, cells_z), F32)]
    return call(shift_kernel, (shape, shape), [SMEM, VMEM, VMEM], "shift_recorded", scratch)(scal, acquired, mask)


def spread_x(hi_ref, lo_ref, index, start, count, refs, row):
    low_ref, own_ref, high_ref = refs
    lanes = own_ref.shape[2]
    depth = hi_ref.shape[2]
    parts = [ref[:, pl.ds(row, 8), :] for ref in refs]
    missing = depth // 8 - sum(part.shape[0] for part in parts)
    if missing:
        parts.append(jnp.zeros((missing, 8, lanes), F32))
    high, low = split(jnp.concatenate(parts, axis=0).reshape(depth, lanes))
    band = hi_ref[index, start:start + count, :]
    out = dot(band, high) + (dot(band, low) + dot(lo_ref[index, start:start + count, :], high))
    return out.reshape(count // 8, 8, lanes)


def blur_x_kernel(hi_ref, lo_ref, low_ref, own_ref, high_ref, first_ref, second_ref):
    planes, rows, lanes = own_ref.shape

    def body(step, carry):
        row = pl.multiple_of(step * 8, 8)
        out = spread_x(hi_ref, lo_ref, 0, 0, hi_ref.shape[1], (low_ref, own_ref, high_ref), row)
        first_ref[:, pl.ds(row, 8), :] = out[:planes]
        second_ref[:, pl.ds(row, 8), :] = out[planes:]
        return carry

    lax.fori_loop(0, rows // 8, body, 0)


def blur_x(tables, low, own, high):
    shape = jax.ShapeDtypeStruct(own.shape, F32)
    return call(blur_x_kernel, (shape, shape), [VMEM] * 5, "blur_x")(*tables[4:], low, own, high)


def spread_y(band, x):
    high, low = split(x)
    parts = [high, low, high]
    rest = band.shape[1] - 3 * x.shape[0]
    if rest:
        parts.append(jnp.zeros((rest, x.shape[1]), BF16))
    return dot(band, jnp.concatenate(parts, axis=0))


def spread_z(x, hi_ref, lo_ref, index):
    high, low = split(x)
    return dot(high, hi_ref[index]) + (dot(low, hi_ref[index]) + dot(high, lo_ref[index]))


def ratio_planes(wide_ref, fetch, yf_ref, ya_ref, zhi_ref, zlo_ref, order, outs):
    out_ref, lower_ref, upper_ref = outs
    planes, rows, _ = out_ref.shape
    radius = lower_ref.shape[0]
    near = yf_ref.shape[1]
    step = 4
    for start in range(0, planes, step):
        block = range(start, min(start + step, planes))
        blurred = jnp.concatenate([spread_y(yf_ref[order], wide_ref[p]) for p in block], axis=0)
        blurred = spread_z(blurred, zhi_ref, zlo_ref, order)
        image = jnp.concatenate([fetch(p) for p in block], axis=0)
        ratio = jnp.where(image >= 0, image / blurred, jnp.ones_like(image))
        spread = jnp.concatenate(
            [spread_y(ya_ref[order], ratio[k * near:(k + 1) * near]) for k in range(len(block))], axis=0
        )
        spread = spread_z(spread, zhi_ref, zlo_ref, 2 + order)
        for k, p in enumerate(block):
            value = spread[k * rows:(k + 1) * rows]
            out_ref[p] = value
            if p < radius:
                lower_ref[p] = value
            if p >= planes - radius:
                upper_ref[p - planes + radius] = value


def first_ratio_kernel(
    shift_ref, place_ref, low_ref, own_ref, high_ref, wide_ref, yf_ref, ya_ref, zhi_ref, zlo_ref,
    out_ref, lower_ref, upper_ref, image_ref, *, order, extent_x, cells_y
):
    planes, near, cells_z = image_ref.shape
    slab, half = place_ref[0], place_ref[1]
    shift_x, shift_y, shift_z = (shift_ref[order, i] for i in range(3))
    lanes = pad_to(cells_y, 128)
    pick = iota((near, lanes), 1) == global_row(half, iota((near, lanes), 0), cells_y)
    mask = own_ref[planes, :planes, :lanes].astype(BF16)
    columns = lax.dot_general(
        pick.astype(F32).astype(BF16), mask, (((1,), (1,)), ((), ())), preferred_element_type=F32
    )
    row = global_row(half, iota((near, cells_z), 0), cells_y) + shift_y
    col = iota((near, cells_z), 1) + shift_z
    inside = (row >= 0) & (row < cells_y) & (col >= 0) & (col < cells_z)

    def fetch(p):
        source = p + shift_x
        x = slab * planes + source
        own = own_ref[jnp.clip(source, 0, planes - 1)]
        low = low_ref[jnp.clip(source + planes, 0, planes - 1)]
        high = high_ref[jnp.clip(source - planes, 0, planes - 1)]
        value = jnp.where(source < 0, low, jnp.where(source < planes, own, high))
        weight = jnp.broadcast_to(columns[:, p:p + 1], (near, cells_z))
        covered = inside & (weight > 0.5) & (x >= 0) & (x < extent_x)
        value = jnp.where(covered, value, jnp.full_like(value, -1.0))
        image_ref[p] = value
        return value

    ratio_planes(wide_ref, fetch, yf_ref, ya_ref, zhi_ref, zlo_ref, order, (out_ref, lower_ref, upper_ref))


def next_ratio_kernel(
    image_ref, wide_ref, yf_ref, ya_ref, zhi_ref, zlo_ref, out_ref, lower_ref, upper_ref, *, order
):
    ratio_planes(
        wide_ref, lambda p: image_ref[p], yf_ref, ya_ref, zhi_ref, zlo_ref, order, (out_ref, lower_ref, upper_ref)
    )


def ratio_shapes(wide, tables, radius):
    planes, _, lanes = wide.shape
    rows = tables[1].shape[1]
    edge = jax.ShapeDtypeStruct((radius, rows, lanes), F32)
    return jax.ShapeDtypeStruct((planes, rows, lanes), F32), edge, edge


def first_ratio(shifts, place, blocks, wide, tables, order, radius, extent_x, cells_y):
    near = tables[0].shape[1]
    kernel = functools.partial(first_ratio_kernel, order=order, extent_x=extent_x, cells_y=cells_y)
    image = jax.ShapeDtypeStruct((wide.shape[0], near, wide.shape[2]), F32)
    out_shape = ratio_shapes(wide, tables, radius) + (image,)
    return call(kernel, out_shape, [SMEM] * 2 + [VMEM] * 8, "image_and_ratio")(
        shifts, place, *blocks, wide, *tables[:4]
    )


def next_ratio(image, wide, tables, order, radius):
    kernel = functools.partial(next_ratio_kernel, order=order)
    return call(kernel, ratio_shapes(wide, tables, radius), [VMEM] * 6, "ratio")(image, wide, *tables[:4])


def factor_kernel(hi_ref, lo_ref, current_ref, *refs, start, share):
    views, out_ref = (refs[:3], refs[3:6]), refs[6]
    planes, rows, _ = out_ref.shape

    def body(step, carry):
        row = pl.multiple_of(step * 8, 8)
        source = pl.multiple_of(start + row, 8)
        total = share * jnp.log(current_ref[:, pl.ds(source, 8), :])
        for order, view in enumerate(views):
            total = total + jnp.log(spread_x(hi_ref, lo_ref, 1, order * 8 * planes, 8 * planes, view, source))
        out_ref[:, pl.ds(row, 8), :] = total
        return carry

    lax.fori_loop(0, rows // 8, body, 0)


def log_factor(tables, current, sides, start, rows, share):
    planes, _, lanes = current.shape
    kernel = functools.partial(factor_kernel, start=start, share=share)
    shape = jax.ShapeDtypeStruct((planes, rows, lanes), F32)
    return call(kernel, shape, [VMEM] * 9, "log_factor")(*tables[4:], current, *sides[0], *sides[1])


def finish_kernel(half_ref, own_ref, *refs, groups):
    out_ref = refs[-1]
    half = half_ref[0]
    cells_y = out_ref.shape[1]
    own = [own_ref] + list(refs[:groups - 1])
    other = list(refs[groups - 1:2 * groups - 1])
    for side, parts in ((half, own), (1 - half, other)):
        for group in range(own_ref.shape[1] // GROUP):
            rows = slice(group * GROUP, (group + 1) * GROUP)
            total = parts[0][:, rows, :]
            for part in parts[1:]:
                total = total + part[:, rows, :]
            start = pl.multiple_of(group_row(side, group, cells_y), GROUP)
            out_ref[:, pl.ds(start, GROUP), :] = jnp.exp(total)


def finish(half, own, own_parts, other_parts, shape):
    groups = len(own_parts) + 1
    kernel = functools.partial(finish_kernel, groups=groups)
    return call(kernel, jax.ShapeDtypeStruct(shape, F32), [SMEM] + [VMEM] * (2 * groups), "update")(
        half.reshape(1), own, *own_parts, *other_parts
    )


def shards(acquired, estimate, offsets, view_mask, kern_x, kern_y, kern_z):
    planes, cells_y, cells_z = estimate.shape
    views, slabs = lax.axis_size("view"), lax.axis_size("tile")
    groups = views // 2
    taps_x, taps_y, taps_z = kern_x.shape[1], kern_y.shape[1], kern_z.shape[1]
    radius = taps_x // 2
    own_rows = cells_y // 2
    near = own_rows + pad_to(taps_y // 2, GROUP)
    wide = own_rows + pad_to(2 * (taps_y // 2), GROUP)
    edge_rows = wide - own_rows
    inner_rows = own_rows - edge_rows
    core = lax.rem(lax.axis_index("view"), 2)
    half = lax.rem(lax.axis_index("tile"), 2)
    slab = lax.axis_index("tile") - half + core
    straight = core == half

    window, crossing = make_windows(half, estimate, wide)
    crossing = send(crossing, lambda g, c, q, r: (g, c, q, 1 - r) if c == r else None)

    scal = jnp.stack([offsets[0, 1], offsets[0, 2], core])
    acquired, window = lax.optimization_barrier((acquired, window))
    first, second = shift_and_cut(scal, acquired[0], view_mask[0], near)

    mine = jnp.concatenate([kern_x[0], kern_y[0], kern_z[0], offsets[0].astype(F32)])
    other = send(mine, to_core_partner)
    both = jnp.where(straight, jnp.stack([mine, other]), jnp.stack([other, mine]))
    kx = both[:, :taps_x]
    ky = both[:, taps_x:taps_x + taps_y]
    kz = both[:, taps_x + taps_y:taps_x + taps_y + taps_z]
    shifts = both[:, taps_x + taps_y + taps_z:].astype(jnp.int32)
    tables = make_tables(half, kx, ky, kz, planes, cells_y, cells_z, (own_rows, near, wide))

    first, crossing = lax.optimization_barrier((first, crossing))
    current = jnp.where(straight, window, crossing)
    low = send(current[planes - radius:], to_next)
    high = send(current[:radius], to_previous)
    first = send(first, lambda g, c, q, r: (g, r, q, c))
    second, first = lax.optimization_barrier((second, first))
    second = send(second, lambda g, c, q, r: (g, r, q, 1 - c))
    place = jnp.stack([slab, half])
    blocks = [(send(block, to_next), block, send(block, to_previous)) for block in (first, second)]
    images = [None, None]

    for step in range(ITERS):
        wides = blur_x(tables, low, current, high)
        sides = []
        for order in range(2):
            if step == 0:
                spread, lower, upper, images[order] = first_ratio(
                    shifts, place, blocks[order], wides[order], tables, order, radius, planes * slabs, cells_y
                )
            else:
                spread, lower, upper = next_ratio(images[order], wides[order], tables, order, radius)
            sides.append((send(upper, to_next), spread, send(lower, to_previous)))
        if step < ITERS - 1:
            edge = log_factor(tables, current, sides, inner_rows, edge_rows, 1.0 / groups)
            inner = log_factor(tables, current, sides, 0, inner_rows, 1.0 / groups)
            edge_sum, inner_sum = edge, inner
            for turn in range(1, groups):
                edge_sum = edge_sum + send(edge, lambda g, c, q, r: ((g + turn) % groups, c, q, r))
            for turn in range(1, groups):
                inner_sum = inner_sum + send(inner, lambda g, c, q, r: ((g + turn) % groups, c, q, r))
            edge = jnp.exp(edge_sum)
            beyond = send(edge, to_row_partner)
            beyond = beyond.reshape(planes, edge_rows // GROUP, GROUP, cells_z)[:, ::-1].reshape(edge.shape)
            current = jnp.concatenate([jnp.exp(inner_sum), edge, beyond], axis=1)
            low = send(current[planes - radius:], to_next)
            high = send(current[:radius], to_previous)

    own = log_factor(tables, current, sides, 0, own_rows, 1.0 / groups)
    own_parts, other_parts = [], []
    for turn in range(groups):
        other_parts.append(
            send(own, lambda g, c, q, r: ((g + turn) % groups, c, q, 1 - r) if c != r else None)
        )
        if turn:
            own_parts.append(send(own, lambda g, c, q, r: ((g + turn) % groups, c, q, r) if c == r else None))
    whole = finish(half, own, own_parts, other_parts, estimate.shape)
    copied = send(whole, lambda g, c, q, r: (g, 1 - c, q, r) if c == r else None)
    return jnp.where(straight, whole, copied)


def solution(mesh):
    in_specs = (
        P("view", "tile", None, None),
        P("tile", None, None),
        P("view", None),
        P("view", "tile", None),
        P("view", None),
        P("view", None),
        P("view", None),
    )
    out_specs = P("tile", None, None)
    return jax.shard_map(shards, mesh=mesh, in_specs=in_specs, out_specs=out_specs, check_vma=False)
```

```python
import functools

import jax
import jax.numpy as jnp
from jax import lax
from jax.experimental import pallas as pl
from jax.experimental.pallas import tpu as pltpu
from jax.sharding import PartitionSpec as P

ITERS = 2
AXES = ("view", "tile")
F32 = jnp.float32
BF16 = jnp.bfloat16
VMEM = pl.BlockSpec(memory_space=pltpu.VMEM)
SMEM = pl.BlockSpec(memory_space=pltpu.SMEM)
PARAMS = pltpu.CompilerParams(vmem_limit_bytes=20 * 1024 * 1024)
GROUP = 16


def moves(move):
    views, tiles = lax.axis_size("view"), lax.axis_size("tile")
    pairs = []
    for view in range(views):
        for tile in range(tiles):
            target = move(view // 2, view % 2, tile // 2, tile % 2)
            if target is not None:
                g, c, q, r = target
                pairs.append((view * tiles + tile, (2 * g + c) * tiles + 2 * q + r))
    return pairs


def send(array, move):
    return lax.ppermute(array, AXES, moves(move))


def to_next(g, c, q, r):
    s = 2 * q + c + 1
    return (g, s % 2, s // 2, r) if s < lax.axis_size("tile") else None


def to_previous(g, c, q, r):
    s = 2 * q + c - 1
    return (g, s % 2, s // 2, r) if s >= 0 else None


def to_row_partner(g, c, q, r):
    return (g, c, q, 1 - r)


def to_core_partner(g, c, q, r):
    return (g, 1 - c, q, r)


def split(x):
    high = x.astype(BF16)
    return high, (x - high.astype(F32)).astype(BF16)


def dot(a, b):
    return jnp.dot(a, b, preferred_element_type=F32)


def iota(shape, dim):
    return lax.broadcasted_iota(jnp.int32, shape, dim)


def group_row(half, group, cells_y):
    return group * GROUP + half * (cells_y - GROUP - 2 * group * GROUP)


def global_row(half, local, cells_y):
    group = local // GROUP
    return group_row(half, group, cells_y) + (local - group * GROUP)


def wide_local(place, own, wide):
    group = (place - own) // GROUP
    return own + (wide - own) - GROUP - group * GROUP + (place - own - group * GROUP)


def wide_group(group, own_groups, groups):
    return group if group < own_groups else own_groups + groups - 1 - group


def pad_to(value, unit):
    return -(-value // unit) * unit


def call(kernel, out_shape, in_specs, name, scratch=()):
    return pl.pallas_call(
        kernel,
        out_shape=out_shape,
        in_specs=in_specs,
        out_specs=jax.tree.map(lambda _: VMEM, out_shape),
        scratch_shapes=list(scratch),
        compiler_params=PARAMS,
        name=name,
    )


def tables_kernel(
    half_ref, ky_ref, tz_ref, tx_ref, yf_ref, ya_ref, zhi_ref, zlo_ref, xhi_ref, xlo_ref, *, sizes, cells_y, radius_z
):
    taps = ky_ref.shape[1]
    radius = taps // 2
    half = half_ref[0]
    own, near, wide = sizes
    for index in range(4):
        adjoint = index >= 2
        out_ref, rows, width = (ya_ref, own, near) if adjoint else (yf_ref, near, wide)
        lanes = out_ref.shape[2]
        row = global_row(half, iota((rows, lanes), 0), cells_y)
        lane = iota((rows, lanes), 1)
        turned = lane if adjoint else jnp.where(lane < own, lane, wide_local(lane, own, wide))
        col = global_row(half, turned, cells_y)
        delta = (row - col if adjoint else col - row) + radius
        delta = jnp.where(lane < width, delta, -1)
        band = jnp.zeros((rows, lanes), F32)
        for a in range(taps):
            band = jnp.where(delta == a, ky_ref[index % 2, a], band)
        high, low = split(band)
        high, low = high.astype(F32), low.astype(F32)
        out_ref[index % 2] = (high + pltpu.roll(high, width, 1) + pltpu.roll(low, 2 * width, 1)).astype(BF16)

    lanes = tz_ref.shape[1]
    near_z = jnp.abs(iota((lanes, lanes), 1) - iota((lanes, lanes), 0)) <= radius_z
    for index in range(4):
        base = pltpu.roll(tz_ref[index:index + 1, :], lanes - radius_z, 1)
        band = pltpu.roll(jnp.broadcast_to(base, (lanes, lanes)), 0, 1, stride=1, stride_axis=0)
        zhi_ref[index], zlo_ref[index] = split(jnp.where(near_z, band, jnp.zeros_like(band)))

    rows, lanes = xhi_ref.shape[1] // 2, tx_ref.shape[1]
    for index in range(4):
        base = jnp.broadcast_to(tx_ref[index:index + 1, :], (rows, lanes))
        band = pltpu.roll(base, 0, 1, stride=1, stride_axis=0)[:, :xhi_ref.shape[2]]
        place = (index // 2, slice(index % 2 * rows, index % 2 * rows + rows))
        xhi_ref[place], xlo_ref[place] = split(band)


def make_tables(half, kx, ky, kz, planes, cells_y, cells_z, sizes):
    own, near, wide = sizes
    taps_x, taps_z = kx.shape[1], kz.shape[1]
    depth = 8 * pad_to(planes + taps_x - 1, 16)
    lanes = max(512, 1 << (depth - 1).bit_length())
    zero = jnp.zeros((), F32)
    tx = jnp.concatenate([kx, kx[:, ::-1]])
    tx = lax.pad(tx, zero, ((0, 0, 0), (0, lanes - 8 * taps_x + 7, 7)))
    tz = jnp.concatenate([kz[:, ::-1], kz])
    tz = lax.pad(tz, zero, ((0, 0, 0), (0, cells_z - taps_z, 0)))
    kernel = functools.partial(tables_kernel, sizes=sizes, cells_y=cells_y, radius_z=taps_z // 2)
    shape = jax.ShapeDtypeStruct
    out_shape = (
        shape((2, near, pad_to(3 * wide, 128)), BF16),
        shape((2, own, pad_to(3 * near, 128)), BF16),
        shape((4, cells_z, cells_z), BF16),
        shape((4, cells_z, cells_z), BF16),
        shape((2, 2 * 8 * planes, depth), BF16),
        shape((2, 2 * 8 * planes, depth), BF16),
    )
    return call(kernel, out_shape, [SMEM, SMEM, VMEM, VMEM], "band_matrices")(half.reshape(1), ky, tz, tx)


def window_kernel(half_ref, estimate_ref, own_ref, other_ref):
    cells_y = estimate_ref.shape[1]
    half = half_ref[0]
    groups = own_ref.shape[1] // GROUP
    for side, out_ref in ((half, own_ref), (1 - half, other_ref)):
        for group in range(groups):
            local = wide_group(group, cells_y // 2 // GROUP, groups)
            start = pl.multiple_of(group_row(side, local, cells_y), GROUP)
            out_ref[:, group * GROUP:(group + 1) * GROUP, :] = estimate_ref[:, pl.ds(start, GROUP), :]


def make_windows(half, estimate, wide):
    planes, _, cells_z = estimate.shape
    shape = jax.ShapeDtypeStruct((planes, wide, cells_z), F32)
    return call(window_kernel, (shape, shape), [SMEM, VMEM], "estimate_windows")(half.reshape(1), estimate)


def assemble_kernel(place_ref, window_ref, *refs):
    pieces, (out_ref, lower_ref, upper_ref) = refs[:-3], refs[-3:]
    straight, group = place_ref[0] != 0, place_ref[1]
    planes, radius, share = out_ref.shape[0], lower_ref.shape[0], pieces[0].shape[0]
    for p in range(planes):
        turn = lax.rem(group - p // share + len(pieces), len(pieces))
        value = pieces[0][p % share]
        for k in range(1, len(pieces)):
            value = jnp.where(turn == k, pieces[k][p % share], value)
        value = jnp.where(straight, window_ref[p], value)
        out_ref[p] = value
        if p < radius:
            lower_ref[p] = value
        if p >= planes - radius:
            upper_ref[p - planes + radius] = value


def edge_shapes(shape, radius):
    edge = jax.ShapeDtypeStruct((radius,) + shape[1:], F32)
    return jax.ShapeDtypeStruct(shape, F32), edge, edge


def assemble(place, window, pieces, radius):
    out_shape = edge_shapes(window.shape, radius)
    return call(assemble_kernel, out_shape, [SMEM] + [VMEM] * (1 + len(pieces)), "estimate")(place, window, *pieces)


def shift_kernel(scal_ref, acq_ref, mask_ref, first_ref, second_ref, turned_ref):
    planes, cells_y, cells_z = acq_ref.shape
    near = first_ref.shape[1]
    shift_y, shift_z, core = scal_ref[0], scal_ref[1], scal_ref[2]
    row = iota((cells_y, cells_z), 0) + shift_y
    col = iota((cells_y, cells_z), 1) + shift_z
    inside = (row >= 0) & (row < cells_y) & (col >= 0) & (col < cells_z)
    turn_y = lax.rem(cells_y - shift_y, cells_y)
    turn_z = lax.rem(cells_z - shift_z, cells_z)

    def body(p, carry):
        x = pltpu.roll(pltpu.roll(acq_ref[p], turn_z, 1), turn_y, 0)
        turned_ref[...] = jnp.where(inside, x, jnp.zeros_like(x))
        for side, out_ref in ((core, first_ref), (1 - core, second_ref)):
            for group in range(near // GROUP):
                start = pl.multiple_of(group_row(side, group, cells_y), GROUP)
                out_ref[p, group * GROUP:(group + 1) * GROUP, :] = turned_ref[pl.ds(start, GROUP), :]
        return carry

    lax.fori_loop(0, planes, body, 0)
    mask = mask_ref[...].astype(F32)
    for out_ref in (first_ref, second_ref):
        out_ref[planes] = jnp.zeros((near, cells_z), F32)
        out_ref[planes, :planes, :cells_y] = mask


def shift_and_cut(scal, acquired, mask, near):
    planes, cells_y, cells_z = acquired.shape
    shape = jax.ShapeDtypeStruct((planes + 1, near, cells_z), F32)
    scratch = [pltpu.VMEM((cells_y, cells_z), F32)]
    return call(shift_kernel, (shape, shape), [SMEM, VMEM, VMEM], "shift_recorded", scratch)(scal, acquired, mask)


def spread_x(hi_ref, lo_ref, index, start, count, refs, row):
    low_ref, own_ref, high_ref = refs
    lanes = own_ref.shape[2]
    depth = hi_ref.shape[2]
    parts = [ref[:, pl.ds(row, 8), :] for ref in refs]
    missing = depth // 8 - sum(part.shape[0] for part in parts)
    if missing:
        parts.append(jnp.zeros((missing, 8, lanes), F32))
    high, low = split(jnp.concatenate(parts, axis=0).reshape(depth, lanes))
    band = hi_ref[index, start:start + count, :]
    out = dot(band, high) + (dot(band, low) + dot(lo_ref[index, start:start + count, :], high))
    return out.reshape(count // 8, 8, lanes)


def blur_x_kernel(hi_ref, lo_ref, low_ref, own_ref, high_ref, first_ref, second_ref):
    planes, rows, lanes = own_ref.shape

    def body(step, carry):
        row = pl.multiple_of(step * 8, 8)
        out = spread_x(hi_ref, lo_ref, 0, 0, hi_ref.shape[1], (low_ref, own_ref, high_ref), row)
        first_ref[:, pl.ds(row, 8), :] = out[:planes]
        second_ref[:, pl.ds(row, 8), :] = out[planes:]
        return carry

    lax.fori_loop(0, rows // 8, body, 0)


def blur_x(tables, low, own, high):
    shape = jax.ShapeDtypeStruct(own.shape, F32)
    return call(blur_x_kernel, (shape, shape), [VMEM] * 5, "blur_x")(*tables[4:], low, own, high)


def spread_y(band, x):
    high, low = split(x)
    parts = [high, low, high]
    rest = band.shape[1] - 3 * x.shape[0]
    if rest:
        parts.append(jnp.zeros((rest, x.shape[1]), BF16))
    return dot(band, jnp.concatenate(parts, axis=0))


def spread_z(x, hi_ref, lo_ref, index):
    high, low = split(x)
    return dot(high, hi_ref[index]) + (dot(low, hi_ref[index]) + dot(high, lo_ref[index]))


def ratio_planes(wide_refs, fetch, yf_ref, ya_ref, zhi_ref, zlo_ref, order, outs):
    out_ref, lower_ref, upper_ref = outs
    planes, rows, _ = out_ref.shape
    radius = lower_ref.shape[0]
    near = yf_ref.shape[1]
    step = 4
    for start in range(0, planes, step):
        block = range(start, min(start + step, planes))
        blurred = jnp.concatenate(
            [spread_y(yf_ref[order], jnp.concatenate([ref[p] for ref in wide_refs], axis=0)) for p in block], axis=0
        )
        blurred = spread_z(blurred, zhi_ref, zlo_ref, order)
        image = jnp.concatenate([fetch(p) for p in block], axis=0)
        ratio = jnp.where(image >= 0, image / blurred, jnp.ones_like(image))
        spread = jnp.concatenate(
            [spread_y(ya_ref[order], ratio[k * near:(k + 1) * near]) for k in range(len(block))], axis=0
        )
        spread = spread_z(spread, zhi_ref, zlo_ref, 2 + order)
        for k, p in enumerate(block):
            value = spread[k * rows:(k + 1) * rows]
            out_ref[p] = value
            if p < radius:
                lower_ref[p] = value
            if p >= planes - radius:
                upper_ref[p - planes + radius] = value


def first_ratio_kernel(shift_ref, place_ref, low_ref, own_ref, high_ref, *refs, order, extent_x, cells_y):
    image_ref = refs[-1]
    planes, near, cells_z = image_ref.shape
    slab, half = place_ref[0], place_ref[1]
    shift_x, shift_y, shift_z = (shift_ref[order, i] for i in range(3))
    lanes = pad_to(cells_y, 128)
    pick = iota((near, lanes), 1) == global_row(half, iota((near, lanes), 0), cells_y)
    mask = own_ref[planes, :planes, :lanes].astype(BF16)
    columns = lax.dot_general(
        pick.astype(F32).astype(BF16), mask, (((1,), (1,)), ((), ())), preferred_element_type=F32
    )
    row = global_row(half, iota((near, cells_z), 0), cells_y) + shift_y
    col = iota((near, cells_z), 1) + shift_z
    inside = (row >= 0) & (row < cells_y) & (col >= 0) & (col < cells_z)

    def fetch(p):
        source = p + shift_x
        x = slab * planes + source
        own = own_ref[jnp.clip(source, 0, planes - 1)]
        low = low_ref[jnp.clip(source + planes, 0, planes - 1)]
        high = high_ref[jnp.clip(source - planes, 0, planes - 1)]
        value = jnp.where(source < 0, low, jnp.where(source < planes, own, high))
        weight = jnp.broadcast_to(columns[:, p:p + 1], (near, cells_z))
        covered = inside & (weight > 0.5) & (x >= 0) & (x < extent_x)
        value = jnp.where(covered, value, jnp.full_like(value, -1.0))
        image_ref[p] = value
        return value

    ratio_planes(refs[:-8], fetch, *refs[-8:-4], order, refs[-4:-1])


def next_ratio_kernel(image_ref, *refs, order):
    ratio_planes(refs[:-7], lambda p: image_ref[p], *refs[-7:-3], order, refs[-3:])


def ratio_shapes(wides, tables, radius):
    planes, _, lanes = wides[0].shape
    return edge_shapes((planes, tables[1].shape[1], lanes), radius)


def first_ratio(shifts, place, blocks, wides, tables, order, radius, extent_x, cells_y):
    planes, _, lanes = wides[0].shape
    kernel = functools.partial(first_ratio_kernel, order=order, extent_x=extent_x, cells_y=cells_y)
    image = jax.ShapeDtypeStruct((planes, tables[0].shape[1], lanes), F32)
    out_shape = ratio_shapes(wides, tables, radius) + (image,)
    return call(kernel, out_shape, [SMEM] * 2 + [VMEM] * (7 + len(wides)), "image_and_ratio")(
        shifts, place, *blocks, *wides, *tables[:4]
    )


def next_ratio(image, wides, tables, order, radius):
    kernel = functools.partial(next_ratio_kernel, order=order)
    return call(kernel, ratio_shapes(wides, tables, radius), [VMEM] * (5 + len(wides)), "ratio")(
        image, *wides, *tables[:4]
    )


def factor_kernel(hi_ref, lo_ref, before_ref, low_ref, own_ref, high_ref, out_ref, *, order, start, share):
    planes, rows, _ = out_ref.shape

    def body(step, carry):
        row = pl.multiple_of(step * 8, 8)
        source = pl.multiple_of(start + row, 8)
        total = before_ref[:, pl.ds(source, 8), :]
        if share:
            total = share * jnp.log(total)
        factor = spread_x(hi_ref, lo_ref, 1, order * 8 * planes, 8 * planes, (low_ref, own_ref, high_ref), source)
        out_ref[:, pl.ds(row, 8), :] = total + jnp.log(factor)
        return carry

    lax.fori_loop(0, rows // 8, body, 0)


def log_factor(tables, before, side, order, start, rows, share):
    planes, _, lanes = side[1].shape
    kernel = functools.partial(factor_kernel, order=order, start=start, share=share)
    shape = jax.ShapeDtypeStruct((planes, rows, lanes), F32)
    return call(kernel, shape, [VMEM] * 6, "log_factor")(*tables[4:], before, *side)


def update_kernel(*refs):
    parts, edge_ref, (out_ref, lower_ref, upper_ref) = refs[:-4], refs[-4], refs[-3:]
    planes, radius, rows = out_ref.shape[0], lower_ref.shape[0], parts[0].shape[1]
    for p in range(planes):
        total = parts[0][p]
        for part in parts[1:]:
            total = total + part[p]
        value = jnp.concatenate([jnp.exp(total), edge_ref[p]], axis=0)
        out_ref[p] = value
        if p < radius:
            lower_ref[p] = value
        if p >= planes - radius:
            upper_ref[p - planes + radius] = value


def update(parts, edge, radius):
    planes, rows, lanes = parts[0].shape
    out_shape = edge_shapes((planes, rows + edge.shape[1], lanes), radius)
    return call(update_kernel, out_shape, [VMEM] * (len(parts) + 1), "update")(*parts, edge)


def finish_kernel(half_ref, own_ref, *refs, groups):
    out_ref = refs[-1]
    half = half_ref[0]
    cells_y = out_ref.shape[1]
    own = [own_ref] + list(refs[:groups - 1])
    other = list(refs[groups - 1:2 * groups - 1])
    for side, parts in ((half, own), (1 - half, other)):
        for group in range(own_ref.shape[1] // GROUP):
            rows = slice(group * GROUP, (group + 1) * GROUP)
            total = parts[0][:, rows, :]
            for part in parts[1:]:
                total = total + part[:, rows, :]
            start = pl.multiple_of(group_row(side, group, cells_y), GROUP)
            out_ref[:, pl.ds(start, GROUP), :] = jnp.exp(total)


def finish(half, own, own_parts, other_parts, shape):
    groups = len(own_parts) + 1
    kernel = functools.partial(finish_kernel, groups=groups)
    return call(kernel, jax.ShapeDtypeStruct(shape, F32), [SMEM] + [VMEM] * (2 * groups), "last_update")(
        half.reshape(1), own, *own_parts, *other_parts
    )


def choose_kernel(flag_ref, one_ref, other_ref, out_ref, semaphore):
    def copy(source_ref):
        move = pltpu.make_async_copy(source_ref, out_ref, semaphore)
        move.start()
        move.wait()

    pl.when(flag_ref[0] != 0)(lambda: copy(one_ref))
    pl.when(flag_ref[0] == 0)(lambda: copy(other_ref))


def choose(flag, one, other):
    anywhere = pl.BlockSpec(memory_space=pl.ANY)
    return pl.pallas_call(
        choose_kernel,
        out_shape=jax.ShapeDtypeStruct(one.shape, one.dtype),
        in_specs=[SMEM, anywhere, anywhere],
        out_specs=anywhere,
        scratch_shapes=[pltpu.SemaphoreType.DMA],
        compiler_params=PARAMS,
        name="choose",
    )(flag, one, other)


def shards(acquired, estimate, offsets, view_mask, kern_x, kern_y, kern_z):
    planes, cells_y, cells_z = estimate.shape
    views, slabs = lax.axis_size("view"), lax.axis_size("tile")
    groups = views // 2
    taps_x, taps_y, taps_z = kern_x.shape[1], kern_y.shape[1], kern_z.shape[1]
    radius = taps_x // 2
    own_rows = cells_y // 2
    near = own_rows + pad_to(taps_y // 2, GROUP)
    wide = own_rows + pad_to(2 * (taps_y // 2), GROUP)
    edge_rows = wide - own_rows
    inner_rows = own_rows - edge_rows
    core = lax.rem(lax.axis_index("view"), 2)
    half = lax.rem(lax.axis_index("tile"), 2)
    slab = lax.axis_index("tile") - half + core
    straight = core == half

    group = lax.axis_index("view") // 2
    flag = jnp.stack([straight.astype(jnp.int32), group])

    def across(turn, half_of=lambda r: r, when=lambda c, r: True):
        return lambda g, c, q, r: ((g + turn) % groups, c, q, half_of(r)) if when(c, r) else None

    window, crossing = make_windows(half, estimate, wide)
    piece = lax.dynamic_slice_in_dim(crossing, group * (planes // groups), planes // groups, 0)
    piece = send(piece, across(0, lambda r: 1 - r, lambda c, r: c == r))

    mine = jnp.concatenate([kern_x[0], kern_y[0], kern_z[0], offsets[0].astype(F32)])
    mine, window = lax.optimization_barrier((mine, window))
    other = send(mine, to_core_partner)

    scal = jnp.stack([offsets[0, 1], offsets[0, 2], core])
    acquired, window = lax.optimization_barrier((acquired, window))
    first, second = shift_and_cut(scal, acquired[0], view_mask[0], near)

    pieces = [piece] + [send(piece, across(turn, when=lambda c, r: c != r)) for turn in range(1, groups)]
    first, piece = lax.optimization_barrier((first, piece))
    arrived = send(first, lambda g, c, q, r: (g, r, q, c) if c != r else None)
    current, lower, upper = assemble(flag, window, pieces, radius)
    low, high = send(upper, to_next), send(lower, to_previous)
    arrived, second = lax.optimization_barrier((arrived, second))
    second = send(second, lambda g, c, q, r: (g, r, q, 1 - c))
    first = jnp.where(straight, first, arrived)

    both = jnp.where(straight, jnp.stack([mine, other]), jnp.stack([other, mine]))
    kx = both[:, :taps_x]
    ky = both[:, taps_x:taps_x + taps_y]
    kz = both[:, taps_x + taps_y:taps_x + taps_y + taps_z]
    shifts = both[:, taps_x + taps_y + taps_z:].astype(jnp.int32)
    tables = make_tables(half, kx, ky, kz, planes, cells_y, cells_z, (own_rows, near, wide))

    place = jnp.stack([slab, half])
    blocks = [(send(block, to_next), block, send(block, to_previous)) for block in (first, second)]
    images = [None, None]
    chunks = [(low, current, high)]

    for step in range(ITERS):
        wides = [blur_x(tables, *chunk) for chunk in chunks]
        sides = []
        for order in range(2):
            parts = [chunk[order] for chunk in wides]
            if step == 0:
                spread, lower, upper, images[order] = first_ratio(
                    shifts, place, blocks[order], parts, tables, order, radius, planes * slabs, cells_y
                )
            else:
                spread, lower, upper = next_ratio(images[order], parts, tables, order, radius)
            sides.append((send(upper, to_next), spread, send(lower, to_previous)))
        total = log_factor(tables, current, sides[0], 0, 0, own_rows, 1.0 / groups)
        if step < ITERS - 1:
            edge = log_factor(tables, total, sides[1], 1, inner_rows, edge_rows, 0)
            inner = log_factor(tables, total, sides[1], 1, 0, inner_rows, 0)
            edge_parts = [edge] + [send(edge, across(turn)) for turn in range(1, groups)]
            inner_parts = [inner] + [send(inner, across(turn)) for turn in range(1, groups)]
            edge = jnp.exp(sum(edge_parts[1:], edge_parts[0]))
            beyond = send(edge, to_row_partner)
            current, lower, upper = update(inner_parts, edge, radius)
            chunks = [
                (send(upper, to_next), current, send(lower, to_previous)),
                (send(beyond[planes - radius:], to_next), beyond, send(beyond[:radius], to_previous)),
            ]

    own = log_factor(tables, total, sides[1], 1, 0, own_rows, 0)
    own_parts, other_parts = [], []
    for turn in range(groups):
        other_parts.append(send(own, across(turn, lambda r: 1 - r, lambda c, r: c != r)))
        if turn:
            own_parts.append(send(own, across(turn, when=lambda c, r: c == r)))
    whole = finish(half, own, own_parts, other_parts, estimate.shape)
    copied = send(whole, lambda g, c, q, r: (g, 1 - c, q, r) if c == r else None)
    return choose(flag, whole, copied)


def solution(mesh):
    in_specs = (
        P("view", "tile", None, None),
        P("tile", None, None),
        P("view", None),
        P("view", "tile", None),
        P("view", None),
        P("view", None),
        P("view", None),
    )
    out_specs = P("tile", None, None)
    return jax.shard_map(shards, mesh=mesh, in_specs=in_specs, out_specs=out_specs, check_vma=False)
```

```python
import functools

import jax
import jax.numpy as jnp
from jax import lax
from jax.experimental import pallas as pl
from jax.experimental.pallas import tpu as pltpu
from jax.sharding import PartitionSpec as P

ITERS = 2
AXES = ("view", "tile")
F32 = jnp.float32
BF16 = jnp.bfloat16
VMEM = pl.BlockSpec(memory_space=pltpu.VMEM)
SMEM = pl.BlockSpec(memory_space=pltpu.SMEM)
PARAMS = pltpu.CompilerParams(vmem_limit_bytes=20 * 1024 * 1024)
GROUP = 16


def moves(move):
    views, tiles = lax.axis_size("view"), lax.axis_size("tile")
    pairs = []
    for view in range(views):
        for tile in range(tiles):
            target = move(view // 2, view % 2, tile // 2, tile % 2)
            if target is not None:
                g, c, q, r = target
                pairs.append((view * tiles + tile, (2 * g + c) * tiles + 2 * q + r))
    return pairs


def send(array, move):
    return lax.ppermute(array, AXES, moves(move))


def after(array, other):
    return lax.optimization_barrier((array, other))[0]


def to_far(g, c, q, r):
    s = 2 * q + c + (1 if c else -1)
    return (g, s % 2, s // 2, r) if 0 <= s < lax.axis_size("tile") else None


def to_row_partner(g, c, q, r):
    return (g, c, q, 1 - r)


def to_core_partner(g, c, q, r):
    return (g, 1 - c, q, r)


def core():
    return lax.rem(lax.axis_index("view"), 2)


def half():
    return lax.rem(lax.axis_index("tile"), 2)


def split(x):
    high = x.astype(BF16)
    return high, (x - high.astype(F32)).astype(BF16)


def dot(a, b):
    return jnp.dot(a, b, preferred_element_type=F32)


def iota(shape, dim):
    return lax.broadcasted_iota(jnp.int32, shape, dim)


def group_row(half, group, cells_y):
    return group * GROUP + half * (cells_y - GROUP - 2 * group * GROUP)


def global_row(half, local, cells_y):
    group = local // GROUP
    return group_row(half, group, cells_y) + (local - group * GROUP)


def wide_local(place, own, wide):
    group = (place - own) // GROUP
    return own + (wide - own) - GROUP - group * GROUP + (place - own - group * GROUP)


def wide_group(group, own_groups, groups):
    return group if group < own_groups else own_groups + groups - 1 - group


def pad_to(value, unit):
    return -(-value // unit) * unit


def call(kernel, out_shape, in_specs, name, scratch=()):
    return pl.pallas_call(
        kernel,
        out_shape=out_shape,
        in_specs=in_specs,
        out_specs=jax.tree.map(lambda _: VMEM, out_shape),
        scratch_shapes=list(scratch),
        compiler_params=PARAMS,
        name=name,
    )


def tables_kernel(
    ky_ref, tz_ref, tx_ref, yf_ref, ya_ref, zhi_ref, zlo_ref, xhi_ref, xlo_ref, *, sizes, cells_y, radius_x, radius_z
):
    taps = ky_ref.shape[1]
    radius = taps // 2
    side = half()
    own, near, wide = sizes
    for index in range(4):
        adjoint = index >= 2
        out_ref, rows, width = (ya_ref, own, near) if adjoint else (yf_ref, near, wide)
        lanes = out_ref.shape[2]
        row = global_row(side, iota((rows, lanes), 0), cells_y)
        lane = iota((rows, lanes), 1)
        turned = lane if adjoint else jnp.where(lane < own, lane, wide_local(lane, own, wide))
        col = global_row(side, turned, cells_y)
        delta = (row - col if adjoint else col - row) + radius
        delta = jnp.where(lane < width, delta, -1)
        band = jnp.zeros((rows, lanes), F32)
        for a in range(taps):
            band = jnp.where(delta == a, ky_ref[index % 2, a], band)
        high, low = split(band)
        high, low = high.astype(F32), low.astype(F32)
        out_ref[index % 2] = (high + pltpu.roll(high, width, 1) + pltpu.roll(low, 2 * width, 1)).astype(BF16)

    lanes = tz_ref.shape[1]
    near_z = jnp.abs(iota((lanes, lanes), 1) - iota((lanes, lanes), 0)) <= radius_z
    for index in range(4):
        base = pltpu.roll(tz_ref[index:index + 1, :], lanes - radius_z, 1)
        band = pltpu.roll(jnp.broadcast_to(base, (lanes, lanes)), 0, 1, stride=1, stride_axis=0)
        zhi_ref[index], zlo_ref[index] = split(jnp.where(near_z, band, jnp.zeros_like(band)))

    rows, lanes = xhi_ref.shape[1] // 2, tx_ref.shape[1]
    for index in range(4):
        base = jnp.broadcast_to(tx_ref[index:index + 1, :], (rows, lanes))
        band = pltpu.roll(base, 0, 1, stride=1, stride_axis=0)
        lane = iota((rows, lanes), 1)
        first, last = 8 * radius_x, 8 * radius_x + rows
        turned = jnp.where(
            lane < first, pltpu.roll(band, lanes - last, 1), jnp.where(lane < last, band, pltpu.roll(band, last, 1))
        )
        turned = jnp.where(lane < last + first, turned, jnp.zeros_like(turned))
        band = jnp.where(core() == 0, band, turned)[:, :xhi_ref.shape[2]]
        place = (index // 2, slice(index % 2 * rows, index % 2 * rows + rows))
        xhi_ref[place], xlo_ref[place] = split(band)


def make_tables(kx, ky, kz, planes, cells_y, cells_z, sizes):
    own, near, wide = sizes
    taps_x, taps_z = kx.shape[1], kz.shape[1]
    depth = 8 * pad_to(planes + taps_x - 1, 16)
    lanes = max(512, 1 << (depth - 1).bit_length())
    zero = jnp.zeros((), F32)
    tx = jnp.concatenate([kx, kx[:, ::-1]])
    tx = lax.pad(tx, zero, ((0, 0, 0), (0, lanes - 8 * taps_x + 7, 7)))
    tz = jnp.concatenate([kz[:, ::-1], kz])
    tz = lax.pad(tz, zero, ((0, 0, 0), (0, cells_z - taps_z, 0)))
    kernel = functools.partial(tables_kernel, sizes=sizes, cells_y=cells_y, radius_x=taps_x // 2, radius_z=taps_z // 2)
    shape = jax.ShapeDtypeStruct
    out_shape = (
        shape((2, near, pad_to(3 * wide, 128)), BF16),
        shape((2, own, pad_to(3 * near, 128)), BF16),
        shape((4, cells_z, cells_z), BF16),
        shape((4, cells_z, cells_z), BF16),
        shape((2, 2 * 8 * planes, depth), BF16),
        shape((2, 2 * 8 * planes, depth), BF16),
    )
    return call(kernel, out_shape, [SMEM, VMEM, VMEM], "band_matrices")(ky, tz, tx)


def window_kernel(estimate_ref, own_ref, other_ref):
    cells_y = estimate_ref.shape[1]
    groups = own_ref.shape[1] // GROUP
    for side, out_ref in ((half(), own_ref), (1 - half(), other_ref)):
        for group in range(groups):
            local = wide_group(group, cells_y // 2 // GROUP, groups)
            start = pl.multiple_of(group_row(side, local, cells_y), GROUP)
            out_ref[:, group * GROUP:(group + 1) * GROUP, :] = estimate_ref[:, pl.ds(start, GROUP), :]


def make_windows(estimate, wide):
    planes, _, cells_z = estimate.shape
    shape = jax.ShapeDtypeStruct((planes, wide, cells_z), F32)
    return call(window_kernel, (shape, shape), [VMEM], "estimate_windows")(estimate)


def put_edges(out_ref, far_ref, near_ref):
    radius = far_ref.shape[0]
    beyond = out_ref.shape[0] - radius
    for p in range(radius):
        far_ref[p] = out_ref[p + core() * beyond]
        near_ref[p] = out_ref[p + (1 - core()) * beyond]


def assemble_kernel(window_ref, *refs):
    pieces, (out_ref, far_ref, near_ref) = refs[:-3], refs[-3:]
    straight, group = core() == half(), lax.axis_index("view") // 2
    planes, share = out_ref.shape[0], pieces[0].shape[0]
    for p in range(planes):
        turn = lax.rem(group - p // share + len(pieces), len(pieces))
        value = pieces[0][p % share]
        for k in range(1, len(pieces)):
            value = jnp.where(turn == k, pieces[k][p % share], value)
        out_ref[p] = jnp.where(straight, window_ref[p], value)
    put_edges(out_ref, far_ref, near_ref)


def edge_shapes(shape, radius):
    edge = jax.ShapeDtypeStruct((radius,) + shape[1:], F32)
    return jax.ShapeDtypeStruct(shape, F32), edge, edge


def assemble(window, pieces, radius):
    out_shape = edge_shapes(window.shape, radius)
    return call(assemble_kernel, out_shape, [VMEM] * (1 + len(pieces)), "estimate")(window, *pieces)


def shift_kernel(offsets_ref, acq_ref, mask_ref, first_ref, second_ref, turned_ref):
    planes, cells_y, cells_z = acq_ref.shape
    near = first_ref.shape[1]
    shift_y, shift_z = offsets_ref[0, 1], offsets_ref[0, 2]
    row = iota((cells_y, cells_z), 0) + shift_y
    col = iota((cells_y, cells_z), 1) + shift_z
    inside = (row >= 0) & (row < cells_y) & (col >= 0) & (col < cells_z)
    turn_y = lax.rem(cells_y - shift_y, cells_y)
    turn_z = lax.rem(cells_z - shift_z, cells_z)

    def body(p, carry):
        x = pltpu.roll(pltpu.roll(acq_ref[p], turn_z, 1), turn_y, 0)
        turned_ref[...] = jnp.where(inside, x, jnp.zeros_like(x))
        for side, out_ref in ((core(), first_ref), (1 - core(), second_ref)):
            for group in range(near // GROUP):
                start = pl.multiple_of(group_row(side, group, cells_y), GROUP)
                out_ref[p, group * GROUP:(group + 1) * GROUP, :] = turned_ref[pl.ds(start, GROUP), :]
        return carry

    lax.fori_loop(0, planes, body, 0)
    mask = mask_ref[...].astype(F32)
    for out_ref in (first_ref, second_ref):
        out_ref[planes] = jnp.zeros((near, cells_z), F32)
        out_ref[planes, :planes, :cells_y] = mask


def shift_and_cut(offsets, acquired, mask, near):
    planes, cells_y, cells_z = acquired.shape
    shape = jax.ShapeDtypeStruct((planes + 1, near, cells_z), F32)
    scratch = [pltpu.VMEM((cells_y, cells_z), F32)]
    return call(shift_kernel, (shape, shape), [SMEM, VMEM, VMEM], "shift_recorded", scratch)(offsets, acquired, mask)


def spread_x(hi_ref, lo_ref, index, start, count, refs, row):
    lanes = refs[1].shape[2]
    depth = hi_ref.shape[2]
    parts = [ref[:, pl.ds(row, 8), :] for ref in refs]
    missing = depth // 8 - sum(part.shape[0] for part in parts)
    if missing:
        parts.append(jnp.zeros((missing, 8, lanes), F32))
    high, low = split(jnp.concatenate(parts, axis=0).reshape(depth, lanes))
    band = hi_ref[index, start:start + count, :]
    out = dot(band, high) + (dot(band, low) + dot(lo_ref[index, start:start + count, :], high))
    return out.reshape(count // 8, 8, lanes)


def blur_x_kernel(hi_ref, lo_ref, far_ref, own_ref, near_ref, first_ref, second_ref):
    planes, rows, lanes = own_ref.shape

    def body(step, carry):
        row = pl.multiple_of(step * 8, 8)
        out = spread_x(hi_ref, lo_ref, 0, 0, hi_ref.shape[1], (far_ref, own_ref, near_ref), row)
        first_ref[:, pl.ds(row, 8), :] = out[:planes]
        second_ref[:, pl.ds(row, 8), :] = out[planes:]
        return carry

    lax.fori_loop(0, rows // 8, body, 0)


def blur_x(tables, far, own, near):
    shape = jax.ShapeDtypeStruct(own.shape, F32)
    return call(blur_x_kernel, (shape, shape), [VMEM] * 5, "blur_x")(*tables[4:], far, own, near)


def spread_y(band, x):
    high, low = split(x)
    parts = [high, low, high]
    rest = band.shape[1] - 3 * x.shape[0]
    if rest:
        parts.append(jnp.zeros((rest, x.shape[1]), BF16))
    return dot(band, jnp.concatenate(parts, axis=0))


def spread_z(x, hi_ref, lo_ref, index):
    high, low = split(x)
    return dot(high, hi_ref[index]) + (dot(low, hi_ref[index]) + dot(high, lo_ref[index]))


def ratio_planes(wide_refs, fetch, yf_ref, ya_ref, zhi_ref, zlo_ref, order, outs):
    out_ref, far_ref, near_ref = outs
    planes, rows, _ = out_ref.shape
    near = yf_ref.shape[1]
    step = 4
    for start in range(0, planes, step):
        block = range(start, min(start + step, planes))
        blurred = jnp.concatenate(
            [spread_y(yf_ref[order], jnp.concatenate([ref[p] for ref in wide_refs], axis=0)) for p in block], axis=0
        )
        blurred = spread_z(blurred, zhi_ref, zlo_ref, order)
        image = jnp.concatenate([fetch(p) for p in block], axis=0)
        ratio = jnp.where(image >= 0, image / blurred, jnp.ones_like(image))
        spread = jnp.concatenate(
            [spread_y(ya_ref[order], ratio[k * near:(k + 1) * near]) for k in range(len(block))], axis=0
        )
        spread = spread_z(spread, zhi_ref, zlo_ref, 2 + order)
        for k, p in enumerate(block):
            out_ref[p] = spread[k * rows:(k + 1) * rows]
    put_edges(out_ref, far_ref, near_ref)


def first_ratio_kernel(shift_ref, far_ref, near_ref, own_ref, *refs, order, extent_x, cells_y):
    image_ref = refs[-1]
    planes, near, cells_z = image_ref.shape
    side = half()
    slab = lax.axis_index("tile") - side + core()
    shift_x, shift_y, shift_z = (shift_ref[order, i] for i in range(3))
    lanes = pad_to(cells_y, 128)
    pick = iota((near, lanes), 1) == global_row(side, iota((near, lanes), 0), cells_y)
    mask = own_ref[planes, :planes, :lanes].astype(BF16)
    columns = lax.dot_general(
        pick.astype(F32).astype(BF16), mask, (((1,), (1,)), ((), ())), preferred_element_type=F32
    )
    row = global_row(side, iota((near, cells_z), 0), cells_y) + shift_y
    col = iota((near, cells_z), 1) + shift_z
    inside = (row >= 0) & (row < cells_y) & (col >= 0) & (col < cells_z)

    def fetch(p):
        source = p + shift_x
        x = slab * planes + source
        beyond = jnp.clip(jnp.where(source < 0, source + planes, source - planes), 0, planes - 1)
        is_far = (source < 0) == (core() == 0)
        outer = jnp.where(is_far, far_ref[beyond], near_ref[beyond])
        is_own = (source >= 0) & (source < planes)
        value = jnp.where(is_own, own_ref[jnp.clip(source, 0, planes - 1)], outer)
        weight = jnp.broadcast_to(columns[:, p:p + 1], (near, cells_z))
        covered = inside & (weight > 0.5) & (x >= 0) & (x < extent_x)
        value = jnp.where(covered, value, jnp.full_like(value, -1.0))
        image_ref[p] = value
        return value

    ratio_planes(refs[:-8], fetch, *refs[-8:-4], order, refs[-4:-1])


def next_ratio_kernel(image_ref, *refs, order):
    ratio_planes(refs[:-7], lambda p: image_ref[p], *refs[-7:-3], order, refs[-3:])


def ratio_shapes(wides, tables, radius):
    planes, _, lanes = wides[0].shape
    return edge_shapes((planes, tables[1].shape[1], lanes), radius)


def first_ratio(shifts, blocks, wides, tables, order, radius, extent_x, cells_y):
    planes, _, lanes = wides[0].shape
    kernel = functools.partial(first_ratio_kernel, order=order, extent_x=extent_x, cells_y=cells_y)
    image = jax.ShapeDtypeStruct((planes, tables[0].shape[1], lanes), F32)
    out_shape = ratio_shapes(wides, tables, radius) + (image,)
    return call(kernel, out_shape, [SMEM] + [VMEM] * (7 + len(wides)), "image_and_ratio")(
        shifts, *blocks, *wides, *tables[:4]
    )


def next_ratio(image, wides, tables, order, radius):
    kernel = functools.partial(next_ratio_kernel, order=order)
    return call(kernel, ratio_shapes(wides, tables, radius), [VMEM] * (5 + len(wides)), "ratio")(
        image, *wides, *tables[:4]
    )


def factor_kernel(hi_ref, lo_ref, before_ref, far_ref, own_ref, near_ref, out_ref, *, order, start, share):
    planes, rows, _ = out_ref.shape

    def body(step, carry):
        row = pl.multiple_of(step * 8, 8)
        source = pl.multiple_of(start + row, 8)
        total = before_ref[:, pl.ds(source, 8), :]
        if share:
            total = share * jnp.log(total)
        factor = spread_x(hi_ref, lo_ref, 1, order * 8 * planes, 8 * planes, (far_ref, own_ref, near_ref), source)
        out_ref[:, pl.ds(row, 8), :] = total + jnp.log(factor)
        return carry

    lax.fori_loop(0, rows // 8, body, 0)


def log_factor(tables, before, side, order, start, rows, share):
    planes, _, lanes = side[1].shape
    kernel = functools.partial(factor_kernel, order=order, start=start, share=share)
    shape = jax.ShapeDtypeStruct((planes, rows, lanes), F32)
    return call(kernel, shape, [VMEM] * 6, "log_factor")(*tables[4:], before, *side)


def update_kernel(*refs):
    parts, edge_ref, (out_ref, far_ref, near_ref) = refs[:-4], refs[-4], refs[-3:]
    for p in range(out_ref.shape[0]):
        total = parts[0][p]
        for part in parts[1:]:
            total = total + part[p]
        out_ref[p] = jnp.concatenate([jnp.exp(total), edge_ref[p]], axis=0)
    put_edges(out_ref, far_ref, near_ref)


def update(parts, edge, radius):
    planes, rows, lanes = parts[0].shape
    out_shape = edge_shapes((planes, rows + edge.shape[1], lanes), radius)
    return call(update_kernel, out_shape, [VMEM] * (len(parts) + 1), "update")(*parts, edge)


def finish_kernel(*refs):
    own, other, out_ref = refs[:(len(refs) - 1) // 2], refs[(len(refs) - 1) // 2:-1], refs[-1]
    straight = core() == half()
    side = jnp.where(straight, half(), 1 - half())
    groups = out_ref.shape[1] // GROUP
    for group in range(groups):
        rows = slice(group * GROUP, (group + 1) * GROUP)
        own_total, other_total = own[0][:, rows, :], other[0][:, rows, :]
        for part in own[1:]:
            own_total = own_total + part[:, rows, :]
        for part in other[1:]:
            other_total = other_total + part[:, rows, :]
        start = jnp.where(side == 0, group, groups - 1 - group) * GROUP
        out_ref[:, pl.ds(pl.multiple_of(start, GROUP), GROUP), :] = jnp.exp(jnp.where(straight, own_total, other_total))


def finish(own_parts, other_parts):
    shape = jax.ShapeDtypeStruct(own_parts[0].shape, F32)
    return call(finish_kernel, shape, [VMEM] * (2 * len(own_parts)), "last_update")(*own_parts, *other_parts)


def join_kernel(mine_ref, theirs_ref, out_ref, semaphores):
    rows = mine_ref.shape[1]
    copies = []
    for index, (source_ref, side) in enumerate(((mine_ref, core()), (theirs_ref, 1 - core()))):
        target = out_ref.at[:, pl.ds(pl.multiple_of(side * rows, rows), rows), :]
        copies.append(pltpu.make_async_copy(source_ref, target, semaphores.at[index]))
    for copy in copies:
        copy.start()
    for copy in copies:
        copy.wait()


def join(mine, theirs):
    planes, rows, lanes = mine.shape
    anywhere = pl.BlockSpec(memory_space=pl.ANY)
    return pl.pallas_call(
        join_kernel,
        out_shape=jax.ShapeDtypeStruct((planes, 2 * rows, lanes), F32),
        in_specs=[anywhere, anywhere],
        out_specs=anywhere,
        scratch_shapes=[pltpu.SemaphoreType.DMA((2,))],
        compiler_params=PARAMS,
        name="join_halves",
    )(mine, theirs)


def shards(acquired, estimate, offsets, view_mask, kern_x, kern_y, kern_z):
    planes, cells_y, cells_z = estimate.shape
    views, slabs = lax.axis_size("view"), lax.axis_size("tile")
    groups = views // 2
    taps_x, taps_y, taps_z = kern_x.shape[1], kern_y.shape[1], kern_z.shape[1]
    radius = taps_x // 2
    own_rows = cells_y // 2
    near = own_rows + pad_to(taps_y // 2, GROUP)
    wide = own_rows + pad_to(2 * (taps_y // 2), GROUP)
    edge_rows = wide - own_rows
    inner_rows = own_rows - edge_rows
    group = lax.axis_index("view") // 2
    straight = core() == half()

    def across(turn, half_of=lambda r: r, core_of=lambda c: c, when=lambda c, r: True):
        return lambda g, c, q, r: ((g + turn) % groups, core_of(c), q, half_of(r)) if when(c, r) else None

    def neighbours(far, near):
        return send(far, to_far), send(near, to_core_partner)

    window, crossing = make_windows(estimate, wide)
    piece = lax.dynamic_slice_in_dim(crossing, group * (planes // groups), planes // groups, 0)
    piece = send(piece, across(0, lambda r: 1 - r, when=lambda c, r: c == r))

    acquired = after(acquired, window)
    first, second = shift_and_cut(offsets, acquired[0], view_mask[0], near)
    piece = after(piece, first)
    arrived = send(first, lambda g, c, q, r: (g, r, q, c) if c != r else None)

    mine = jnp.concatenate([kern_x[0], kern_y[0], kern_z[0], offsets[0].astype(F32)])
    mine = after(mine, first)
    other = send(mine, to_core_partner)
    both = jnp.where(straight, jnp.stack([mine, other]), jnp.stack([other, mine]))
    kx = both[:, :taps_x]
    ky = both[:, taps_x:taps_x + taps_y]
    kz = both[:, taps_x + taps_y:taps_x + taps_y + taps_z]
    shifts = both[:, taps_x + taps_y + taps_z:].astype(jnp.int32)
    tables = make_tables(kx, ky, kz, planes, cells_y, cells_z, (own_rows, near, wide))

    pieces = [piece] + [send(piece, across(turn, when=lambda c, r: c != r)) for turn in range(1, groups)]
    current, distant, close = assemble(window, pieces, radius)
    second = after(second, distant)
    distant, close = neighbours(distant, close)
    chunks = [(distant, current, close)]
    second = send(second, lambda g, c, q, r: (g, r, q, 1 - c))
    first = jnp.where(straight, first, arrived)
    blocks = [(*neighbours(first, first), first)]

    blocks.append((*neighbours(second, second), second))
    images = [None, None]

    for step in range(ITERS):
        wides = [blur_x(tables, *chunk) for chunk in chunks]
        sides = []
        for order in range(2):
            parts = [chunk[order] for chunk in wides]
            if step == 0:
                spread, distant, close, images[order] = first_ratio(
                    shifts, blocks[order], parts, tables, order, radius, planes * slabs, cells_y
                )
            else:
                spread, distant, close = next_ratio(images[order], parts, tables, order, radius)
            distant, close = neighbours(distant, close)
            sides.append((distant, spread, close))
        total = log_factor(tables, current, sides[0], 0, 0, own_rows, 1.0 / groups)
        if step < ITERS - 1:
            edge = log_factor(tables, total, sides[1], 1, inner_rows, edge_rows, 0)
            inner = log_factor(tables, total, sides[1], 1, 0, inner_rows, 0)
            edge_parts = [edge] + [send(edge, across(turn)) for turn in range(1, groups)]
            inner_parts = [inner] + [send(inner, across(turn)) for turn in range(1, groups)]
            edge = jnp.exp(sum(edge_parts[1:], edge_parts[0]))
            beyond = send(edge, to_row_partner)
            current, distant, close = update(inner_parts, edge, radius)
            distant, close = neighbours(distant, close)
            chunks = [(distant, current, close)]
            rest = planes - radius
            distant, close = neighbours(
                lax.dynamic_slice_in_dim(beyond, core() * rest, radius, 0),
                lax.dynamic_slice_in_dim(beyond, (1 - core()) * rest, radius, 0),
            )
            chunks.append((distant, beyond, close))

    own = log_factor(tables, total, sides[1], 1, 0, own_rows, 0)
    other_parts = [
        send(own, across(turn, lambda r: 1 - r, lambda c: 1 - c, lambda c, r: c != r)) for turn in reversed(range(groups))
    ]
    own_parts = [own] + [send(own, across(turn, when=lambda c, r: c == r)) for turn in range(1, groups)]
    mine = finish(own_parts, other_parts)
    return join(mine, send(mine, to_core_partner))


def solution(mesh):
    in_specs = (
        P("view", "tile", None, None),
        P("tile", None, None),
        P("view", None),
        P("view", "tile", None),
        P("view", None),
        P("view", None),
        P("view", None),
    )
    out_specs = P("tile", None, None)
    return jax.shard_map(shards, mesh=mesh, in_specs=in_specs, out_specs=out_specs, check_vma=False)
```

```python
import functools

import jax
import jax.numpy as jnp
from jax import lax
from jax.experimental import pallas as pl
from jax.experimental.pallas import tpu as pltpu
from jax.sharding import PartitionSpec as P

ITERS = 2
AXES = ("view", "tile")
F32 = jnp.float32
BF16 = jnp.bfloat16
VMEM = pl.BlockSpec(memory_space=pltpu.VMEM)
SMEM = pl.BlockSpec(memory_space=pltpu.SMEM)
PARAMS = pltpu.CompilerParams(vmem_limit_bytes=12 * 1024 * 1024)
GROUP = 16


def moves(move):
    views, tiles = lax.axis_size("view"), lax.axis_size("tile")
    pairs = []
    for view in range(views):
        for tile in range(tiles):
            target = move(view // 2, view % 2, tile // 2, tile % 2)
            if target is not None:
                g, c, q, r = target
                pairs.append((view * tiles + tile, (2 * g + c) * tiles + 2 * q + r))
    return pairs


def send(array, move):
    return lax.ppermute(array, AXES, moves(move))


def after(array, other):
    return lax.optimization_barrier((array, other))[0]


def to_far(g, c, q, r):
    s = 2 * q + c + (1 if c else -1)
    return (g, s % 2, s // 2, r) if 0 <= s < lax.axis_size("tile") else None


def to_row_partner(g, c, q, r):
    return (g, c, q, 1 - r)


def to_core_partner(g, c, q, r):
    return (g, 1 - c, q, r)


def core():
    return lax.rem(lax.axis_index("view"), 2)


def half():
    return lax.rem(lax.axis_index("tile"), 2)


def split(x):
    high = x.astype(BF16)
    return high, (x - high.astype(F32)).astype(BF16)


def dot(a, b):
    return jnp.dot(a, b, preferred_element_type=F32)


def iota(shape, dim):
    return lax.broadcasted_iota(jnp.int32, shape, dim)


def group_row(half, group, cells_y):
    return group * GROUP + half * (cells_y - GROUP - 2 * group * GROUP)


def global_row(half, local, cells_y):
    group = local // GROUP
    return group_row(half, group, cells_y) + (local - group * GROUP)


def wide_local(place, own, wide):
    group = (place - own) // GROUP
    return own + (wide - own) - GROUP - group * GROUP + (place - own - group * GROUP)


def wide_group(group, own_groups, groups):
    return group if group < own_groups else own_groups + groups - 1 - group


def pad_to(value, unit):
    return -(-value // unit) * unit


def call(kernel, out_shape, in_specs, name, scratch=()):
    return pl.pallas_call(
        kernel,
        out_shape=out_shape,
        in_specs=in_specs,
        out_specs=jax.tree.map(lambda _: VMEM, out_shape),
        scratch_shapes=list(scratch),
        compiler_params=PARAMS,
        name=name,
    )


def tables_kernel(
    ky_ref, tz_ref, tx_ref, yf_ref, ya_ref, zhi_ref, zlo_ref, xhi_ref, xlo_ref, *, sizes, cells_y, radius_x, radius_z
):
    taps = ky_ref.shape[1]
    radius = taps // 2
    side = half()
    own, near, wide = sizes
    for index in range(4):
        adjoint = index >= 2
        out_ref, rows, width = (ya_ref, own, near) if adjoint else (yf_ref, near, wide)
        lanes = out_ref.shape[2]
        row = global_row(side, iota((rows, lanes), 0), cells_y)
        lane = iota((rows, lanes), 1)
        turned = lane if adjoint else jnp.where(lane < own, lane, wide_local(lane, own, wide))
        col = global_row(side, turned, cells_y)
        delta = (row - col if adjoint else col - row) + radius
        delta = jnp.where(lane < width, delta, -1)
        band = jnp.zeros((rows, lanes), F32)
        for a in range(taps):
            band = jnp.where(delta == a, ky_ref[index % 2, a], band)
        high, low = split(band)
        high, low = high.astype(F32), low.astype(F32)
        out_ref[index % 2] = (high + pltpu.roll(high, width, 1) + pltpu.roll(low, 2 * width, 1)).astype(BF16)

    lanes = tz_ref.shape[1]
    near_z = jnp.abs(iota((lanes, lanes), 1) - iota((lanes, lanes), 0)) <= radius_z
    for index in range(4):
        base = pltpu.roll(tz_ref[index:index + 1, :], lanes - radius_z, 1)
        band = pltpu.roll(jnp.broadcast_to(base, (lanes, lanes)), 0, 1, stride=1, stride_axis=0)
        zhi_ref[index], zlo_ref[index] = split(jnp.where(near_z, band, jnp.zeros_like(band)))

    rows, lanes = xhi_ref.shape[1] // 2, tx_ref.shape[1]
    for index in range(4):
        base = jnp.broadcast_to(tx_ref[index:index + 1, :], (rows, lanes))
        band = pltpu.roll(base, 0, 1, stride=1, stride_axis=0)
        lane = iota((rows, lanes), 1)
        edge = 8 * radius_x
        far = pad_to(rows + edge, 128)
        next_near = pltpu.roll(band, lanes - edge, 1)
        next_far = pltpu.roll(band, far - rows - edge, 1)
        near_part = jnp.where((lane < rows) | (core() == 0), next_near, pltpu.roll(band, rows, 1))
        far_part = jnp.where(core() == 0, pltpu.roll(band, far, 1), next_far)
        zero = jnp.zeros_like(band)
        band = jnp.where(
            lane < rows + edge, near_part, jnp.where((lane >= far) & (lane < far + edge), far_part, zero)
        )[:, :xhi_ref.shape[2]]
        place = (index // 2, slice(index % 2 * rows, index % 2 * rows + rows))
        xhi_ref[place], xlo_ref[place] = split(band)


def make_tables(kx, ky, kz, planes, cells_y, cells_z, sizes):
    own, near, wide = sizes
    taps_x, taps_z = kx.shape[1], kz.shape[1]
    depth = pad_to(8 * (planes + taps_x // 2), 128) + pad_to(8 * (taps_x // 2), 128)
    lanes = max(512, 1 << (depth - 1).bit_length())
    zero = jnp.zeros((), F32)
    tx = jnp.concatenate([kx, kx[:, ::-1]])
    tx = lax.pad(tx, zero, ((0, 0, 0), (0, lanes - 8 * taps_x + 7, 7)))
    tz = jnp.concatenate([kz[:, ::-1], kz])
    tz = lax.pad(tz, zero, ((0, 0, 0), (0, cells_z - taps_z, 0)))
    kernel = functools.partial(tables_kernel, sizes=sizes, cells_y=cells_y, radius_x=taps_x // 2, radius_z=taps_z // 2)
    shape = jax.ShapeDtypeStruct
    out_shape = (
        shape((2, near, pad_to(3 * wide, 128)), BF16),
        shape((2, own, pad_to(3 * near, 128)), BF16),
        shape((4, cells_z, cells_z), BF16),
        shape((4, cells_z, cells_z), BF16),
        shape((2, 2 * 8 * planes, depth), BF16),
        shape((2, 2 * 8 * planes, depth), BF16),
    )
    return call(kernel, out_shape, [SMEM, VMEM, VMEM], "band_matrices")(ky, tz, tx)


def window_kernel(estimate_ref, own_ref, other_ref):
    cells_y = estimate_ref.shape[1]
    groups = own_ref.shape[1] // GROUP
    for side, out_ref in ((half(), own_ref), (1 - half(), other_ref)):
        for group in range(groups):
            local = wide_group(group, cells_y // 2 // GROUP, groups)
            start = pl.multiple_of(group_row(side, local, cells_y), GROUP)
            out_ref[:, group * GROUP:(group + 1) * GROUP, :] = estimate_ref[:, pl.ds(start, GROUP), :]


def make_windows(estimate, wide):
    planes, _, cells_z = estimate.shape
    shape = jax.ShapeDtypeStruct((planes, wide, cells_z), F32)
    return call(window_kernel, (shape, shape), [VMEM], "estimate_windows")(estimate)


def put_edges(out_ref, edge_refs):
    start = 0
    for far_ref, near_ref in zip(edge_refs[::2], edge_refs[1::2]):
        radius, rows = far_ref.shape[0], slice(start, start + far_ref.shape[1])
        beyond = out_ref.shape[0] - radius
        for p in range(radius):
            far_ref[p] = out_ref[p + core() * beyond, rows]
            near_ref[p] = out_ref[p + (1 - core()) * beyond, rows]
        start += far_ref.shape[1]


def assemble_kernel(*refs, count):
    pieces, window, out_ref, edge_refs = refs[:count], refs[count:-1], refs[-1], ()
    if len(refs) > count + 1:
        window, out_ref, edge_refs = refs[count], refs[count + 1], refs[count + 2:]
    straight, group = core() == half(), lax.axis_index("view") // 2
    planes, share = out_ref.shape[0], pieces[0].shape[0]
    for p in range(planes):
        turn = lax.rem(group - p // share + count, count)
        value = pieces[0][p % share]
        for k in range(1, count):
            value = jnp.where(turn == k, pieces[k][p % share], value)
        out_ref[p] = jnp.where(straight, window[p], value) if edge_refs else value
    put_edges(out_ref, edge_refs)


def edge_shapes(shape, radius, chunks):
    planes, _, lanes = shape
    edges = [jax.ShapeDtypeStruct((radius, rows, lanes), F32) for rows in chunks for _ in range(2)]
    return (jax.ShapeDtypeStruct(shape, F32), *edges)


def assemble(window, pieces, radius):
    out_shape = edge_shapes(window.shape, radius, window.shape[1:2])
    kernel = functools.partial(assemble_kernel, count=len(pieces))
    return call(kernel, out_shape, [VMEM] * (1 + len(pieces)), "estimate")(*pieces, window)


def assemble_far(pieces):
    share, rows, lanes = pieces[0].shape
    shape = jax.ShapeDtypeStruct((share * len(pieces), rows, lanes), F32)
    kernel = functools.partial(assemble_kernel, count=len(pieces))
    return call(kernel, (shape,), [VMEM] * len(pieces), "far_slab")(*pieces)[0]


def shift_kernel(offsets_ref, acq_ref, mask_ref, first_ref, second_ref, turned_ref):
    planes, cells_y, cells_z = acq_ref.shape
    near = first_ref.shape[1]
    shift_y, shift_z = offsets_ref[0, 1], offsets_ref[0, 2]
    row = iota((cells_y, cells_z), 0) + shift_y
    col = iota((cells_y, cells_z), 1) + shift_z
    inside = (row >= 0) & (row < cells_y) & (col >= 0) & (col < cells_z)
    turn_y = lax.rem(cells_y - shift_y, cells_y)
    turn_z = lax.rem(cells_z - shift_z, cells_z)

    def body(p, carry):
        x = pltpu.roll(pltpu.roll(acq_ref[p], turn_z, 1), turn_y, 0)
        turned_ref[...] = jnp.where(inside, x, jnp.zeros_like(x))
        for side, out_ref in ((core(), first_ref), (1 - core(), second_ref)):
            for group in range(near // GROUP):
                start = pl.multiple_of(group_row(side, group, cells_y), GROUP)
                out_ref[p, group * GROUP:(group + 1) * GROUP, :] = turned_ref[pl.ds(start, GROUP), :]
        return carry

    lax.fori_loop(0, planes, body, 0)
    mask = mask_ref[...].astype(F32)
    for out_ref in (first_ref, second_ref):
        out_ref[planes] = jnp.zeros((near, cells_z), F32)
        out_ref[planes, :planes, :cells_y] = mask


def shift_and_cut(offsets, acquired, mask, near):
    planes, cells_y, cells_z = acquired.shape
    shape = jax.ShapeDtypeStruct((planes + 1, near, cells_z), F32)
    scratch = [pltpu.VMEM((cells_y, cells_z), F32)]
    return call(shift_kernel, (shape, shape), [SMEM, VMEM, VMEM], "shift_recorded", scratch)(offsets, acquired, mask)


def gather(ref, row, radius=None):
    if radius is None or ref.shape[0] == radius:
        return ref[:, pl.ds(row, 8), :]
    return ref[pl.ds((1 - core()) * (ref.shape[0] - radius), radius), pl.ds(row, 8), :]


def spread_x(hi_ref, lo_ref, index, band_rows, band_lanes, blocks):
    lanes = blocks[0][0].shape[2]
    filled = []
    for parts in blocks:
        count = 8 * sum(part.shape[0] for part in parts)
        missing = (pad_to(count, 128) - count) // 8
        filled += list(parts) + ([jnp.zeros((missing, 8, lanes), F32)] if missing else [])
    high, low = split(jnp.concatenate(filled, axis=0).reshape(-1, lanes))
    band = hi_ref[index, band_rows, band_lanes]
    out = dot(band, high) + (dot(band, low) + dot(lo_ref[index, band_rows, band_lanes], high))
    return out.reshape(-1, 8, lanes)


def near_lanes(planes, radius):
    return pad_to(8 * (planes + radius), 128)


def blur_near_kernel(hi_ref, lo_ref, own_ref, near_ref, first_ref, second_ref):
    planes, rows, _ = own_ref.shape
    lanes = slice(0, near_lanes(planes, near_ref.shape[0]))

    def body(step, carry):
        row = pl.multiple_of(step * 8, 8)
        block = [gather(own_ref, row), gather(near_ref, row)]
        out = spread_x(hi_ref, lo_ref, 0, slice(None), lanes, [block])
        first_ref[:, pl.ds(row, 8), :] = out[:planes]
        second_ref[:, pl.ds(row, 8), :] = out[planes:]
        return carry

    lax.fori_loop(0, rows // 8, body, 0)


def blur_far_kernel(hi_ref, lo_ref, far_ref, first_ref, second_ref, first_out, second_out, *, radius):
    planes, rows, _ = first_ref.shape
    lanes = slice(near_lanes(planes, radius), None)

    def body(step, carry):
        row = pl.multiple_of(step * 8, 8)
        place = (slice(None), pl.ds(row, 8), slice(None))
        out = spread_x(hi_ref, lo_ref, 0, slice(None), lanes, [[gather(far_ref, row, radius)]])
        first_out[place] = first_ref[place] + out[:planes]
        second_out[place] = second_ref[place] + out[planes:]
        return carry

    lax.fori_loop(0, rows // 8, body, 0)


def blur_x(tables, far, own, near):
    shape = jax.ShapeDtypeStruct(own.shape, F32)
    shapes = (shape, shape)
    parts = call(blur_near_kernel, shapes, [VMEM] * 4, "blur_x_near")(*tables[4:], own, near)
    kernel = functools.partial(blur_far_kernel, radius=near.shape[0])
    return call(kernel, shapes, [VMEM] * 5, "blur_x_far")(*tables[4:], far, *parts)


def spread_y(band, x):
    high, low = split(x)
    parts = [high, low, high]
    rest = band.shape[1] - 3 * x.shape[0]
    if rest:
        parts.append(jnp.zeros((rest, x.shape[1]), BF16))
    return dot(band, jnp.concatenate(parts, axis=0))


def spread_z(x, hi_ref, lo_ref, index):
    high, low = split(x)
    return dot(high, hi_ref[index]) + (dot(low, hi_ref[index]) + dot(high, lo_ref[index]))


def ratio_planes(wide_refs, fetch, yf_ref, ya_ref, zhi_ref, zlo_ref, order, outs):
    out_ref, edge_refs = outs[0], outs[1:]
    planes, rows, _ = out_ref.shape
    near = yf_ref.shape[1]
    step = 4
    for start in range(0, planes, step):
        block = range(start, min(start + step, planes))
        blurred = jnp.concatenate(
            [spread_y(yf_ref[order], jnp.concatenate([ref[p] for ref in wide_refs], axis=0)) for p in block], axis=0
        )
        blurred = spread_z(blurred, zhi_ref, zlo_ref, order)
        image = jnp.concatenate([fetch(p) for p in block], axis=0)
        ratio = jnp.where(image >= 0, image / blurred, jnp.ones_like(image))
        spread = jnp.concatenate(
            [spread_y(ya_ref[order], ratio[k * near:(k + 1) * near]) for k in range(len(block))], axis=0
        )
        spread = spread_z(spread, zhi_ref, zlo_ref, 2 + order)
        for k, p in enumerate(block):
            out_ref[p] = spread[k * rows:(k + 1) * rows]
    put_edges(out_ref, edge_refs)


def first_ratio_kernel(shift_ref, far_ref, near_ref, own_ref, *refs, order, wides, extent_x, cells_y):
    image_ref = refs[-1]
    planes, near, cells_z = image_ref.shape
    side = half()
    slab = lax.axis_index("tile") - side + core()
    shift_x, shift_y, shift_z = (shift_ref[order, i] for i in range(3))
    lanes = pad_to(cells_y, 128)
    pick = iota((near, lanes), 1) == global_row(side, iota((near, lanes), 0), cells_y)
    mask = own_ref[planes, :planes, :lanes].astype(BF16)
    columns = lax.dot_general(
        pick.astype(F32).astype(BF16), mask, (((1,), (1,)), ((), ())), preferred_element_type=F32
    )
    row = global_row(side, iota((near, cells_z), 0), cells_y) + shift_y
    col = iota((near, cells_z), 1) + shift_z
    inside = (row >= 0) & (row < cells_y) & (col >= 0) & (col < cells_z)

    def fetch(p):
        source = p + shift_x
        x = slab * planes + source
        beyond = jnp.clip(jnp.where(source < 0, source + planes, source - planes), 0, planes - 1)
        is_far = (source < 0) == (core() == 0)
        outer = jnp.where(is_far, far_ref[beyond], near_ref[beyond])
        is_own = (source >= 0) & (source < planes)
        value = jnp.where(is_own, own_ref[jnp.clip(source, 0, planes - 1)], outer)
        weight = jnp.broadcast_to(columns[:, p:p + 1], (near, cells_z))
        covered = inside & (weight > 0.5) & (x >= 0) & (x < extent_x)
        value = jnp.where(covered, value, jnp.full_like(value, -1.0))
        image_ref[p] = value
        return value

    ratio_planes(refs[:wides], fetch, *refs[wides:wides + 4], order, refs[wides + 4:-1])


def next_ratio_kernel(image_ref, *refs, order, wides):
    ratio_planes(refs[:wides], lambda p: image_ref[p], *refs[wides:wides + 4], order, refs[wides + 4:])


def ratio_shapes(wides, tables, radius, chunks):
    planes, _, lanes = wides[0].shape
    return edge_shapes((planes, tables[1].shape[1], lanes), radius, chunks)


def first_ratio(shifts, blocks, wides, tables, order, radius, chunks, extent_x, cells_y):
    planes, _, lanes = wides[0].shape
    kernel = functools.partial(
        first_ratio_kernel, order=order, wides=len(wides), extent_x=extent_x, cells_y=cells_y
    )
    image = jax.ShapeDtypeStruct((planes, tables[0].shape[1], lanes), F32)
    out_shape = ratio_shapes(wides, tables, radius, chunks) + (image,)
    return call(kernel, out_shape, [SMEM] + [VMEM] * (7 + len(wides)), "image_and_ratio")(
        shifts, *blocks, *wides, *tables[:4]
    )


def next_ratio(image, wides, tables, order, radius, chunks):
    kernel = functools.partial(next_ratio_kernel, order=order, wides=len(wides))
    return call(kernel, ratio_shapes(wides, tables, radius, chunks), [VMEM] * (5 + len(wides)), "ratio")(
        image, *wides, *tables[:4]
    )


def factor_kernel(hi_ref, lo_ref, before_ref, far_ref, own_ref, near_ref, out_ref, *, order, start, share):
    planes, rows, _ = out_ref.shape
    band_rows = slice(order * 8 * planes, (order + 1) * 8 * planes)

    def body(step, carry):
        row = pl.multiple_of(step * 8, 8)
        source = pl.multiple_of(start + row, 8)
        if share:
            total = share * jnp.log(before_ref[:, pl.ds(source, 8), :])
        else:
            total = before_ref[:, pl.ds(row, 8), :]
        blocks = [[gather(own_ref, source), gather(near_ref, row)], [gather(far_ref, row)]]
        factor = spread_x(hi_ref, lo_ref, 1, band_rows, slice(None), blocks)
        out_ref[:, pl.ds(row, 8), :] = total + jnp.log(factor)
        return carry

    lax.fori_loop(0, rows // 8, body, 0)


def log_factor(tables, before, side, order, start, share):
    far, own, near = side
    kernel = functools.partial(factor_kernel, order=order, start=start, share=share)
    shape = jax.ShapeDtypeStruct((own.shape[0],) + far.shape[1:], F32)
    return call(kernel, shape, [VMEM] * 6, "log_factor")(*tables[4:], before, far, own, near)


def update_kernel(*refs):
    parts, edge_ref, out_ref, edge_refs = refs[:-4], refs[-4], refs[-3], refs[-2:]
    for p in range(out_ref.shape[0]):
        total = parts[0][p]
        for part in parts[1:]:
            total = total + part[p]
        out_ref[p] = jnp.concatenate([jnp.exp(total), edge_ref[p]], axis=0)
    put_edges(out_ref, edge_refs)


def update(parts, edge, radius):
    planes, rows, lanes = parts[0].shape
    rows += edge.shape[1]
    out_shape = edge_shapes((planes, rows, lanes), radius, [rows])
    return call(update_kernel, out_shape, [VMEM] * (len(parts) + 1), "update")(*parts, edge)


def finish_kernel(*refs):
    own, other, out_ref = refs[:(len(refs) - 1) // 2], refs[(len(refs) - 1) // 2:-1], refs[-1]
    straight = core() == half()
    groups = out_ref.shape[1] // GROUP
    for group in range(groups):
        rows = slice(group * GROUP, (group + 1) * GROUP)
        own_total, other_total = own[0][:, rows, :], other[0][:, rows, :]
        for part in own[1:]:
            own_total = own_total + part[:, rows, :]
        for part in other[1:]:
            other_total = other_total + part[:, rows, :]
        start = jnp.where(core() == 0, group, groups - 1 - group) * GROUP
        out_ref[:, pl.ds(pl.multiple_of(start, GROUP), GROUP), :] = jnp.exp(jnp.where(straight, own_total, other_total))


def finish(own_parts, other_parts):
    shape = jax.ShapeDtypeStruct(own_parts[0].shape, F32)
    return call(finish_kernel, shape, [VMEM] * (2 * len(own_parts)), "last_update")(*own_parts, *other_parts)


def join_kernel(*refs, starts):
    sources, out_ref, semaphores = refs[:-2], refs[-2], refs[-1]
    cells_y = out_ref.shape[1]
    copies = []
    for index, source_ref in enumerate(sources):
        rows, start = source_ref.shape[1], starts[index // 2]
        side = core() if index % 2 == 0 else 1 - core()
        place = pl.multiple_of(jnp.where(side == 0, start, cells_y - start - rows), GROUP)
        target = out_ref.at[:, pl.ds(place, rows), :]
        copies.append(pltpu.make_async_copy(source_ref, target, semaphores.at[index]))
    for copy in copies:
        copy.start()
    for copy in copies:
        copy.wait()


def join(pieces, starts, shape):
    anywhere = pl.BlockSpec(memory_space=pl.ANY)
    return pl.pallas_call(
        functools.partial(join_kernel, starts=starts),
        out_shape=jax.ShapeDtypeStruct(shape, F32),
        in_specs=[anywhere] * len(pieces),
        out_specs=anywhere,
        scratch_shapes=[pltpu.SemaphoreType.DMA((len(pieces),))],
        compiler_params=PARAMS,
        name="join_halves",
    )(*pieces)


def shards(acquired, estimate, offsets, view_mask, kern_x, kern_y, kern_z):
    planes, cells_y, cells_z = estimate.shape
    views, slabs = lax.axis_size("view"), lax.axis_size("tile")
    groups = views // 2
    taps_x, taps_y, taps_z = kern_x.shape[1], kern_y.shape[1], kern_z.shape[1]
    radius = taps_x // 2
    own_rows = cells_y // 2
    near = own_rows + pad_to(taps_y // 2, GROUP)
    wide = own_rows + pad_to(2 * (taps_y // 2), GROUP)
    edge_rows = wide - own_rows
    inner_rows = own_rows - edge_rows
    group = lax.axis_index("view") // 2
    straight = core() == half()

    def across(turn, half_of=lambda r: r, core_of=lambda c: c, when=lambda c, r: True):
        return lambda g, c, q, r: ((g + turn) % groups, core_of(c), q, half_of(r)) if when(c, r) else None

    def neighbours(far, near):
        return send(far, to_far), send(near, to_core_partner)

    window, crossing = make_windows(estimate, wide)
    piece = lax.dynamic_slice_in_dim(crossing, group * (planes // groups), planes // groups, 0)
    piece = send(piece, across(0, lambda r: 1 - r, when=lambda c, r: c == r))

    acquired = after(acquired, window)
    first, second = shift_and_cut(offsets, acquired[0], view_mask[0], near)
    piece = after(piece, first)
    arrived = send(first, lambda g, c, q, r: (g, r, q, c) if c != r else None)

    mine = jnp.concatenate([kern_x[0], kern_y[0], kern_z[0], offsets[0].astype(F32)])
    mine = after(mine, first)
    other = send(mine, to_core_partner)
    both = jnp.where(straight, jnp.stack([mine, other]), jnp.stack([other, mine]))
    kx = both[:, :taps_x]
    ky = both[:, taps_x:taps_x + taps_y]
    kz = both[:, taps_x + taps_y:taps_x + taps_y + taps_z]
    shifts = both[:, taps_x + taps_y + taps_z:].astype(jnp.int32)
    tables = make_tables(kx, ky, kz, planes, cells_y, cells_z, (own_rows, near, wide))

    start = group * (planes // groups)
    share = jnp.where(straight, lax.dynamic_slice_in_dim(window, start, planes // groups, 0), piece)
    share = send(share, to_far)
    pieces = [piece] + [send(piece, across(turn, when=lambda c, r: c != r)) for turn in range(1, groups)]
    current, _, close = assemble(window, pieces, radius)
    second = after(second, current)
    second = send(second, lambda g, c, q, r: (g, r, q, 1 - c))
    distant = assemble_far([share] + [send(share, across(turn)) for turn in range(1, groups)])
    chunks = [(distant, current, send(close, to_core_partner))]
    first = jnp.where(straight, first, arrived)
    blocks = [(*neighbours(block, block), block) for block in (first, second)]
    images = [None, None]

    row_chunks = [(0, inner_rows), (inner_rows, edge_rows)]
    sizes = [size for _, size in row_chunks]

    for step in range(ITERS):
        last = step == ITERS - 1
        wides = [blur_x(tables, *chunk) for chunk in chunks]
        spreads, edges = [], []
        for order in range(2):
            parts = [chunk[order] for chunk in wides]
            if step == 0:
                spread, *edge, images[order] = first_ratio(
                    shifts, blocks[order], parts, tables, order, radius, sizes, planes * slabs, cells_y
                )
            else:
                spread, *edge = next_ratio(images[order], parts, tables, order, radius, sizes)
            spreads.append(spread)
            edges.append(edge)

        totals = [None, None]
        hook = None
        for index in (1, 0):
            total = current
            for order in range(2):
                distant, close = edges[order][2 * index:2 * index + 2]
                if hook is not None:
                    distant, close = after(distant, hook), after(close, hook)
                distant, close = neighbours(distant, close)
                side = (distant, spreads[order], close)
                total = log_factor(tables, total, side, order, row_chunks[index][0], 0 if order else 1.0 / groups)
                if index == 1 and order == 0:
                    first_total = total
            hook = first_total
            totals[index] = total

        if not last:
            inner, edge = totals
            edge_parts = [edge] + [send(edge, across(turn)) for turn in range(1, groups)]
            inner_parts = [inner] + [send(inner, across(turn)) for turn in range(1, groups)]
            edge = jnp.exp(sum(edge_parts[1:], edge_parts[0]))
            beyond = send(edge, to_row_partner)
            current, distant, close = update(inner_parts, edge, radius)
            distant, close = neighbours(distant, close)
            chunks = [(distant, current, close)]
            rest = planes - radius
            distant, close = neighbours(
                lax.dynamic_slice_in_dim(beyond, core() * rest, radius, 0),
                lax.dynamic_slice_in_dim(beyond, (1 - core()) * rest, radius, 0),
            )
            chunks.append((distant, beyond, close))

    pieces = []
    for index in (1, 0):
        own = totals[index]
        other_parts = [
            send(own, across(turn, lambda r: 1 - r, lambda c: 1 - c, lambda c, r: c != r))
            for turn in reversed(range(groups))
        ]
        own_parts = [own] + [send(own, across(turn, when=lambda c, r: c == r)) for turn in range(1, groups)]
        mine = finish(own_parts, other_parts)
        pieces += [mine, send(mine, to_core_partner)]
    return join(pieces, [row_chunks[1][0], row_chunks[0][0]], estimate.shape)


def solution(mesh):
    in_specs = (
        P("view", "tile", None, None),
        P("tile", None, None),
        P("view", None),
        P("view", "tile", None),
        P("view", None),
        P("view", None),
        P("view", None),
    )
    out_specs = P("tile", None, None)
    return jax.shard_map(shards, mesh=mesh, in_specs=in_specs, out_specs=out_specs, check_vma=False)
```

```python
import functools

import jax
import jax.numpy as jnp
from jax import lax
from jax.experimental import pallas as pl
from jax.experimental.pallas import tpu as pltpu
from jax.sharding import PartitionSpec as P

ITERS = 2
AXES = ("view", "tile")
F32 = jnp.float32
BF16 = jnp.bfloat16
VMEM = pl.BlockSpec(memory_space=pltpu.VMEM)
SMEM = pl.BlockSpec(memory_space=pltpu.SMEM)
PARAMS = pltpu.CompilerParams(vmem_limit_bytes=12 * 1024 * 1024)
GROUP = 16


def moves(move):
    views, tiles = lax.axis_size("view"), lax.axis_size("tile")
    pairs = []
    for view in range(views):
        for tile in range(tiles):
            target = move(view // 2, view % 2, tile // 2, tile % 2)
            if target is not None:
                g, c, q, r = target
                pairs.append((view * tiles + tile, (2 * g + c) * tiles + 2 * q + r))
    return pairs


def send(array, move):
    return lax.ppermute(array, AXES, moves(move))


def after(array, other):
    return lax.optimization_barrier((array, other))[0]


def to_far(g, c, q, r):
    s = 2 * q + c + (1 if c else -1)
    return (g, s % 2, s // 2, r) if 0 <= s < lax.axis_size("tile") else None


def to_row_partner(g, c, q, r):
    return (g, c, q, 1 - r)


def to_core_partner(g, c, q, r):
    return (g, 1 - c, q, r)


def core():
    return lax.rem(lax.axis_index("view"), 2)


def half():
    return lax.rem(lax.axis_index("tile"), 2)


def split(x):
    high = x.astype(BF16)
    return high, (x - high.astype(F32)).astype(BF16)


def dot(a, b):
    return jnp.dot(a, b, preferred_element_type=F32)


def iota(shape, dim):
    return lax.broadcasted_iota(jnp.int32, shape, dim)


def group_row(half, group, cells_y):
    return group * GROUP + half * (cells_y - GROUP - 2 * group * GROUP)


def global_row(half, local, cells_y):
    group = local // GROUP
    return group_row(half, group, cells_y) + (local - group * GROUP)


def wide_local(place, own, wide):
    group = (place - own) // GROUP
    return own + (wide - own) - GROUP - group * GROUP + (place - own - group * GROUP)


def wide_group(group, own_groups, groups):
    return group if group < own_groups else own_groups + groups - 1 - group


def pad_to(value, unit):
    return -(-value // unit) * unit


def call(kernel, out_shape, in_specs, name, scratch=()):
    return pl.pallas_call(
        kernel,
        out_shape=out_shape,
        in_specs=in_specs,
        out_specs=jax.tree.map(lambda _: VMEM, out_shape),
        scratch_shapes=list(scratch),
        compiler_params=PARAMS,
        name=name,
    )


def place(row, count, width, turned, spacing):
    source, target = iota((row.shape[1], width), 0), iota((row.shape[1], width), 1)
    index = count - 1 - source if turned else source
    ones = (target == spacing * index) & (source < count)
    return jnp.dot(row, ones.astype(F32), precision=lax.Precision.HIGHEST, preferred_element_type=F32)


def tables_kernel(mine_ref, other_ref, yf_ref, ya_ref, zhi_ref, zlo_ref, xhi_ref, xlo_ref, *, sizes, cells_y, taps):
    taps_x, taps_y, taps_z = taps
    straight = core() == half()
    mine, other = mine_ref[...], other_ref[...]
    both = (jnp.where(straight, mine, other), jnp.where(straight, other, mine))
    radius, radius_x, radius_z = taps_y // 2, taps_x // 2, taps_z // 2
    side = half()
    own, near, wide = sizes
    for index in range(4):
        adjoint = index >= 2
        out_ref, rows, width = (ya_ref, own, near) if adjoint else (yf_ref, near, wide)
        lanes = out_ref.shape[2]
        row = global_row(side, iota((rows, lanes), 0), cells_y)
        lane = iota((rows, lanes), 1)
        turned = lane if adjoint else jnp.where(lane < own, lane, wide_local(lane, own, wide))
        col = global_row(side, turned, cells_y)
        delta = (row - col if adjoint else col - row) + radius
        delta = jnp.where(lane < width, delta, -1)
        band = jnp.zeros((rows, lanes), F32)
        values = both[index % 2][:, 128:256]
        for a in range(taps_y):
            band = jnp.where(delta == a, jnp.broadcast_to(values[:, a:a + 1], (rows, lanes)), band)
        high, low = split(band)
        high, low = high.astype(F32), low.astype(F32)
        out_ref[index % 2] = (high + pltpu.roll(high, width, 1) + pltpu.roll(low, 2 * width, 1)).astype(BF16)

    lanes = zhi_ref.shape[2]
    near_z = jnp.abs(iota((lanes, lanes), 1) - iota((lanes, lanes), 0)) <= radius_z
    for index in range(4):
        base = place(both[index % 2][:, 256:384], taps_z, lanes, index < 2, 1)
        base = pltpu.roll(base, lanes - radius_z, 1)
        band = pltpu.roll(jnp.broadcast_to(base, (lanes, lanes)), 0, 1, stride=1, stride_axis=0)
        zhi_ref[index], zlo_ref[index] = split(jnp.where(near_z, band, jnp.zeros_like(band)))

    rows = xhi_ref.shape[1] // 2
    lanes = max(512, 1 << (xhi_ref.shape[2] - 1).bit_length())
    for index in range(4):
        base = place(both[index % 2][:, :128], taps_x, lanes, index >= 2, 8)
        base = jnp.broadcast_to(base, (rows, lanes))
        band = pltpu.roll(base, 0, 1, stride=1, stride_axis=0)
        lane = iota((rows, lanes), 1)
        edge = 8 * radius_x
        far = pad_to(rows + edge, 128)
        next_near = pltpu.roll(band, lanes - edge, 1)
        next_far = pltpu.roll(band, far - rows - edge, 1)
        near_part = jnp.where((lane < rows) | (core() == 0), next_near, pltpu.roll(band, rows, 1))
        far_part = jnp.where(core() == 0, pltpu.roll(band, far, 1), next_far)
        zero = jnp.zeros_like(band)
        band = jnp.where(
            lane < rows + edge, near_part, jnp.where((lane >= far) & (lane < far + edge), far_part, zero)
        )[:, :xhi_ref.shape[2]]
        block = (index // 2, slice(index % 2 * rows, index % 2 * rows + rows))
        xhi_ref[block], xlo_ref[block] = split(band)


def make_tables(mine, other, taps, planes, cells_y, cells_z, sizes):
    own, near, wide = sizes
    radius = taps[0] // 2
    depth = pad_to(8 * (planes + radius), 128) + pad_to(8 * radius, 128)
    kernel = functools.partial(tables_kernel, sizes=sizes, cells_y=cells_y, taps=taps)
    shape = jax.ShapeDtypeStruct
    out_shape = (
        shape((2, near, pad_to(3 * wide, 128)), BF16),
        shape((2, own, pad_to(3 * near, 128)), BF16),
        shape((4, cells_z, cells_z), BF16),
        shape((4, cells_z, cells_z), BF16),
        shape((2, 2 * 8 * planes, depth), BF16),
        shape((2, 2 * 8 * planes, depth), BF16),
    )
    return call(kernel, out_shape, [VMEM, VMEM], "band_matrices")(mine, other)


def window_kernel(estimate_ref, own_ref, other_ref):
    cells_y = estimate_ref.shape[1]
    groups = own_ref.shape[1] // GROUP
    for side, out_ref in ((half(), own_ref), (1 - half(), other_ref)):
        for group in range(groups):
            local = wide_group(group, cells_y // 2 // GROUP, groups)
            start = pl.multiple_of(group_row(side, local, cells_y), GROUP)
            out_ref[:, group * GROUP:(group + 1) * GROUP, :] = estimate_ref[:, pl.ds(start, GROUP), :]


def make_windows(estimate, wide):
    planes, _, cells_z = estimate.shape
    shape = jax.ShapeDtypeStruct((planes, wide, cells_z), F32)
    return call(window_kernel, (shape, shape), [VMEM], "estimate_windows")(estimate)


def put_edges(out_ref, edge_refs):
    start = 0
    for far_ref, near_ref in zip(edge_refs[::2], edge_refs[1::2]):
        radius, rows = far_ref.shape[0], slice(start, start + far_ref.shape[1])
        beyond = out_ref.shape[0] - radius
        for p in range(radius):
            far_ref[p] = out_ref[p + core() * beyond, rows]
            near_ref[p] = out_ref[p + (1 - core()) * beyond, rows]
        start += far_ref.shape[1]


def assemble_kernel(*refs, count):
    pieces, window, out_ref, edge_refs = refs[:count], refs[count:-1], refs[-1], ()
    if len(refs) > count + 1:
        window, out_ref, edge_refs = refs[count], refs[count + 1], refs[count + 2:]
    straight, group = core() == half(), lax.axis_index("view") // 2
    planes, share = out_ref.shape[0], pieces[0].shape[0]
    for p in range(planes):
        turn = lax.rem(group - p // share + count, count)
        value = pieces[0][p % share]
        for k in range(1, count):
            value = jnp.where(turn == k, pieces[k][p % share], value)
        out_ref[p] = jnp.where(straight, window[p], value) if edge_refs else value
    put_edges(out_ref, edge_refs)


def edge_shapes(shape, radius, chunks):
    planes, _, lanes = shape
    edges = [jax.ShapeDtypeStruct((radius, rows, lanes), F32) for rows in chunks for _ in range(2)]
    return (jax.ShapeDtypeStruct(shape, F32), *edges)


def assemble(window, pieces, radius):
    out_shape = edge_shapes(window.shape, radius, window.shape[1:2])
    kernel = functools.partial(assemble_kernel, count=len(pieces))
    return call(kernel, out_shape, [VMEM] * (1 + len(pieces)), "estimate")(*pieces, window)


def assemble_far(pieces):
    share, rows, lanes = pieces[0].shape
    shape = jax.ShapeDtypeStruct((share * len(pieces), rows, lanes), F32)
    kernel = functools.partial(assemble_kernel, count=len(pieces))
    return call(kernel, (shape,), [VMEM] * len(pieces), "far_slab")(*pieces)[0]


def shift_kernel(offsets_ref, acq_ref, mask_ref, first_ref, second_ref, turned_ref):
    planes, cells_y, cells_z = acq_ref.shape
    near = first_ref.shape[1]
    shift_y, shift_z = offsets_ref[0, 1], offsets_ref[0, 2]
    row = iota((cells_y, cells_z), 0) + shift_y
    col = iota((cells_y, cells_z), 1) + shift_z
    inside = (row >= 0) & (row < cells_y) & (col >= 0) & (col < cells_z)
    turn_y = lax.rem(cells_y - shift_y, cells_y)
    turn_z = lax.rem(cells_z - shift_z, cells_z)

    def body(p, carry):
        x = pltpu.roll(pltpu.roll(acq_ref[p], turn_z, 1), turn_y, 0)
        turned_ref[...] = jnp.where(inside, x, jnp.zeros_like(x))
        for side, out_ref in ((core(), first_ref), (1 - core(), second_ref)):
            for group in range(near // GROUP):
                start = pl.multiple_of(group_row(side, group, cells_y), GROUP)
                out_ref[p, group * GROUP:(group + 1) * GROUP, :] = turned_ref[pl.ds(start, GROUP), :]
        return carry

    lax.fori_loop(0, planes, body, 0)
    mask = mask_ref[...].astype(F32)
    for out_ref in (first_ref, second_ref):
        out_ref[planes] = jnp.zeros((near, cells_z), F32)
        out_ref[planes, :planes, :cells_y] = mask


def shift_and_cut(offsets, acquired, mask, near):
    planes, cells_y, cells_z = acquired.shape
    shape = jax.ShapeDtypeStruct((planes + 1, near, cells_z), F32)
    scratch = [pltpu.VMEM((cells_y, cells_z), F32)]
    return call(shift_kernel, (shape, shape), [SMEM, VMEM, VMEM], "shift_recorded", scratch)(offsets, acquired, mask)


def gather(ref, row, radius=None):
    if radius is None or ref.shape[0] == radius:
        return ref[:, pl.ds(row, 8), :]
    return ref[pl.ds((1 - core()) * (ref.shape[0] - radius), radius), pl.ds(row, 8), :]


def spread_x(hi_ref, lo_ref, index, band_rows, band_lanes, blocks):
    lanes = blocks[0][0].shape[2]
    filled = []
    for parts in blocks:
        count = 8 * sum(part.shape[0] for part in parts)
        missing = (pad_to(count, 128) - count) // 8
        filled += list(parts) + ([jnp.zeros((missing, 8, lanes), F32)] if missing else [])
    high, low = split(jnp.concatenate(filled, axis=0).reshape(-1, lanes))
    band = hi_ref[index, band_rows, band_lanes]
    out = dot(band, high) + (dot(band, low) + dot(lo_ref[index, band_rows, band_lanes], high))
    return out.reshape(-1, 8, lanes)


def near_lanes(planes, radius):
    return pad_to(8 * (planes + radius), 128)


def blur_near_kernel(hi_ref, lo_ref, own_ref, near_ref, first_ref, second_ref):
    planes, rows, _ = own_ref.shape
    lanes = slice(0, near_lanes(planes, near_ref.shape[0]))

    def body(step, carry):
        row = pl.multiple_of(step * 8, 8)
        block = [gather(own_ref, row), gather(near_ref, row)]
        out = spread_x(hi_ref, lo_ref, 0, slice(None), lanes, [block])
        first_ref[:, pl.ds(row, 8), :] = out[:planes]
        second_ref[:, pl.ds(row, 8), :] = out[planes:]
        return carry

    lax.fori_loop(0, rows // 8, body, 0)


def blur_far_kernel(hi_ref, lo_ref, far_ref, first_ref, second_ref, first_out, second_out, *, radius):
    planes, rows, _ = first_ref.shape
    lanes = slice(near_lanes(planes, radius), None)

    def body(step, carry):
        row = pl.multiple_of(step * 8, 8)
        place = (slice(None), pl.ds(row, 8), slice(None))
        out = spread_x(hi_ref, lo_ref, 0, slice(None), lanes, [[gather(far_ref, row, radius)]])
        first_out[place] = first_ref[place] + out[:planes]
        second_out[place] = second_ref[place] + out[planes:]
        return carry

    lax.fori_loop(0, rows // 8, body, 0)


def blur_near(tables, own, near):
    shape = jax.ShapeDtypeStruct(own.shape, F32)
    return call(blur_near_kernel, (shape, shape), [VMEM] * 4, "blur_x_near")(*tables[4:], own, near)


def blur_far(tables, far, parts, radius):
    shape = jax.ShapeDtypeStruct(parts[0].shape, F32)
    kernel = functools.partial(blur_far_kernel, radius=radius)
    return call(kernel, (shape, shape), [VMEM] * 5, "blur_x_far")(*tables[4:], far, *parts)


def spread_y(band, x):
    high, low = split(x)
    parts = [high, low, high]
    rest = band.shape[1] - 3 * x.shape[0]
    if rest:
        parts.append(jnp.zeros((rest, x.shape[1]), BF16))
    return dot(band, jnp.concatenate(parts, axis=0))


def spread_z(x, hi_ref, lo_ref, index):
    high, low = split(x)
    return dot(high, hi_ref[index]) + (dot(low, hi_ref[index]) + dot(high, lo_ref[index]))


def ratio_planes(wide_refs, fetch, yf_ref, ya_ref, zhi_ref, zlo_ref, order, outs):
    out_ref, edge_refs = outs[0], outs[1:]
    planes, rows, _ = out_ref.shape
    near = yf_ref.shape[1]
    step = 4
    for start in range(0, planes, step):
        block = range(start, min(start + step, planes))
        blurred = jnp.concatenate(
            [spread_y(yf_ref[order], jnp.concatenate([ref[p] for ref in wide_refs], axis=0)) for p in block], axis=0
        )
        blurred = spread_z(blurred, zhi_ref, zlo_ref, order)
        image = jnp.concatenate([fetch(p) for p in block], axis=0)
        ratio = jnp.where(image >= 0, image / blurred, jnp.ones_like(image))
        spread = jnp.concatenate(
            [spread_y(ya_ref[order], ratio[k * near:(k + 1) * near]) for k in range(len(block))], axis=0
        )
        spread = spread_z(spread, zhi_ref, zlo_ref, 2 + order)
        for k, p in enumerate(block):
            out_ref[p] = spread[k * rows:(k + 1) * rows]
    put_edges(out_ref, edge_refs)


def first_ratio_kernel(shift_ref, far_ref, near_ref, own_ref, *refs, order, wides, extent_x, cells_y):
    refs, image_ref, (planes_ref, mask_ref, semaphores) = refs[:-4], refs[-4], refs[-3:]
    planes, near, cells_z = image_ref.shape
    side = half()
    slab = lax.axis_index("tile") - side + core()
    shift_x, shift_y, shift_z = (shift_ref[order, i] for i in range(3))
    lanes = pad_to(cells_y, 128)
    pick = iota((near, lanes), 1) == global_row(side, iota((near, lanes), 0), cells_y)

    def copy(ref, index, p):
        return pltpu.make_async_copy(ref.at[index], planes_ref.at[p], semaphores.at[p])

    mask_copy = pltpu.make_async_copy(own_ref.at[planes, pl.ds(0, planes)], mask_ref, semaphores.at[planes])
    mask_copy.start()
    for p in range(planes):
        source = p + shift_x
        is_own = (source >= 0) & (source < planes)
        is_far = (source < 0) == (core() == 0)
        beyond = jnp.clip(jnp.where(source < 0, source + planes, source - planes), 0, planes - 1)
        pl.when(is_own)(copy(own_ref, jnp.clip(source, 0, planes - 1), p).start)
        pl.when(jnp.logical_not(is_own) & is_far)(copy(far_ref, beyond, p).start)
        pl.when(jnp.logical_not(is_own) & jnp.logical_not(is_far))(copy(near_ref, beyond, p).start)
    mask_copy.wait()
    mask = mask_ref[:, :lanes].astype(BF16)
    columns = lax.dot_general(
        pick.astype(F32).astype(BF16), mask, (((1,), (1,)), ((), ())), preferred_element_type=F32
    )
    row = global_row(side, iota((near, cells_z), 0), cells_y) + shift_y
    col = iota((near, cells_z), 1) + shift_z
    inside = (row >= 0) & (row < cells_y) & (col >= 0) & (col < cells_z)

    def fetch(p):
        copy(own_ref, 0, p).wait()
        x = slab * planes + p + shift_x
        value = planes_ref[p]
        weight = jnp.broadcast_to(columns[:, p:p + 1], (near, cells_z))
        covered = inside & (weight > 0.5) & (x >= 0) & (x < extent_x)
        value = jnp.where(covered, value, jnp.full_like(value, -1.0))
        image_ref[p] = value
        return value

    ratio_planes(refs[:wides], fetch, *refs[wides:wides + 4], order, refs[wides + 4:])


def next_ratio_kernel(image_ref, *refs, order, wides):
    ratio_planes(refs[:wides], lambda p: image_ref[p], *refs[wides:wides + 4], order, refs[wides + 4:])


def ratio_shapes(wides, tables, radius, chunks):
    planes, _, lanes = wides[0].shape
    return edge_shapes((planes, tables[1].shape[1], lanes), radius, chunks)


def first_ratio(shifts, blocks, wides, tables, order, radius, chunks, extent_x, cells_y):
    planes, _, lanes = wides[0].shape
    kernel = functools.partial(
        first_ratio_kernel, order=order, wides=len(wides), extent_x=extent_x, cells_y=cells_y
    )
    image = jax.ShapeDtypeStruct((planes, tables[0].shape[1], lanes), F32)
    out_shape = ratio_shapes(wides, tables, radius, chunks) + (image,)
    scratch = [
        pltpu.VMEM(image.shape, F32), pltpu.VMEM((planes, lanes), F32), pltpu.SemaphoreType.DMA((planes + 1,))
    ]
    in_specs = [SMEM] + [pl.BlockSpec(memory_space=pl.ANY)] * 3 + [VMEM] * (4 + len(wides))
    return call(kernel, out_shape, in_specs, "image_and_ratio", scratch)(shifts, *blocks, *wides, *tables[:4])


def next_ratio(image, wides, tables, order, radius, chunks):
    kernel = functools.partial(next_ratio_kernel, order=order, wides=len(wides))
    return call(kernel, ratio_shapes(wides, tables, radius, chunks), [VMEM] * (5 + len(wides)), "ratio")(
        image, *wides, *tables[:4]
    )


def factor_kernel(hi_ref, lo_ref, before_ref, far_ref, near_ref, own_ref, out_ref, *, order, starts, share):
    planes, rows, _ = out_ref.shape
    band_rows = slice(order * 8 * planes, (order + 1) * 8 * planes)

    def body(step, carry):
        row = pl.multiple_of(step * 8, 8)
        total = before_ref[:, pl.ds(pl.multiple_of(starts[0] + row, 8), 8), :]
        if share:
            total = share * jnp.log(total)
        own = gather(own_ref, pl.multiple_of(starts[1] + row, 8))
        blocks = [[own, gather(near_ref, row)], [gather(far_ref, row)]]
        factor = spread_x(hi_ref, lo_ref, 1, band_rows, slice(None), blocks)
        out_ref[:, pl.ds(row, 8), :] = total + jnp.log(factor)
        return carry

    lax.fori_loop(0, rows // 8, body, 0)


def log_factor(tables, before, side, order, before_start, own_start, share):
    far, near, own = side
    kernel = functools.partial(factor_kernel, order=order, starts=(before_start, own_start), share=share)
    shape = jax.ShapeDtypeStruct((own.shape[0],) + far.shape[1:], F32)
    return call(kernel, shape, [VMEM] * 6, "log_factor")(*tables[4:], before, far, near, own)


def update_kernel(*refs):
    parts, edge_ref, out_ref, edge_refs = refs[:-4], refs[-4], refs[-3], refs[-2:]
    for p in range(out_ref.shape[0]):
        total = parts[0][p]
        for part in parts[1:]:
            total = total + part[p]
        out_ref[p] = jnp.concatenate([jnp.exp(total), edge_ref[p]], axis=0)
    put_edges(out_ref, edge_refs)


def update(parts, edge, radius):
    planes, rows, lanes = parts[0].shape
    rows += edge.shape[1]
    out_shape = edge_shapes((planes, rows, lanes), radius, [rows])
    return call(update_kernel, out_shape, [VMEM] * (len(parts) + 1), "update")(*parts, edge)


def finish_kernel(*refs):
    own, other, out_ref = refs[:(len(refs) - 1) // 2], refs[(len(refs) - 1) // 2:-1], refs[-1]
    straight = core() == half()
    groups = out_ref.shape[1] // GROUP
    for group in range(groups):
        rows = slice(group * GROUP, (group + 1) * GROUP)
        own_total, other_total = own[0][:, rows, :], other[0][:, rows, :]
        for part in own[1:]:
            own_total = own_total + part[:, rows, :]
        for part in other[1:]:
            other_total = other_total + part[:, rows, :]
        start = jnp.where(core() == 0, group, groups - 1 - group) * GROUP
        out_ref[:, pl.ds(pl.multiple_of(start, GROUP), GROUP), :] = jnp.exp(jnp.where(straight, own_total, other_total))


def finish(own_parts, other_parts):
    shape = jax.ShapeDtypeStruct(own_parts[0].shape, F32)
    return call(finish_kernel, shape, [VMEM] * (2 * len(own_parts)), "last_update")(*own_parts, *other_parts)


def join_kernel(*refs, starts):
    sources, out_ref, semaphores = refs[:-2], refs[-2], refs[-1]
    cells_y = out_ref.shape[1]
    copies = []
    for index, source_ref in enumerate(sources):
        rows, start = source_ref.shape[1], starts[index // 2]
        side = core() if index % 2 == 0 else 1 - core()
        place = pl.multiple_of(jnp.where(side == 0, start, cells_y - start - rows), GROUP)
        target = out_ref.at[:, pl.ds(place, rows), :]
        copies.append(pltpu.make_async_copy(source_ref, target, semaphores.at[index]))
    for copy in copies:
        copy.start()
    for copy in copies:
        copy.wait()


def join(pieces, starts, shape):
    anywhere = pl.BlockSpec(memory_space=pl.ANY)
    return pl.pallas_call(
        functools.partial(join_kernel, starts=starts),
        out_shape=jax.ShapeDtypeStruct(shape, F32),
        in_specs=[anywhere] * len(pieces),
        out_specs=anywhere,
        scratch_shapes=[pltpu.SemaphoreType.DMA((len(pieces),))],
        compiler_params=PARAMS,
        name="join_halves",
    )(*pieces)


def shards(acquired, estimate, offsets, view_mask, kern_x, kern_y, kern_z):
    planes, cells_y, cells_z = estimate.shape
    views, slabs = lax.axis_size("view"), lax.axis_size("tile")
    groups = views // 2
    taps_y = kern_y.shape[1]
    radius = kern_x.shape[1] // 2
    own_rows = cells_y // 2
    near = own_rows + pad_to(taps_y // 2, GROUP)
    wide = own_rows + pad_to(2 * (taps_y // 2), GROUP)
    edge_rows = wide - own_rows
    inner_rows = own_rows - edge_rows
    group = lax.axis_index("view") // 2
    straight = core() == half()

    def across(turn, half_of=lambda r: r, core_of=lambda c: c, when=lambda c, r: True):
        return lambda g, c, q, r: ((g + turn) % groups, core_of(c), q, half_of(r)) if when(c, r) else None

    def neighbours(far, near):
        return send(far, to_far), send(near, to_core_partner)

    window, crossing = make_windows(estimate, wide)
    piece = lax.dynamic_slice_in_dim(crossing, group * (planes // groups), planes // groups, 0)
    piece = send(piece, across(0, lambda r: 1 - r, when=lambda c, r: c == r))

    acquired = after(acquired, window)
    first, second = shift_and_cut(offsets, acquired[0], view_mask[0], near)
    piece = after(piece, first)
    arrived = send(first, lambda g, c, q, r: (g, r, q, c) if c != r else None)

    mine = [jnp.pad(row, ((0, 0), (0, 128 - row.shape[1]))) for row in (kern_x, kern_y, kern_z, offsets.astype(F32))]
    mine = jnp.concatenate(mine, axis=1)
    other = send(mine, to_core_partner)
    taps = kern_x.shape[1], taps_y, kern_z.shape[1]
    tables = make_tables(mine, other, taps, planes, cells_y, cells_z, (own_rows, near, wide))
    shifts = jnp.where(straight, jnp.concatenate([mine, other]), jnp.concatenate([other, mine]))
    shifts = shifts[:, 384:384 + offsets.shape[1]].astype(jnp.int32)

    start = group * (planes // groups)
    share = jnp.where(straight, lax.dynamic_slice_in_dim(window, start, planes // groups, 0), piece)
    later = after(after(piece, tables[0]), share)
    share = send(share, to_far)
    pieces = [piece] + [send(later, across(turn, when=lambda c, r: c != r)) for turn in range(1, groups)]
    current, _, close = assemble(after(window, share), pieces, radius)
    second = after(second, current)
    second = send(second, lambda g, c, q, r: (g, r, q, 1 - c))
    distant = assemble_far([share] + [send(share, across(turn)) for turn in range(1, groups)])
    chunks = [(distant, blur_near(tables, current, after(send(close, to_core_partner), distant)))]
    first = jnp.where(straight, first, arrived)
    second = after(second, chunks[0][1][0])
    blocks = [(*neighbours(block, block), block) for block in (first, second)]
    images = [None, None]

    sizes = [[own_rows], [inner_rows, edge_rows]]

    for step in range(ITERS):
        wides = []
        for distant, parts in chunks:
            distant = after(distant, wides[-1][0]) if wides else distant
            wides.append(blur_far(tables, distant, parts, radius))
        sides = []
        for order in range(2):
            parts = [chunk[order] for chunk in wides]
            if step == 0:
                spread, *edges, images[order] = first_ratio(
                    shifts, blocks[order], parts, tables, order, radius, sizes[order], planes * slabs, cells_y
                )
            else:
                spread, *edges = next_ratio(images[order], parts, tables, order, radius, sizes[order])
            sides += [(*neighbours(*edges[k:k + 2]), spread) for k in range(0, len(edges), 2)]

        total = log_factor(tables, current, sides[0], 0, 0, 0, 1.0 / groups)
        edge = log_factor(tables, after(total, sides[1][1]), sides[2], 1, inner_rows, inner_rows, 0)
        inner = log_factor(tables, total, sides[1], 1, 0, 0, 0)

        if step < ITERS - 1:
            edge_parts = [edge] + [send(edge, across(turn)) for turn in range(1, groups)]
            inner_parts = [inner] + [send(inner, across(turn)) for turn in range(1, groups)]
            edge = jnp.exp(sum(edge_parts[1:], edge_parts[0]))
            beyond = send(edge, to_row_partner)
            current, distant, close = update(inner_parts, edge, radius)
            distant, close = neighbours(distant, close)
            chunks = [(distant, blur_near(tables, current, close))]
            rest = planes - radius
            distant, close = neighbours(
                lax.dynamic_slice_in_dim(beyond, core() * rest, radius, 0),
                lax.dynamic_slice_in_dim(beyond, (1 - core()) * rest, radius, 0),
            )
            chunks.append((distant, blur_near(tables, beyond, after(close, chunks[0][1][0]))))

    pieces = []
    for own in (edge, inner):
        other_parts = [
            send(own, across(turn, lambda r: 1 - r, lambda c: 1 - c, lambda c, r: c != r))
            for turn in reversed(range(groups))
        ]
        own_parts = [own] + [send(own, across(turn, when=lambda c, r: c == r)) for turn in range(1, groups)]
        mine = finish(own_parts, other_parts)
        pieces += [mine, send(mine, to_core_partner)]
    return join(pieces, [inner_rows, 0], estimate.shape)


def solution(mesh):
    in_specs = (
        P("view", "tile", None, None),
        P("tile", None, None),
        P("view", None),
        P("view", "tile", None),
        P("view", None),
        P("view", None),
        P("view", None),
    )
    out_specs = P("tile", None, None)
    return jax.shard_map(shards, mesh=mesh, in_specs=in_specs, out_specs=out_specs, check_vma=False)
```

```python
import functools

import jax
import jax.numpy as jnp
from jax import lax
from jax.experimental import pallas as pl
from jax.experimental.pallas import tpu as pltpu
from jax.sharding import PartitionSpec as P

ITERS = 2
AXES = ("view", "tile")
F32 = jnp.float32
BF16 = jnp.bfloat16
VMEM = pl.BlockSpec(memory_space=pltpu.VMEM)
SMEM = pl.BlockSpec(memory_space=pltpu.SMEM)
PARAMS = pltpu.CompilerParams(vmem_limit_bytes=12 * 1024 * 1024)
GROUP = 16


def moves(move):
    views, tiles = lax.axis_size("view"), lax.axis_size("tile")
    pairs = []
    for view in range(views):
        for tile in range(tiles):
            target = move(view // 2, view % 2, tile // 2, tile % 2)
            if target is not None:
                g, c, q, r = target
                pairs.append((view * tiles + tile, (2 * g + c) * tiles + 2 * q + r))
    return pairs


def send(array, move):
    return lax.ppermute(array, AXES, moves(move))


def after(array, other):
    return lax.optimization_barrier((array, other))[0]


def to_far(g, c, q, r):
    s = 2 * q + c + (1 if c else -1)
    return (g, s % 2, s // 2, r) if 0 <= s < lax.axis_size("tile") else None


def to_row_partner(g, c, q, r):
    return (g, c, q, 1 - r)


def to_core_partner(g, c, q, r):
    return (g, 1 - c, q, r)


def core():
    return lax.rem(lax.axis_index("view"), 2)


def half():
    return lax.rem(lax.axis_index("tile"), 2)


def split(x):
    high = x.astype(BF16)
    return high, (x - high.astype(F32)).astype(BF16)


def dot(a, b):
    return jnp.dot(a, b, preferred_element_type=F32)


def iota(shape, dim):
    return lax.broadcasted_iota(jnp.int32, shape, dim)


def group_row(half, group, cells_y):
    return group * GROUP + half * (cells_y - GROUP - 2 * group * GROUP)


def global_row(half, local, cells_y):
    group = local // GROUP
    return group_row(half, group, cells_y) + (local - group * GROUP)


def wide_local(place, own, wide):
    group = (place - own) // GROUP
    return own + (wide - own) - GROUP - group * GROUP + (place - own - group * GROUP)


def wide_group(group, own_groups, groups):
    return group if group < own_groups else own_groups + groups - 1 - group


def pad_to(value, unit):
    return -(-value // unit) * unit


def call(kernel, out_shape, in_specs, name, scratch=()):
    return pl.pallas_call(
        kernel,
        out_shape=out_shape,
        in_specs=in_specs,
        out_specs=jax.tree.map(lambda _: VMEM, out_shape),
        scratch_shapes=list(scratch),
        compiler_params=PARAMS,
        name=name,
    )


def place(row, count, width, turned, spacing):
    source, target = iota((row.shape[1], width), 0), iota((row.shape[1], width), 1)
    index = count - 1 - source if turned else source
    ones = (target == spacing * index) & (source < count)
    return jnp.dot(row, ones.astype(F32), precision=lax.Precision.HIGHEST, preferred_element_type=F32)


def tables_kernel(mine_ref, other_ref, yf_ref, ya_ref, zhi_ref, zlo_ref, xhi_ref, xlo_ref, *, sizes, cells_y, taps):
    taps_x, taps_y, taps_z = taps
    straight = core() == half()
    mine, other = mine_ref[...], other_ref[...]
    both = (jnp.where(straight, mine, other), jnp.where(straight, other, mine))
    radius, radius_x, radius_z = taps_y // 2, taps_x // 2, taps_z // 2
    side = half()
    own, near, wide = sizes
    for index in range(4):
        adjoint = index >= 2
        out_ref, rows, width = (ya_ref, own, near) if adjoint else (yf_ref, near, wide)
        lanes = out_ref.shape[2]
        row = global_row(side, iota((rows, lanes), 0), cells_y)
        lane = iota((rows, lanes), 1)
        turned = lane if adjoint else jnp.where(lane < own, lane, wide_local(lane, own, wide))
        col = global_row(side, turned, cells_y)
        delta = (row - col if adjoint else col - row) + radius
        delta = jnp.where(lane < width, delta, -1)
        band = jnp.zeros((rows, lanes), F32)
        values = both[index % 2][:, 128:256]
        for a in range(taps_y):
            band = jnp.where(delta == a, jnp.broadcast_to(values[:, a:a + 1], (rows, lanes)), band)
        high, low = split(band)
        high, low = high.astype(F32), low.astype(F32)
        out_ref[index % 2] = (high + pltpu.roll(high, width, 1) + pltpu.roll(low, 2 * width, 1)).astype(BF16)

    lanes = zhi_ref.shape[2]
    near_z = jnp.abs(iota((lanes, lanes), 1) - iota((lanes, lanes), 0)) <= radius_z
    for index in range(4):
        base = place(both[index % 2][:, 256:384], taps_z, lanes, index < 2, 1)
        base = pltpu.roll(base, lanes - radius_z, 1)
        band = pltpu.roll(jnp.broadcast_to(base, (lanes, lanes)), 0, 1, stride=1, stride_axis=0)
        zhi_ref[index], zlo_ref[index] = split(jnp.where(near_z, band, jnp.zeros_like(band)))

    rows = xhi_ref.shape[1] // 2
    lanes = max(512, 1 << (xhi_ref.shape[2] - 1).bit_length())
    for index in range(4):
        base = place(both[index % 2][:, :128], taps_x, lanes, index >= 2, 8)
        base = jnp.broadcast_to(base, (rows, lanes))
        band = pltpu.roll(base, 0, 1, stride=1, stride_axis=0)
        lane = iota((rows, lanes), 1)
        edge = 8 * radius_x
        far = pad_to(rows + edge, 128)
        next_near = pltpu.roll(band, lanes - edge, 1)
        next_far = pltpu.roll(band, far - rows - edge, 1)
        near_part = jnp.where((lane < rows) | (core() == 0), next_near, pltpu.roll(band, rows, 1))
        far_part = jnp.where(core() == 0, pltpu.roll(band, far, 1), next_far)
        zero = jnp.zeros_like(band)
        band = jnp.where(
            lane < rows + edge, near_part, jnp.where((lane >= far) & (lane < far + edge), far_part, zero)
        )[:, :xhi_ref.shape[2]]
        block = (index // 2, slice(index % 2 * rows, index % 2 * rows + rows))
        xhi_ref[block], xlo_ref[block] = split(band)


def make_tables(mine, other, taps, planes, cells_y, cells_z, sizes):
    own, near, wide = sizes
    radius = taps[0] // 2
    depth = pad_to(8 * (planes + radius), 128) + pad_to(8 * radius, 128)
    kernel = functools.partial(tables_kernel, sizes=sizes, cells_y=cells_y, taps=taps)
    shape = jax.ShapeDtypeStruct
    out_shape = (
        shape((2, near, pad_to(3 * wide, 128)), BF16),
        shape((2, own, pad_to(3 * near, 128)), BF16),
        shape((4, cells_z, cells_z), BF16),
        shape((4, cells_z, cells_z), BF16),
        shape((2, 2 * 8 * planes, depth), BF16),
        shape((2, 2 * 8 * planes, depth), BF16),
    )
    return call(kernel, out_shape, [VMEM, VMEM], "band_matrices")(mine, other)


def window_kernel(estimate_ref, own_ref, other_ref):
    cells_y = estimate_ref.shape[1]
    groups = own_ref.shape[1] // GROUP
    for side, out_ref in ((half(), own_ref), (1 - half(), other_ref)):
        for group in range(groups):
            local = wide_group(group, cells_y // 2 // GROUP, groups)
            start = pl.multiple_of(group_row(side, local, cells_y), GROUP)
            out_ref[:, group * GROUP:(group + 1) * GROUP, :] = estimate_ref[:, pl.ds(start, GROUP), :]


def make_windows(estimate, wide):
    planes, _, cells_z = estimate.shape
    shape = jax.ShapeDtypeStruct((planes, wide, cells_z), F32)
    return call(window_kernel, (shape, shape), [VMEM], "estimate_windows")(estimate)


def put_edges(out_ref, edge_refs):
    start = 0
    for far_ref, near_ref in zip(edge_refs[::2], edge_refs[1::2]):
        radius, rows = far_ref.shape[0], slice(start, start + far_ref.shape[1])
        beyond = out_ref.shape[0] - radius
        for p in range(radius):
            far_ref[p] = out_ref[p + core() * beyond, rows]
            near_ref[p] = out_ref[p + (1 - core()) * beyond, rows]
        start += far_ref.shape[1]


def choose_kernel(window_ref, crossed_ref, out_ref, *edge_refs):
    straight = core() == half()
    for p in range(out_ref.shape[0]):
        out_ref[p] = jnp.where(straight, window_ref[p], crossed_ref[p])
    put_edges(out_ref, edge_refs)


def edge_shapes(shape, radius, chunks):
    planes, _, lanes = shape
    edges = [jax.ShapeDtypeStruct((radius, rows, lanes), F32) for rows in chunks for _ in range(2)]
    return (jax.ShapeDtypeStruct(shape, F32), *edges)


def choose(window, crossed, radius):
    out_shape = edge_shapes(window.shape, radius, window.shape[1:2])
    return call(choose_kernel, out_shape, [VMEM] * 2, "estimate")(window, crossed)


def shift_kernel(offsets_ref, acq_ref, mask_ref, first_ref, second_ref, turned_ref):
    planes, cells_y, cells_z = acq_ref.shape
    near = first_ref.shape[1]
    shift_y, shift_z = offsets_ref[0, 1], offsets_ref[0, 2]
    row = iota((cells_y, cells_z), 0) + shift_y
    col = iota((cells_y, cells_z), 1) + shift_z
    inside = (row >= 0) & (row < cells_y) & (col >= 0) & (col < cells_z)
    turn_y = lax.rem(cells_y - shift_y, cells_y)
    turn_z = lax.rem(cells_z - shift_z, cells_z)

    def body(p, carry):
        x = pltpu.roll(pltpu.roll(acq_ref[p], turn_z, 1), turn_y, 0)
        turned_ref[...] = jnp.where(inside, x, jnp.zeros_like(x))
        for side, out_ref in ((core(), first_ref), (1 - core(), second_ref)):
            for group in range(near // GROUP):
                start = pl.multiple_of(group_row(side, group, cells_y), GROUP)
                out_ref[p, group * GROUP:(group + 1) * GROUP, :] = turned_ref[pl.ds(start, GROUP), :]
        return carry

    lax.fori_loop(0, planes, body, 0)
    mask = mask_ref[...].astype(F32)
    for out_ref in (first_ref, second_ref):
        out_ref[planes] = jnp.zeros((near, cells_z), F32)
        out_ref[planes, :planes, :cells_y] = mask


def shift_and_cut(offsets, acquired, mask, near):
    planes, cells_y, cells_z = acquired.shape
    shape = jax.ShapeDtypeStruct((planes + 1, near, cells_z), F32)
    scratch = [pltpu.VMEM((cells_y, cells_z), F32)]
    return call(shift_kernel, (shape, shape), [SMEM, VMEM, VMEM], "shift_recorded", scratch)(offsets, acquired, mask)


def gather(ref, row):
    return ref[:, pl.ds(pl.multiple_of(row, 8), 8), :]


def spread_x(hi_ref, lo_ref, index, band_rows, band_lanes, blocks):
    lanes = blocks[0][0].shape[2]
    filled = []
    for parts in blocks:
        count = 8 * sum(part.shape[0] for part in parts)
        missing = (pad_to(count, 128) - count) // 8
        filled += list(parts) + ([jnp.zeros((missing, 8, lanes), F32)] if missing else [])
    high, low = split(jnp.concatenate(filled, axis=0).reshape(-1, lanes))
    band = hi_ref[index, band_rows, band_lanes]
    out = dot(band, high) + (dot(band, low) + dot(lo_ref[index, band_rows, band_lanes], high))
    return out.reshape(-1, 8, lanes)


def near_lanes(planes, radius):
    return pad_to(8 * (planes + radius), 128)


def blur_near_kernel(hi_ref, lo_ref, own_ref, near_ref, first_ref, second_ref):
    planes, rows, _ = own_ref.shape
    lanes = slice(0, near_lanes(planes, near_ref.shape[0]))

    def body(step, carry):
        row = pl.multiple_of(step * 8, 8)
        block = [gather(own_ref, row), gather(near_ref, row)]
        out = spread_x(hi_ref, lo_ref, 0, slice(None), lanes, [block])
        first_ref[:, pl.ds(row, 8), :] = out[:planes]
        second_ref[:, pl.ds(row, 8), :] = out[planes:]
        return carry

    lax.fori_loop(0, rows // 8, body, 0)


def blur_far_kernel(hi_ref, lo_ref, far_ref, first_ref, second_ref, first_out, second_out):
    planes, rows, _ = first_ref.shape
    lanes = slice(near_lanes(planes, far_ref.shape[0]), None)

    def body(step, carry):
        row = pl.multiple_of(step * 8, 8)
        place = (slice(None), pl.ds(row, 8), slice(None))
        out = spread_x(hi_ref, lo_ref, 0, slice(None), lanes, [[gather(far_ref, row)]])
        first_out[place] = first_ref[place] + out[:planes]
        second_out[place] = second_ref[place] + out[planes:]
        return carry

    lax.fori_loop(0, rows // 8, body, 0)


def blur_near(tables, own, near):
    shape = jax.ShapeDtypeStruct(own.shape, F32)
    return call(blur_near_kernel, (shape, shape), [VMEM] * 4, "blur_x_near")(*tables[4:], own, near)


def blur_far(tables, far, parts):
    shape = jax.ShapeDtypeStruct(parts[0].shape, F32)
    return call(blur_far_kernel, (shape, shape), [VMEM] * 5, "blur_x_far")(*tables[4:], far, *parts)


def spread_y(band, x):
    high, low = split(x)
    parts = [high, low, high]
    rest = band.shape[1] - 3 * x.shape[0]
    if rest:
        parts.append(jnp.zeros((rest, x.shape[1]), BF16))
    return dot(band, jnp.concatenate(parts, axis=0))


def spread_z(x, hi_ref, lo_ref, index):
    high, low = split(x)
    return dot(high, hi_ref[index]) + (dot(low, hi_ref[index]) + dot(high, lo_ref[index]))


def blurred_planes(wide_refs, yf_ref, zhi_ref, zlo_ref, order, block):
    wide = [jnp.concatenate([ref[p] for ref in wide_refs], axis=0) for p in block]
    spread = jnp.concatenate([spread_y(yf_ref[order], rows) for rows in wide], axis=0)
    return spread_z(spread, zhi_ref, zlo_ref, order)


def plane_blocks(planes, step=4):
    return [range(start, min(start + step, planes)) for start in range(0, planes, step)]


def blur_yz_kernel(*refs, order):
    wide_refs, (yf_ref, zhi_ref, zlo_ref, out_ref) = refs[:-4], refs[-4:]
    near = yf_ref.shape[1]
    for block in plane_blocks(out_ref.shape[0]):
        blurred = blurred_planes(wide_refs, yf_ref, zhi_ref, zlo_ref, order, block)
        for k, p in enumerate(block):
            out_ref[p] = blurred[k * near:(k + 1) * near]


def blur_yz(wides, tables, order):
    planes, _, lanes = wides[0].shape
    shape = jax.ShapeDtypeStruct((planes, tables[0].shape[1], lanes), F32)
    kernel = functools.partial(blur_yz_kernel, order=order)
    return call(kernel, shape, [VMEM] * (3 + len(wides)), "blur_yz")(*wides, tables[0], *tables[2:4])


def adjoint_planes(blurred_of, image_of, ya_ref, zhi_ref, zlo_ref, order, out_ref, edge_refs):
    planes, rows, _ = out_ref.shape
    for block in plane_blocks(planes):
        blurred = blurred_of(block)
        image = jnp.concatenate([image_of(p) for p in block], axis=0)
        ratio = jnp.where(image >= 0, image / blurred, jnp.ones_like(image))
        near = ratio.shape[0] // len(block)
        spread = jnp.concatenate(
            [spread_y(ya_ref[order], ratio[k * near:(k + 1) * near]) for k in range(len(block))], axis=0
        )
        spread = spread_z(spread, zhi_ref, zlo_ref, 2 + order)
        for k, p in enumerate(block):
            out_ref[p] = spread[k * rows:(k + 1) * rows]
    put_edges(out_ref, edge_refs)


def first_ratio_kernel(
    shift_ref, far_ref, near_ref, own_ref, blurred_ref, ya_ref, zhi_ref, zlo_ref, out_ref, *refs, order, extent_x, cells_y
):
    edge_refs, image_ref, (mine_ref, beyond_ref, semaphores) = refs[:-4], refs[-4], refs[-3:]
    planes, near, cells_z = image_ref.shape
    side = half()
    slab = lax.axis_index("tile") - side + core()
    shift_x, shift_y, shift_z = (shift_ref[order, i] for i in range(3))
    lanes = pad_to(cells_y, 128)
    pick = iota((near, lanes), 1) == global_row(side, iota((near, lanes), 0), cells_y)
    is_far = (shift_x > 0) == (core() == 1)
    copy = pltpu.make_async_copy(own_ref, mine_ref, semaphores.at[0])
    far_copy = pltpu.make_async_copy(far_ref.at[pl.ds(0, planes)], beyond_ref, semaphores.at[1])
    near_copy = pltpu.make_async_copy(near_ref.at[pl.ds(0, planes)], beyond_ref, semaphores.at[1])
    copy.start()
    pl.when(is_far)(far_copy.start)
    pl.when(jnp.logical_not(is_far))(near_copy.start)
    copy.wait()
    far_copy.wait()
    mask = mine_ref[planes, :planes, :lanes].astype(BF16)
    columns = lax.dot_general(
        pick.astype(F32).astype(BF16), mask, (((1,), (1,)), ((), ())), preferred_element_type=F32
    )
    row = global_row(side, iota((near, cells_z), 0), cells_y) + shift_y
    col = iota((near, cells_z), 1) + shift_z
    inside = (row >= 0) & (row < cells_y) & (col >= 0) & (col < cells_z)

    def fetch(p):
        source = p + shift_x
        x = slab * planes + source
        is_own = (source >= 0) & (source < planes)
        beyond = jnp.clip(jnp.where(source < 0, source + planes, source - planes), 0, planes - 1)
        value = jnp.where(is_own, mine_ref[jnp.clip(source, 0, planes - 1)], beyond_ref[beyond])
        weight = jnp.broadcast_to(columns[:, p:p + 1], (near, cells_z))
        covered = inside & (weight > 0.5) & (x >= 0) & (x < extent_x)
        value = jnp.where(covered, value, jnp.full_like(value, -1.0))
        image_ref[p] = value
        return value

    def blurred_of(block):
        return jnp.concatenate([blurred_ref[p] for p in block], axis=0)

    adjoint_planes(blurred_of, fetch, ya_ref, zhi_ref, zlo_ref, order, out_ref, edge_refs)


def next_ratio_kernel(image_ref, *refs, order, wides):
    wide_refs, (yf_ref, ya_ref, zhi_ref, zlo_ref, out_ref) = refs[:wides], refs[wides:wides + 5]

    def blurred_of(block):
        return blurred_planes(wide_refs, yf_ref, zhi_ref, zlo_ref, order, block)

    adjoint_planes(
        blurred_of, lambda p: image_ref[p], ya_ref, zhi_ref, zlo_ref, order, out_ref, refs[wides + 5:]
    )


def ratio_shapes(planes, lanes, tables, radius, chunks):
    return edge_shapes((planes, tables[1].shape[1], lanes), radius, chunks)


def first_ratio(shifts, blocks, blurred, tables, order, radius, chunks, extent_x, cells_y):
    planes, near, lanes = blurred.shape
    kernel = functools.partial(first_ratio_kernel, order=order, extent_x=extent_x, cells_y=cells_y)
    out_shape = ratio_shapes(planes, lanes, tables, radius, chunks) + (jax.ShapeDtypeStruct(blurred.shape, F32),)
    scratch = [
        pltpu.VMEM((planes + 1, near, lanes), F32), pltpu.VMEM(blurred.shape, F32), pltpu.SemaphoreType.DMA((2,))
    ]
    in_specs = [SMEM] + [pl.BlockSpec(memory_space=pl.ANY)] * 3 + [VMEM] * 4
    return call(kernel, out_shape, in_specs, "image_and_ratio", scratch)(shifts, *blocks, blurred, *tables[1:4])


def next_ratio(image, wides, tables, order, radius, chunks):
    planes, _, lanes = image.shape
    kernel = functools.partial(next_ratio_kernel, order=order, wides=len(wides))
    out_shape = ratio_shapes(planes, lanes, tables, radius, chunks)
    return call(kernel, out_shape, [VMEM] * (5 + len(wides)), "ratio")(image, *wides, *tables[:4])


def factor_kernel(hi_ref, lo_ref, before_ref, far_ref, near_ref, own_ref, out_ref, *, order, starts, share):
    planes, rows, _ = out_ref.shape
    band_rows = slice(order * 8 * planes, (order + 1) * 8 * planes)

    def body(step, carry):
        row = pl.multiple_of(step * 8, 8)
        total = gather(before_ref, starts[0] + row)
        if share:
            total = share * jnp.log(total)
        own = gather(own_ref, starts[1] + row)
        edge_row = starts[2] + row
        blocks = [[own, gather(near_ref, edge_row)], [gather(far_ref, edge_row)]]
        factor = spread_x(hi_ref, lo_ref, 1, band_rows, slice(None), blocks)
        out_ref[:, pl.ds(row, 8), :] = total + jnp.log(factor)
        return carry

    lax.fori_loop(0, rows // 8, body, 0)


def log_factor(tables, before, side, order, rows, starts, share):
    far, near, own = side
    kernel = functools.partial(factor_kernel, order=order, starts=starts, share=share)
    shape = jax.ShapeDtypeStruct((own.shape[0], rows, own.shape[2]), F32)
    return call(kernel, shape, [VMEM] * 6, "log_factor")(*tables[4:], before, far, near, own)


def update_kernel(*refs):
    parts, edge_ref, out_ref, edge_refs = refs[:-4], refs[-4], refs[-3], refs[-2:]
    for p in range(out_ref.shape[0]):
        total = parts[0][p]
        for part in parts[1:]:
            total = total + part[p]
        out_ref[p] = jnp.concatenate([jnp.exp(total), edge_ref[p]], axis=0)
    put_edges(out_ref, edge_refs)


def update(parts, edge, radius):
    planes, rows, lanes = parts[0].shape
    rows += edge.shape[1]
    out_shape = edge_shapes((planes, rows, lanes), radius, [rows])
    return call(update_kernel, out_shape, [VMEM] * (len(parts) + 1), "update")(*parts, edge)


def finish_kernel(*refs):
    own, other, out_ref = refs[:(len(refs) - 1) // 2], refs[(len(refs) - 1) // 2:-1], refs[-1]
    straight = core() == half()
    groups = out_ref.shape[1] // GROUP
    for group in range(groups):
        rows = slice(group * GROUP, (group + 1) * GROUP)
        own_total, other_total = own[0][:, rows, :], other[0][:, rows, :]
        for part in own[1:]:
            own_total = own_total + part[:, rows, :]
        for part in other[1:]:
            other_total = other_total + part[:, rows, :]
        start = jnp.where(core() == 0, group, groups - 1 - group) * GROUP
        out_ref[:, pl.ds(pl.multiple_of(start, GROUP), GROUP), :] = jnp.exp(jnp.where(straight, own_total, other_total))


def finish(own_parts, other_parts):
    shape = jax.ShapeDtypeStruct(own_parts[0].shape, F32)
    return call(finish_kernel, shape, [VMEM] * (2 * len(own_parts)), "last_update")(*own_parts, *other_parts)


def join_kernel(*refs, starts):
    sources, out_ref, semaphores = refs[:-2], refs[-2], refs[-1]
    cells_y = out_ref.shape[1]
    copies = []
    for index, source_ref in enumerate(sources):
        rows, start = source_ref.shape[1], starts[index // 2]
        side = core() if index % 2 == 0 else 1 - core()
        place = pl.multiple_of(jnp.where(side == 0, start, cells_y - start - rows), GROUP)
        target = out_ref.at[:, pl.ds(place, rows), :]
        copies.append(pltpu.make_async_copy(source_ref, target, semaphores.at[index]))
    for copy in copies:
        copy.start()
    for copy in copies:
        copy.wait()


def join(pieces, starts, shape):
    anywhere = pl.BlockSpec(memory_space=pl.ANY)
    return pl.pallas_call(
        functools.partial(join_kernel, starts=starts),
        out_shape=jax.ShapeDtypeStruct(shape, F32),
        in_specs=[anywhere] * len(pieces),
        out_specs=anywhere,
        scratch_shapes=[pltpu.SemaphoreType.DMA((len(pieces),))],
        compiler_params=PARAMS,
        name="join_halves",
    )(*pieces)


def shards(acquired, estimate, offsets, view_mask, kern_x, kern_y, kern_z):
    planes, cells_y, cells_z = estimate.shape
    views, slabs = lax.axis_size("view"), lax.axis_size("tile")
    groups = views // 2
    taps_y = kern_y.shape[1]
    radius = kern_x.shape[1] // 2
    own_rows = cells_y // 2
    near = own_rows + pad_to(taps_y // 2, GROUP)
    wide = own_rows + pad_to(2 * (taps_y // 2), GROUP)
    edge_rows = wide - own_rows
    inner_rows = own_rows - edge_rows
    group = lax.axis_index("view") // 2
    straight = core() == half()

    def across(turn, half_of=lambda r: r, core_of=lambda c: c, when=lambda c, r: True):
        return lambda g, c, q, r: ((g + turn) % groups, core_of(c), q, half_of(r)) if when(c, r) else None

    def neighbours(far, near):
        return send(far, to_far), send(near, to_core_partner)

    window, crossed = make_windows(estimate, wide)
    crossed = send(crossed, across(0, lambda r: 1 - r, when=lambda c, r: c == r))

    acquired = after(acquired, window)
    first, second = shift_and_cut(offsets, acquired[0], view_mask[0], near)
    mine = [jnp.pad(row, ((0, 0), (0, 128 - row.shape[1]))) for row in (kern_x, kern_y, kern_z, offsets.astype(F32))]
    mine = jnp.concatenate(mine, axis=1)
    other = send(mine, to_core_partner)
    taps = kern_x.shape[1], taps_y, kern_z.shape[1]
    tables = make_tables(mine, other, taps, planes, cells_y, cells_z, (own_rows, near, wide))
    shifts = jnp.where(straight, jnp.concatenate([mine, other]), jnp.concatenate([other, mine]))
    shifts = shifts[:, 384:384 + offsets.shape[1]].astype(jnp.int32)

    arrived = send(after(first, tables[0]), lambda g, c, q, r: (g, r, q, c) if c != r else None)
    current, distant, close = choose(after(window, first), crossed, radius)
    second = send(after(second, current), lambda g, c, q, r: (g, r, q, 1 - c))
    distant, close = neighbours(distant, close)
    chunks = [(distant, blur_near(tables, current, close))]
    first = jnp.where(straight, first, arrived)
    blocks = [(*neighbours(block, block), block) for block in (first, second)]
    images = [None, None]

    sizes = [[own_rows], [inner_rows, edge_rows]]

    for step in range(ITERS):
        last = step == ITERS - 1
        if last:
            sizes = [[own_rows], [own_rows]]
        wides = []
        for distant, parts in chunks:
            distant = after(distant, wides[-1][0]) if wides else distant
            wides.append(blur_far(tables, distant, parts))
        sides = []
        if step == 0:
            blurred = [blur_yz([chunk[order] for chunk in wides], tables, order) for order in range(2)]
        for order in range(2):
            if step == 0:
                spread, *edges, images[order] = first_ratio(
                    shifts, blocks[order], blurred[order], tables, order, radius, sizes[order], planes * slabs, cells_y
                )
            else:
                parts = [chunk[order] for chunk in wides]
                spread, *edges = next_ratio(images[order], parts, tables, order, radius, sizes[order])
            sides += [(*neighbours(*edges[k:k + 2]), spread) for k in range(0, len(edges), 2)]

        total = log_factor(tables, current, sides[0], 0, own_rows, (0, 0, 0), 1.0 / groups)
        starts = (inner_rows, inner_rows, inner_rows if last else 0)
        edge = log_factor(tables, total, sides[-1], 1, edge_rows, starts, 0)
        inner = log_factor(tables, total, sides[1], 1, inner_rows, (0, 0, 0), 0)

        if not last:
            edge_parts = [edge] + [send(edge, across(turn)) for turn in range(1, groups)]
            inner_parts = [inner] + [send(inner, across(turn)) for turn in range(1, groups)]
            edge = jnp.exp(sum(edge_parts[1:], edge_parts[0]))
            beyond = send(edge, to_row_partner)
            current, distant, close = update(inner_parts, edge, radius)
            distant, close = neighbours(distant, close)
            chunks = [(distant, blur_near(tables, current, close))]
            rest = planes - radius
            distant, close = neighbours(
                lax.dynamic_slice_in_dim(beyond, core() * rest, radius, 0),
                lax.dynamic_slice_in_dim(beyond, (1 - core()) * rest, radius, 0),
            )
            chunks.append((distant, blur_near(tables, beyond, after(close, chunks[0][1][0]))))

    pieces = []
    for own in (edge, inner):
        other_parts = [
            send(own, across(turn, lambda r: 1 - r, lambda c: 1 - c, lambda c, r: c != r))
            for turn in reversed(range(groups))
        ]
        own_parts = [own] + [send(own, across(turn, when=lambda c, r: c == r)) for turn in range(1, groups)]
        mine = finish(own_parts, other_parts)
        pieces += [mine, send(mine, to_core_partner)]
    return join(pieces, [inner_rows, 0], estimate.shape)


def solution(mesh):
    in_specs = (
        P("view", "tile", None, None),
        P("tile", None, None),
        P("view", None),
        P("view", "tile", None),
        P("view", None),
        P("view", None),
        P("view", None),
    )
    out_specs = P("tile", None, None)
    return jax.shard_map(shards, mesh=mesh, in_specs=in_specs, out_specs=out_specs, check_vma=False)
```

```python
import functools

import jax
import jax.numpy as jnp
from jax import lax
from jax.experimental import pallas as pl
from jax.experimental.pallas import tpu as pltpu
from jax.sharding import PartitionSpec as P

ITERS = 2
AXES = ("view", "tile")
F32 = jnp.float32
BF16 = jnp.bfloat16
VMEM = pl.BlockSpec(memory_space=pltpu.VMEM)
SMEM = pl.BlockSpec(memory_space=pltpu.SMEM)
PARAMS = pltpu.CompilerParams(vmem_limit_bytes=12 * 1024 * 1024)
GROUP = 16


def moves(move):
    views, tiles = lax.axis_size("view"), lax.axis_size("tile")
    pairs = []
    for view in range(views):
        for tile in range(tiles):
            target = move(view // 2, view % 2, tile // 2, tile % 2)
            if target is not None:
                g, c, q, r = target
                pairs.append((view * tiles + tile, (2 * g + c) * tiles + 2 * q + r))
    return pairs


def send(array, move):
    return lax.ppermute(array, AXES, moves(move))


def after(array, other):
    return lax.optimization_barrier((array, other))[0]


def to_far(g, c, q, r):
    s = 2 * q + c + (1 if c else -1)
    return (g, s % 2, s // 2, r) if 0 <= s < lax.axis_size("tile") else None


def to_row_partner(g, c, q, r):
    return (g, c, q, 1 - r)


def to_core_partner(g, c, q, r):
    return (g, 1 - c, q, r)


def core():
    return lax.rem(lax.axis_index("view"), 2)


def half():
    return lax.rem(lax.axis_index("tile"), 2)


def split(x):
    high = x.astype(BF16)
    return high, (x - high.astype(F32)).astype(BF16)


def dot(a, b):
    return jnp.dot(a, b, preferred_element_type=F32)


def iota(shape, dim):
    return lax.broadcasted_iota(jnp.int32, shape, dim)


def group_row(half, group, cells_y):
    return group * GROUP + half * (cells_y - GROUP - 2 * group * GROUP)


def global_row(half, local, cells_y):
    group = local // GROUP
    return group_row(half, group, cells_y) + (local - group * GROUP)


def wide_local(place, own, wide):
    group = (place - own) // GROUP
    return own + (wide - own) - GROUP - group * GROUP + (place - own - group * GROUP)


def wide_group(group, own_groups, groups):
    return group if group < own_groups else own_groups + groups - 1 - group


def pad_to(value, unit):
    return -(-value // unit) * unit


def call(kernel, out_shape, in_specs, name, scratch=()):
    return pl.pallas_call(
        kernel,
        out_shape=out_shape,
        in_specs=in_specs,
        out_specs=jax.tree.map(lambda _: VMEM, out_shape),
        scratch_shapes=list(scratch),
        compiler_params=PARAMS,
        name=name,
    )


def place(row, count, width, turned, spacing):
    source, target = iota((row.shape[1], width), 0), iota((row.shape[1], width), 1)
    index = count - 1 - source if turned else source
    ones = (target == spacing * index) & (source < count)
    return jnp.dot(row, ones.astype(F32), precision=lax.Precision.HIGHEST, preferred_element_type=F32)


def tables_kernel(mine_ref, other_ref, yf_ref, ya_ref, zhi_ref, zlo_ref, xhi_ref, xlo_ref, *, sizes, cells_y, taps):
    taps_x, taps_y, taps_z = taps
    straight = core() == half()
    mine, other = mine_ref[...], other_ref[...]
    both = (jnp.where(straight, mine, other), jnp.where(straight, other, mine))
    radius, radius_x, radius_z = taps_y // 2, taps_x // 2, taps_z // 2
    side = half()
    own, near, wide = sizes
    for index in range(4):
        adjoint = index >= 2
        out_ref, rows, width = (ya_ref, own, near) if adjoint else (yf_ref, near, wide)
        lanes = out_ref.shape[2]
        row = global_row(side, iota((rows, lanes), 0), cells_y)
        lane = iota((rows, lanes), 1)
        turned = lane if adjoint else jnp.where(lane < own, lane, wide_local(lane, own, wide))
        col = global_row(side, turned, cells_y)
        delta = (row - col if adjoint else col - row) + radius
        delta = jnp.where(lane < width, delta, -1)
        band = jnp.zeros((rows, lanes), F32)
        values = both[index % 2][:, 128:256]
        for a in range(taps_y):
            band = jnp.where(delta == a, jnp.broadcast_to(values[:, a:a + 1], (rows, lanes)), band)
        high, low = split(band)
        high, low = high.astype(F32), low.astype(F32)
        out_ref[index % 2] = (high + pltpu.roll(high, width, 1) + pltpu.roll(low, 2 * width, 1)).astype(BF16)

    lanes = zhi_ref.shape[2]
    near_z = jnp.abs(iota((lanes, lanes), 1) - iota((lanes, lanes), 0)) <= radius_z
    for index in range(4):
        base = place(both[index % 2][:, 256:384], taps_z, lanes, index < 2, 1)
        base = pltpu.roll(base, lanes - radius_z, 1)
        band = pltpu.roll(jnp.broadcast_to(base, (lanes, lanes)), 0, 1, stride=1, stride_axis=0)
        zhi_ref[index], zlo_ref[index] = split(jnp.where(near_z, band, jnp.zeros_like(band)))

    rows = xhi_ref.shape[1] // 2
    lanes = max(512, 1 << (xhi_ref.shape[2] - 1).bit_length())
    for index in range(4):
        base = place(both[index % 2][:, :128], taps_x, lanes, index >= 2, 8)
        base = jnp.broadcast_to(base, (rows, lanes))
        band = pltpu.roll(base, 0, 1, stride=1, stride_axis=0)
        lane = iota((rows, lanes), 1)
        edge = 8 * radius_x
        far = pad_to(rows + edge, 128)
        next_near = pltpu.roll(band, lanes - edge, 1)
        next_far = pltpu.roll(band, far - rows - edge, 1)
        near_part = jnp.where((lane < rows) | (core() == 0), next_near, pltpu.roll(band, rows, 1))
        far_part = jnp.where(core() == 0, pltpu.roll(band, far, 1), next_far)
        zero = jnp.zeros_like(band)
        band = jnp.where(
            lane < rows + edge, near_part, jnp.where((lane >= far) & (lane < far + edge), far_part, zero)
        )[:, :xhi_ref.shape[2]]
        block = (index // 2, slice(index % 2 * rows, index % 2 * rows + rows))
        xhi_ref[block], xlo_ref[block] = split(band)


def make_tables(mine, other, taps, planes, cells_y, cells_z, sizes):
    own, near, wide = sizes
    radius = taps[0] // 2
    depth = pad_to(8 * (planes + radius), 128) + pad_to(8 * radius, 128)
    kernel = functools.partial(tables_kernel, sizes=sizes, cells_y=cells_y, taps=taps)
    shape = jax.ShapeDtypeStruct
    out_shape = (
        shape((2, near, pad_to(3 * wide, 128)), BF16),
        shape((2, own, pad_to(3 * near, 128)), BF16),
        shape((4, cells_z, cells_z), BF16),
        shape((4, cells_z, cells_z), BF16),
        shape((2, 2 * 8 * planes, depth), BF16),
        shape((2, 2 * 8 * planes, depth), BF16),
    )
    return call(kernel, out_shape, [VMEM, VMEM], "band_matrices")(mine, other)


def window_kernel(estimate_ref, own_ref, other_ref):
    cells_y = estimate_ref.shape[1]
    groups = own_ref.shape[1] // GROUP
    for side, out_ref in ((half(), own_ref), (1 - half(), other_ref)):
        for group in range(groups):
            local = wide_group(group, cells_y // 2 // GROUP, groups)
            start = pl.multiple_of(group_row(side, local, cells_y), GROUP)
            out_ref[:, group * GROUP:(group + 1) * GROUP, :] = estimate_ref[:, pl.ds(start, GROUP), :]


def make_windows(estimate, wide):
    planes, _, cells_z = estimate.shape
    shape = jax.ShapeDtypeStruct((planes, wide, cells_z), F32)
    return call(window_kernel, (shape, shape), [VMEM], "estimate_windows")(estimate)


def put_edges(out_ref, edge_refs):
    end = out_ref.shape[1]
    for far_ref, near_ref in zip(edge_refs[::2], edge_refs[1::2]):
        radius, rows = far_ref.shape[0], slice(end - far_ref.shape[1], end)
        beyond = out_ref.shape[0] - radius
        for p in range(radius):
            far_ref[p] = out_ref[p + core() * beyond, rows]
            near_ref[p] = out_ref[p + (1 - core()) * beyond, rows]
        end -= far_ref.shape[1]


def assemble_kernel(*refs, count):
    pieces, window, out_ref, edge_refs = refs[:count], refs[count:-1], refs[-1], ()
    if len(refs) > count + 1:
        window, out_ref, edge_refs = refs[count], refs[count + 1], refs[count + 2:]
    straight, group = core() == half(), lax.axis_index("view") // 2
    planes, share = out_ref.shape[0], pieces[0].shape[0]
    for p in range(planes):
        turn = lax.rem(group - p // share + count, count)
        value = pieces[0][p % share]
        for k in range(1, count):
            value = jnp.where(turn == k, pieces[k][p % share], value)
        out_ref[p] = jnp.where(straight, window[p], value) if edge_refs else value
    put_edges(out_ref, edge_refs)


def edge_shapes(shape, radius, chunks):
    planes, _, lanes = shape
    edges = [jax.ShapeDtypeStruct((radius, rows, lanes), F32) for rows in chunks for _ in range(2)]
    return (jax.ShapeDtypeStruct(shape, F32), *edges)


def assemble(window, pieces, radius):
    out_shape = edge_shapes(window.shape, radius, window.shape[1:2])
    kernel = functools.partial(assemble_kernel, count=len(pieces))
    return call(kernel, out_shape, [VMEM] * (1 + len(pieces)), "estimate")(*pieces, window)


def assemble_far(pieces):
    share, rows, lanes = pieces[0].shape
    shape = jax.ShapeDtypeStruct((share * len(pieces), rows, lanes), F32)
    kernel = functools.partial(assemble_kernel, count=len(pieces))
    return call(kernel, (shape,), [VMEM] * len(pieces), "far_slab")(*pieces)[0]


def shift_kernel(offsets_ref, acq_ref, mask_ref, first_ref, second_ref, turned_ref):
    planes, cells_y, cells_z = acq_ref.shape
    near = first_ref.shape[1]
    shift_y, shift_z = offsets_ref[0, 1], offsets_ref[0, 2]
    row = iota((cells_y, cells_z), 0) + shift_y
    col = iota((cells_y, cells_z), 1) + shift_z
    inside = (row >= 0) & (row < cells_y) & (col >= 0) & (col < cells_z)
    turn_y = lax.rem(cells_y - shift_y, cells_y)
    turn_z = lax.rem(cells_z - shift_z, cells_z)

    def body(p, carry):
        x = pltpu.roll(pltpu.roll(acq_ref[p], turn_z, 1), turn_y, 0)
        turned_ref[...] = jnp.where(inside, x, jnp.zeros_like(x))
        for side, out_ref in ((core(), first_ref), (1 - core(), second_ref)):
            for group in range(near // GROUP):
                start = pl.multiple_of(group_row(side, group, cells_y), GROUP)
                out_ref[p, group * GROUP:(group + 1) * GROUP, :] = turned_ref[pl.ds(start, GROUP), :]
        return carry

    lax.fori_loop(0, planes, body, 0)
    mask = mask_ref[...].astype(F32)
    for out_ref in (first_ref, second_ref):
        out_ref[planes] = jnp.zeros((near, cells_z), F32)
        out_ref[planes, :planes, :cells_y] = mask


def shift_and_cut(offsets, acquired, mask, near):
    planes, cells_y, cells_z = acquired.shape
    shape = jax.ShapeDtypeStruct((planes + 1, near, cells_z), F32)
    scratch = [pltpu.VMEM((cells_y, cells_z), F32)]
    return call(shift_kernel, (shape, shape), [SMEM, VMEM, VMEM], "shift_recorded", scratch)(offsets, acquired, mask)


def gather(ref, row, radius=None):
    rows = pl.ds(pl.multiple_of(row, 8), 8)
    if radius is None or ref.shape[0] == radius:
        return ref[:, rows, :]
    return ref[pl.ds((1 - core()) * (ref.shape[0] - radius), radius), rows, :]


def spread_x(hi_ref, lo_ref, index, band_rows, band_lanes, blocks):
    lanes = blocks[0][0].shape[2]
    filled = []
    for parts in blocks:
        count = 8 * sum(part.shape[0] for part in parts)
        missing = (pad_to(count, 128) - count) // 8
        filled += list(parts) + ([jnp.zeros((missing, 8, lanes), F32)] if missing else [])
    high, low = split(jnp.concatenate(filled, axis=0).reshape(-1, lanes))
    band = hi_ref[index, band_rows, band_lanes]
    out = dot(band, high) + (dot(band, low) + dot(lo_ref[index, band_rows, band_lanes], high))
    return out.reshape(-1, 8, lanes)


def near_lanes(planes, radius):
    return pad_to(8 * (planes + radius), 128)


def blur_near_kernel(hi_ref, lo_ref, own_ref, near_ref, first_ref, second_ref):
    planes, rows, _ = own_ref.shape
    lanes = slice(0, near_lanes(planes, near_ref.shape[0]))

    def body(step, carry):
        row = pl.multiple_of(step * 8, 8)
        block = [gather(own_ref, row), gather(near_ref, row)]
        out = spread_x(hi_ref, lo_ref, 0, slice(None), lanes, [block])
        first_ref[:, pl.ds(row, 8), :] = out[:planes]
        second_ref[:, pl.ds(row, 8), :] = out[planes:]
        return carry

    lax.fori_loop(0, rows // 8, body, 0)


def blur_far_kernel(hi_ref, lo_ref, far_ref, first_ref, second_ref, first_out, second_out, *, radius):
    planes, rows, _ = first_ref.shape
    lanes = slice(near_lanes(planes, radius), None)

    def body(step, carry):
        row = pl.multiple_of(step * 8, 8)
        place = (slice(None), pl.ds(row, 8), slice(None))
        out = spread_x(hi_ref, lo_ref, 0, slice(None), lanes, [[gather(far_ref, row, radius)]])
        first_out[place] = first_ref[place] + out[:planes]
        second_out[place] = second_ref[place] + out[planes:]
        return carry

    lax.fori_loop(0, rows // 8, body, 0)


def blur_near(tables, own, near):
    shape = jax.ShapeDtypeStruct(own.shape, F32)
    return call(blur_near_kernel, (shape, shape), [VMEM] * 4, "blur_x_near")(*tables[4:], own, near)


def blur_far(tables, far, parts, radius):
    shape = jax.ShapeDtypeStruct(parts[0].shape, F32)
    kernel = functools.partial(blur_far_kernel, radius=radius)
    return call(kernel, (shape, shape), [VMEM] * 5, "blur_x_far")(*tables[4:], far, *parts)


def spread_y(band, x):
    high, low = split(x)
    parts = [high, low, high]
    rest = band.shape[1] - 3 * x.shape[0]
    if rest:
        parts.append(jnp.zeros((rest, x.shape[1]), BF16))
    return dot(band, jnp.concatenate(parts, axis=0))


def spread_z(x, hi_ref, lo_ref, index):
    high, low = split(x)
    return dot(high, hi_ref[index]) + (dot(low, hi_ref[index]) + dot(high, lo_ref[index]))


def blurred_planes(wide_refs, yf_ref, zhi_ref, zlo_ref, order, block):
    wide = [jnp.concatenate([ref[p] for ref in wide_refs], axis=0) for p in block]
    spread = jnp.concatenate([spread_y(yf_ref[order], rows) for rows in wide], axis=0)
    return spread_z(spread, zhi_ref, zlo_ref, order)


def plane_blocks(planes, step=4):
    return [range(start, min(start + step, planes)) for start in range(0, planes, step)]


def blur_yz_kernel(*refs, order):
    wide_refs, (yf_ref, zhi_ref, zlo_ref, out_ref) = refs[:-4], refs[-4:]
    near = yf_ref.shape[1]
    for block in plane_blocks(out_ref.shape[0]):
        blurred = blurred_planes(wide_refs, yf_ref, zhi_ref, zlo_ref, order, block)
        for k, p in enumerate(block):
            out_ref[p] = blurred[k * near:(k + 1) * near]


def blur_yz(wides, tables, order):
    planes, _, lanes = wides[0].shape
    shape = jax.ShapeDtypeStruct((planes, tables[0].shape[1], lanes), F32)
    kernel = functools.partial(blur_yz_kernel, order=order)
    return call(kernel, shape, [VMEM] * (3 + len(wides)), "blur_yz")(*wides, tables[0], *tables[2:4])


def adjoint_planes(blurred_of, image_of, ya_ref, zhi_ref, zlo_ref, order, out_ref, edge_refs):
    planes, rows, _ = out_ref.shape
    for block in plane_blocks(planes):
        blurred = blurred_of(block)
        image = jnp.concatenate([image_of(p) for p in block], axis=0)
        ratio = jnp.where(image >= 0, image / blurred, jnp.ones_like(image))
        near = ratio.shape[0] // len(block)
        spread = jnp.concatenate(
            [spread_y(ya_ref[order], ratio[k * near:(k + 1) * near]) for k in range(len(block))], axis=0
        )
        spread = spread_z(spread, zhi_ref, zlo_ref, 2 + order)
        for k, p in enumerate(block):
            out_ref[p] = spread[k * rows:(k + 1) * rows]
    put_edges(out_ref, edge_refs)


def first_ratio_kernel(
    shift_ref, far_ref, near_ref, own_ref, blurred_ref, ya_ref, zhi_ref, zlo_ref, out_ref, *refs, order, extent_x, cells_y
):
    edge_refs, image_ref, (mine_ref, beyond_ref, semaphores) = refs[:-4], refs[-4], refs[-3:]
    planes, near, cells_z = image_ref.shape
    side = half()
    slab = lax.axis_index("tile") - side + core()
    shift_x, shift_y, shift_z = (shift_ref[order, i] for i in range(3))
    lanes = pad_to(cells_y, 128)
    pick = iota((near, lanes), 1) == global_row(side, iota((near, lanes), 0), cells_y)
    is_far = (shift_x > 0) == (core() == 1)
    copy = pltpu.make_async_copy(own_ref, mine_ref, semaphores.at[0])
    far_copy = pltpu.make_async_copy(far_ref.at[pl.ds(0, planes)], beyond_ref, semaphores.at[1])
    near_copy = pltpu.make_async_copy(near_ref.at[pl.ds(0, planes)], beyond_ref, semaphores.at[1])
    copy.start()
    pl.when(is_far)(far_copy.start)
    pl.when(jnp.logical_not(is_far))(near_copy.start)
    copy.wait()
    far_copy.wait()
    mask = mine_ref[planes, :planes, :lanes].astype(BF16)
    columns = lax.dot_general(
        pick.astype(F32).astype(BF16), mask, (((1,), (1,)), ((), ())), preferred_element_type=F32
    )
    row = global_row(side, iota((near, cells_z), 0), cells_y) + shift_y
    col = iota((near, cells_z), 1) + shift_z
    inside = (row >= 0) & (row < cells_y) & (col >= 0) & (col < cells_z)

    def fetch(p):
        source = p + shift_x
        x = slab * planes + source
        is_own = (source >= 0) & (source < planes)
        beyond = jnp.clip(jnp.where(source < 0, source + planes, source - planes), 0, planes - 1)
        value = jnp.where(is_own, mine_ref[jnp.clip(source, 0, planes - 1)], beyond_ref[beyond])
        weight = jnp.broadcast_to(columns[:, p:p + 1], (near, cells_z))
        covered = inside & (weight > 0.5) & (x >= 0) & (x < extent_x)
        value = jnp.where(covered, value, jnp.full_like(value, -1.0))
        image_ref[p] = value
        return value

    def blurred_of(block):
        return jnp.concatenate([blurred_ref[p] for p in block], axis=0)

    adjoint_planes(blurred_of, fetch, ya_ref, zhi_ref, zlo_ref, order, out_ref, edge_refs)


def next_ratio_kernel(*refs, wides):
    image_refs, refs = refs[:2], refs[2:]
    wide_refs, refs = (refs[:wides], refs[wides:2 * wides]), refs[2 * wides:]
    (yf_ref, ya_ref, zhi_ref, zlo_ref), out_refs, edge_refs = refs[:4], refs[4:6], refs[6:]
    for order in range(2):

        def blurred_of(block, order=order):
            return blurred_planes(wide_refs[order], yf_ref, zhi_ref, zlo_ref, order, block)

        def image_of(p, order=order):
            return image_refs[order][p]

        edges = [ref.at[order] for ref in edge_refs]
        adjoint_planes(blurred_of, image_of, ya_ref, zhi_ref, zlo_ref, order, out_refs[order], edges)


def ratio_shapes(planes, lanes, tables, radius, chunks):
    return edge_shapes((planes, tables[1].shape[1], lanes), radius, chunks)


def first_ratio(shifts, blocks, blurred, tables, order, radius, chunks, extent_x, cells_y):
    planes, near, lanes = blurred.shape
    kernel = functools.partial(first_ratio_kernel, order=order, extent_x=extent_x, cells_y=cells_y)
    out_shape = ratio_shapes(planes, lanes, tables, radius, chunks) + (jax.ShapeDtypeStruct(blurred.shape, F32),)
    scratch = [
        pltpu.VMEM((planes + 1, near, lanes), F32), pltpu.VMEM(blurred.shape, F32), pltpu.SemaphoreType.DMA((2,))
    ]
    in_specs = [SMEM] + [pl.BlockSpec(memory_space=pl.ANY)] * 3 + [VMEM] * 4
    return call(kernel, out_shape, in_specs, "image_and_ratio", scratch)(shifts, *blocks, blurred, *tables[1:4])


def next_ratio(images, wides, tables, radius, chunks):
    planes, _, lanes = images[0].shape
    kernel = functools.partial(next_ratio_kernel, wides=len(wides[0]))
    whole, *edges = ratio_shapes(planes, lanes, tables, radius, chunks)
    edges = [jax.ShapeDtypeStruct((2,) + edge.shape, F32) for edge in edges]
    return call(kernel, (whole, whole, *edges), [VMEM] * (6 + 2 * len(wides[0])), "ratio")(
        *images, *wides[0], *wides[1], *tables[:4]
    )


def factor_kernel(hi_ref, lo_ref, before_ref, *refs, orders, starts, share):
    out_ref = refs[-1]
    planes, rows, _ = out_ref.shape

    def body(step, carry):
        row = pl.multiple_of(step * 8, 8)
        total = gather(before_ref, starts[0] + row)
        if share:
            total = share * jnp.log(total)
        for index, order in enumerate(orders):
            far_ref, near_ref, own_ref = refs[3 * index:3 * index + 3]
            if len(far_ref.shape) == 4:
                far_ref, near_ref = far_ref.at[order], near_ref.at[order]
            own = gather(own_ref, starts[1] + row)
            blocks = [[own, gather(near_ref, row)], [gather(far_ref, row)]]
            band_rows = slice(order * 8 * planes, (order + 1) * 8 * planes)
            total = total + jnp.log(spread_x(hi_ref, lo_ref, 1, band_rows, slice(None), blocks))
        out_ref[:, pl.ds(row, 8), :] = total
        return carry

    lax.fori_loop(0, rows // 8, body, 0)


def log_factor(tables, before, sides, orders, rows, starts, share):
    kernel = functools.partial(factor_kernel, orders=orders, starts=starts, share=share)
    planes, _, lanes = sides[0][2].shape
    shape = jax.ShapeDtypeStruct((planes, rows, lanes), F32)
    parts = [part for side in sides for part in side]
    return call(kernel, shape, [VMEM] * (3 + len(parts)), "log_factor")(*tables[4:], before, *parts)


def update_kernel(*refs, count):
    parts, out_ref, edge_refs = refs[:count], refs[count], refs[count + 1:]
    for p in range(out_ref.shape[0]):
        total = parts[0][p]
        for part in parts[1:]:
            total = total + part[p]
        out_ref[p] = jnp.exp(total)
    put_edges(out_ref, edge_refs)


def update(parts, radius):
    kernel = functools.partial(update_kernel, count=len(parts))
    out_shape = edge_shapes(parts[0].shape, radius, parts[0].shape[1:2])
    return call(kernel, out_shape, [VMEM] * len(parts), "update")(*parts)


def finish_kernel(*refs):
    own, other, out_ref = refs[:(len(refs) - 1) // 2], refs[(len(refs) - 1) // 2:-1], refs[-1]
    straight = core() == half()
    groups = out_ref.shape[1] // GROUP
    for group in range(groups):
        rows = slice(group * GROUP, (group + 1) * GROUP)
        own_total, other_total = own[0][:, rows, :], other[0][:, rows, :]
        for part in own[1:]:
            own_total = own_total + part[:, rows, :]
        for part in other[1:]:
            other_total = other_total + part[:, rows, :]
        start = jnp.where(core() == 0, group, groups - 1 - group) * GROUP
        out_ref[:, pl.ds(pl.multiple_of(start, GROUP), GROUP), :] = jnp.exp(jnp.where(straight, own_total, other_total))


def finish(own_parts, other_parts):
    shape = jax.ShapeDtypeStruct(own_parts[0].shape, F32)
    return call(finish_kernel, shape, [VMEM] * (2 * len(own_parts)), "last_update")(*own_parts, *other_parts)


def join_kernel(*refs, starts):
    sources, out_ref, semaphores = refs[:-2], refs[-2], refs[-1]
    cells_y = out_ref.shape[1]
    copies = []
    for index, source_ref in enumerate(sources):
        rows, start = source_ref.shape[1], starts[index // 2]
        side = core() if index % 2 == 0 else 1 - core()
        place = pl.multiple_of(jnp.where(side == 0, start, cells_y - start - rows), GROUP)
        target = out_ref.at[:, pl.ds(place, rows), :]
        copies.append(pltpu.make_async_copy(source_ref, target, semaphores.at[index]))
    for copy in copies:
        copy.start()
    for copy in copies:
        copy.wait()


def join(pieces, starts, shape):
    anywhere = pl.BlockSpec(memory_space=pl.ANY)
    return pl.pallas_call(
        functools.partial(join_kernel, starts=starts),
        out_shape=jax.ShapeDtypeStruct(shape, F32),
        in_specs=[anywhere] * len(pieces),
        out_specs=anywhere,
        scratch_shapes=[pltpu.SemaphoreType.DMA((len(pieces),))],
        compiler_params=PARAMS,
        name="join_halves",
    )(*pieces)


def shards(acquired, estimate, offsets, view_mask, kern_x, kern_y, kern_z):
    planes, cells_y, cells_z = estimate.shape
    views, slabs = lax.axis_size("view"), lax.axis_size("tile")
    groups = views // 2
    taps_y = kern_y.shape[1]
    radius = kern_x.shape[1] // 2
    own_rows = cells_y // 2
    near = own_rows + pad_to(taps_y // 2, GROUP)
    wide = own_rows + pad_to(2 * (taps_y // 2), GROUP)
    edge_rows = wide - own_rows
    inner_rows = own_rows - edge_rows
    group = lax.axis_index("view") // 2
    straight = core() == half()

    def across(turn, half_of=lambda r: r, core_of=lambda c: c, when=lambda c, r: True):
        return lambda g, c, q, r: ((g + turn) % groups, core_of(c), q, half_of(r)) if when(c, r) else None

    def neighbours(far, near):
        return send(far, to_far), send(near, to_core_partner)

    window, crossing = make_windows(estimate, wide)
    piece = lax.dynamic_slice_in_dim(crossing, group * (planes // groups), planes // groups, 0)
    piece = send(piece, across(0, lambda r: 1 - r, when=lambda c, r: c == r))

    acquired = after(acquired, window)
    first, second = shift_and_cut(offsets, acquired[0], view_mask[0], near)
    piece = after(piece, first)

    mine = [jnp.pad(row, ((0, 0), (0, 128 - row.shape[1]))) for row in (kern_x, kern_y, kern_z, offsets.astype(F32))]
    mine = jnp.concatenate(mine, axis=1)
    other = send(mine, to_core_partner)
    taps = kern_x.shape[1], taps_y, kern_z.shape[1]
    tables = make_tables(mine, other, taps, planes, cells_y, cells_z, (own_rows, near, wide))
    shifts = jnp.where(straight, jnp.concatenate([mine, other]), jnp.concatenate([other, mine]))
    shifts = shifts[:, 384:384 + offsets.shape[1]].astype(jnp.int32)

    arrived = send(first, lambda g, c, q, r: (g, r, q, c) if c != r else None)
    start = group * (planes // groups)
    share = jnp.where(straight, lax.dynamic_slice_in_dim(window, start, planes // groups, 0), piece)
    later = after(after(piece, tables[0]), share)
    pieces = [piece] + [send(later, across(turn, when=lambda c, r: c != r)) for turn in range(1, groups)]
    share = send(share, to_far)
    shares = [share] + [send(share, across(turn)) for turn in range(1, groups)]
    second = send(after(second, share), lambda g, c, q, r: (g, r, q, 1 - c))
    current, _, close = assemble(after(window, shares[-1]), pieces, radius)
    chunks = [(assemble_far(shares), blur_near(tables, current, send(close, to_core_partner)))]
    first = jnp.where(straight, first, arrived)
    blocks = [(*neighbours(block, block), block) for block in (first, second)]
    images = [None, None]

    row_chunks = [(inner_rows, edge_rows), (0, inner_rows)]
    share = 1.0 / groups
    wide_parts = [blur_far(tables, *chunk, radius) for chunk in chunks]
    blurred = [blur_yz([parts[order] for parts in wide_parts], tables, order) for order in range(2)]
    images, sides = [], []
    for order, chunk_sizes in enumerate(([own_rows], [edge_rows, inner_rows])):
        spread, *edges, image = first_ratio(
            shifts, blocks[order], blurred[order], tables, order, radius, chunk_sizes, planes * slabs, cells_y
        )
        images.append(image)
        sides.append([(*neighbours(*edges[k:k + 2]), spread) for k in range(0, len(edges), 2)])
    total = log_factor(tables, current, sides[0], [0], own_rows, (0, 0), share)
    totals = [
        log_factor(tables, total, [side], [1], rows, (start, start), 0)
        for (start, rows), side in zip(row_chunks, sides[1])
    ]

    for step in range(1, ITERS):
        chunks, before = [], []
        for total in totals:
            parts = [total] + [send(total, across(turn)) for turn in range(1, groups)]
            rows, distant, close = update(parts, radius)
            if total is totals[0]:
                beyond = send(rows, to_row_partner)
            distant, close = neighbours(distant, close)
            chunks.append((distant, blur_near(tables, rows, close)))
            before.append(rows)
        rest = planes - radius
        distant, close = neighbours(
            lax.dynamic_slice_in_dim(beyond, core() * rest, radius, 0),
            lax.dynamic_slice_in_dim(beyond, (1 - core()) * rest, radius, 0),
        )
        chunks.append((distant, blur_near(tables, beyond, close)))
        edge_parts, inner_parts, halo_parts = [blur_far(tables, *chunk, radius) for chunk in chunks]
        wides = [[parts[order] for parts in (inner_parts, edge_parts, halo_parts)] for order in range(2)]
        *spreads, edge_far, edge_near, inner_far, inner_near = next_ratio(
            images, wides, tables, radius, [edge_rows, inner_rows]
        )
        sides = [neighbours(edge_far, edge_near), neighbours(inner_far, inner_near)]
        totals = [
            log_factor(tables, estimate_rows, [(*side, spread) for spread in spreads], [0, 1], rows, (0, start), share)
            for (start, rows), side, estimate_rows in zip(row_chunks, sides, before)
        ]

    pieces = []
    for own in totals:
        other_parts = [
            send(own, across(turn, lambda r: 1 - r, lambda c: 1 - c, lambda c, r: c != r))
            for turn in reversed(range(groups))
        ]
        own_parts = [own] + [send(own, across(turn, when=lambda c, r: c == r)) for turn in range(1, groups)]
        mine = finish(own_parts, other_parts)
        pieces += [mine, send(mine, to_core_partner)]
    return join(pieces, [start for start, _ in row_chunks], estimate.shape)


def solution(mesh):
    in_specs = (
        P("view", "tile", None, None),
        P("tile", None, None),
        P("view", None),
        P("view", "tile", None),
        P("view", None),
        P("view", None),
        P("view", None),
    )
    out_specs = P("tile", None, None)
    return jax.shard_map(shards, mesh=mesh, in_specs=in_specs, out_specs=out_specs, check_vma=False)
```

```python
import functools
import typing

import jax
import jax.numpy as jnp
from jax import lax
from jax.experimental import pallas as pl
from jax.experimental.pallas import tpu as pltpu
from jax.sharding import PartitionSpec as P

ITERS = 2
AXES = ("view", "tile")
F32 = jnp.float32
BF16 = jnp.bfloat16
VMEM = pl.BlockSpec(memory_space=pltpu.VMEM)
SMEM = pl.BlockSpec(memory_space=pltpu.SMEM)
PARAMS = pltpu.CompilerParams(vmem_limit_bytes=12 * 1024 * 1024)
GROUP = 16


def moves(move):
    views, tiles = lax.axis_size("view"), lax.axis_size("tile")
    pairs = []
    for view in range(views):
        for tile in range(tiles):
            target = move(view // 2, view % 2, tile // 2, tile % 2)
            if target is not None:
                g, c, q, r = target
                pairs.append((view * tiles + tile, (2 * g + c) * tiles + 2 * q + r))
    return pairs


def send(array, move):
    return lax.ppermute(array, AXES, moves(move))


def after(array, other):
    return lax.optimization_barrier((array, other))[0]


def to_far(g, c, q, r):
    s = 2 * q + c + (1 if c else -1)
    return (g, s % 2, s // 2, r) if 0 <= s < lax.axis_size("tile") else None


def to_row_partner(g, c, q, r):
    return (g, c, q, 1 - r)


def to_core_partner(g, c, q, r):
    return (g, 1 - c, q, r)


def core():
    return lax.rem(lax.axis_index("view"), 2)


def half():
    return lax.rem(lax.axis_index("tile"), 2)


def split(x):
    high = x.astype(BF16)
    return high, (x - high.astype(F32)).astype(BF16)


def dot(a, b):
    return jnp.dot(a, b, preferred_element_type=F32)


def iota(shape, dim):
    return lax.broadcasted_iota(jnp.int32, shape, dim)


def group_row(half, group, cells_y):
    return group * GROUP + half * (cells_y - GROUP - 2 * group * GROUP)


def global_row(half, local, cells_y):
    group = local // GROUP
    return group_row(half, group, cells_y) + (local - group * GROUP)


def wide_local(place, own, wide):
    group = (place - own) // GROUP
    return own + (wide - own) - GROUP - group * GROUP + (place - own - group * GROUP)


def wide_group(group, own_groups, groups):
    return group if group < own_groups else own_groups + groups - 1 - group


def pad_to(value, unit):
    return -(-value // unit) * unit


def call(kernel, out_shape, in_specs, name, scratch=()):
    return pl.pallas_call(
        kernel,
        out_shape=out_shape,
        in_specs=in_specs,
        out_specs=jax.tree.map(lambda _: VMEM, out_shape),
        scratch_shapes=list(scratch),
        compiler_params=PARAMS,
        name=name,
    )


class Tables(typing.NamedTuple):
    whole: tuple
    inner: tuple
    edge: tuple
    z: tuple
    x: tuple


def place(row, count, width, turned, spacing):
    source, target = iota((row.shape[1], width), 0), iota((row.shape[1], width), 1)
    index = count - 1 - source if turned else source
    ones = (target == spacing * index) & (source < count)
    return jnp.dot(row, ones.astype(F32), precision=lax.Precision.HIGHEST, preferred_element_type=F32)


def tables_kernel(mine_ref, other_ref, *refs, blocks, sizes, cells_y, taps):
    y_refs, (zhi_ref, zlo_ref, xhi_ref, xlo_ref) = refs[:-4], refs[-4:]
    taps_x, taps_y, taps_z = taps
    straight = core() == half()
    mine, other = mine_ref[...], other_ref[...]
    both = (jnp.where(straight, mine, other), jnp.where(straight, other, mine))
    radius, radius_x, radius_z = taps_y // 2, taps_x // 2, taps_z // 2
    side = half()
    own, wide = sizes
    for out_ref, adjoint, first_row, first_col, width in zip(y_refs, *zip(*blocks)):
        _, rows, lanes = out_ref.shape
        row = global_row(side, first_row + iota((rows, lanes), 0), cells_y)
        lane = iota((rows, lanes), 1)
        place_of = lane + first_col
        turned = place_of if adjoint else jnp.where(place_of < own, place_of, wide_local(place_of, own, wide))
        col = global_row(side, turned, cells_y)
        delta = (row - col if adjoint else col - row) + radius
        delta = jnp.where(lane < width, delta, -1)
        for order in range(2):
            band = jnp.zeros((rows, lanes), F32)
            values = both[order][:, 128:256]
            for a in range(taps_y):
                band = jnp.where(delta == a, jnp.broadcast_to(values[:, a:a + 1], (rows, lanes)), band)
            high, low = split(band)
            high, low = high.astype(F32), low.astype(F32)
            out_ref[order] = (high + pltpu.roll(high, width, 1) + pltpu.roll(low, 2 * width, 1)).astype(BF16)

    lanes = zhi_ref.shape[2]
    near_z = jnp.abs(iota((lanes, lanes), 1) - iota((lanes, lanes), 0)) <= radius_z
    for index in range(4):
        base = place(both[index % 2][:, 256:384], taps_z, lanes, index < 2, 1)
        base = pltpu.roll(base, lanes - radius_z, 1)
        band = pltpu.roll(jnp.broadcast_to(base, (lanes, lanes)), 0, 1, stride=1, stride_axis=0)
        zhi_ref[index], zlo_ref[index] = split(jnp.where(near_z, band, jnp.zeros_like(band)))

    rows = xhi_ref.shape[1] // 2
    lanes = max(512, 1 << (xhi_ref.shape[2] - 1).bit_length())
    for index in range(4):
        base = place(both[index % 2][:, :128], taps_x, lanes, index >= 2, 8)
        base = jnp.broadcast_to(base, (rows, lanes))
        band = pltpu.roll(base, 0, 1, stride=1, stride_axis=0)
        lane = iota((rows, lanes), 1)
        edge = 8 * radius_x
        far = pad_to(rows + edge, 128)
        next_near = pltpu.roll(band, lanes - edge, 1)
        next_far = pltpu.roll(band, far - rows - edge, 1)
        near_part = jnp.where((lane < rows) | (core() == 0), next_near, pltpu.roll(band, rows, 1))
        far_part = jnp.where(core() == 0, pltpu.roll(band, far, 1), next_far)
        zero = jnp.zeros_like(band)
        band = jnp.where(
            lane < rows + edge, near_part, jnp.where((lane >= far) & (lane < far + edge), far_part, zero)
        )[:, :xhi_ref.shape[2]]
        block = (index // 2, slice(index % 2 * rows, index % 2 * rows + rows))
        xhi_ref[block], xlo_ref[block] = split(band)


def make_tables(mine, other, taps, planes, cells_y, cells_z, sizes):
    own, near, wide = sizes
    inner, beyond = 2 * own - wide, near - own
    radius = taps[0] // 2
    depth = pad_to(8 * (planes + radius), 128) + pad_to(8 * radius, 128)
    blocks = [
        (False, near, 0, 0, wide), (True, own, 0, 0, near),
        (False, inner + beyond, 0, 0, own), (True, inner, 0, 0, inner + beyond),
        (False, near - inner - beyond, inner + beyond, inner, wide - inner),
        (True, own - inner, inner, inner - beyond, near - inner + beyond),
    ]
    kernel = functools.partial(
        tables_kernel, blocks=[block[:1] + block[2:] for block in blocks], sizes=(own, wide), cells_y=cells_y, taps=taps
    )
    shape = jax.ShapeDtypeStruct
    out_shape = tuple(shape((2, block[1], pad_to(3 * block[4], 128)), BF16) for block in blocks) + (
        shape((4, cells_z, cells_z), BF16),
        shape((4, cells_z, cells_z), BF16),
        shape((2, 2 * 8 * planes, depth), BF16),
        shape((2, 2 * 8 * planes, depth), BF16),
    )
    tables = call(kernel, out_shape, [VMEM, VMEM], "band_matrices")(mine, other)
    whole, inner_rows, edge_rows = tables[0:2], tables[2:4], tables[4:6]
    return Tables(whole, inner_rows, edge_rows, tables[6:8], tables[8:10])


def window_kernel(estimate_ref, own_ref, other_ref):
    cells_y = estimate_ref.shape[1]
    groups = own_ref.shape[1] // GROUP
    for side, out_ref in ((half(), own_ref), (1 - half(), other_ref)):
        for group in range(groups):
            local = wide_group(group, cells_y // 2 // GROUP, groups)
            start = pl.multiple_of(group_row(side, local, cells_y), GROUP)
            out_ref[:, group * GROUP:(group + 1) * GROUP, :] = estimate_ref[:, pl.ds(start, GROUP), :]


def make_windows(estimate, wide):
    planes, _, cells_z = estimate.shape
    shape = jax.ShapeDtypeStruct((planes, wide, cells_z), F32)
    return call(window_kernel, (shape, shape), [VMEM], "estimate_windows")(estimate)


def put_edges(out_ref, edge_refs):
    end = out_ref.shape[1]
    for far_ref, near_ref in zip(edge_refs[::2], edge_refs[1::2]):
        radius, rows = far_ref.shape[0], slice(end - far_ref.shape[1], end)
        beyond = out_ref.shape[0] - radius
        for p in range(radius):
            far_ref[p] = out_ref[p + core() * beyond, rows]
            near_ref[p] = out_ref[p + (1 - core()) * beyond, rows]
        end -= far_ref.shape[1]


def choose_kernel(window_ref, crossed_ref, out_ref, *edge_refs):
    straight = core() == half()
    for p in range(out_ref.shape[0]):
        out_ref[p] = jnp.where(straight, window_ref[p], crossed_ref[p])
    put_edges(out_ref, edge_refs)


def edge_shapes(shape, radius, chunks):
    planes, _, lanes = shape
    edges = [jax.ShapeDtypeStruct((radius, rows, lanes), F32) for rows in chunks for _ in range(2)]
    return (jax.ShapeDtypeStruct(shape, F32), *edges)


def choose(window, crossed, radius):
    out_shape = edge_shapes(window.shape, radius, window.shape[1:2])
    return call(choose_kernel, out_shape, [VMEM] * 2, "estimate")(window, crossed)


def shift_kernel(offsets_ref, acq_ref, mask_ref, first_ref, second_ref, turned_ref):
    planes, cells_y, cells_z = acq_ref.shape
    near = first_ref.shape[1]
    shift_y, shift_z = offsets_ref[0, 1], offsets_ref[0, 2]
    row = iota((cells_y, cells_z), 0) + shift_y
    col = iota((cells_y, cells_z), 1) + shift_z
    inside = (row >= 0) & (row < cells_y) & (col >= 0) & (col < cells_z)
    turn_y = lax.rem(cells_y - shift_y, cells_y)
    turn_z = lax.rem(cells_z - shift_z, cells_z)

    def body(p, carry):
        x = pltpu.roll(pltpu.roll(acq_ref[p], turn_z, 1), turn_y, 0)
        turned_ref[...] = jnp.where(inside, x, jnp.zeros_like(x))
        for side, out_ref in ((core(), first_ref), (1 - core(), second_ref)):
            for group in range(near // GROUP):
                start = pl.multiple_of(group_row(side, group, cells_y), GROUP)
                out_ref[p, group * GROUP:(group + 1) * GROUP, :] = turned_ref[pl.ds(start, GROUP), :]
        return carry

    lax.fori_loop(0, planes, body, 0)
    mask = mask_ref[...].astype(F32)
    for out_ref in (first_ref, second_ref):
        out_ref[planes] = jnp.zeros((near, cells_z), F32)
        out_ref[planes, :planes, :cells_y] = mask


def shift_and_cut(offsets, acquired, mask, near):
    planes, cells_y, cells_z = acquired.shape
    shape = jax.ShapeDtypeStruct((planes + 1, near, cells_z), F32)
    scratch = [pltpu.VMEM((cells_y, cells_z), F32)]
    return call(shift_kernel, (shape, shape), [SMEM, VMEM, VMEM], "shift_recorded", scratch)(offsets, acquired, mask)


def gather(ref, row):
    return ref[:, pl.ds(pl.multiple_of(row, 8), 8), :]


def spread_x(hi_ref, lo_ref, index, band_rows, band_lanes, blocks):
    lanes = blocks[0][0].shape[2]
    filled = []
    for parts in blocks:
        count = 8 * sum(part.shape[0] for part in parts)
        missing = (pad_to(count, 128) - count) // 8
        filled += list(parts) + ([jnp.zeros((missing, 8, lanes), F32)] if missing else [])
    high, low = split(jnp.concatenate(filled, axis=0).reshape(-1, lanes))
    band = hi_ref[index, band_rows, band_lanes]
    out = dot(band, high) + (dot(band, low) + dot(lo_ref[index, band_rows, band_lanes], high))
    return out.reshape(-1, 8, lanes)


def near_lanes(planes, radius):
    return pad_to(8 * (planes + radius), 128)


def blur_near_kernel(hi_ref, lo_ref, own_ref, near_ref, first_ref, second_ref):
    planes, rows, _ = own_ref.shape
    lanes = slice(0, near_lanes(planes, near_ref.shape[0]))

    def body(step, carry):
        row = pl.multiple_of(step * 8, 8)
        block = [gather(own_ref, row), gather(near_ref, row)]
        out = spread_x(hi_ref, lo_ref, 0, slice(None), lanes, [block])
        first_ref[:, pl.ds(row, 8), :] = out[:planes]
        second_ref[:, pl.ds(row, 8), :] = out[planes:]
        return carry

    lax.fori_loop(0, rows // 8, body, 0)


def blur_far_kernel(hi_ref, lo_ref, far_ref, first_ref, second_ref, first_out, second_out):
    planes, rows, _ = first_ref.shape
    lanes = slice(near_lanes(planes, far_ref.shape[0]), None)

    def body(step, carry):
        row = pl.multiple_of(step * 8, 8)
        place = (slice(None), pl.ds(row, 8), slice(None))
        out = spread_x(hi_ref, lo_ref, 0, slice(None), lanes, [[gather(far_ref, row)]])
        first_out[place] = first_ref[place] + out[:planes]
        second_out[place] = second_ref[place] + out[planes:]
        return carry

    lax.fori_loop(0, rows // 8, body, 0)


def blur_near(tables, own, near):
    shape = jax.ShapeDtypeStruct(own.shape, F32)
    return call(blur_near_kernel, (shape, shape), [VMEM] * 4, "blur_x_near")(*tables.x, own, near)


def blur_far(tables, far, parts):
    shape = jax.ShapeDtypeStruct(parts[0].shape, F32)
    return call(blur_far_kernel, (shape, shape), [VMEM] * 5, "blur_x_far")(*tables.x, far, *parts)


def spread_y(band, x):
    high, low = split(x)
    parts = [high, low, high]
    rest = band.shape[1] - 3 * x.shape[0]
    if rest:
        parts.append(jnp.zeros((rest, x.shape[1]), BF16))
    return dot(band, jnp.concatenate(parts, axis=0))


def spread_z(x, hi_ref, lo_ref, index):
    high, low = split(x)
    return dot(high, hi_ref[index]) + (dot(low, hi_ref[index]) + dot(high, lo_ref[index]))


def blurred_planes(wide_refs, yf_ref, zhi_ref, zlo_ref, order, block):
    wide = [jnp.concatenate([ref[p] for ref in wide_refs], axis=0) for p in block]
    spread = jnp.concatenate([spread_y(yf_ref[order], rows) for rows in wide], axis=0)
    return spread_z(spread, zhi_ref, zlo_ref, order)


def plane_blocks(planes, step=4):
    return [range(start, min(start + step, planes)) for start in range(0, planes, step)]


def blur_yz_kernel(*refs, order):
    wide_refs, (yf_ref, zhi_ref, zlo_ref, out_ref) = refs[:-4], refs[-4:]
    near = yf_ref.shape[1]
    for block in plane_blocks(out_ref.shape[0]):
        blurred = blurred_planes(wide_refs, yf_ref, zhi_ref, zlo_ref, order, block)
        for k, p in enumerate(block):
            out_ref[p] = blurred[k * near:(k + 1) * near]


def blur_yz(wides, tables, order):
    planes, _, lanes = wides[0].shape
    shape = jax.ShapeDtypeStruct((planes, tables.whole[0].shape[1], lanes), F32)
    kernel = functools.partial(blur_yz_kernel, order=order)
    return call(kernel, shape, [VMEM] * (3 + len(wides)), "blur_yz")(*wides, tables.whole[0], *tables.z)


def adjoint_planes(blurred_of, image_of, ya_ref, zhi_ref, zlo_ref, order, out_ref, edge_refs, complete=None):
    planes, rows, _ = out_ref.shape
    for block in plane_blocks(planes):
        blurred = blurred_of(block)
        image = jnp.concatenate([image_of(p) for p in block], axis=0)
        ratio = jnp.where(image >= 0, image / blurred, jnp.ones_like(image))
        near = ratio.shape[0] // len(block)
        ratios = [ratio[k * near:(k + 1) * near] for k in range(len(block))]
        if complete:
            ratios = [complete(p, rows_of) for p, rows_of in zip(block, ratios)]
        spread = jnp.concatenate([spread_y(ya_ref[order], rows_of) for rows_of in ratios], axis=0)
        spread = spread_z(spread, zhi_ref, zlo_ref, 2 + order)
        for k, p in enumerate(block):
            out_ref[p] = spread[k * rows:(k + 1) * rows]
    put_edges(out_ref, edge_refs)


def first_ratio_kernel(
    shift_ref, far_ref, near_ref, own_ref, blurred_ref, ya_ref, zhi_ref, zlo_ref, out_ref, *refs, order, extent_x, cells_y
):
    edge_refs, image_ref, (mine_ref, beyond_ref, semaphores) = refs[:-4], refs[-4], refs[-3:]
    planes, near, cells_z = image_ref.shape
    side = half()
    slab = lax.axis_index("tile") - side + core()
    shift_x, shift_y, shift_z = (shift_ref[order, i] for i in range(3))
    lanes = pad_to(cells_y, 128)
    pick = iota((near, lanes), 1) == global_row(side, iota((near, lanes), 0), cells_y)
    is_far = (shift_x > 0) == (core() == 1)
    copy = pltpu.make_async_copy(own_ref, mine_ref, semaphores.at[0])
    far_copy = pltpu.make_async_copy(far_ref.at[pl.ds(0, planes)], beyond_ref, semaphores.at[1])
    near_copy = pltpu.make_async_copy(near_ref.at[pl.ds(0, planes)], beyond_ref, semaphores.at[1])
    copy.start()
    pl.when(is_far)(far_copy.start)
    pl.when(jnp.logical_not(is_far))(near_copy.start)
    copy.wait()
    far_copy.wait()
    mask = mine_ref[planes, :planes, :lanes].astype(BF16)
    columns = lax.dot_general(
        pick.astype(F32).astype(BF16), mask, (((1,), (1,)), ((), ())), preferred_element_type=F32
    )
    row = global_row(side, iota((near, cells_z), 0), cells_y) + shift_y
    col = iota((near, cells_z), 1) + shift_z
    inside = (row >= 0) & (row < cells_y) & (col >= 0) & (col < cells_z)

    def fetch(p):
        source = p + shift_x
        x = slab * planes + source
        is_own = (source >= 0) & (source < planes)
        beyond = jnp.clip(jnp.where(source < 0, source + planes, source - planes), 0, planes - 1)
        value = jnp.where(is_own, mine_ref[jnp.clip(source, 0, planes - 1)], beyond_ref[beyond])
        weight = jnp.broadcast_to(columns[:, p:p + 1], (near, cells_z))
        covered = inside & (weight > 0.5) & (x >= 0) & (x < extent_x)
        value = jnp.where(covered, value, jnp.full_like(value, -1.0))
        image_ref[p] = value
        return value

    def blurred_of(block):
        return jnp.concatenate([blurred_ref[p] for p in block], axis=0)

    adjoint_planes(blurred_of, fetch, ya_ref, zhi_ref, zlo_ref, order, out_ref, edge_refs)


def next_ratio_kernel(*refs, inner, count, first_row):
    image_refs, wide_refs, refs = refs[:2], (refs[2:4], refs[4:6]), refs[6:]
    passed_ref, refs = (None, refs) if inner else (refs[0], refs[1:])
    (yf_ref, ya_ref, zhi_ref, zlo_ref), out_refs, (far_ref, near_ref), refs = refs[:4], refs[4:6], refs[6:8], refs[8:]
    planes = out_refs[0].shape[0]
    rows = yf_ref.shape[1]
    for order in range(2):

        def blurred_of(block):
            return blurred_planes(wide_refs[order], yf_ref, zhi_ref, zlo_ref, order, block)

        def image_of(p):
            return image_refs[order][p, first_row:first_row + rows]

        def complete(p, ratio):
            if inner:
                refs[0][order, p] = ratio[rows - count:]
                return ratio
            return jnp.concatenate([passed_ref[order, p], ratio], axis=0)

        edges = (far_ref.at[order], near_ref.at[order])
        adjoint_planes(blurred_of, image_of, ya_ref, zhi_ref, zlo_ref, order, out_refs[order], edges, complete)


def next_ratio(images, wides, passed, y_tables, z_tables, radius, count, first_row):
    planes, _, lanes = images[0].shape
    rows = y_tables[1].shape[1]
    kernel = functools.partial(next_ratio_kernel, inner=passed is None, count=count, first_row=first_row)
    shape = jax.ShapeDtypeStruct
    whole, edge = shape((planes, rows, lanes), F32), shape((2, radius, rows, lanes), F32)
    out_shape = (whole, whole, edge, edge)
    if passed is None:
        out_shape += (shape((2, planes, count, lanes), F32),)
    operands = [*images, *wides[0], *wides[1]] + ([] if passed is None else [passed]) + [*y_tables, *z_tables]
    return call(kernel, out_shape, [VMEM] * len(operands), "ratio")(*operands)


def first_ratio(shifts, blocks, blurred, tables, order, radius, chunks, extent_x, cells_y):
    planes, near, lanes = blurred.shape
    kernel = functools.partial(first_ratio_kernel, order=order, extent_x=extent_x, cells_y=cells_y)
    rows = tables.whole[1].shape[1]
    out_shape = edge_shapes((planes, rows, lanes), radius, chunks) + (jax.ShapeDtypeStruct(blurred.shape, F32),)
    scratch = [
        pltpu.VMEM((planes + 1, near, lanes), F32), pltpu.VMEM(blurred.shape, F32), pltpu.SemaphoreType.DMA((2,))
    ]
    in_specs = [SMEM] + [pl.BlockSpec(memory_space=pl.ANY)] * 3 + [VMEM] * 4
    return call(kernel, out_shape, in_specs, "image_and_ratio", scratch)(
        shifts, *blocks, blurred, tables.whole[1], *tables.z
    )


def factor_kernel(hi_ref, lo_ref, before_ref, *refs, orders, starts, share):
    out_ref = refs[-1]
    planes, rows, _ = out_ref.shape

    def body(step, carry):
        row = pl.multiple_of(step * 8, 8)
        total = gather(before_ref, starts[0] + row)
        if share:
            total = share * jnp.log(total)
        for index, order in enumerate(orders):
            far_ref, near_ref, own_ref = refs[3 * index:3 * index + 3]
            if len(far_ref.shape) == 4:
                far_ref, near_ref = far_ref.at[order], near_ref.at[order]
            own = gather(own_ref, starts[1] + row)
            blocks = [[own, gather(near_ref, row)], [gather(far_ref, row)]]
            band_rows = slice(order * 8 * planes, (order + 1) * 8 * planes)
            total = total + jnp.log(spread_x(hi_ref, lo_ref, 1, band_rows, slice(None), blocks))
        out_ref[:, pl.ds(row, 8), :] = total
        return carry

    lax.fori_loop(0, rows // 8, body, 0)


def log_factor(tables, before, sides, orders, rows, starts, share):
    kernel = functools.partial(factor_kernel, orders=orders, starts=starts, share=share)
    planes, _, lanes = sides[0][2].shape
    shape = jax.ShapeDtypeStruct((planes, rows, lanes), F32)
    parts = [part for side in sides for part in side]
    return call(kernel, shape, [VMEM] * (3 + len(parts)), "log_factor")(*tables.x, before, *parts)


def update_kernel(*refs, count):
    parts, out_ref, edge_refs = refs[:count], refs[count], refs[count + 1:]
    for p in range(out_ref.shape[0]):
        total = parts[0][p]
        for part in parts[1:]:
            total = total + part[p]
        out_ref[p] = jnp.exp(total)
    put_edges(out_ref, edge_refs)


def update(parts, radius):
    kernel = functools.partial(update_kernel, count=len(parts))
    out_shape = edge_shapes(parts[0].shape, radius, parts[0].shape[1:2])
    return call(kernel, out_shape, [VMEM] * len(parts), "update")(*parts)


def finish_kernel(*refs):
    own, other, out_ref = refs[:(len(refs) - 1) // 2], refs[(len(refs) - 1) // 2:-1], refs[-1]
    straight = core() == half()
    groups = out_ref.shape[1] // GROUP
    for group in range(groups):
        rows = slice(group * GROUP, (group + 1) * GROUP)
        own_total, other_total = own[0][:, rows, :], other[0][:, rows, :]
        for part in own[1:]:
            own_total = own_total + part[:, rows, :]
        for part in other[1:]:
            other_total = other_total + part[:, rows, :]
        start = jnp.where(core() == 0, group, groups - 1 - group) * GROUP
        out_ref[:, pl.ds(pl.multiple_of(start, GROUP), GROUP), :] = jnp.exp(jnp.where(straight, own_total, other_total))


def finish(own_parts, other_parts):
    shape = jax.ShapeDtypeStruct(own_parts[0].shape, F32)
    return call(finish_kernel, shape, [VMEM] * (2 * len(own_parts)), "last_update")(*own_parts, *other_parts)


def join_kernel(*refs, starts):
    sources, out_ref, semaphores = refs[:-2], refs[-2], refs[-1]
    cells_y = out_ref.shape[1]
    copies = []
    for index, source_ref in enumerate(sources):
        rows, start = source_ref.shape[1], starts[index // 2]
        side = core() if index % 2 == 0 else 1 - core()
        place = pl.multiple_of(jnp.where(side == 0, start, cells_y - start - rows), GROUP)
        target = out_ref.at[:, pl.ds(place, rows), :]
        copies.append(pltpu.make_async_copy(source_ref, target, semaphores.at[index]))
    for copy in copies:
        copy.start()
    for copy in copies:
        copy.wait()


def join(pieces, starts, shape):
    anywhere = pl.BlockSpec(memory_space=pl.ANY)
    return pl.pallas_call(
        functools.partial(join_kernel, starts=starts),
        out_shape=jax.ShapeDtypeStruct(shape, F32),
        in_specs=[anywhere] * len(pieces),
        out_specs=anywhere,
        scratch_shapes=[pltpu.SemaphoreType.DMA((len(pieces),))],
        compiler_params=PARAMS,
        name="join_halves",
    )(*pieces)


def shards(acquired, estimate, offsets, view_mask, kern_x, kern_y, kern_z):
    planes, cells_y, cells_z = estimate.shape
    views, slabs = lax.axis_size("view"), lax.axis_size("tile")
    groups = views // 2
    taps_y = kern_y.shape[1]
    radius = kern_x.shape[1] // 2
    own_rows = cells_y // 2
    near = own_rows + pad_to(taps_y // 2, GROUP)
    wide = own_rows + pad_to(2 * (taps_y // 2), GROUP)
    edge_rows = wide - own_rows
    inner_rows = own_rows - edge_rows
    group = lax.axis_index("view") // 2
    straight = core() == half()

    def across(turn, half_of=lambda r: r, core_of=lambda c: c, when=lambda c, r: True):
        return lambda g, c, q, r: ((g + turn) % groups, core_of(c), q, half_of(r)) if when(c, r) else None

    def neighbours(far, near):
        return send(far, to_far), send(near, to_core_partner)

    window, crossed = make_windows(estimate, wide)
    crossed = send(crossed, across(0, lambda r: 1 - r, when=lambda c, r: c == r))

    acquired = after(acquired, window)
    first, second = shift_and_cut(offsets, acquired[0], view_mask[0], near)

    mine = [jnp.pad(row, ((0, 0), (0, 128 - row.shape[1]))) for row in (kern_x, kern_y, kern_z, offsets.astype(F32))]
    mine = jnp.concatenate(mine, axis=1)
    other = send(mine, to_core_partner)
    taps = kern_x.shape[1], taps_y, kern_z.shape[1]
    tables = make_tables(mine, other, taps, planes, cells_y, cells_z, (own_rows, near, wide))
    shifts = jnp.where(straight, jnp.concatenate([mine, other]), jnp.concatenate([other, mine]))
    shifts = shifts[:, 384:384 + offsets.shape[1]].astype(jnp.int32)

    arrived = send(first, lambda g, c, q, r: (g, r, q, c) if c != r else None)
    current, distant, close = choose(after(after(window, first), tables.whole[0]), crossed, radius)
    distant = send(distant, to_far)
    second = send(after(second, current), lambda g, c, q, r: (g, r, q, 1 - c))
    first = jnp.where(straight, first, arrived)
    close = send(after(close, distant), to_core_partner)
    blocks = [(*neighbours(block, block), block) for block in (first, second)]
    wide_parts = blur_far(tables, distant, blur_near(tables, current, close))
    blurred = [blur_yz([part], tables, order) for order, part in enumerate(wide_parts)]

    row_chunks = [(inner_rows, edge_rows), (0, inner_rows)]
    share = 1.0 / groups
    images, sides = [], []
    for order, chunk_sizes in enumerate(([own_rows], [edge_rows, inner_rows])):
        spread, *edges, image = first_ratio(
            shifts, blocks[order], blurred[order], tables, order, radius, chunk_sizes, planes * slabs, cells_y
        )
        images.append(image)
        sides.append([(*neighbours(*edges[k:k + 2]), spread) for k in range(0, len(edges), 2)])
    total = log_factor(tables, current, sides[0], [0], own_rows, (0, 0), share)
    totals = [
        log_factor(tables, total, [side], [1], rows, (start, start), 0)
        for (start, rows), side in zip(row_chunks, sides[1])
    ]

    for step in range(1, ITERS):
        chunks, before = [], []
        for total in totals:
            parts = [total] + [send(total, across(turn)) for turn in range(1, groups)]
            if chunks:
                parts[-1] = after(parts[-1], chunks[0][0])
            rows, distant, close = update(parts, radius)
            if total is totals[0]:
                beyond = send(rows, to_row_partner)
            distant, close = neighbours(distant, close)
            chunks.append((distant, blur_near(tables, rows, close)))
            before.append(rows)
        rest = planes - radius
        distant, close = neighbours(
            lax.dynamic_slice_in_dim(beyond, core() * rest, radius, 0),
            lax.dynamic_slice_in_dim(beyond, (1 - core()) * rest, radius, 0),
        )
        edge_parts, inner_parts = [blur_far(tables, *chunk) for chunk in chunks]
        *inner_spreads, distant_inner, close_inner, passed = next_ratio(
            images, list(zip([after(after(part, distant), close) for part in inner_parts], edge_parts)), None, tables.inner, tables.z, radius, 2 * (near - own_rows), 0
        )
        halo_parts = blur_far(tables, distant, blur_near(tables, beyond, close))
        inner_side = neighbours(distant_inner, close_inner)
        *edge_spreads, distant, close = next_ratio(
            images, list(zip(edge_parts, halo_parts)), passed, tables.edge, tables.z, radius, 0,
            inner_rows + near - own_rows,
        )
        edge_side = neighbours(distant, close)
        totals = [
            log_factor(tables, rows_of, [(*side, spread) for spread in spreads], [0, 1], rows, (0, 0), share)
            for rows_of, side, spreads, rows in (
                (before[0], edge_side, edge_spreads, edge_rows), (before[1], inner_side, inner_spreads, inner_rows)
            )
        ]

    pieces = []
    for own in totals[::-1]:
        other_parts = [
            send(own, across(turn, lambda r: 1 - r, lambda c: 1 - c, lambda c, r: c != r))
            for turn in reversed(range(groups))
        ]
        own_parts = [own] + [send(own, across(turn, when=lambda c, r: c == r)) for turn in range(1, groups)]
        mine = finish(own_parts, other_parts)
        pieces += [mine, send(mine, to_core_partner)]
    return join(pieces, [start for start, _ in row_chunks[::-1]], estimate.shape)


def solution(mesh):
    in_specs = (
        P("view", "tile", None, None),
        P("tile", None, None),
        P("view", None),
        P("view", "tile", None),
        P("view", None),
        P("view", None),
        P("view", None),
    )
    out_specs = P("tile", None, None)
    return jax.shard_map(shards, mesh=mesh, in_specs=in_specs, out_specs=out_specs, check_vma=False)
```

```python
import functools
import typing

import jax
import jax.numpy as jnp
from jax import lax
from jax.experimental import pallas as pl
from jax.experimental.pallas import tpu as pltpu
from jax.sharding import PartitionSpec as P

ITERS = 2
AXES = ("view", "tile")
F32 = jnp.float32
BF16 = jnp.bfloat16
VMEM = pl.BlockSpec(memory_space=pltpu.VMEM)
SMEM = pl.BlockSpec(memory_space=pltpu.SMEM)
PARAMS = pltpu.CompilerParams(vmem_limit_bytes=12 * 1024 * 1024)
GROUP = 16


def moves(move):
    views, tiles = lax.axis_size("view"), lax.axis_size("tile")
    pairs = []
    for view in range(views):
        for tile in range(tiles):
            target = move(view // 2, view % 2, tile // 2, tile % 2)
            if target is not None:
                g, c, q, r = target
                pairs.append((view * tiles + tile, (2 * g + c) * tiles + 2 * q + r))
    return pairs


def send(array, move):
    return lax.ppermute(array, AXES, moves(move))


def after(array, other):
    return lax.optimization_barrier((array, other))[0]


def to_far(g, c, q, r):
    s = 2 * q + c + (1 if c else -1)
    return (g, s % 2, s // 2, r) if 0 <= s < lax.axis_size("tile") else None


def to_row_partner(g, c, q, r):
    return (g, c, q, 1 - r)


def to_core_partner(g, c, q, r):
    return (g, 1 - c, q, r)


def core():
    return lax.rem(lax.axis_index("view"), 2)


def half():
    return lax.rem(lax.axis_index("tile"), 2)


def split(x):
    high = x.astype(BF16)
    return high, (x - high.astype(F32)).astype(BF16)


def dot(a, b):
    return jnp.dot(a, b, preferred_element_type=F32)


def iota(shape, dim):
    return lax.broadcasted_iota(jnp.int32, shape, dim)


def group_row(half, group, cells_y):
    return group * GROUP + half * (cells_y - GROUP - 2 * group * GROUP)


def global_row(half, local, cells_y):
    group = local // GROUP
    return group_row(half, group, cells_y) + (local - group * GROUP)


def wide_local(place, own, wide):
    group = (place - own) // GROUP
    return own + (wide - own) - GROUP - group * GROUP + (place - own - group * GROUP)


def wide_group(group, own_groups, groups):
    return group if group < own_groups else own_groups + groups - 1 - group


def pad_to(value, unit):
    return -(-value // unit) * unit


def call(kernel, out_shape, in_specs, name, scratch=()):
    return pl.pallas_call(
        kernel,
        out_shape=out_shape,
        in_specs=in_specs,
        out_specs=jax.tree.map(lambda _: VMEM, out_shape),
        scratch_shapes=list(scratch),
        compiler_params=PARAMS,
        name=name,
    )


class Tables(typing.NamedTuple):
    whole: tuple
    inner: tuple
    edge: tuple
    z: tuple
    x: tuple


def place(row, count, width, turned, spacing):
    source, target = iota((row.shape[1], width), 0), iota((row.shape[1], width), 1)
    index = count - 1 - source if turned else source
    ones = (target == spacing * index) & (source < count)
    return jnp.dot(row, ones.astype(F32), precision=lax.Precision.HIGHEST, preferred_element_type=F32)


def tables_kernel(mine_ref, other_ref, *refs, blocks, sizes, cells_y, taps):
    y_refs, (zhi_ref, zlo_ref, xhi_ref, xlo_ref) = refs[:-4], refs[-4:]
    taps_x, taps_y, taps_z = taps
    straight = core() == half()
    mine, other = mine_ref[...], other_ref[...]
    both = (jnp.where(straight, mine, other), jnp.where(straight, other, mine))
    radius, radius_x, radius_z = taps_y // 2, taps_x // 2, taps_z // 2
    side = half()
    own, wide = sizes
    for out_ref, adjoint, first_row, first_col, width in zip(y_refs, *zip(*blocks)):
        _, rows, lanes = out_ref.shape
        row = global_row(side, first_row + iota((rows, lanes), 0), cells_y)
        lane = iota((rows, lanes), 1)
        place_of = lane + first_col
        turned = place_of if adjoint else jnp.where(place_of < own, place_of, wide_local(place_of, own, wide))
        col = global_row(side, turned, cells_y)
        delta = (row - col if adjoint else col - row) + radius
        delta = jnp.where(lane < width, delta, -1)
        for order in range(2):
            band = jnp.zeros((rows, lanes), F32)
            values = both[order][:, 128:256]
            for a in range(taps_y):
                band = jnp.where(delta == a, jnp.broadcast_to(values[:, a:a + 1], (rows, lanes)), band)
            high, low = split(band)
            high, low = high.astype(F32), low.astype(F32)
            out_ref[order] = (high + pltpu.roll(high, width, 1) + pltpu.roll(low, 2 * width, 1)).astype(BF16)

    lanes = zhi_ref.shape[2]
    near_z = jnp.abs(iota((lanes, lanes), 1) - iota((lanes, lanes), 0)) <= radius_z
    for index in range(4):
        base = place(both[index % 2][:, 256:384], taps_z, lanes, index < 2, 1)
        base = pltpu.roll(base, lanes - radius_z, 1)
        band = pltpu.roll(jnp.broadcast_to(base, (lanes, lanes)), 0, 1, stride=1, stride_axis=0)
        zhi_ref[index], zlo_ref[index] = split(jnp.where(near_z, band, jnp.zeros_like(band)))

    rows = xhi_ref.shape[1] // 2
    lanes = max(512, 1 << (xhi_ref.shape[2] - 1).bit_length())
    for index in range(4):
        base = place(both[index % 2][:, :128], taps_x, lanes, index >= 2, 8)
        base = jnp.broadcast_to(base, (rows, lanes))
        band = pltpu.roll(base, 0, 1, stride=1, stride_axis=0)
        lane = iota((rows, lanes), 1)
        edge = 8 * radius_x
        far = pad_to(rows + edge, 128)
        next_near = pltpu.roll(band, lanes - edge, 1)
        next_far = pltpu.roll(band, far - rows - edge, 1)
        near_part = jnp.where((lane < rows) | (core() == 0), next_near, pltpu.roll(band, rows, 1))
        far_part = jnp.where(core() == 0, pltpu.roll(band, far, 1), next_far)
        zero = jnp.zeros_like(band)
        band = jnp.where(
            lane < rows + edge, near_part, jnp.where((lane >= far) & (lane < far + edge), far_part, zero)
        )[:, :xhi_ref.shape[2]]
        block = (index // 2, slice(index % 2 * rows, index % 2 * rows + rows))
        xhi_ref[block], xlo_ref[block] = split(band)


def make_tables(mine, other, taps, planes, cells_y, cells_z, sizes):
    own, near, wide = sizes
    inner, beyond = 2 * own - wide, near - own
    radius = taps[0] // 2
    depth = pad_to(8 * (planes + radius), 128) + pad_to(8 * radius, 128)
    blocks = [
        (False, near, 0, 0, wide), (True, own, 0, 0, near),
        (False, inner + beyond, 0, 0, own), (True, inner, 0, 0, inner + beyond),
        (False, near - inner - beyond, inner + beyond, inner, wide - inner),
        (True, own - inner, inner, inner - beyond, near - inner + beyond),
    ]
    kernel = functools.partial(
        tables_kernel, blocks=[block[:1] + block[2:] for block in blocks], sizes=(own, wide), cells_y=cells_y, taps=taps
    )
    shape = jax.ShapeDtypeStruct
    out_shape = tuple(shape((2, block[1], pad_to(3 * block[4], 128)), BF16) for block in blocks) + (
        shape((4, cells_z, cells_z), BF16),
        shape((4, cells_z, cells_z), BF16),
        shape((2, 2 * 8 * planes, depth), BF16),
        shape((2, 2 * 8 * planes, depth), BF16),
    )
    tables = call(kernel, out_shape, [VMEM, VMEM], "band_matrices")(mine, other)
    whole, inner_rows, edge_rows = tables[0:2], tables[2:4], tables[4:6]
    return Tables(whole, inner_rows, edge_rows, tables[6:8], tables[8:10])


def window_kernel(estimate_ref, own_ref, other_ref):
    cells_y = estimate_ref.shape[1]
    groups = own_ref.shape[1] // GROUP
    for side, out_ref in ((half(), own_ref), (1 - half(), other_ref)):
        for group in range(groups):
            local = wide_group(group, cells_y // 2 // GROUP, groups)
            start = pl.multiple_of(group_row(side, local, cells_y), GROUP)
            out_ref[:, group * GROUP:(group + 1) * GROUP, :] = estimate_ref[:, pl.ds(start, GROUP), :]


def make_windows(estimate, wide):
    planes, _, cells_z = estimate.shape
    shape = jax.ShapeDtypeStruct((planes, wide, cells_z), F32)
    return call(window_kernel, (shape, shape), [VMEM], "estimate_windows")(estimate)


def put_edges(out_ref, edge_refs):
    end = out_ref.shape[1]
    for far_ref, near_ref in zip(edge_refs[::2], edge_refs[1::2]):
        radius, rows = far_ref.shape[0], slice(end - far_ref.shape[1], end)
        beyond = out_ref.shape[0] - radius
        for p in range(radius):
            far_ref[p] = out_ref[p + core() * beyond, rows]
            near_ref[p] = out_ref[p + (1 - core()) * beyond, rows]
        end -= far_ref.shape[1]


def choose_kernel(window_ref, crossed_ref, out_ref, *edge_refs):
    straight = core() == half()
    for p in range(out_ref.shape[0]):
        out_ref[p] = jnp.where(straight, window_ref[p], crossed_ref[p])
    put_edges(out_ref, edge_refs)


def edge_shapes(shape, radius, chunks):
    planes, _, lanes = shape
    edges = [jax.ShapeDtypeStruct((radius, rows, lanes), F32) for rows in chunks for _ in range(2)]
    return (jax.ShapeDtypeStruct(shape, F32), *edges)


def choose(window, crossed, radius):
    out_shape = edge_shapes(window.shape, radius, window.shape[1:2])
    return call(choose_kernel, out_shape, [VMEM] * 2, "estimate")(window, crossed)


def shift_kernel(offsets_ref, acq_ref, mask_ref, first_ref, second_ref, turned_ref):
    planes, cells_y, cells_z = acq_ref.shape
    near = first_ref.shape[1]
    shift_y, shift_z = offsets_ref[0, 1], offsets_ref[0, 2]
    row = iota((cells_y, cells_z), 0) + shift_y
    col = iota((cells_y, cells_z), 1) + shift_z
    inside = (row >= 0) & (row < cells_y) & (col >= 0) & (col < cells_z)
    turn_y = lax.rem(cells_y - shift_y, cells_y)
    turn_z = lax.rem(cells_z - shift_z, cells_z)

    def body(p, carry):
        x = pltpu.roll(pltpu.roll(acq_ref[p], turn_z, 1), turn_y, 0)
        turned_ref[...] = jnp.where(inside, x, jnp.zeros_like(x))
        for side, out_ref in ((core(), first_ref), (1 - core(), second_ref)):
            for group in range(near // GROUP):
                start = pl.multiple_of(group_row(side, group, cells_y), GROUP)
                out_ref[p, group * GROUP:(group + 1) * GROUP, :] = turned_ref[pl.ds(start, GROUP), :]
        return carry

    lax.fori_loop(0, planes, body, 0)
    mask = mask_ref[...].astype(F32)
    for out_ref in (first_ref, second_ref):
        out_ref[planes] = jnp.zeros((near, cells_z), F32)
        out_ref[planes, :planes, :cells_y] = mask


def shift_and_cut(offsets, acquired, mask, near):
    planes, cells_y, cells_z = acquired.shape
    shape = jax.ShapeDtypeStruct((planes + 1, near, cells_z), F32)
    scratch = [pltpu.VMEM((cells_y, cells_z), F32)]
    return call(shift_kernel, (shape, shape), [SMEM, VMEM, VMEM], "shift_recorded", scratch)(offsets, acquired, mask)


def gather(ref, row):
    return ref[:, pl.ds(pl.multiple_of(row, 8), 8), :]


def spread_x(hi_ref, lo_ref, index, band_rows, band_lanes, blocks):
    lanes = blocks[0][0].shape[2]
    filled = []
    for parts in blocks:
        count = 8 * sum(part.shape[0] for part in parts)
        missing = (pad_to(count, 128) - count) // 8
        filled += list(parts) + ([jnp.zeros((missing, 8, lanes), F32)] if missing else [])
    high, low = split(jnp.concatenate(filled, axis=0).reshape(-1, lanes))
    band = hi_ref[index, band_rows, band_lanes]
    out = dot(band, high) + (dot(band, low) + dot(lo_ref[index, band_rows, band_lanes], high))
    return out.reshape(-1, 8, lanes)


def near_lanes(planes, radius):
    return pad_to(8 * (planes + radius), 128)


def blur_x_kernel(hi_ref, lo_ref, *refs, far, radius):
    planes_of, before, (first_ref, second_ref) = refs[:2 - far], refs[2 - far:-2], refs[-2:]
    planes, rows, _ = first_ref.shape
    split_at = near_lanes(planes, radius)
    lanes = slice(split_at, None) if far else slice(0, split_at)

    def body(step, carry):
        row = pl.multiple_of(step * 8, 8)
        place = (slice(None), pl.ds(row, 8), slice(None))
        out = spread_x(hi_ref, lo_ref, 0, slice(None), lanes, [[gather(ref, row) for ref in planes_of]])
        out = [out[:planes], out[planes:]]
        if before:
            out = [ref[place] + part for ref, part in zip(before, out)]
        first_ref[place], second_ref[place] = out
        return carry

    lax.fori_loop(0, rows // 8, body, 0)


def blur_x(tables, planes_of, before, planes):
    far, (radius, rows, lanes) = len(planes_of) == 1, planes_of[-1].shape
    shape = jax.ShapeDtypeStruct((planes, rows, lanes), F32)
    kernel = functools.partial(blur_x_kernel, far=far, radius=radius)
    operands = [*tables.x, *planes_of, *before]
    return call(kernel, (shape, shape), [VMEM] * len(operands), "blur_x_far" if far else "blur_x_near")(*operands)


def blur_near(tables, own, near):
    return blur_x(tables, (own, near), (), own.shape[0])


def blur_far(tables, far, parts):
    return blur_x(tables, (far,), parts, parts[0].shape[0])


def spread_y(band, x):
    high, low = split(x)
    parts = [high, low, high]
    rest = band.shape[1] - 3 * x.shape[0]
    if rest:
        parts.append(jnp.zeros((rest, x.shape[1]), BF16))
    return dot(band, jnp.concatenate(parts, axis=0))


def spread_z(x, hi_ref, lo_ref, index):
    high, low = split(x)
    return dot(high, hi_ref[index]) + (dot(low, hi_ref[index]) + dot(high, lo_ref[index]))


def blurred_planes(wide_refs, yf_ref, zhi_ref, zlo_ref, order, block):
    wide = [jnp.concatenate([ref[p] for ref in wide_refs], axis=0) for p in block]
    spread = jnp.concatenate([spread_y(yf_ref[order], rows) for rows in wide], axis=0)
    return spread_z(spread, zhi_ref, zlo_ref, order)


def plane_blocks(planes, step=4):
    return [range(start, min(start + step, planes)) for start in range(0, planes, step)]


def blur_yz_kernel(*refs, order):
    wide_refs, (yf_ref, zhi_ref, zlo_ref, out_ref) = refs[:-4], refs[-4:]
    near = yf_ref.shape[1]
    for block in plane_blocks(out_ref.shape[0]):
        blurred = blurred_planes(wide_refs, yf_ref, zhi_ref, zlo_ref, order, block)
        for k, p in enumerate(block):
            out_ref[p] = blurred[k * near:(k + 1) * near]


def blur_yz(wides, tables, order):
    planes, _, lanes = wides[0].shape
    shape = jax.ShapeDtypeStruct((planes, tables.whole[0].shape[1], lanes), F32)
    kernel = functools.partial(blur_yz_kernel, order=order)
    return call(kernel, shape, [VMEM] * (3 + len(wides)), "blur_yz")(*wides, tables.whole[0], *tables.z)


def adjoint_planes(blurred_of, image_of, ya_ref, zhi_ref, zlo_ref, order, out_ref, edge_refs, complete=None):
    planes, rows, _ = out_ref.shape
    for block in plane_blocks(planes):
        blurred = blurred_of(block)
        image = jnp.concatenate([image_of(p) for p in block], axis=0)
        ratio = jnp.where(image >= 0, image / blurred, jnp.ones_like(image))
        near = ratio.shape[0] // len(block)
        ratios = [ratio[k * near:(k + 1) * near] for k in range(len(block))]
        if complete:
            ratios = [complete(p, rows_of) for p, rows_of in zip(block, ratios)]
        spread = jnp.concatenate([spread_y(ya_ref[order], rows_of) for rows_of in ratios], axis=0)
        spread = spread_z(spread, zhi_ref, zlo_ref, 2 + order)
        for k, p in enumerate(block):
            out_ref[p] = spread[k * rows:(k + 1) * rows]
    put_edges(out_ref, edge_refs)


def first_ratio_kernel(
    shift_ref, far_ref, near_ref, own_ref, blurred_ref, ya_ref, zhi_ref, zlo_ref, out_ref, *refs, order, extent_x, cells_y
):
    edge_refs, image_ref, (mine_ref, beyond_ref, semaphores) = refs[:-4], refs[-4], refs[-3:]
    planes, near, cells_z = image_ref.shape
    side = half()
    slab = lax.axis_index("tile") - side + core()
    shift_x, shift_y, shift_z = (shift_ref[order, i] for i in range(3))
    lanes = pad_to(cells_y, 128)
    pick = iota((near, lanes), 1) == global_row(side, iota((near, lanes), 0), cells_y)
    is_far = (shift_x > 0) == (core() == 1)
    copy = pltpu.make_async_copy(own_ref, mine_ref, semaphores.at[0])
    far_copy = pltpu.make_async_copy(far_ref.at[pl.ds(0, planes)], beyond_ref, semaphores.at[1])
    near_copy = pltpu.make_async_copy(near_ref.at[pl.ds(0, planes)], beyond_ref, semaphores.at[1])
    copy.start()
    pl.when(is_far)(far_copy.start)
    pl.when(jnp.logical_not(is_far))(near_copy.start)
    copy.wait()
    far_copy.wait()
    mask = mine_ref[planes, :planes, :lanes].astype(BF16)
    columns = lax.dot_general(
        pick.astype(F32).astype(BF16), mask, (((1,), (1,)), ((), ())), preferred_element_type=F32
    )
    row = global_row(side, iota((near, cells_z), 0), cells_y) + shift_y
    col = iota((near, cells_z), 1) + shift_z
    inside = (row >= 0) & (row < cells_y) & (col >= 0) & (col < cells_z)

    def fetch(p):
        source = p + shift_x
        x = slab * planes + source
        is_own = (source >= 0) & (source < planes)
        beyond = jnp.clip(jnp.where(source < 0, source + planes, source - planes), 0, planes - 1)
        value = jnp.where(is_own, mine_ref[jnp.clip(source, 0, planes - 1)], beyond_ref[beyond])
        weight = jnp.broadcast_to(columns[:, p:p + 1], (near, cells_z))
        covered = inside & (weight > 0.5) & (x >= 0) & (x < extent_x)
        value = jnp.where(covered, value, jnp.full_like(value, -1.0))
        image_ref[p] = value
        return value

    def blurred_of(block):
        return jnp.concatenate([blurred_ref[p] for p in block], axis=0)

    adjoint_planes(blurred_of, fetch, ya_ref, zhi_ref, zlo_ref, order, out_ref, edge_refs)


def next_ratio_kernel(*refs, inner, count, first_row):
    image_refs, wide_refs, refs = refs[:2], (refs[2:4], refs[4:6]), refs[6:]
    passed_ref, refs = (None, refs) if inner else (refs[0], refs[1:])
    (yf_ref, ya_ref, zhi_ref, zlo_ref), out_refs, (far_ref, near_ref), refs = refs[:4], refs[4:6], refs[6:8], refs[8:]
    planes = out_refs[0].shape[0]
    rows = yf_ref.shape[1]
    for order in range(2):

        def blurred_of(block):
            return blurred_planes(wide_refs[order], yf_ref, zhi_ref, zlo_ref, order, block)

        def image_of(p):
            return image_refs[order][p, first_row:first_row + rows]

        def complete(p, ratio):
            if inner:
                refs[0][order, p] = ratio[rows - count:]
                return ratio
            return jnp.concatenate([passed_ref[order, p], ratio], axis=0)

        edges = (far_ref.at[order], near_ref.at[order])
        adjoint_planes(blurred_of, image_of, ya_ref, zhi_ref, zlo_ref, order, out_refs[order], edges, complete)


def next_ratio(images, wides, passed, y_tables, z_tables, radius, count, first_row):
    planes, _, lanes = images[0].shape
    rows = y_tables[1].shape[1]
    kernel = functools.partial(next_ratio_kernel, inner=passed is None, count=count, first_row=first_row)
    shape = jax.ShapeDtypeStruct
    whole, edge = shape((planes, rows, lanes), F32), shape((2, radius, rows, lanes), F32)
    out_shape = (whole, whole, edge, edge)
    if passed is None:
        out_shape += (shape((2, planes, count, lanes), F32),)
    operands = [*images, *wides[0], *wides[1]] + ([] if passed is None else [passed]) + [*y_tables, *z_tables]
    return call(kernel, out_shape, [VMEM] * len(operands), "ratio")(*operands)


def first_ratio(shifts, blocks, blurred, tables, order, radius, chunks, extent_x, cells_y):
    planes, near, lanes = blurred.shape
    kernel = functools.partial(first_ratio_kernel, order=order, extent_x=extent_x, cells_y=cells_y)
    rows = tables.whole[1].shape[1]
    out_shape = edge_shapes((planes, rows, lanes), radius, chunks) + (jax.ShapeDtypeStruct(blurred.shape, F32),)
    scratch = [
        pltpu.VMEM((planes + 1, near, lanes), F32), pltpu.VMEM(blurred.shape, F32), pltpu.SemaphoreType.DMA((2,))
    ]
    in_specs = [SMEM] + [pl.BlockSpec(memory_space=pl.ANY)] * 3 + [VMEM] * 4
    return call(kernel, out_shape, in_specs, "image_and_ratio", scratch)(
        shifts, *blocks, blurred, tables.whole[1], *tables.z
    )


def factor_kernel(hi_ref, lo_ref, before_ref, *refs, orders, starts, share):
    out_ref = refs[-1]
    planes, rows, _ = out_ref.shape

    def body(step, carry):
        row = pl.multiple_of(step * 8, 8)
        total = gather(before_ref, starts[0] + row)
        if share:
            total = share * jnp.log(total)
        for index, order in enumerate(orders):
            far_ref, near_ref, own_ref = refs[3 * index:3 * index + 3]
            if len(far_ref.shape) == 4:
                far_ref, near_ref = far_ref.at[order], near_ref.at[order]
            own = gather(own_ref, starts[1] + row)
            blocks = [[own, gather(near_ref, row)], [gather(far_ref, row)]]
            band_rows = slice(order * 8 * planes, (order + 1) * 8 * planes)
            total = total + jnp.log(spread_x(hi_ref, lo_ref, 1, band_rows, slice(None), blocks))
        out_ref[:, pl.ds(row, 8), :] = total
        return carry

    lax.fori_loop(0, rows // 8, body, 0)


def log_factor(tables, before, sides, orders, rows, starts, share):
    kernel = functools.partial(factor_kernel, orders=orders, starts=starts, share=share)
    planes, _, lanes = sides[0][2].shape
    shape = jax.ShapeDtypeStruct((planes, rows, lanes), F32)
    parts = [part for side in sides for part in side]
    return call(kernel, shape, [VMEM] * (3 + len(parts)), "log_factor")(*tables.x, before, *parts)


def update_kernel(*refs, count):
    parts, out_ref, edge_refs = refs[:count], refs[count], refs[count + 1:]
    for p in range(out_ref.shape[0]):
        total = parts[0][p]
        for part in parts[1:]:
            total = total + part[p]
        out_ref[p] = jnp.exp(total)
    put_edges(out_ref, edge_refs)


def update(parts, radius):
    kernel = functools.partial(update_kernel, count=len(parts))
    out_shape = edge_shapes(parts[0].shape, radius, parts[0].shape[1:2])
    return call(kernel, out_shape, [VMEM] * len(parts), "update")(*parts)


def finish_kernel(*refs):
    own, other, out_ref = refs[:(len(refs) - 1) // 2], refs[(len(refs) - 1) // 2:-1], refs[-1]
    straight = core() == half()
    groups = out_ref.shape[1] // GROUP
    for group in range(groups):
        rows = slice(group * GROUP, (group + 1) * GROUP)
        own_total, other_total = own[0][:, rows, :], other[0][:, rows, :]
        for part in own[1:]:
            own_total = own_total + part[:, rows, :]
        for part in other[1:]:
            other_total = other_total + part[:, rows, :]
        start = jnp.where(core() == 0, group, groups - 1 - group) * GROUP
        out_ref[:, pl.ds(pl.multiple_of(start, GROUP), GROUP), :] = jnp.exp(jnp.where(straight, own_total, other_total))


def finish(own_parts, other_parts):
    shape = jax.ShapeDtypeStruct(own_parts[0].shape, F32)
    return call(finish_kernel, shape, [VMEM] * (2 * len(own_parts)), "last_update")(*own_parts, *other_parts)


def join_kernel(*refs, starts):
    sources, out_ref, semaphores = refs[:-2], refs[-2], refs[-1]
    cells_y = out_ref.shape[1]
    copies = []
    for index, source_ref in enumerate(sources):
        rows, start = source_ref.shape[1], starts[index // 2]
        side = core() if index % 2 == 0 else 1 - core()
        place = pl.multiple_of(jnp.where(side == 0, start, cells_y - start - rows), GROUP)
        target = out_ref.at[:, pl.ds(place, rows), :]
        copies.append(pltpu.make_async_copy(source_ref, target, semaphores.at[index]))
    for copy in copies:
        copy.start()
    for copy in copies:
        copy.wait()


def join(pieces, starts, shape):
    anywhere = pl.BlockSpec(memory_space=pl.ANY)
    return pl.pallas_call(
        functools.partial(join_kernel, starts=starts),
        out_shape=jax.ShapeDtypeStruct(shape, F32),
        in_specs=[anywhere] * len(pieces),
        out_specs=anywhere,
        scratch_shapes=[pltpu.SemaphoreType.DMA((len(pieces),))],
        compiler_params=PARAMS,
        name="join_halves",
    )(*pieces)


def shards(acquired, estimate, offsets, view_mask, kern_x, kern_y, kern_z):
    planes, cells_y, cells_z = estimate.shape
    views, slabs = lax.axis_size("view"), lax.axis_size("tile")
    groups = views // 2
    taps_y = kern_y.shape[1]
    radius = kern_x.shape[1] // 2
    own_rows = cells_y // 2
    near = own_rows + pad_to(taps_y // 2, GROUP)
    wide = own_rows + pad_to(2 * (taps_y // 2), GROUP)
    edge_rows = wide - own_rows
    inner_rows = own_rows - edge_rows
    group = lax.axis_index("view") // 2
    straight = core() == half()

    def across(turn, half_of=lambda r: r, core_of=lambda c: c, when=lambda c, r: True):
        return lambda g, c, q, r: ((g + turn) % groups, core_of(c), q, half_of(r)) if when(c, r) else None

    def neighbours(far, near):
        return send(far, to_far), send(near, to_core_partner)

    window, crossed = make_windows(estimate, wide)
    crossed = send(crossed, across(0, lambda r: 1 - r, when=lambda c, r: c == r))

    acquired = after(acquired, window)
    first, second = shift_and_cut(offsets, acquired[0], view_mask[0], near)

    mine = [jnp.pad(row, ((0, 0), (0, 128 - row.shape[1]))) for row in (kern_x, kern_y, kern_z, offsets.astype(F32))]
    mine = jnp.concatenate(mine, axis=1)
    other = send(mine, to_core_partner)
    taps = kern_x.shape[1], taps_y, kern_z.shape[1]
    tables = make_tables(mine, other, taps, planes, cells_y, cells_z, (own_rows, near, wide))
    shifts = jnp.where(straight, jnp.concatenate([mine, other]), jnp.concatenate([other, mine]))
    shifts = shifts[:, 384:384 + offsets.shape[1]].astype(jnp.int32)

    arrived = send(after(first, tables.whole[0]), lambda g, c, q, r: (g, r, q, c) if c != r else None)
    current, distant, close = choose(after(window, first), crossed, radius)
    second = send(after(second, current), lambda g, c, q, r: (g, r, q, 1 - c))
    distant, close = neighbours(distant, close)
    first = jnp.where(straight, first, arrived)
    blocks = [(*neighbours(block, block), block) for block in (first, second)]
    wide_parts = blur_x(tables, (current, close), blur_x(tables, (distant,), (), planes), planes)
    blurred = [blur_yz([part], tables, order) for order, part in enumerate(wide_parts)]

    row_chunks = [(inner_rows, edge_rows), (0, inner_rows)]
    share = 1.0 / groups
    images, sides = [], []
    for order, chunk_sizes in enumerate(([own_rows], [edge_rows, inner_rows])):
        spread, *edges, image = first_ratio(
            shifts, blocks[order], blurred[order], tables, order, radius, chunk_sizes, planes * slabs, cells_y
        )
        images.append(image)
        sides.append([(*neighbours(*edges[k:k + 2]), spread) for k in range(0, len(edges), 2)])
    total = log_factor(tables, current, sides[0], [0], own_rows, (0, 0), share)
    totals = [
        log_factor(tables, total, [side], [1], rows, (start, start), 0)
        for (start, rows), side in zip(row_chunks, sides[1])
    ]

    for step in range(1, ITERS):
        chunks, before = [], []
        for total in totals:
            parts = [total] + [send(total, across(turn)) for turn in range(1, groups)]
            if chunks:
                parts[-1] = after(parts[-1], chunks[0][0])
            rows, distant, close = update(parts, radius)
            if total is totals[0]:
                beyond = send(rows, to_row_partner)
            distant, close = neighbours(distant, close)
            chunks.append((distant, blur_near(tables, rows, close)))
            before.append(rows)
        rest = planes - radius
        distant, close = neighbours(
            lax.dynamic_slice_in_dim(beyond, core() * rest, radius, 0),
            lax.dynamic_slice_in_dim(beyond, (1 - core()) * rest, radius, 0),
        )
        edge_parts, inner_parts = [blur_far(tables, *chunk) for chunk in chunks]
        *inner_spreads, distant_inner, close_inner, passed = next_ratio(
            images, list(zip([after(after(part, distant), close) for part in inner_parts], edge_parts)), None, tables.inner, tables.z, radius, 2 * (near - own_rows), 0
        )
        halo_parts = blur_far(tables, distant, blur_near(tables, beyond, close))
        inner_side = neighbours(distant_inner, close_inner)
        *edge_spreads, distant, close = next_ratio(
            images, list(zip(edge_parts, halo_parts)), passed, tables.edge, tables.z, radius, 0,
            inner_rows + near - own_rows,
        )
        edge_side = neighbours(distant, close)
        totals = [
            log_factor(tables, rows_of, [(*side, spread) for spread in spreads], [0, 1], rows, (0, 0), share)
            for rows_of, side, spreads, rows in (
                (before[0], edge_side, edge_spreads, edge_rows), (before[1], inner_side, inner_spreads, inner_rows)
            )
        ]

    pieces = []
    for own in totals[::-1]:
        other_parts = [
            send(own, across(turn, lambda r: 1 - r, lambda c: 1 - c, lambda c, r: c != r))
            for turn in reversed(range(groups))
        ]
        own_parts = [own] + [send(own, across(turn, when=lambda c, r: c == r)) for turn in range(1, groups)]
        mine = finish(own_parts, other_parts)
        pieces += [mine, send(mine, to_core_partner)]
    return join(pieces, [start for start, _ in row_chunks[::-1]], estimate.shape)


def solution(mesh):
    in_specs = (
        P("view", "tile", None, None),
        P("tile", None, None),
        P("view", None),
        P("view", "tile", None),
        P("view", None),
        P("view", None),
        P("view", None),
    )
    out_specs = P("tile", None, None)
    return jax.shard_map(shards, mesh=mesh, in_specs=in_specs, out_specs=out_specs, check_vma=False)
```

```python
import functools
import typing

import jax
import jax.numpy as jnp
from jax import lax
from jax.experimental import pallas as pl
from jax.experimental.pallas import tpu as pltpu
from jax.sharding import PartitionSpec as P

ITERS = 2
AXES = ("view", "tile")
F32 = jnp.float32
BF16 = jnp.bfloat16
VMEM = pl.BlockSpec(memory_space=pltpu.VMEM)
SMEM = pl.BlockSpec(memory_space=pltpu.SMEM)
PARAMS = pltpu.CompilerParams(vmem_limit_bytes=12 * 1024 * 1024)
GROUP = 16


def moves(move):
    views, tiles = lax.axis_size("view"), lax.axis_size("tile")
    pairs = []
    for view in range(views):
        for tile in range(tiles):
            target = move(view // 2, view % 2, tile // 2, tile % 2)
            if target is not None:
                g, c, q, r = target
                pairs.append((view * tiles + tile, (2 * g + c) * tiles + 2 * q + r))
    return pairs


def send(array, move):
    return lax.ppermute(array, AXES, moves(move))


def after(array, other):
    return lax.optimization_barrier((array, other))[0]


def to_far(g, c, q, r):
    s = 2 * q + c + (1 if c else -1)
    return (g, s % 2, s // 2, r) if 0 <= s < lax.axis_size("tile") else None


def to_row_partner(g, c, q, r):
    return (g, c, q, 1 - r)


def to_core_partner(g, c, q, r):
    return (g, 1 - c, q, r)


def core():
    return lax.rem(lax.axis_index("view"), 2)


def half():
    return lax.rem(lax.axis_index("tile"), 2)


def split(x):
    high = x.astype(BF16)
    return high, (x - high.astype(F32)).astype(BF16)


def dot(a, b):
    return jnp.dot(a, b, preferred_element_type=F32)


def iota(shape, dim):
    return lax.broadcasted_iota(jnp.int32, shape, dim)


def group_row(half, group, cells_y):
    return group * GROUP + half * (cells_y - GROUP - 2 * group * GROUP)


def global_row(half, local, cells_y):
    group = local // GROUP
    return group_row(half, group, cells_y) + (local - group * GROUP)


def wide_local(place, own, wide):
    group = (place - own) // GROUP
    return own + (wide - own) - GROUP - group * GROUP + (place - own - group * GROUP)


def wide_group(group, own_groups, groups):
    return group if group < own_groups else own_groups + groups - 1 - group


def pad_to(value, unit):
    return -(-value // unit) * unit


def call(kernel, out_shape, in_specs, name, scratch=()):
    return pl.pallas_call(
        kernel,
        out_shape=out_shape,
        in_specs=in_specs,
        out_specs=jax.tree.map(lambda _: VMEM, out_shape),
        scratch_shapes=list(scratch),
        compiler_params=PARAMS,
        name=name,
    )


class Tables(typing.NamedTuple):
    whole: tuple
    inner: tuple
    edge: tuple
    z: tuple
    x: tuple


def place(row, count, width, turned, spacing):
    source, target = iota((row.shape[1], width), 0), iota((row.shape[1], width), 1)
    index = count - 1 - source if turned else source
    ones = (target == spacing * index) & (source < count)
    return jnp.dot(row, ones.astype(F32), precision=lax.Precision.HIGHEST, preferred_element_type=F32)


def tables_kernel(mine_ref, other_ref, *refs, blocks, sizes, cells_y, taps):
    y_refs, (zhi_ref, zlo_ref, xhi_ref, xlo_ref) = refs[:-4], refs[-4:]
    taps_x, taps_y, taps_z = taps
    straight = core() == half()
    mine, other = mine_ref[...], other_ref[...]
    both = (jnp.where(straight, mine, other), jnp.where(straight, other, mine))
    radius, radius_x, radius_z = taps_y // 2, taps_x // 2, taps_z // 2
    side = half()
    own, wide = sizes
    for out_ref, adjoint, first_row, first_col, width in zip(y_refs, *zip(*blocks)):
        _, rows, lanes = out_ref.shape
        row = global_row(side, first_row + iota((rows, lanes), 0), cells_y)
        lane = iota((rows, lanes), 1)
        place_of = lane + first_col
        turned = place_of if adjoint else jnp.where(place_of < own, place_of, wide_local(place_of, own, wide))
        col = global_row(side, turned, cells_y)
        delta = (row - col if adjoint else col - row) + radius
        delta = jnp.where(lane < width, delta, -1)
        for order in range(2):
            band = jnp.zeros((rows, lanes), F32)
            values = both[order][:, 128:256]
            for a in range(taps_y):
                band = jnp.where(delta == a, jnp.broadcast_to(values[:, a:a + 1], (rows, lanes)), band)
            high, low = split(band)
            high, low = high.astype(F32), low.astype(F32)
            out_ref[order] = (high + pltpu.roll(high, width, 1) + pltpu.roll(low, 2 * width, 1)).astype(BF16)

    lanes = zhi_ref.shape[2]
    near_z = jnp.abs(iota((lanes, lanes), 1) - iota((lanes, lanes), 0)) <= radius_z
    for index in range(4):
        base = place(both[index % 2][:, 256:384], taps_z, lanes, index < 2, 1)
        base = pltpu.roll(base, lanes - radius_z, 1)
        band = pltpu.roll(jnp.broadcast_to(base, (lanes, lanes)), 0, 1, stride=1, stride_axis=0)
        zhi_ref[index], zlo_ref[index] = split(jnp.where(near_z, band, jnp.zeros_like(band)))

    rows = xhi_ref.shape[1] // 2
    lanes = max(512, 1 << (xhi_ref.shape[2] - 1).bit_length())
    for index in range(4):
        base = place(both[index % 2][:, :128], taps_x, lanes, index >= 2, 8)
        base = jnp.broadcast_to(base, (rows, lanes))
        band = pltpu.roll(base, 0, 1, stride=1, stride_axis=0)
        lane = iota((rows, lanes), 1)
        edge = 8 * radius_x
        far = pad_to(rows + edge, 128)
        next_near = pltpu.roll(band, lanes - edge, 1)
        next_far = pltpu.roll(band, far - rows - edge, 1)
        near_part = jnp.where((lane < rows) | (core() == 0), next_near, pltpu.roll(band, rows, 1))
        far_part = jnp.where(core() == 0, pltpu.roll(band, far, 1), next_far)
        zero = jnp.zeros_like(band)
        band = jnp.where(
            lane < rows + edge, near_part, jnp.where((lane >= far) & (lane < far + edge), far_part, zero)
        )[:, :xhi_ref.shape[2]]
        block = (index // 2, slice(index % 2 * rows, index % 2 * rows + rows))
        xhi_ref[block], xlo_ref[block] = split(band)


def make_tables(mine, other, taps, planes, cells_y, cells_z, sizes):
    own, near, wide = sizes
    inner, beyond = 2 * own - wide, near - own
    radius = taps[0] // 2
    depth = pad_to(8 * (planes + radius), 128) + pad_to(8 * radius, 128)
    blocks = [
        (False, near, 0, 0, wide), (True, own, 0, 0, near),
        (False, inner + beyond, 0, 0, own), (True, inner, 0, 0, inner + beyond),
        (False, near - inner - beyond, inner + beyond, inner, wide - inner),
        (True, own - inner, inner, inner - beyond, near - inner + beyond),
    ]
    kernel = functools.partial(
        tables_kernel, blocks=[block[:1] + block[2:] for block in blocks], sizes=(own, wide), cells_y=cells_y, taps=taps
    )
    shape = jax.ShapeDtypeStruct
    out_shape = tuple(shape((2, block[1], pad_to(3 * block[4], 128)), BF16) for block in blocks) + (
        shape((4, cells_z, cells_z), BF16),
        shape((4, cells_z, cells_z), BF16),
        shape((2, 2 * 8 * planes, depth), BF16),
        shape((2, 2 * 8 * planes, depth), BF16),
    )
    tables = call(kernel, out_shape, [VMEM, VMEM], "band_matrices")(mine, other)
    whole, inner_rows, edge_rows = tables[0:2], tables[2:4], tables[4:6]
    return Tables(whole, inner_rows, edge_rows, tables[6:8], tables[8:10])


def window_kernel(estimate_ref, own_ref, other_ref):
    cells_y = estimate_ref.shape[1]
    groups = own_ref.shape[1] // GROUP
    for side, out_ref in ((half(), own_ref), (1 - half(), other_ref)):
        for group in range(groups):
            local = wide_group(group, cells_y // 2 // GROUP, groups)
            start = pl.multiple_of(group_row(side, local, cells_y), GROUP)
            out_ref[:, group * GROUP:(group + 1) * GROUP, :] = estimate_ref[:, pl.ds(start, GROUP), :]


def make_windows(estimate, wide):
    planes, _, cells_z = estimate.shape
    shape = jax.ShapeDtypeStruct((planes, wide, cells_z), F32)
    return call(window_kernel, (shape, shape), [VMEM], "estimate_windows")(estimate)


def put_edges(out_ref, edge_refs):
    end = out_ref.shape[1]
    for far_ref, near_ref in zip(edge_refs[::2], edge_refs[1::2]):
        radius, rows = far_ref.shape[0], slice(end - far_ref.shape[1], end)
        beyond = out_ref.shape[0] - radius
        for p in range(radius):
            far_ref[p] = out_ref[p + core() * beyond, rows]
            near_ref[p] = out_ref[p + (1 - core()) * beyond, rows]
        end -= far_ref.shape[1]


def choose_kernel(window_ref, crossed_ref, out_ref, *edge_refs):
    straight = core() == half()
    for p in range(out_ref.shape[0]):
        out_ref[p] = jnp.where(straight, window_ref[p], crossed_ref[p])
    put_edges(out_ref, edge_refs)


def edge_shapes(shape, radius, chunks):
    planes, _, lanes = shape
    edges = [jax.ShapeDtypeStruct((radius, rows, lanes), F32) for rows in chunks for _ in range(2)]
    return (jax.ShapeDtypeStruct(shape, F32), *edges)


def choose(window, crossed, radius):
    out_shape = edge_shapes(window.shape, radius, window.shape[1:2])
    return call(choose_kernel, out_shape, [VMEM] * 2, "estimate")(window, crossed)


def shift_kernel(offsets_ref, acq_ref, mask_ref, first_ref, second_ref, turned_ref):
    planes, cells_y, cells_z = acq_ref.shape
    near = first_ref.shape[1]
    shift_y, shift_z = offsets_ref[0, 1], offsets_ref[0, 2]
    row = iota((cells_y, cells_z), 0) + shift_y
    col = iota((cells_y, cells_z), 1) + shift_z
    inside = (row >= 0) & (row < cells_y) & (col >= 0) & (col < cells_z)
    turn_y = lax.rem(cells_y - shift_y, cells_y)
    turn_z = lax.rem(cells_z - shift_z, cells_z)

    def body(p, carry):
        x = pltpu.roll(pltpu.roll(acq_ref[p], turn_z, 1), turn_y, 0)
        turned_ref[...] = jnp.where(inside, x, jnp.zeros_like(x))
        for side, out_ref in ((core(), first_ref), (1 - core(), second_ref)):
            for group in range(near // GROUP):
                start = pl.multiple_of(group_row(side, group, cells_y), GROUP)
                out_ref[p, group * GROUP:(group + 1) * GROUP, :] = turned_ref[pl.ds(start, GROUP), :]
        return carry

    lax.fori_loop(0, planes, body, 0)
    mask = mask_ref[...].astype(F32)
    for out_ref in (first_ref, second_ref):
        out_ref[planes] = jnp.zeros((near, cells_z), F32)
        out_ref[planes, :planes, :cells_y] = mask


def shift_and_cut(offsets, acquired, mask, near):
    planes, cells_y, cells_z = acquired.shape
    shape = jax.ShapeDtypeStruct((planes + 1, near, cells_z), F32)
    scratch = [pltpu.VMEM((cells_y, cells_z), F32)]
    return call(shift_kernel, (shape, shape), [SMEM, VMEM, VMEM], "shift_recorded", scratch)(offsets, acquired, mask)


def gather(ref, row):
    return ref[:, pl.ds(pl.multiple_of(row, 8), 8), :]


def spread_x(hi_ref, lo_ref, index, band_rows, band_lanes, blocks):
    lanes = blocks[0][0].shape[2]
    filled = []
    for parts in blocks:
        count = 8 * sum(part.shape[0] for part in parts)
        missing = (pad_to(count, 128) - count) // 8
        filled += list(parts) + ([jnp.zeros((missing, 8, lanes), F32)] if missing else [])
    high, low = split(jnp.concatenate(filled, axis=0).reshape(-1, lanes))
    band = hi_ref[index, band_rows, band_lanes]
    out = dot(band, high) + (dot(band, low) + dot(lo_ref[index, band_rows, band_lanes], high))
    return out.reshape(-1, 8, lanes)


def near_lanes(planes, radius):
    return pad_to(8 * (planes + radius), 128)


def blur_x_kernel(hi_ref, lo_ref, *refs, far, radius):
    planes_of, before, (first_ref, second_ref) = refs[:2 - far], refs[2 - far:-2], refs[-2:]
    planes, rows, _ = first_ref.shape
    split_at = near_lanes(planes, radius)
    lanes = slice(split_at, None) if far else slice(0, split_at)

    def body(step, carry):
        row = pl.multiple_of(step * 8, 8)
        place = (slice(None), pl.ds(row, 8), slice(None))
        out = spread_x(hi_ref, lo_ref, 0, slice(None), lanes, [[gather(ref, row) for ref in planes_of]])
        out = [out[:planes], out[planes:]]
        if before:
            out = [ref[place] + part for ref, part in zip(before, out)]
        first_ref[place], second_ref[place] = out
        return carry

    lax.fori_loop(0, rows // 8, body, 0)


def blur_x(tables, planes_of, before, planes):
    far, (radius, rows, lanes) = len(planes_of) == 1, planes_of[-1].shape
    shape = jax.ShapeDtypeStruct((planes, rows, lanes), F32)
    kernel = functools.partial(blur_x_kernel, far=far, radius=radius)
    operands = [*tables.x, *planes_of, *before]
    return call(kernel, (shape, shape), [VMEM] * len(operands), "blur_x_far" if far else "blur_x_near")(*operands)


def blur_near(tables, own, near):
    return blur_x(tables, (own, near), (), own.shape[0])


def blur_far(tables, far, parts):
    return blur_x(tables, (far,), parts, parts[0].shape[0])


def spread_y(band, x):
    high, low = split(x)
    parts = [high, low, high]
    rest = band.shape[1] - 3 * x.shape[0]
    if rest:
        parts.append(jnp.zeros((rest, x.shape[1]), BF16))
    return dot(band, jnp.concatenate(parts, axis=0))


def spread_z(x, hi_ref, lo_ref, index):
    high, low = split(x)
    return dot(high, hi_ref[index]) + (dot(low, hi_ref[index]) + dot(high, lo_ref[index]))


def blurred_planes(wide_refs, yf_ref, zhi_ref, zlo_ref, order, block):
    wide = [jnp.concatenate([ref[p] for ref in wide_refs], axis=0) for p in block]
    spread = jnp.concatenate([spread_y(yf_ref[order], rows) for rows in wide], axis=0)
    return spread_z(spread, zhi_ref, zlo_ref, order)


def plane_blocks(planes, step=4):
    return [range(start, min(start + step, planes)) for start in range(0, planes, step)]


def blur_yz_kernel(*refs, order):
    wide_refs, (yf_ref, zhi_ref, zlo_ref, out_ref) = refs[:-4], refs[-4:]
    near = yf_ref.shape[1]
    for block in plane_blocks(out_ref.shape[0]):
        blurred = blurred_planes(wide_refs, yf_ref, zhi_ref, zlo_ref, order, block)
        for k, p in enumerate(block):
            out_ref[p] = blurred[k * near:(k + 1) * near]


def blur_yz(wides, tables, order):
    planes, _, lanes = wides[0].shape
    shape = jax.ShapeDtypeStruct((planes, tables.whole[0].shape[1], lanes), F32)
    kernel = functools.partial(blur_yz_kernel, order=order)
    return call(kernel, shape, [VMEM] * (3 + len(wides)), "blur_yz")(*wides, tables.whole[0], *tables.z)


def adjoint_planes(blurred_of, image_of, ya_ref, zhi_ref, zlo_ref, order, out_ref, edge_refs, complete=None):
    planes, rows, _ = out_ref.shape
    for block in plane_blocks(planes):
        blurred = blurred_of(block)
        image = jnp.concatenate([image_of(p) for p in block], axis=0)
        ratio = jnp.where(image >= 0, image / blurred, jnp.ones_like(image))
        near = ratio.shape[0] // len(block)
        ratios = [ratio[k * near:(k + 1) * near] for k in range(len(block))]
        if complete:
            ratios = [complete(p, rows_of) for p, rows_of in zip(block, ratios)]
        spread = jnp.concatenate([spread_y(ya_ref[order], rows_of) for rows_of in ratios], axis=0)
        spread = spread_z(spread, zhi_ref, zlo_ref, 2 + order)
        for k, p in enumerate(block):
            out_ref[p] = spread[k * rows:(k + 1) * rows]
    put_edges(out_ref, edge_refs)


def first_ratio_kernel(
    shift_ref, far_ref, near_ref, own_ref, blurred_ref, ya_ref, zhi_ref, zlo_ref, out_ref, *refs, order, extent_x, cells_y
):
    edge_refs, image_ref, (mine_ref, beyond_ref, semaphores) = refs[:-4], refs[-4], refs[-3:]
    planes, near, cells_z = image_ref.shape
    side = half()
    slab = lax.axis_index("tile") - side + core()
    shift_x, shift_y, shift_z = (shift_ref[order, i] for i in range(3))
    lanes = pad_to(cells_y, 128)
    pick = iota((near, lanes), 1) == global_row(side, iota((near, lanes), 0), cells_y)
    is_far = (shift_x > 0) == (core() == 1)
    copy = pltpu.make_async_copy(own_ref, mine_ref, semaphores.at[0])
    far_copy = pltpu.make_async_copy(far_ref.at[pl.ds(0, planes)], beyond_ref, semaphores.at[1])
    near_copy = pltpu.make_async_copy(near_ref.at[pl.ds(0, planes)], beyond_ref, semaphores.at[1])
    copy.start()
    pl.when(is_far)(far_copy.start)
    pl.when(jnp.logical_not(is_far))(near_copy.start)
    copy.wait()
    far_copy.wait()
    mask = mine_ref[planes, :planes, :lanes].astype(BF16)
    columns = lax.dot_general(
        pick.astype(F32).astype(BF16), mask, (((1,), (1,)), ((), ())), preferred_element_type=F32
    )
    row = global_row(side, iota((near, cells_z), 0), cells_y) + shift_y
    col = iota((near, cells_z), 1) + shift_z
    inside = (row >= 0) & (row < cells_y) & (col >= 0) & (col < cells_z)

    def fetch(p):
        source = p + shift_x
        x = slab * planes + source
        is_own = (source >= 0) & (source < planes)
        beyond = jnp.clip(jnp.where(source < 0, source + planes, source - planes), 0, planes - 1)
        value = jnp.where(is_own, mine_ref[jnp.clip(source, 0, planes - 1)], beyond_ref[beyond])
        weight = jnp.broadcast_to(columns[:, p:p + 1], (near, cells_z))
        covered = inside & (weight > 0.5) & (x >= 0) & (x < extent_x)
        value = jnp.where(covered, value, jnp.full_like(value, -1.0))
        image_ref[p] = value
        return value

    def blurred_of(block):
        return jnp.concatenate([blurred_ref[p] for p in block], axis=0)

    adjoint_planes(blurred_of, fetch, ya_ref, zhi_ref, zlo_ref, order, out_ref, edge_refs)


def next_ratio_kernel(*refs, inner, count, first_row):
    image_refs, wide_refs, refs = refs[:2], (refs[2:4], refs[4:6]), refs[6:]
    passed_ref, refs = (None, refs) if inner else (refs[0], refs[1:])
    (yf_ref, ya_ref, zhi_ref, zlo_ref), out_refs, (far_ref, near_ref), refs = refs[:4], refs[4:6], refs[6:8], refs[8:]
    planes = out_refs[0].shape[0]
    rows = yf_ref.shape[1]
    for order in range(2):

        def blurred_of(block):
            return blurred_planes(wide_refs[order], yf_ref, zhi_ref, zlo_ref, order, block)

        def image_of(p):
            return image_refs[order][p, first_row:first_row + rows]

        def complete(p, ratio):
            if inner:
                refs[0][order, p] = ratio[rows - count:]
                return ratio
            return jnp.concatenate([passed_ref[order, p], ratio], axis=0)

        edges = (far_ref.at[order], near_ref.at[order])
        adjoint_planes(blurred_of, image_of, ya_ref, zhi_ref, zlo_ref, order, out_refs[order], edges, complete)


def next_ratio(images, wides, passed, y_tables, z_tables, radius, count, first_row):
    planes, _, lanes = images[0].shape
    rows = y_tables[1].shape[1]
    kernel = functools.partial(next_ratio_kernel, inner=passed is None, count=count, first_row=first_row)
    shape = jax.ShapeDtypeStruct
    whole, edge = shape((planes, rows, lanes), F32), shape((2, radius, rows, lanes), F32)
    out_shape = (whole, whole, edge, edge)
    if passed is None:
        out_shape += (shape((2, planes, count, lanes), F32),)
    operands = [*images, *wides[0], *wides[1]] + ([] if passed is None else [passed]) + [*y_tables, *z_tables]
    return call(kernel, out_shape, [VMEM] * len(operands), "ratio")(*operands)


def first_ratio(shifts, blocks, blurred, tables, order, radius, chunks, extent_x, cells_y):
    planes, near, lanes = blurred.shape
    kernel = functools.partial(first_ratio_kernel, order=order, extent_x=extent_x, cells_y=cells_y)
    rows = tables.whole[1].shape[1]
    out_shape = edge_shapes((planes, rows, lanes), radius, chunks) + (jax.ShapeDtypeStruct(blurred.shape, F32),)
    scratch = [
        pltpu.VMEM((planes + 1, near, lanes), F32), pltpu.VMEM(blurred.shape, F32), pltpu.SemaphoreType.DMA((2,))
    ]
    in_specs = [SMEM] + [pl.BlockSpec(memory_space=pl.ANY)] * 3 + [VMEM] * 4
    return call(kernel, out_shape, in_specs, "image_and_ratio", scratch)(
        shifts, *blocks, blurred, tables.whole[1], *tables.z
    )


def factor_kernel(hi_ref, lo_ref, before_ref, *refs, orders, starts, share):
    out_ref = refs[-1]
    planes, rows, _ = out_ref.shape

    def body(step, carry):
        row = pl.multiple_of(step * 8, 8)
        total = gather(before_ref, starts[0] + row)
        if share:
            total = share * jnp.log(total)
        for index, order in enumerate(orders):
            far_ref, near_ref, own_ref = refs[3 * index:3 * index + 3]
            if len(far_ref.shape) == 4:
                far_ref, near_ref = far_ref.at[order], near_ref.at[order]
            own = gather(own_ref, starts[1] + row)
            blocks = [[own, gather(near_ref, row)], [gather(far_ref, row)]]
            band_rows = slice(order * 8 * planes, (order + 1) * 8 * planes)
            total = total + jnp.log(spread_x(hi_ref, lo_ref, 1, band_rows, slice(None), blocks))
        out_ref[:, pl.ds(row, 8), :] = total
        return carry

    lax.fori_loop(0, rows // 8, body, 0)


def log_factor(tables, before, sides, orders, rows, starts, share):
    kernel = functools.partial(factor_kernel, orders=orders, starts=starts, share=share)
    planes, _, lanes = sides[0][2].shape
    shape = jax.ShapeDtypeStruct((planes, rows, lanes), F32)
    parts = [part for side in sides for part in side]
    return call(kernel, shape, [VMEM] * (3 + len(parts)), "log_factor")(*tables.x, before, *parts)


def update_kernel(*refs, count):
    parts, out_ref, edge_refs = refs[:count], refs[count], refs[count + 1:]
    for p in range(out_ref.shape[0]):
        total = parts[0][p]
        for part in parts[1:]:
            total = total + part[p]
        out_ref[p] = jnp.exp(total)
    put_edges(out_ref, edge_refs)


def update(parts, radius):
    kernel = functools.partial(update_kernel, count=len(parts))
    out_shape = edge_shapes(parts[0].shape, radius, parts[0].shape[1:2])
    return call(kernel, out_shape, [VMEM] * len(parts), "update")(*parts)


def finish_kernel(*refs):
    own, other, out_ref = refs[:(len(refs) - 1) // 2], refs[(len(refs) - 1) // 2:-1], refs[-1]
    straight = core() == half()
    groups = out_ref.shape[1] // GROUP
    for group in range(groups):
        rows = slice(group * GROUP, (group + 1) * GROUP)
        own_total, other_total = own[0][:, rows, :], other[0][:, rows, :]
        for part in own[1:]:
            own_total = own_total + part[:, rows, :]
        for part in other[1:]:
            other_total = other_total + part[:, rows, :]
        start = jnp.where(core() == 0, group, groups - 1 - group) * GROUP
        out_ref[:, pl.ds(pl.multiple_of(start, GROUP), GROUP), :] = jnp.exp(jnp.where(straight, own_total, other_total))


def finish(own_parts, other_parts):
    shape = jax.ShapeDtypeStruct(own_parts[0].shape, F32)
    return call(finish_kernel, shape, [VMEM] * (2 * len(own_parts)), "last_update")(*own_parts, *other_parts)


def join_kernel(*refs, starts):
    sources, out_ref, semaphores = refs[:-2], refs[-2], refs[-1]
    cells_y = out_ref.shape[1]
    copies = []
    for index, source_ref in enumerate(sources):
        rows, start = source_ref.shape[1], starts[index // 2]
        side = core() if index % 2 == 0 else 1 - core()
        place = pl.multiple_of(jnp.where(side == 0, start, cells_y - start - rows), GROUP)
        target = out_ref.at[:, pl.ds(place, rows), :]
        copies.append(pltpu.make_async_copy(source_ref, target, semaphores.at[index]))
    for copy in copies:
        copy.start()
    for copy in copies:
        copy.wait()


def join(pieces, starts, shape):
    anywhere = pl.BlockSpec(memory_space=pl.ANY)
    return pl.pallas_call(
        functools.partial(join_kernel, starts=starts),
        out_shape=jax.ShapeDtypeStruct(shape, F32),
        in_specs=[anywhere] * len(pieces),
        out_specs=anywhere,
        scratch_shapes=[pltpu.SemaphoreType.DMA((len(pieces),))],
        compiler_params=PARAMS,
        name="join_halves",
    )(*pieces)


def shards(acquired, estimate, offsets, view_mask, kern_x, kern_y, kern_z):
    planes, cells_y, cells_z = estimate.shape
    views, slabs = lax.axis_size("view"), lax.axis_size("tile")
    groups = views // 2
    taps_y = kern_y.shape[1]
    radius = kern_x.shape[1] // 2
    own_rows = cells_y // 2
    near = own_rows + pad_to(taps_y // 2, GROUP)
    wide = own_rows + pad_to(2 * (taps_y // 2), GROUP)
    edge_rows = wide - own_rows
    inner_rows = own_rows - edge_rows
    group = lax.axis_index("view") // 2
    straight = core() == half()

    def across(turn, half_of=lambda r: r, core_of=lambda c: c, when=lambda c, r: True):
        return lambda g, c, q, r: ((g + turn) % groups, core_of(c), q, half_of(r)) if when(c, r) else None

    def neighbours(far, near):
        return send(far, to_far), send(near, to_core_partner)

    window, crossed = make_windows(estimate, wide)
    crossed = send(crossed, across(0, lambda r: 1 - r, when=lambda c, r: c == r))

    acquired = after(acquired, window)
    first, second = shift_and_cut(offsets, acquired[0], view_mask[0], near)

    mine = [jnp.pad(row, ((0, 0), (0, 128 - row.shape[1]))) for row in (kern_x, kern_y, kern_z)]
    mine = jnp.concatenate(mine, axis=1)
    other = send(mine, to_core_partner)
    taps = kern_x.shape[1], taps_y, kern_z.shape[1]
    tables = make_tables(mine, other, taps, planes, cells_y, cells_z, (own_rows, near, wide))
    mine = after(offsets.astype(F32), tables.whole[0])
    other = send(mine, to_core_partner)
    shifts = jnp.where(straight, jnp.concatenate([mine, other]), jnp.concatenate([other, mine])).astype(jnp.int32)

    arrived = send(after(first, other), lambda g, c, q, r: (g, r, q, c) if c != r else None)
    current, distant, close = choose(after(window, first), crossed, radius)
    second = send(after(second, current), lambda g, c, q, r: (g, r, q, 1 - c))
    distant, close = neighbours(distant, close)
    first = jnp.where(straight, first, arrived)
    blocks = [(*neighbours(block, block), block) for block in (first, second)]
    wide_parts = blur_x(tables, (current, close), blur_x(tables, (distant,), (), planes), planes)
    blurred = [blur_yz([part], tables, order) for order, part in enumerate(wide_parts)]

    row_chunks = [(inner_rows, edge_rows), (0, inner_rows)]
    share = 1.0 / groups
    images, sides = [], []
    for order, chunk_sizes in enumerate(([own_rows], [edge_rows, inner_rows])):
        spread, *edges, image = first_ratio(
            shifts, blocks[order], blurred[order], tables, order, radius, chunk_sizes, planes * slabs, cells_y
        )
        images.append(image)
        sides.append([(*neighbours(*edges[k:k + 2]), spread) for k in range(0, len(edges), 2)])
    total = log_factor(tables, current, sides[0], [0], own_rows, (0, 0), share)
    totals = [
        log_factor(tables, total, [side], [1], rows, (start, start), 0)
        for (start, rows), side in zip(row_chunks, sides[1])
    ]

    for step in range(1, ITERS):
        chunks, before = [], []
        for total in totals:
            parts = [total] + [send(total, across(turn)) for turn in range(1, groups)]
            rows, distant, close = update(parts, radius)
            if total is totals[0]:
                beyond = send(rows, to_row_partner)
            distant = after(distant, chunks[0][0]) if chunks else distant
            distant, close = neighbours(distant, close)
            chunks.append((distant, blur_near(tables, rows, close)))
            before.append(rows)
        rest = planes - radius
        distant, close = neighbours(
            lax.dynamic_slice_in_dim(beyond, core() * rest, radius, 0),
            lax.dynamic_slice_in_dim(beyond, (1 - core()) * rest, radius, 0),
        )
        edge_parts, inner_parts = [blur_far(tables, *chunk) for chunk in chunks]
        halo_parts = blur_near(tables, beyond, close)
        *inner_spreads, distant_inner, close_inner, passed = next_ratio(
            images, list(zip([after(after(part, distant), halo_parts[0]) for part in inner_parts], edge_parts)), None, tables.inner, tables.z, radius, 2 * (near - own_rows), 0
        )
        halo_parts = blur_far(tables, distant, halo_parts)
        inner_side = neighbours(distant_inner, close_inner)
        *edge_spreads, distant, close = next_ratio(
            images, list(zip(edge_parts, halo_parts)), passed, tables.edge, tables.z, radius, 0,
            inner_rows + near - own_rows,
        )
        edge_side = neighbours(distant, close)
        totals = [
            log_factor(tables, rows_of, [(*side, spread) for spread in spreads], [0, 1], rows, (0, 0), share)
            for rows_of, side, spreads, rows in (
                (before[0], edge_side, edge_spreads, edge_rows), (before[1], inner_side, inner_spreads, inner_rows)
            )
        ]

    pieces = []
    for own in totals[::-1]:
        other_parts = [
            send(own, across(turn, lambda r: 1 - r, lambda c: 1 - c, lambda c, r: c != r))
            for turn in reversed(range(groups))
        ]
        own_parts = [own] + [send(own, across(turn, when=lambda c, r: c == r)) for turn in range(1, groups)]
        mine = finish(own_parts, other_parts)
        pieces += [mine, send(mine, to_core_partner)]
    return join(pieces, [start for start, _ in row_chunks[::-1]], estimate.shape)


def solution(mesh):
    in_specs = (
        P("view", "tile", None, None),
        P("tile", None, None),
        P("view", None),
        P("view", "tile", None),
        P("view", None),
        P("view", None),
        P("view", None),
    )
    out_specs = P("tile", None, None)
    return jax.shard_map(shards, mesh=mesh, in_specs=in_specs, out_specs=out_specs, check_vma=False)
```

```python
import functools
import typing

import jax
import jax.numpy as jnp
from jax import lax
from jax.experimental import pallas as pl
from jax.experimental.pallas import tpu as pltpu
from jax.sharding import PartitionSpec as P

ITERS = 2
AXES = ("view", "tile")
F32 = jnp.float32
BF16 = jnp.bfloat16
VMEM = pl.BlockSpec(memory_space=pltpu.VMEM)
SMEM = pl.BlockSpec(memory_space=pltpu.SMEM)
PARAMS = pltpu.CompilerParams(vmem_limit_bytes=12 * 1024 * 1024)
GROUP = 16


def moves(move):
    views, tiles = lax.axis_size("view"), lax.axis_size("tile")
    pairs = []
    for view in range(views):
        for tile in range(tiles):
            target = move(view // 2, view % 2, tile // 2, tile % 2)
            if target is not None:
                g, c, q, r = target
                pairs.append((view * tiles + tile, (2 * g + c) * tiles + 2 * q + r))
    return pairs


def send(array, move):
    return lax.ppermute(array, AXES, moves(move))


def after(array, other):
    return lax.optimization_barrier((array, other))[0]


def to_far(g, c, q, r):
    s = 2 * q + c + (1 if c else -1)
    return (g, s % 2, s // 2, r) if 0 <= s < lax.axis_size("tile") else None


def to_row_partner(g, c, q, r):
    return (g, c, q, 1 - r)


def to_core_partner(g, c, q, r):
    return (g, 1 - c, q, r)


def core():
    return lax.rem(lax.axis_index("view"), 2)


def half():
    return lax.rem(lax.axis_index("tile"), 2)


def split(x):
    high = x.astype(BF16)
    return high, (x - high.astype(F32)).astype(BF16)


def dot(a, b):
    return jnp.dot(a, b, preferred_element_type=F32)


def iota(shape, dim):
    return lax.broadcasted_iota(jnp.int32, shape, dim)


def group_row(half, group, cells_y):
    return group * GROUP + half * (cells_y - GROUP - 2 * group * GROUP)


def global_row(half, local, cells_y):
    group = local // GROUP
    return group_row(half, group, cells_y) + (local - group * GROUP)


def wide_local(place, own, wide):
    group = (place - own) // GROUP
    return own + (wide - own) - GROUP - group * GROUP + (place - own - group * GROUP)


def wide_group(group, own_groups, groups):
    return group if group < own_groups else own_groups + groups - 1 - group


def pad_to(value, unit):
    return -(-value // unit) * unit


def call(kernel, out_shape, in_specs, name, scratch=()):
    return pl.pallas_call(
        kernel,
        out_shape=out_shape,
        in_specs=in_specs,
        out_specs=jax.tree.map(lambda _: VMEM, out_shape),
        scratch_shapes=list(scratch),
        compiler_params=PARAMS,
        name=name,
    )


class Tables(typing.NamedTuple):
    whole: tuple
    inner: tuple
    edge: tuple
    z: tuple
    x: tuple


def place(row, count, width, turned, spacing):
    source, target = iota((row.shape[1], width), 0), iota((row.shape[1], width), 1)
    index = count - 1 - source if turned else source
    ones = (target == spacing * index) & (source < count)
    return jnp.dot(row, ones.astype(F32), precision=lax.Precision.HIGHEST, preferred_element_type=F32)


def tables_kernel(mine_ref, other_ref, *refs, blocks, sizes, cells_y, taps):
    y_refs, (zhi_ref, zlo_ref, xhi_ref, xlo_ref) = refs[:-4], refs[-4:]
    taps_x, taps_y, taps_z = taps
    straight = core() == half()
    mine, other = mine_ref[...], other_ref[...]
    both = (jnp.where(straight, mine, other), jnp.where(straight, other, mine))
    radius, radius_x, radius_z = taps_y // 2, taps_x // 2, taps_z // 2
    side = half()
    own, wide = sizes
    for out_ref, adjoint, first_row, first_col, width in zip(y_refs, *zip(*blocks)):
        _, rows, lanes = out_ref.shape
        row = global_row(side, first_row + iota((rows, lanes), 0), cells_y)
        lane = iota((rows, lanes), 1)
        place_of = lane + first_col
        turned = place_of if adjoint else jnp.where(place_of < own, place_of, wide_local(place_of, own, wide))
        col = global_row(side, turned, cells_y)
        delta = (row - col if adjoint else col - row) + radius
        delta = jnp.where(lane < width, delta, -1)
        for order in range(2):
            band = jnp.zeros((rows, lanes), F32)
            values = both[order][:, 128:256]
            for a in range(taps_y):
                band = jnp.where(delta == a, jnp.broadcast_to(values[:, a:a + 1], (rows, lanes)), band)
            high, low = split(band)
            high, low = high.astype(F32), low.astype(F32)
            out_ref[order] = (high + pltpu.roll(high, width, 1) + pltpu.roll(low, 2 * width, 1)).astype(BF16)

    lanes = zhi_ref.shape[2]
    near_z = jnp.abs(iota((lanes, lanes), 1) - iota((lanes, lanes), 0)) <= radius_z
    for index in range(4):
        base = place(both[index % 2][:, 256:384], taps_z, lanes, index < 2, 1)
        base = pltpu.roll(base, lanes - radius_z, 1)
        band = pltpu.roll(jnp.broadcast_to(base, (lanes, lanes)), 0, 1, stride=1, stride_axis=0)
        zhi_ref[index], zlo_ref[index] = split(jnp.where(near_z, band, jnp.zeros_like(band)))

    rows = xhi_ref.shape[1] // 2
    lanes = max(512, 1 << (xhi_ref.shape[2] - 1).bit_length())
    for index in range(4):
        base = place(both[index % 2][:, :128], taps_x, lanes, index >= 2, 8)
        base = jnp.broadcast_to(base, (rows, lanes))
        band = pltpu.roll(base, 0, 1, stride=1, stride_axis=0)
        lane = iota((rows, lanes), 1)
        edge = 8 * radius_x
        far = pad_to(rows + edge, 128)
        next_near = pltpu.roll(band, lanes - edge, 1)
        next_far = pltpu.roll(band, far - rows - edge, 1)
        near_part = jnp.where((lane < rows) | (core() == 0), next_near, pltpu.roll(band, rows, 1))
        far_part = jnp.where(core() == 0, pltpu.roll(band, far, 1), next_far)
        zero = jnp.zeros_like(band)
        band = jnp.where(
            lane < rows + edge, near_part, jnp.where((lane >= far) & (lane < far + edge), far_part, zero)
        )[:, :xhi_ref.shape[2]]
        block = (index // 2, slice(index % 2 * rows, index % 2 * rows + rows))
        xhi_ref[block], xlo_ref[block] = split(band)


def make_tables(mine, other, taps, planes, cells_y, cells_z, sizes):
    own, near, wide = sizes
    inner, beyond = 2 * own - wide, near - own
    radius = taps[0] // 2
    depth = pad_to(8 * (planes + radius), 128) + pad_to(8 * radius, 128)
    blocks = [
        (False, near, 0, 0, wide), (True, own, 0, 0, near),
        (False, inner + beyond, 0, 0, own), (True, inner, 0, 0, inner + beyond),
        (False, near - inner - beyond, inner + beyond, inner, wide - inner),
        (True, own - inner, inner, inner - beyond, near - inner + beyond),
    ]
    kernel = functools.partial(
        tables_kernel, blocks=[block[:1] + block[2:] for block in blocks], sizes=(own, wide), cells_y=cells_y, taps=taps
    )
    shape = jax.ShapeDtypeStruct
    out_shape = tuple(shape((2, block[1], pad_to(3 * block[4], 128)), BF16) for block in blocks) + (
        shape((4, cells_z, cells_z), BF16),
        shape((4, cells_z, cells_z), BF16),
        shape((2, 2 * 8 * planes, depth), BF16),
        shape((2, 2 * 8 * planes, depth), BF16),
    )
    tables = call(kernel, out_shape, [VMEM, VMEM], "band_matrices")(mine, other)
    whole, inner_rows, edge_rows = tables[0:2], tables[2:4], tables[4:6]
    return Tables(whole, inner_rows, edge_rows, tables[6:8], tables[8:10])


def window_kernel(estimate_ref, own_ref, other_ref):
    cells_y = estimate_ref.shape[1]
    groups = own_ref.shape[1] // GROUP
    for side, out_ref in ((half(), own_ref), (1 - half(), other_ref)):
        for group in range(groups):
            local = wide_group(group, cells_y // 2 // GROUP, groups)
            start = pl.multiple_of(group_row(side, local, cells_y), GROUP)
            out_ref[:, group * GROUP:(group + 1) * GROUP, :] = estimate_ref[:, pl.ds(start, GROUP), :]


def make_windows(estimate, wide):
    planes, _, cells_z = estimate.shape
    shape = jax.ShapeDtypeStruct((planes, wide, cells_z), F32)
    return call(window_kernel, (shape, shape), [VMEM], "estimate_windows")(estimate)


def put_edges(out_ref, edge_refs):
    end = out_ref.shape[1]
    for far_ref, near_ref in zip(edge_refs[::2], edge_refs[1::2]):
        radius, rows = far_ref.shape[0], slice(end - far_ref.shape[1], end)
        beyond = out_ref.shape[0] - radius
        for p in range(radius):
            far_ref[p] = out_ref[p + core() * beyond, rows]
            near_ref[p] = out_ref[p + (1 - core()) * beyond, rows]
        end -= far_ref.shape[1]


def choose_kernel(window_ref, crossed_ref, out_ref, *edge_refs):
    straight = core() == half()
    for p in range(out_ref.shape[0]):
        out_ref[p] = jnp.where(straight, window_ref[p], crossed_ref[p])
    put_edges(out_ref, edge_refs)


def edge_shapes(shape, radius, chunks):
    planes, _, lanes = shape
    edges = [jax.ShapeDtypeStruct((radius, rows, lanes), F32) for rows in chunks for _ in range(2)]
    return (jax.ShapeDtypeStruct(shape, F32), *edges)


def choose(window, crossed, radius):
    out_shape = edge_shapes(window.shape, radius, window.shape[1:2])
    return call(choose_kernel, out_shape, [VMEM] * 2, "estimate")(window, crossed)


def shift_kernel(offsets_ref, acq_ref, first_ref, second_ref, turned_ref):
    planes, cells_y, cells_z = acq_ref.shape
    near = first_ref.shape[1]
    shift_y, shift_z = offsets_ref[0, 1], offsets_ref[0, 2]
    row = iota((cells_y, cells_z), 0) + shift_y
    col = iota((cells_y, cells_z), 1) + shift_z
    inside = (row >= 0) & (row < cells_y) & (col >= 0) & (col < cells_z)
    turn_y = lax.rem(cells_y - shift_y, cells_y)
    turn_z = lax.rem(cells_z - shift_z, cells_z)

    def body(p, carry):
        x = pltpu.roll(pltpu.roll(acq_ref[p], turn_z, 1), turn_y, 0)
        turned_ref[...] = jnp.where(inside, x, jnp.zeros_like(x))
        for side, out_ref in ((core(), first_ref), (1 - core(), second_ref)):
            for group in range(near // GROUP):
                start = pl.multiple_of(group_row(side, group, cells_y), GROUP)
                out_ref[p, group * GROUP:(group + 1) * GROUP, :] = turned_ref[pl.ds(start, GROUP), :]
        return carry

    lax.fori_loop(0, planes, body, 0)


def shift_and_cut(offsets, acquired, near):
    planes, cells_y, cells_z = acquired.shape
    shape = jax.ShapeDtypeStruct((planes, near, cells_z), F32)
    scratch = [pltpu.VMEM((cells_y, cells_z), F32)]
    return call(shift_kernel, (shape, shape), [SMEM, VMEM], "shift_recorded", scratch)(offsets, acquired)


def gather(ref, row):
    return ref[:, pl.ds(pl.multiple_of(row, 8), 8), :]


def spread_x(hi_ref, lo_ref, index, band_rows, band_lanes, blocks):
    lanes = blocks[0][0].shape[2]
    filled = []
    for parts in blocks:
        count = 8 * sum(part.shape[0] for part in parts)
        missing = (pad_to(count, 128) - count) // 8
        filled += list(parts) + ([jnp.zeros((missing, 8, lanes), F32)] if missing else [])
    high, low = split(jnp.concatenate(filled, axis=0).reshape(-1, lanes))
    band = hi_ref[index, band_rows, band_lanes]
    out = dot(band, high) + (dot(band, low) + dot(lo_ref[index, band_rows, band_lanes], high))
    return out.reshape(-1, 8, lanes)


def near_lanes(planes, radius):
    return pad_to(8 * (planes + radius), 128)


def blur_x_kernel(hi_ref, lo_ref, *refs, far, radius):
    planes_of, before, (first_ref, second_ref) = refs[:2 - far], refs[2 - far:-2], refs[-2:]
    planes, rows, _ = first_ref.shape
    split_at = near_lanes(planes, radius)
    lanes = slice(split_at, None) if far else slice(0, split_at)

    def body(step, carry):
        row = pl.multiple_of(step * 8, 8)
        place = (slice(None), pl.ds(row, 8), slice(None))
        out = spread_x(hi_ref, lo_ref, 0, slice(None), lanes, [[gather(ref, row) for ref in planes_of]])
        out = [out[:planes], out[planes:]]
        if before:
            out = [ref[place] + part for ref, part in zip(before, out)]
        first_ref[place], second_ref[place] = out
        return carry

    lax.fori_loop(0, rows // 8, body, 0)


def blur_x(tables, planes_of, before, planes):
    far, (radius, rows, lanes) = len(planes_of) == 1, planes_of[-1].shape
    shape = jax.ShapeDtypeStruct((planes, rows, lanes), F32)
    kernel = functools.partial(blur_x_kernel, far=far, radius=radius)
    operands = [*tables.x, *planes_of, *before]
    return call(kernel, (shape, shape), [VMEM] * len(operands), "blur_x_far" if far else "blur_x_near")(*operands)


def blur_near(tables, own, near):
    return blur_x(tables, (own, near), (), own.shape[0])


def blur_far(tables, far, parts):
    return blur_x(tables, (far,), parts, parts[0].shape[0])


def spread_y(band, x):
    high, low = split(x)
    return dot(band[:, :3 * x.shape[0]], jnp.concatenate([high, low, high], axis=0))


def spread_z(x, hi_ref, lo_ref, index):
    high, low = split(x)
    return dot(high, hi_ref[index]) + (dot(low, hi_ref[index]) + dot(high, lo_ref[index]))


def blurred_planes(wide_refs, yf_ref, zhi_ref, zlo_ref, order, block):
    wide = [jnp.concatenate([ref[p] for ref in wide_refs], axis=0) for p in block]
    spread = jnp.concatenate([spread_y(yf_ref[order], rows) for rows in wide], axis=0)
    return spread_z(spread, zhi_ref, zlo_ref, order)


def plane_blocks(planes, step=4):
    return [range(start, min(start + step, planes)) for start in range(0, planes, step)]


def blur_yz_kernel(*refs, order):
    wide_refs, (yf_ref, zhi_ref, zlo_ref, out_ref) = refs[:-4], refs[-4:]
    near = yf_ref.shape[1]
    for block in plane_blocks(out_ref.shape[0]):
        blurred = blurred_planes(wide_refs, yf_ref, zhi_ref, zlo_ref, order, block)
        for k, p in enumerate(block):
            out_ref[p] = blurred[k * near:(k + 1) * near]


def blur_yz(wides, tables, order):
    planes, _, lanes = wides[0].shape
    shape = jax.ShapeDtypeStruct((planes, tables.whole[0].shape[1], lanes), F32)
    kernel = functools.partial(blur_yz_kernel, order=order)
    return call(kernel, shape, [VMEM] * (3 + len(wides)), "blur_yz")(*wides, tables.whole[0], *tables.z)


def adjoint_planes(blurred_of, image_of, ya_ref, zhi_ref, zlo_ref, order, out_ref, edge_refs, complete=None):
    planes, rows, _ = out_ref.shape
    for block in plane_blocks(planes):
        blurred = blurred_of(block)
        image = jnp.concatenate([image_of(p) for p in block], axis=0)
        ratio = jnp.where(image >= 0, image / blurred, jnp.ones_like(image))
        near = ratio.shape[0] // len(block)
        ratios = [ratio[k * near:(k + 1) * near] for k in range(len(block))]
        if complete:
            ratios = [complete(p, rows_of) for p, rows_of in zip(block, ratios)]
        spread = jnp.concatenate([spread_y(ya_ref[order], rows_of) for rows_of in ratios], axis=0)
        spread = spread_z(spread, zhi_ref, zlo_ref, 2 + order)
        for k, p in enumerate(block):
            out_ref[p] = spread[k * rows:(k + 1) * rows]
    put_edges(out_ref, edge_refs)


def first_ratio_kernel(
    shift_ref, far_ref, near_ref, own_ref, masks_ref, blurred_ref, ya_ref, zhi_ref, zlo_ref, out_ref, *refs, order, extent_x, cells_y
):
    edge_refs, image_ref, (mine_ref, beyond_ref, semaphores) = refs[:-4], refs[-4], refs[-3:]
    planes, near, cells_z = image_ref.shape
    side = half()
    slab = lax.axis_index("tile") - side + core()
    shift_x, shift_y, shift_z = (shift_ref[order, i] for i in range(3))
    lanes = masks_ref.shape[2]
    pick = iota((near, lanes), 1) == global_row(side, iota((near, lanes), 0), cells_y)
    is_far = (shift_x > 0) == (core() == 1)
    copy = pltpu.make_async_copy(own_ref, mine_ref, semaphores.at[0])
    far_copy = pltpu.make_async_copy(far_ref, beyond_ref, semaphores.at[1])
    near_copy = pltpu.make_async_copy(near_ref, beyond_ref, semaphores.at[1])
    copy.start()
    pl.when(is_far)(far_copy.start)
    pl.when(jnp.logical_not(is_far))(near_copy.start)
    copy.wait()
    far_copy.wait()
    mask = masks_ref[half() if order == 0 else 1 - half()].astype(BF16)
    columns = lax.dot_general(
        pick.astype(F32).astype(BF16), mask, (((1,), (1,)), ((), ())), preferred_element_type=F32
    )
    row = global_row(side, iota((near, cells_z), 0), cells_y) + shift_y
    col = iota((near, cells_z), 1) + shift_z
    inside = (row >= 0) & (row < cells_y) & (col >= 0) & (col < cells_z)

    def fetch(p):
        source = p + shift_x
        x = slab * planes + source
        is_own = (source >= 0) & (source < planes)
        beyond = jnp.clip(jnp.where(source < 0, source + planes, source - planes), 0, planes - 1)
        value = jnp.where(is_own, mine_ref[jnp.clip(source, 0, planes - 1)], beyond_ref[beyond])
        weight = jnp.broadcast_to(columns[:, p:p + 1], (near, cells_z))
        covered = inside & (weight > 0.5) & (x >= 0) & (x < extent_x)
        value = jnp.where(covered, value, jnp.full_like(value, -1.0))
        image_ref[p] = value
        return value

    def blurred_of(block):
        return jnp.concatenate([blurred_ref[p] for p in block], axis=0)

    adjoint_planes(blurred_of, fetch, ya_ref, zhi_ref, zlo_ref, order, out_ref, edge_refs)


def next_ratio_kernel(*refs, inner, count, first_row):
    image_refs, wide_refs, refs = refs[:2], (refs[2:4], refs[4:6]), refs[6:]
    passed_ref, refs = (None, refs) if inner else (refs[0], refs[1:])
    (yf_ref, ya_ref, zhi_ref, zlo_ref), out_refs, (far_ref, near_ref), refs = refs[:4], refs[4:6], refs[6:8], refs[8:]
    planes = out_refs[0].shape[0]
    rows = yf_ref.shape[1]
    for order in range(2):

        def blurred_of(block):
            return blurred_planes(wide_refs[order], yf_ref, zhi_ref, zlo_ref, order, block)

        def image_of(p):
            return image_refs[order][p, first_row:first_row + rows]

        def complete(p, ratio):
            if inner:
                refs[0][order, p] = ratio[rows - count:]
                return ratio
            return jnp.concatenate([passed_ref[order, p], ratio], axis=0)

        edges = (far_ref.at[order], near_ref.at[order])
        adjoint_planes(blurred_of, image_of, ya_ref, zhi_ref, zlo_ref, order, out_refs[order], edges, complete)


def next_ratio(images, wides, passed, y_tables, z_tables, radius, count, first_row):
    planes, _, lanes = images[0].shape
    rows = y_tables[1].shape[1]
    kernel = functools.partial(next_ratio_kernel, inner=passed is None, count=count, first_row=first_row)
    shape = jax.ShapeDtypeStruct
    whole, edge = shape((planes, rows, lanes), F32), shape((2, radius, rows, lanes), F32)
    out_shape = (whole, whole, edge, edge)
    if passed is None:
        out_shape += (shape((2, planes, count, lanes), F32),)
    operands = [*images, *wides[0], *wides[1]] + ([] if passed is None else [passed]) + [*y_tables, *z_tables]
    return call(kernel, out_shape, [VMEM] * len(operands), "ratio")(*operands)


def first_ratio(shifts, blocks, masks, blurred, tables, order, radius, chunks, extent_x, cells_y):
    planes, near, lanes = blurred.shape
    kernel = functools.partial(first_ratio_kernel, order=order, extent_x=extent_x, cells_y=cells_y)
    rows = tables.whole[1].shape[1]
    out_shape = edge_shapes((planes, rows, lanes), radius, chunks) + (jax.ShapeDtypeStruct(blurred.shape, F32),)
    scratch = [
        pltpu.VMEM(blurred.shape, F32), pltpu.VMEM(blurred.shape, F32), pltpu.SemaphoreType.DMA((2,))
    ]
    in_specs = [SMEM] + [pl.BlockSpec(memory_space=pl.ANY)] * 3 + [VMEM] * 5
    return call(kernel, out_shape, in_specs, "image_and_ratio", scratch)(
        shifts, *blocks, masks, blurred, tables.whole[1], *tables.z
    )


def factor_kernel(hi_ref, lo_ref, before_ref, *refs, orders, starts, share):
    out_ref = refs[-1]
    planes, rows, _ = out_ref.shape

    def body(step, carry):
        row = pl.multiple_of(step * 8, 8)
        total = gather(before_ref, starts[0] + row)
        if share:
            total = share * jnp.log(total)
        for index, order in enumerate(orders):
            far_ref, near_ref, own_ref = refs[3 * index:3 * index + 3]
            if len(far_ref.shape) == 4:
                far_ref, near_ref = far_ref.at[order], near_ref.at[order]
            own = gather(own_ref, starts[1] + row)
            blocks = [[own, gather(near_ref, row)], [gather(far_ref, row)]]
            band_rows = slice(order * 8 * planes, (order + 1) * 8 * planes)
            total = total + jnp.log(spread_x(hi_ref, lo_ref, 1, band_rows, slice(None), blocks))
        out_ref[:, pl.ds(row, 8), :] = total
        return carry

    lax.fori_loop(0, rows // 8, body, 0)


def log_factor(tables, before, sides, orders, rows, starts, share):
    kernel = functools.partial(factor_kernel, orders=orders, starts=starts, share=share)
    planes, _, lanes = sides[0][2].shape
    shape = jax.ShapeDtypeStruct((planes, rows, lanes), F32)
    parts = [part for side in sides for part in side]
    return call(kernel, shape, [VMEM] * (3 + len(parts)), "log_factor")(*tables.x, before, *parts)


def update_kernel(*refs, count):
    parts, out_ref, edge_refs = refs[:count], refs[count], refs[count + 1:]
    for p in range(out_ref.shape[0]):
        total = parts[0][p]
        for part in parts[1:]:
            total = total + part[p]
        out_ref[p] = jnp.exp(total)
    put_edges(out_ref, edge_refs)


def update(parts, radius):
    kernel = functools.partial(update_kernel, count=len(parts))
    out_shape = edge_shapes(parts[0].shape, radius, parts[0].shape[1:2])
    return call(kernel, out_shape, [VMEM] * len(parts), "update")(*parts)


def finish_kernel(*refs):
    own, other, out_ref = refs[:(len(refs) - 1) // 2], refs[(len(refs) - 1) // 2:-1], refs[-1]
    straight = core() == half()
    groups = out_ref.shape[1] // GROUP
    for group in range(groups):
        rows = slice(group * GROUP, (group + 1) * GROUP)
        own_total, other_total = own[0][:, rows, :], other[0][:, rows, :]
        for part in own[1:]:
            own_total = own_total + part[:, rows, :]
        for part in other[1:]:
            other_total = other_total + part[:, rows, :]
        start = jnp.where(core() == 0, group, groups - 1 - group) * GROUP
        out_ref[:, pl.ds(pl.multiple_of(start, GROUP), GROUP), :] = jnp.exp(jnp.where(straight, own_total, other_total))


def finish(own_parts, other_parts):
    shape = jax.ShapeDtypeStruct(own_parts[0].shape, F32)
    return call(finish_kernel, shape, [VMEM] * (2 * len(own_parts)), "last_update")(*own_parts, *other_parts)


def join_kernel(*refs, starts):
    sources, out_ref, semaphores = refs[:-2], refs[-2], refs[-1]
    cells_y = out_ref.shape[1]
    copies = []
    for index, source_ref in enumerate(sources):
        rows, start = source_ref.shape[1], starts[index // 2]
        side = core() if index % 2 == 0 else 1 - core()
        place = pl.multiple_of(jnp.where(side == 0, start, cells_y - start - rows), GROUP)
        target = out_ref.at[:, pl.ds(place, rows), :]
        copies.append(pltpu.make_async_copy(source_ref, target, semaphores.at[index]))
    for copy in copies:
        copy.start()
    for copy in copies:
        copy.wait()


def join(pieces, starts, shape):
    anywhere = pl.BlockSpec(memory_space=pl.ANY)
    return pl.pallas_call(
        functools.partial(join_kernel, starts=starts),
        out_shape=jax.ShapeDtypeStruct(shape, F32),
        in_specs=[anywhere] * len(pieces),
        out_specs=anywhere,
        scratch_shapes=[pltpu.SemaphoreType.DMA((len(pieces),))],
        compiler_params=PARAMS,
        name="join_halves",
    )(*pieces)


def shards(acquired, estimate, offsets, view_mask, kern_x, kern_y, kern_z):
    planes, cells_y, cells_z = estimate.shape
    views, slabs = lax.axis_size("view"), lax.axis_size("tile")
    groups = views // 2
    taps_y = kern_y.shape[1]
    radius = kern_x.shape[1] // 2
    own_rows = cells_y // 2
    near = own_rows + pad_to(taps_y // 2, GROUP)
    wide = own_rows + pad_to(2 * (taps_y // 2), GROUP)
    edge_rows = wide - own_rows
    inner_rows = own_rows - edge_rows
    group = lax.axis_index("view") // 2
    straight = core() == half()

    def across(turn, half_of=lambda r: r, core_of=lambda c: c, when=lambda c, r: True):
        return lambda g, c, q, r: ((g + turn) % groups, core_of(c), q, half_of(r)) if when(c, r) else None

    def neighbours(far, near):
        return send(far, to_far), send(near, to_core_partner)

    window, crossed = make_windows(estimate, wide)
    crossed = send(crossed, across(0, lambda r: 1 - r, when=lambda c, r: c == r))

    acquired = after(acquired, window)
    first, second = shift_and_cut(offsets, acquired[0], near)

    mine = [jnp.pad(row, ((0, 0), (0, 128 - row.shape[1]))) for row in (kern_x, kern_y, kern_z)]
    mine = jnp.concatenate(mine, axis=1)
    other = send(mine, to_core_partner)
    taps = kern_x.shape[1], taps_y, kern_z.shape[1]
    tables = make_tables(mine, other, taps, planes, cells_y, cells_z, (own_rows, near, wide))
    offset = offsets.astype(F32)
    other = send(offset, to_core_partner)
    shifts = jnp.where(straight, jnp.concatenate([offset, other]), jnp.concatenate([other, offset])).astype(jnp.int32)

    mask = view_mask.astype(F32)
    other = send(mask, to_core_partner)
    masks = jnp.where(core() == 0, jnp.concatenate([mask, other]), jnp.concatenate([other, mask]))
    beyond = send(after(masks, tables.whole[0]), to_row_partner)
    masks = jnp.where(straight, masks, beyond)

    arrived = send(after(first, masks), lambda g, c, q, r: (g, r, q, c) if c != r else None)
    current, distant, close = choose(after(window, first), crossed, radius)
    second = send(after(second, current), lambda g, c, q, r: (g, r, q, 1 - c))
    distant, close = neighbours(distant, close)
    first = jnp.where(straight, first, arrived)
    blocks = [(*neighbours(block, block), block) for block in (first, second)]
    wide_parts = blur_x(tables, (current, close), blur_x(tables, (distant,), (), planes), planes)
    blurred = [blur_yz([part], tables, order) for order, part in enumerate(wide_parts)]

    row_chunks = [(inner_rows, edge_rows), (0, inner_rows)]
    share = 1.0 / groups
    images, sides = [], []
    for order, chunk_sizes in enumerate(([own_rows], [edge_rows, inner_rows])):
        spread, *edges, image = first_ratio(
            shifts, blocks[order], masks, blurred[order], tables, order, radius, chunk_sizes, planes * slabs, cells_y
        )
        images.append(image)
        sides.append([(*neighbours(*edges[k:k + 2]), spread) for k in range(0, len(edges), 2)])
    total = log_factor(tables, current, sides[0], [0], own_rows, (0, 0), share)
    totals = [
        log_factor(tables, total, [side], [1], rows, (start, start), 0)
        for (start, rows), side in zip(row_chunks, sides[1])
    ]

    for step in range(1, ITERS):
        chunks, before = [], []
        for total in totals:
            parts = [total] + [send(total, across(turn)) for turn in range(1, groups)]
            rows, distant, close = update(parts, radius)
            if total is totals[0]:
                beyond = send(rows, to_row_partner)
            distant = after(distant, chunks[0][0]) if chunks else distant
            distant, close = neighbours(distant, close)
            chunks.append((distant, blur_near(tables, rows, close)))
            before.append(rows)
        rest = planes - radius
        distant, close = neighbours(
            lax.dynamic_slice_in_dim(beyond, core() * rest, radius, 0),
            lax.dynamic_slice_in_dim(beyond, (1 - core()) * rest, radius, 0),
        )
        edge_parts, inner_parts = [blur_far(tables, *chunk) for chunk in chunks]
        halo_parts = blur_near(tables, beyond, close)
        *inner_spreads, distant_inner, close_inner, passed = next_ratio(
            images, list(zip([after(after(part, distant), halo_parts[0]) for part in inner_parts], edge_parts)), None, tables.inner, tables.z, radius, 2 * (near - own_rows), 0
        )
        halo_parts = blur_far(tables, distant, halo_parts)
        inner_side = neighbours(distant_inner, close_inner)
        *edge_spreads, distant, close = next_ratio(
            images, list(zip(edge_parts, halo_parts)), passed, tables.edge, tables.z, radius, 0,
            inner_rows + near - own_rows,
        )
        edge_side = neighbours(distant, close)
        totals = [
            log_factor(tables, rows_of, [(*side, spread) for spread in spreads], [0, 1], rows, (0, 0), share)
            for rows_of, side, spreads, rows in (
                (before[0], edge_side, edge_spreads, edge_rows), (before[1], inner_side, inner_spreads, inner_rows)
            )
        ]

    pieces = []
    for own in totals[::-1]:
        other_parts = [
            send(own, across(turn, lambda r: 1 - r, lambda c: 1 - c, lambda c, r: c != r))
            for turn in reversed(range(groups))
        ]
        own_parts = [own] + [send(own, across(turn, when=lambda c, r: c == r)) for turn in range(1, groups)]
        mine = finish(own_parts, other_parts)
        pieces += [mine, send(mine, to_core_partner)]
    return join(pieces, [start for start, _ in row_chunks[::-1]], estimate.shape)


def solution(mesh):
    in_specs = (
        P("view", "tile", None, None),
        P("tile", None, None),
        P("view", None),
        P("view", "tile", None),
        P("view", None),
        P("view", None),
        P("view", None),
    )
    out_specs = P("tile", None, None)
    return jax.shard_map(shards, mesh=mesh, in_specs=in_specs, out_specs=out_specs, check_vma=False)
```

```python
import functools
import typing

import jax
import jax.numpy as jnp
from jax import lax
from jax.experimental import pallas as pl
from jax.experimental.pallas import tpu as pltpu
from jax.sharding import PartitionSpec as P

ITERS = 2
AXES = ("view", "tile")
F32 = jnp.float32
BF16 = jnp.bfloat16
VMEM = pl.BlockSpec(memory_space=pltpu.VMEM)
SMEM = pl.BlockSpec(memory_space=pltpu.SMEM)
PARAMS = pltpu.CompilerParams(vmem_limit_bytes=12 * 1024 * 1024)
GROUP = 16


def moves(move):
    views, tiles = lax.axis_size("view"), lax.axis_size("tile")
    pairs = []
    for view in range(views):
        for tile in range(tiles):
            target = move(view // 2, view % 2, tile // 2, tile % 2)
            if target is not None:
                g, c, q, r = target
                pairs.append((view * tiles + tile, (2 * g + c) * tiles + 2 * q + r))
    return pairs


def send(array, move):
    return lax.ppermute(array, AXES, moves(move))


def after(array, other):
    return lax.optimization_barrier((array, other))[0]


def to_far(g, c, q, r):
    s = 2 * q + c + (1 if c else -1)
    return (g, s % 2, s // 2, r) if 0 <= s < lax.axis_size("tile") else None


def to_row_partner(g, c, q, r):
    return (g, c, q, 1 - r)


def to_core_partner(g, c, q, r):
    return (g, 1 - c, q, r)


def core():
    return lax.rem(lax.axis_index("view"), 2)


def half():
    return lax.rem(lax.axis_index("tile"), 2)


def split(x):
    high = x.astype(BF16)
    return high, (x - high.astype(F32)).astype(BF16)


def dot(a, b):
    return jnp.dot(a, b, preferred_element_type=F32)


def iota(shape, dim):
    return lax.broadcasted_iota(jnp.int32, shape, dim)


def group_row(half, group, cells_y):
    return group * GROUP + half * (cells_y - GROUP - 2 * group * GROUP)


def global_row(half, local, cells_y):
    group = local // GROUP
    return group_row(half, group, cells_y) + (local - group * GROUP)


def wide_local(place, own, wide):
    group = (place - own) // GROUP
    return own + (wide - own) - GROUP - group * GROUP + (place - own - group * GROUP)


def wide_group(group, own_groups, groups):
    return group if group < own_groups else own_groups + groups - 1 - group


def pad_to(value, unit):
    return -(-value // unit) * unit


def call(kernel, out_shape, in_specs, name, scratch=()):
    return pl.pallas_call(
        kernel,
        out_shape=out_shape,
        in_specs=in_specs,
        out_specs=jax.tree.map(lambda _: VMEM, out_shape),
        scratch_shapes=list(scratch),
        compiler_params=PARAMS,
        name=name,
    )


class Tables(typing.NamedTuple):
    whole: tuple
    inner: tuple
    edge: tuple
    z: tuple
    x: tuple


def place(row, count, width, turned, spacing):
    source, target = iota((row.shape[1], width), 0), iota((row.shape[1], width), 1)
    index = count - 1 - source if turned else source
    ones = (target == spacing * index) & (source < count)
    return jnp.dot(row, ones.astype(F32), precision=lax.Precision.HIGHEST, preferred_element_type=F32)


def tables_kernel(mine_ref, other_ref, *refs, blocks, sizes, cells_y, taps):
    y_refs, (zhi_ref, zlo_ref, xhi_ref, xlo_ref) = refs[:-4], refs[-4:]
    taps_x, taps_y, taps_z = taps
    straight = core() == half()
    mine, other = mine_ref[...], other_ref[...]
    both = (jnp.where(straight, mine, other), jnp.where(straight, other, mine))
    radius, radius_x, radius_z = taps_y // 2, taps_x // 2, taps_z // 2
    side = half()
    own, wide = sizes
    for out_ref, adjoint, first_row, first_col, width in zip(y_refs, *zip(*blocks)):
        _, rows, lanes = out_ref.shape
        row = global_row(side, first_row + iota((rows, lanes), 0), cells_y)
        lane = iota((rows, lanes), 1)
        place_of = lane + first_col
        turned = place_of if adjoint else jnp.where(place_of < own, place_of, wide_local(place_of, own, wide))
        col = global_row(side, turned, cells_y)
        delta = (row - col if adjoint else col - row) + radius
        delta = jnp.where(lane < width, delta, -1)
        for order in range(2):
            band = jnp.zeros((rows, lanes), F32)
            values = both[order][:, 128:256]
            for a in range(taps_y):
                band = jnp.where(delta == a, jnp.broadcast_to(values[:, a:a + 1], (rows, lanes)), band)
            high, low = split(band)
            high, low = high.astype(F32), low.astype(F32)
            out_ref[order] = (high + pltpu.roll(high, width, 1) + pltpu.roll(low, 2 * width, 1)).astype(BF16)

    lanes = zhi_ref.shape[2]
    near_z = jnp.abs(iota((lanes, lanes), 1) - iota((lanes, lanes), 0)) <= radius_z
    for index in range(4):
        base = place(both[index % 2][:, 256:384], taps_z, lanes, index < 2, 1)
        base = pltpu.roll(base, lanes - radius_z, 1)
        band = pltpu.roll(jnp.broadcast_to(base, (lanes, lanes)), 0, 1, stride=1, stride_axis=0)
        zhi_ref[index], zlo_ref[index] = split(jnp.where(near_z, band, jnp.zeros_like(band)))

    rows = xhi_ref.shape[1] // 2
    lanes = max(512, 1 << (xhi_ref.shape[2] - 1).bit_length())
    for index in range(4):
        base = place(both[index % 2][:, :128], taps_x, lanes, index >= 2, 8)
        base = jnp.broadcast_to(base, (rows, lanes))
        band = pltpu.roll(base, 0, 1, stride=1, stride_axis=0)
        lane = iota((rows, lanes), 1)
        edge = 8 * radius_x
        far = pad_to(rows + edge, 128)
        next_near = pltpu.roll(band, lanes - edge, 1)
        next_far = pltpu.roll(band, far - rows - edge, 1)
        near_part = jnp.where((lane < rows) | (core() == 0), next_near, pltpu.roll(band, rows, 1))
        far_part = jnp.where(core() == 0, pltpu.roll(band, far, 1), next_far)
        zero = jnp.zeros_like(band)
        band = jnp.where(
            lane < rows + edge, near_part, jnp.where((lane >= far) & (lane < far + edge), far_part, zero)
        )[:, :xhi_ref.shape[2]]
        block = (index // 2, slice(index % 2 * rows, index % 2 * rows + rows))
        xhi_ref[block], xlo_ref[block] = split(band)


def make_tables(mine, other, taps, planes, cells_y, cells_z, sizes):
    own, near, wide = sizes
    inner, beyond = 2 * own - wide, near - own
    radius = taps[0] // 2
    depth = pad_to(8 * (planes + radius), 128) + pad_to(8 * radius, 128)
    blocks = [
        (False, near, 0, 0, wide), (True, own, 0, 0, near),
        (False, inner + beyond, 0, 0, own), (True, inner, 0, 0, inner + beyond),
        (False, near - inner - beyond, inner + beyond, inner, wide - inner),
        (True, own - inner, inner, inner - beyond, near - inner + beyond),
    ]
    kernel = functools.partial(
        tables_kernel, blocks=[block[:1] + block[2:] for block in blocks], sizes=(own, wide), cells_y=cells_y, taps=taps
    )
    shape = jax.ShapeDtypeStruct
    out_shape = tuple(shape((2, block[1], pad_to(3 * block[4], 128)), BF16) for block in blocks) + (
        shape((4, cells_z, cells_z), BF16),
        shape((4, cells_z, cells_z), BF16),
        shape((2, 2 * 8 * planes, depth), BF16),
        shape((2, 2 * 8 * planes, depth), BF16),
    )
    tables = call(kernel, out_shape, [VMEM, VMEM], "band_matrices")(mine, other)
    whole, inner_rows, edge_rows = tables[0:2], tables[2:4], tables[4:6]
    return Tables(whole, inner_rows, edge_rows, tables[6:8], tables[8:10])


def window_kernel(estimate_ref, own_ref, other_ref):
    cells_y = estimate_ref.shape[1]
    groups = own_ref.shape[1] // GROUP
    for side, out_ref in ((half(), own_ref), (1 - half(), other_ref)):
        for group in range(groups):
            local = wide_group(group, cells_y // 2 // GROUP, groups)
            start = pl.multiple_of(group_row(side, local, cells_y), GROUP)
            out_ref[:, group * GROUP:(group + 1) * GROUP, :] = estimate_ref[:, pl.ds(start, GROUP), :]


def make_windows(estimate, wide):
    planes, _, cells_z = estimate.shape
    shape = jax.ShapeDtypeStruct((planes, wide, cells_z), F32)
    return call(window_kernel, (shape, shape), [VMEM], "estimate_windows")(estimate)


def put_edges(out_ref, edge_refs):
    end = out_ref.shape[1]
    for far_ref, near_ref in zip(edge_refs[::2], edge_refs[1::2]):
        radius, rows = far_ref.shape[0], slice(end - far_ref.shape[1], end)
        beyond = out_ref.shape[0] - radius
        for p in range(radius):
            far_ref[p] = out_ref[p + core() * beyond, rows]
            near_ref[p] = out_ref[p + (1 - core()) * beyond, rows]
        end -= far_ref.shape[1]


def choose_kernel(window_ref, crossed_ref, out_ref, *edge_refs):
    straight = core() == half()
    for p in range(out_ref.shape[0]):
        out_ref[p] = jnp.where(straight, window_ref[p], crossed_ref[p])
    put_edges(out_ref, edge_refs)


def edge_shapes(shape, radius, chunks):
    planes, _, lanes = shape
    edges = [jax.ShapeDtypeStruct((radius, rows, lanes), F32) for rows in chunks for _ in range(2)]
    return (jax.ShapeDtypeStruct(shape, F32), *edges)


def choose(window, crossed, radius):
    out_shape = edge_shapes(window.shape, radius, window.shape[1:2])
    return call(choose_kernel, out_shape, [VMEM] * 2, "estimate")(window, crossed)


def shift_kernel(offsets_ref, acq_ref, first_ref, second_ref, turned_ref):
    planes, cells_y, cells_z = acq_ref.shape
    near = first_ref.shape[1]
    shift_y, shift_z = offsets_ref[0, 1], offsets_ref[0, 2]
    row = iota((cells_y, cells_z), 0) + shift_y
    col = iota((cells_y, cells_z), 1) + shift_z
    inside = (row >= 0) & (row < cells_y) & (col >= 0) & (col < cells_z)
    turn_y = lax.rem(cells_y - shift_y, cells_y)
    turn_z = lax.rem(cells_z - shift_z, cells_z)

    def body(p, carry):
        x = pltpu.roll(pltpu.roll(acq_ref[p], turn_z, 1), turn_y, 0)
        turned_ref[...] = jnp.where(inside, x, jnp.zeros_like(x))
        for side, out_ref in ((core(), first_ref), (1 - core(), second_ref)):
            for group in range(near // GROUP):
                start = pl.multiple_of(group_row(side, group, cells_y), GROUP)
                out_ref[p, group * GROUP:(group + 1) * GROUP, :] = turned_ref[pl.ds(start, GROUP), :]
        return carry

    lax.fori_loop(0, planes, body, 0)


def shift_and_cut(offsets, acquired, near):
    planes, cells_y, cells_z = acquired.shape
    shape = jax.ShapeDtypeStruct((planes, near, cells_z), F32)
    scratch = [pltpu.VMEM((cells_y, cells_z), F32)]
    return call(shift_kernel, (shape, shape), [SMEM, VMEM], "shift_recorded", scratch)(offsets, acquired)


def gather(ref, row):
    return ref[:, pl.ds(pl.multiple_of(row, 8), 8), :]


def spread_x(hi_ref, lo_ref, index, band_rows, band_lanes, blocks):
    lanes = blocks[0][0].shape[2]
    filled = []
    for parts in blocks:
        count = 8 * sum(part.shape[0] for part in parts)
        missing = (pad_to(count, 128) - count) // 8
        filled += list(parts) + ([jnp.zeros((missing, 8, lanes), F32)] if missing else [])
    high, low = split(jnp.concatenate(filled, axis=0).reshape(-1, lanes))
    band = hi_ref[index, band_rows, band_lanes]
    out = dot(band, high) + (dot(band, low) + dot(lo_ref[index, band_rows, band_lanes], high))
    return out.reshape(-1, 8, lanes)


def near_lanes(planes, radius):
    return pad_to(8 * (planes + radius), 128)


def blur_x_kernel(hi_ref, lo_ref, *refs, far, radius):
    planes_of, before, (first_ref, second_ref) = refs[:2 - far], refs[2 - far:-2], refs[-2:]
    planes, rows, _ = first_ref.shape
    split_at = near_lanes(planes, radius)
    lanes = slice(split_at, None) if far else slice(0, split_at)

    def body(step, carry):
        row = pl.multiple_of(step * 8, 8)
        place = (slice(None), pl.ds(row, 8), slice(None))
        out = spread_x(hi_ref, lo_ref, 0, slice(None), lanes, [[gather(ref, row) for ref in planes_of]])
        out = [out[:planes], out[planes:]]
        if before:
            out = [ref[place] + part for ref, part in zip(before, out)]
        first_ref[place], second_ref[place] = out
        return carry

    lax.fori_loop(0, rows // 8, body, 0)


def blur_x(tables, planes_of, before, planes):
    far, (radius, rows, lanes) = len(planes_of) == 1, planes_of[-1].shape
    shape = jax.ShapeDtypeStruct((planes, rows, lanes), F32)
    kernel = functools.partial(blur_x_kernel, far=far, radius=radius)
    operands = [*tables.x, *planes_of, *before]
    return call(kernel, (shape, shape), [VMEM] * len(operands), "blur_x_far" if far else "blur_x_near")(*operands)


def blur_near(tables, own, near):
    return blur_x(tables, (own, near), (), own.shape[0])


def blur_far(tables, far, parts):
    return blur_x(tables, (far,), parts, parts[0].shape[0])


def spread_y(band, x):
    high, low = split(x)
    return dot(band[:, :3 * x.shape[0]], jnp.concatenate([high, low, high], axis=0))


def spread_z(x, hi_ref, lo_ref, index):
    high, low = split(x)
    return dot(high, hi_ref[index]) + (dot(low, hi_ref[index]) + dot(high, lo_ref[index]))


def blurred_planes(wide_refs, yf_ref, zhi_ref, zlo_ref, order, block):
    wide = [jnp.concatenate([ref[p] for ref in wide_refs], axis=0) for p in block]
    spread = jnp.concatenate([spread_y(yf_ref[order], rows) for rows in wide], axis=0)
    return spread_z(spread, zhi_ref, zlo_ref, order)


def plane_blocks(planes, step=4):
    return [range(start, min(start + step, planes)) for start in range(0, planes, step)]


def blur_yz_kernel(*refs, order):
    wide_refs, (yf_ref, zhi_ref, zlo_ref, out_ref) = refs[:-4], refs[-4:]
    near = yf_ref.shape[1]
    for block in plane_blocks(out_ref.shape[0]):
        blurred = blurred_planes(wide_refs, yf_ref, zhi_ref, zlo_ref, order, block)
        for k, p in enumerate(block):
            out_ref[p] = blurred[k * near:(k + 1) * near]


def blur_yz(wides, tables, order):
    planes, _, lanes = wides[0].shape
    shape = jax.ShapeDtypeStruct((planes, tables.whole[0].shape[1], lanes), F32)
    kernel = functools.partial(blur_yz_kernel, order=order)
    return call(kernel, shape, [VMEM] * (3 + len(wides)), "blur_yz")(*wides, tables.whole[0], *tables.z)


def adjoint_planes(blurred_of, image_of, ya_ref, zhi_ref, zlo_ref, order, out_ref, edge_refs, complete=None):
    planes, rows, _ = out_ref.shape
    for block in plane_blocks(planes):
        blurred = blurred_of(block)
        image = jnp.concatenate([image_of(p) for p in block], axis=0)
        ratio = jnp.where(image >= 0, image / blurred, jnp.ones_like(image))
        near = ratio.shape[0] // len(block)
        ratios = [ratio[k * near:(k + 1) * near] for k in range(len(block))]
        if complete:
            ratios = [complete(p, rows_of) for p, rows_of in zip(block, ratios)]
        spread = jnp.concatenate([spread_y(ya_ref[order], rows_of) for rows_of in ratios], axis=0)
        spread = spread_z(spread, zhi_ref, zlo_ref, 2 + order)
        for k, p in enumerate(block):
            out_ref[p] = spread[k * rows:(k + 1) * rows]
    put_edges(out_ref, edge_refs)


def first_ratio_kernel(
    shift_ref, far_ref, near_ref, own_ref, masks_ref, blurred_ref, ya_ref, zhi_ref, zlo_ref, out_ref, *refs, order, extent_x, cells_y
):
    edge_refs, image_ref, (mine_ref, beyond_ref, semaphores) = refs[:-4], refs[-4], refs[-3:]
    planes, near, cells_z = image_ref.shape
    side = half()
    slab = lax.axis_index("tile") - side + core()
    shift_x, shift_y, shift_z = (shift_ref[order, i] for i in range(3))
    lanes = masks_ref.shape[2]
    pick = iota((near, lanes), 1) == global_row(side, iota((near, lanes), 0), cells_y)
    is_far = (shift_x > 0) == (core() == 1)
    copy = pltpu.make_async_copy(own_ref, mine_ref, semaphores.at[0])
    far_copy = pltpu.make_async_copy(far_ref, beyond_ref, semaphores.at[1])
    near_copy = pltpu.make_async_copy(near_ref, beyond_ref, semaphores.at[1])
    copy.start()
    pl.when(is_far)(far_copy.start)
    pl.when(jnp.logical_not(is_far))(near_copy.start)
    copy.wait()
    far_copy.wait()
    mask = masks_ref[half() if order == 0 else 1 - half()].astype(BF16)
    columns = lax.dot_general(
        pick.astype(F32).astype(BF16), mask, (((1,), (1,)), ((), ())), preferred_element_type=F32
    )
    row = global_row(side, iota((near, cells_z), 0), cells_y) + shift_y
    col = iota((near, cells_z), 1) + shift_z
    inside = (row >= 0) & (row < cells_y) & (col >= 0) & (col < cells_z)

    def fetch(p):
        source = p + shift_x
        x = slab * planes + source
        is_own = (source >= 0) & (source < planes)
        beyond = jnp.clip(jnp.where(source < 0, source + planes, source - planes), 0, planes - 1)
        value = jnp.where(is_own, mine_ref[jnp.clip(source, 0, planes - 1)], beyond_ref[beyond])
        weight = jnp.broadcast_to(columns[:, p:p + 1], (near, cells_z))
        covered = inside & (weight > 0.5) & (x >= 0) & (x < extent_x)
        value = jnp.where(covered, value, jnp.full_like(value, -1.0))
        image_ref[p] = value
        return value

    def blurred_of(block):
        return jnp.concatenate([blurred_ref[p] for p in block], axis=0)

    adjoint_planes(blurred_of, fetch, ya_ref, zhi_ref, zlo_ref, order, out_ref, edge_refs)


def next_ratio_kernel(*refs, inner, count, first_row):
    image_refs, wide_refs, refs = refs[:2], (refs[2:4], refs[4:6]), refs[6:]
    passed_ref, refs = (None, refs) if inner else (refs[0], refs[1:])
    (yf_ref, ya_ref, zhi_ref, zlo_ref), out_refs, (far_ref, near_ref), refs = refs[:4], refs[4:6], refs[6:8], refs[8:]
    planes = out_refs[0].shape[0]
    rows = yf_ref.shape[1]
    for order in range(2):

        def blurred_of(block):
            return blurred_planes(wide_refs[order], yf_ref, zhi_ref, zlo_ref, order, block)

        def image_of(p):
            return image_refs[order][p, first_row:first_row + rows]

        def complete(p, ratio):
            if inner:
                refs[0][order, p] = ratio[rows - count:]
                return ratio
            return jnp.concatenate([passed_ref[order, p], ratio], axis=0)

        edges = (far_ref.at[order], near_ref.at[order])
        adjoint_planes(blurred_of, image_of, ya_ref, zhi_ref, zlo_ref, order, out_refs[order], edges, complete)


def next_ratio(images, wides, passed, y_tables, z_tables, radius, count, first_row):
    planes, _, lanes = images[0].shape
    rows = y_tables[1].shape[1]
    kernel = functools.partial(next_ratio_kernel, inner=passed is None, count=count, first_row=first_row)
    shape = jax.ShapeDtypeStruct
    whole, edge = shape((planes, rows, lanes), F32), shape((2, radius, rows, lanes), F32)
    out_shape = (whole, whole, edge, edge)
    if passed is None:
        out_shape += (shape((2, planes, count, lanes), F32),)
    operands = [*images, *wides[0], *wides[1]] + ([] if passed is None else [passed]) + [*y_tables, *z_tables]
    return call(kernel, out_shape, [VMEM] * len(operands), "ratio")(*operands)


def first_ratio(shifts, blocks, masks, blurred, tables, order, radius, chunks, extent_x, cells_y):
    planes, near, lanes = blurred.shape
    kernel = functools.partial(first_ratio_kernel, order=order, extent_x=extent_x, cells_y=cells_y)
    rows = tables.whole[1].shape[1]
    out_shape = edge_shapes((planes, rows, lanes), radius, chunks) + (jax.ShapeDtypeStruct(blurred.shape, F32),)
    scratch = [
        pltpu.VMEM(blurred.shape, F32), pltpu.VMEM(blurred.shape, F32), pltpu.SemaphoreType.DMA((2,))
    ]
    in_specs = [SMEM] + [pl.BlockSpec(memory_space=pl.ANY)] * 3 + [VMEM] * 5
    return call(kernel, out_shape, in_specs, "image_and_ratio", scratch)(
        shifts, *blocks, masks, blurred, tables.whole[1], *tables.z
    )


def factor_kernel(hi_ref, lo_ref, before_ref, *refs, orders, starts, share):
    out_ref = refs[-1]
    planes, rows, _ = out_ref.shape

    def body(step, carry):
        row = pl.multiple_of(step * 8, 8)
        total = gather(before_ref, starts[0] + row)
        if share:
            total = share * jnp.log(total)
        for index, order in enumerate(orders):
            far_ref, near_ref, own_ref = refs[3 * index:3 * index + 3]
            if len(far_ref.shape) == 4:
                far_ref, near_ref = far_ref.at[order], near_ref.at[order]
            own = gather(own_ref, starts[1] + row)
            blocks = [[own, gather(near_ref, row)], [gather(far_ref, row)]]
            band_rows = slice(order * 8 * planes, (order + 1) * 8 * planes)
            total = total + jnp.log(spread_x(hi_ref, lo_ref, 1, band_rows, slice(None), blocks))
        out_ref[:, pl.ds(row, 8), :] = total
        return carry

    lax.fori_loop(0, rows // 8, body, 0)


def log_factor(tables, before, sides, orders, rows, starts, share):
    kernel = functools.partial(factor_kernel, orders=orders, starts=starts, share=share)
    planes, _, lanes = sides[0][2].shape
    shape = jax.ShapeDtypeStruct((planes, rows, lanes), F32)
    parts = [part for side in sides for part in side]
    return call(kernel, shape, [VMEM] * (3 + len(parts)), "log_factor")(*tables.x, before, *parts)


def update_kernel(*refs, count):
    parts, out_ref, edge_refs = refs[:count], refs[count], refs[count + 1:]
    for p in range(out_ref.shape[0]):
        total = parts[0][p]
        for part in parts[1:]:
            total = total + part[p]
        out_ref[p] = jnp.exp(total)
    put_edges(out_ref, edge_refs)


def update(parts, radius):
    kernel = functools.partial(update_kernel, count=len(parts))
    out_shape = edge_shapes(parts[0].shape, radius, parts[0].shape[1:2])
    return call(kernel, out_shape, [VMEM] * len(parts), "update")(*parts)


def finish_kernel(*refs):
    own, other, out_ref = refs[:(len(refs) - 1) // 2], refs[(len(refs) - 1) // 2:-1], refs[-1]
    straight = core() == half()
    groups = out_ref.shape[1] // GROUP
    for group in range(groups):
        rows = slice(group * GROUP, (group + 1) * GROUP)
        own_total, other_total = own[0][:, rows, :], other[0][:, rows, :]
        for part in own[1:]:
            own_total = own_total + part[:, rows, :]
        for part in other[1:]:
            other_total = other_total + part[:, rows, :]
        start = jnp.where(core() == 0, group, groups - 1 - group) * GROUP
        out_ref[:, pl.ds(pl.multiple_of(start, GROUP), GROUP), :] = jnp.exp(jnp.where(straight, own_total, other_total))


def finish(own_parts, other_parts):
    shape = jax.ShapeDtypeStruct(own_parts[0].shape, F32)
    return call(finish_kernel, shape, [VMEM] * (2 * len(own_parts)), "last_update")(*own_parts, *other_parts)


def join_kernel(*refs, starts):
    sources, out_ref, semaphores = refs[:-2], refs[-2], refs[-1]
    cells_y = out_ref.shape[1]
    copies = []
    for index, source_ref in enumerate(sources):
        rows, start = source_ref.shape[1], starts[index // 2]
        side = core() if index % 2 == 0 else 1 - core()
        place = pl.multiple_of(jnp.where(side == 0, start, cells_y - start - rows), GROUP)
        target = out_ref.at[:, pl.ds(place, rows), :]
        copies.append(pltpu.make_async_copy(source_ref, target, semaphores.at[index]))
    for copy in copies:
        copy.start()
    for copy in copies:
        copy.wait()


def join(pieces, starts, shape):
    anywhere = pl.BlockSpec(memory_space=pl.ANY)
    return pl.pallas_call(
        functools.partial(join_kernel, starts=starts),
        out_shape=jax.ShapeDtypeStruct(shape, F32),
        in_specs=[anywhere] * len(pieces),
        out_specs=anywhere,
        scratch_shapes=[pltpu.SemaphoreType.DMA((len(pieces),))],
        compiler_params=PARAMS,
        name="join_halves",
    )(*pieces)


def shards(acquired, estimate, offsets, view_mask, kern_x, kern_y, kern_z):
    planes, cells_y, cells_z = estimate.shape
    views, slabs = lax.axis_size("view"), lax.axis_size("tile")
    groups = views // 2
    taps_y = kern_y.shape[1]
    radius = kern_x.shape[1] // 2
    own_rows = cells_y // 2
    near = own_rows + pad_to(taps_y // 2, GROUP)
    wide = own_rows + pad_to(2 * (taps_y // 2), GROUP)
    edge_rows = wide - own_rows
    inner_rows = own_rows - edge_rows
    group = lax.axis_index("view") // 2
    straight = core() == half()

    def across(turn, half_of=lambda r: r, core_of=lambda c: c, when=lambda c, r: True):
        return lambda g, c, q, r: ((g + turn) % groups, core_of(c), q, half_of(r)) if when(c, r) else None

    def neighbours(far, near):
        return send(far, to_far), send(near, to_core_partner)

    window, crossed = make_windows(estimate, wide)
    crossed = send(crossed, across(0, lambda r: 1 - r, when=lambda c, r: c == r))

    acquired = after(acquired, window)
    first, second = shift_and_cut(offsets, acquired[0], near)

    mine = [jnp.pad(row, ((0, 0), (0, 128 - row.shape[1]))) for row in (kern_x, kern_y, kern_z)]
    mine = jnp.concatenate(mine, axis=1)
    other = send(mine, to_core_partner)
    taps = kern_x.shape[1], taps_y, kern_z.shape[1]
    tables = make_tables(mine, other, taps, planes, cells_y, cells_z, (own_rows, near, wide))
    offset = after(offsets.astype(F32), tables.whole[0])
    other = send(offset, to_core_partner)
    shifts = jnp.where(straight, jnp.concatenate([offset, other]), jnp.concatenate([other, offset])).astype(jnp.int32)

    arrived = send(after(first, tables.whole[0]), lambda g, c, q, r: (g, r, q, c) if c != r else None)
    current, distant, close = choose(after(window, first), crossed, radius)
    second = send(after(second, current), lambda g, c, q, r: (g, r, q, 1 - c))
    distant, close = neighbours(distant, close)
    first = jnp.where(straight, first, arrived)

    mask = after(view_mask.astype(F32), current)
    other = send(mask, to_core_partner)
    masks = jnp.where(core() == 0, jnp.concatenate([mask, other]), jnp.concatenate([other, mask]))
    masks = jnp.where(straight, masks, send(masks, to_row_partner))

    blocks = [(*neighbours(block, block), block) for block in (first, second)]
    wide_parts = blur_x(tables, (current, close), blur_x(tables, (distant,), (), planes), planes)
    blurred = [blur_yz([part], tables, order) for order, part in enumerate(wide_parts)]

    row_chunks = [(inner_rows, edge_rows), (0, inner_rows)]
    share = 1.0 / groups
    images, sides = [], []
    for order, chunk_sizes in enumerate(([own_rows], [edge_rows, inner_rows])):
        spread, *edges, image = first_ratio(
            shifts, blocks[order], masks, blurred[order], tables, order, radius, chunk_sizes, planes * slabs, cells_y
        )
        images.append(image)
        sides.append([(*neighbours(*edges[k:k + 2]), spread) for k in range(0, len(edges), 2)])
    total = log_factor(tables, current, sides[0], [0], own_rows, (0, 0), share)
    totals = [
        log_factor(tables, total, [side], [1], rows, (start, start), 0)
        for (start, rows), side in zip(row_chunks, sides[1])
    ]

    for step in range(1, ITERS):
        chunks, before = [], []
        for total in totals:
            parts = [total] + [send(total, across(turn)) for turn in range(1, groups)]
            rows, distant, close = update(parts, radius)
            if total is totals[0]:
                beyond = send(rows, to_row_partner)
            distant = after(distant, chunks[0][0]) if chunks else distant
            distant, close = neighbours(distant, close)
            chunks.append((distant, blur_near(tables, rows, close)))
            before.append(rows)
        rest = planes - radius
        distant, close = neighbours(
            lax.dynamic_slice_in_dim(beyond, core() * rest, radius, 0),
            lax.dynamic_slice_in_dim(beyond, (1 - core()) * rest, radius, 0),
        )
        edge_parts, inner_parts = [blur_far(tables, *chunk) for chunk in chunks]
        halo_parts = blur_near(tables, beyond, close)
        *inner_spreads, distant_inner, close_inner, passed = next_ratio(
            images, list(zip([after(after(part, distant), halo_parts[0]) for part in inner_parts], edge_parts)), None, tables.inner, tables.z, radius, 2 * (near - own_rows), 0
        )
        halo_parts = blur_far(tables, distant, halo_parts)
        inner_side = neighbours(distant_inner, close_inner)
        *edge_spreads, distant, close = next_ratio(
            images, list(zip(edge_parts, halo_parts)), passed, tables.edge, tables.z, radius, 0,
            inner_rows + near - own_rows,
        )
        edge_side = neighbours(distant, close)
        totals = [
            log_factor(tables, rows_of, [(*side, spread) for spread in spreads], [0, 1], rows, (0, 0), share)
            for rows_of, side, spreads, rows in (
                (before[0], edge_side, edge_spreads, edge_rows), (before[1], inner_side, inner_spreads, inner_rows)
            )
        ]

    pieces = []
    for own in totals[::-1]:
        other_parts = [
            send(own, across(turn, lambda r: 1 - r, lambda c: 1 - c, lambda c, r: c != r))
            for turn in reversed(range(groups))
        ]
        own_parts = [own] + [send(own, across(turn, when=lambda c, r: c == r)) for turn in range(1, groups)]
        mine = finish(own_parts, other_parts)
        pieces += [mine, send(mine, to_core_partner)]
    return join(pieces, [start for start, _ in row_chunks[::-1]], estimate.shape)


def solution(mesh):
    in_specs = (
        P("view", "tile", None, None),
        P("tile", None, None),
        P("view", None),
        P("view", "tile", None),
        P("view", None),
        P("view", None),
        P("view", None),
    )
    out_specs = P("tile", None, None)
    return jax.shard_map(shards, mesh=mesh, in_specs=in_specs, out_specs=out_specs, check_vma=False)
```

```python
import functools
import typing

import jax
import jax.numpy as jnp
from jax import lax
from jax.experimental import pallas as pl
from jax.experimental.pallas import tpu as pltpu
from jax.sharding import PartitionSpec as P

ITERS = 2
AXES = ("view", "tile")
F32 = jnp.float32
BF16 = jnp.bfloat16
VMEM = pl.BlockSpec(memory_space=pltpu.VMEM)
SMEM = pl.BlockSpec(memory_space=pltpu.SMEM)
PARAMS = pltpu.CompilerParams(vmem_limit_bytes=12 * 1024 * 1024)
GROUP = 16


def moves(move):
    views, tiles = lax.axis_size("view"), lax.axis_size("tile")
    pairs = []
    for view in range(views):
        for tile in range(tiles):
            target = move(view // 2, view % 2, tile // 2, tile % 2)
            if target is not None:
                g, c, q, r = target
                pairs.append((view * tiles + tile, (2 * g + c) * tiles + 2 * q + r))
    return pairs


def send(array, move):
    return lax.ppermute(array, AXES, moves(move))


def after(array, other):
    return lax.optimization_barrier((array, other))[0]


def to_far(g, c, q, r):
    s = 2 * q + c + (1 if c else -1)
    return (g, s % 2, s // 2, r) if 0 <= s < lax.axis_size("tile") else None


def to_row_partner(g, c, q, r):
    return (g, c, q, 1 - r)


def to_core_partner(g, c, q, r):
    return (g, 1 - c, q, r)


def core():
    return lax.rem(lax.axis_index("view"), 2)


def half():
    return lax.rem(lax.axis_index("tile"), 2)


def split(x):
    high = x.astype(BF16)
    return high, (x - high.astype(F32)).astype(BF16)


def dot(a, b):
    return jnp.dot(a, b, preferred_element_type=F32)


def iota(shape, dim):
    return lax.broadcasted_iota(jnp.int32, shape, dim)


def group_row(half, group, cells_y):
    return group * GROUP + half * (cells_y - GROUP - 2 * group * GROUP)


def global_row(half, local, cells_y):
    group = local // GROUP
    return group_row(half, group, cells_y) + (local - group * GROUP)


def wide_local(place, own, wide):
    group = (place - own) // GROUP
    return own + (wide - own) - GROUP - group * GROUP + (place - own - group * GROUP)


def wide_group(group, own_groups, groups):
    return group if group < own_groups else own_groups + groups - 1 - group


def pad_to(value, unit):
    return -(-value // unit) * unit


def call(kernel, out_shape, in_specs, name, scratch=()):
    return pl.pallas_call(
        kernel,
        out_shape=out_shape,
        in_specs=in_specs,
        out_specs=jax.tree.map(lambda _: VMEM, out_shape),
        scratch_shapes=list(scratch),
        compiler_params=PARAMS,
        name=name,
    )


class Tables(typing.NamedTuple):
    whole: tuple
    inner: tuple
    edge: tuple
    z: tuple
    x: tuple


def place(row, count, width, turned, spacing):
    source, target = iota((row.shape[1], width), 0), iota((row.shape[1], width), 1)
    index = count - 1 - source if turned else source
    ones = (target == spacing * index) & (source < count)
    return jnp.dot(row, ones.astype(F32), precision=lax.Precision.HIGHEST, preferred_element_type=F32)


def tables_kernel(mine_ref, other_ref, *refs, blocks, sizes, cells_y, taps):
    y_refs, (zhi_ref, zlo_ref, xhi_ref, xlo_ref) = refs[:-4], refs[-4:]
    taps_x, taps_y, taps_z = taps
    straight = core() == half()
    mine, other = mine_ref[...], other_ref[...]
    both = (jnp.where(straight, mine, other), jnp.where(straight, other, mine))
    radius, radius_x, radius_z = taps_y // 2, taps_x // 2, taps_z // 2
    side = half()
    own, wide = sizes
    for out_ref, adjoint, first_row, first_col, width in zip(y_refs, *zip(*blocks)):
        _, rows, lanes = out_ref.shape
        row = global_row(side, first_row + iota((rows, lanes), 0), cells_y)
        lane = iota((rows, lanes), 1)
        place_of = lane + first_col
        turned = place_of if adjoint else jnp.where(place_of < own, place_of, wide_local(place_of, own, wide))
        col = global_row(side, turned, cells_y)
        delta = (row - col if adjoint else col - row) + radius
        delta = jnp.where(lane < width, delta, -1)
        for order in range(2):
            band = jnp.zeros((rows, lanes), F32)
            values = both[order][:, 128:256]
            for a in range(taps_y):
                band = jnp.where(delta == a, jnp.broadcast_to(values[:, a:a + 1], (rows, lanes)), band)
            high, low = split(band)
            high, low = high.astype(F32), low.astype(F32)
            out_ref[order] = (high + pltpu.roll(high, width, 1) + pltpu.roll(low, 2 * width, 1)).astype(BF16)

    lanes = zhi_ref.shape[2]
    near_z = jnp.abs(iota((lanes, lanes), 1) - iota((lanes, lanes), 0)) <= radius_z
    for index in range(4):
        base = place(both[index % 2][:, 256:384], taps_z, lanes, index < 2, 1)
        base = pltpu.roll(base, lanes - radius_z, 1)
        band = pltpu.roll(jnp.broadcast_to(base, (lanes, lanes)), 0, 1, stride=1, stride_axis=0)
        zhi_ref[index], zlo_ref[index] = split(jnp.where(near_z, band, jnp.zeros_like(band)))

    rows = xhi_ref.shape[1] // 2
    lanes = max(512, 1 << (xhi_ref.shape[2] - 1).bit_length())
    for index in range(4):
        base = place(both[index % 2][:, :128], taps_x, lanes, index >= 2, 8)
        base = jnp.broadcast_to(base, (rows, lanes))
        band = pltpu.roll(base, 0, 1, stride=1, stride_axis=0)
        lane = iota((rows, lanes), 1)
        edge = 8 * radius_x
        far = pad_to(rows + edge, 128)
        next_near = pltpu.roll(band, lanes - edge, 1)
        next_far = pltpu.roll(band, far - rows - edge, 1)
        near_part = jnp.where((lane < rows) | (core() == 0), next_near, pltpu.roll(band, rows, 1))
        far_part = jnp.where(core() == 0, pltpu.roll(band, far, 1), next_far)
        zero = jnp.zeros_like(band)
        band = jnp.where(
            lane < rows + edge, near_part, jnp.where((lane >= far) & (lane < far + edge), far_part, zero)
        )[:, :xhi_ref.shape[2]]
        block = (index // 2, slice(index % 2 * rows, index % 2 * rows + rows))
        xhi_ref[block], xlo_ref[block] = split(band)


def make_tables(mine, other, taps, planes, cells_y, cells_z, sizes):
    own, near, wide = sizes
    inner, beyond = 2 * own - wide, near - own
    radius = taps[0] // 2
    depth = pad_to(8 * (planes + radius), 128) + pad_to(8 * radius, 128)
    blocks = [
        (False, near, 0, 0, wide), (True, own, 0, 0, near),
        (False, inner + beyond, 0, 0, own), (True, inner, 0, 0, inner + beyond),
        (False, near - inner - beyond, inner + beyond, inner, wide - inner),
        (True, own - inner, inner, inner - beyond, near - inner + beyond),
    ]
    kernel = functools.partial(
        tables_kernel, blocks=[block[:1] + block[2:] for block in blocks], sizes=(own, wide), cells_y=cells_y, taps=taps
    )
    shape = jax.ShapeDtypeStruct
    out_shape = tuple(shape((2, block[1], pad_to(3 * block[4], 128)), BF16) for block in blocks) + (
        shape((4, cells_z, cells_z), BF16),
        shape((4, cells_z, cells_z), BF16),
        shape((2, 2 * 8 * planes, depth), BF16),
        shape((2, 2 * 8 * planes, depth), BF16),
    )
    tables = call(kernel, out_shape, [VMEM, VMEM], "band_matrices")(mine, other)
    whole, inner_rows, edge_rows = tables[0:2], tables[2:4], tables[4:6]
    return Tables(whole, inner_rows, edge_rows, tables[6:8], tables[8:10])


def window_kernel(estimate_ref, own_ref, other_ref):
    cells_y = estimate_ref.shape[1]
    groups = own_ref.shape[1] // GROUP
    for side, out_ref in ((half(), own_ref), (1 - half(), other_ref)):
        for group in range(groups):
            local = wide_group(group, cells_y // 2 // GROUP, groups)
            start = pl.multiple_of(group_row(side, local, cells_y), GROUP)
            out_ref[:, group * GROUP:(group + 1) * GROUP, :] = estimate_ref[:, pl.ds(start, GROUP), :]


def make_windows(estimate, wide):
    planes, _, cells_z = estimate.shape
    shape = jax.ShapeDtypeStruct((planes, wide, cells_z), F32)
    return call(window_kernel, (shape, shape), [VMEM], "estimate_windows")(estimate)


def put_edges(out_ref, edge_refs):
    end = out_ref.shape[1]
    for far_ref, near_ref in zip(edge_refs[::2], edge_refs[1::2]):
        radius, rows = far_ref.shape[0], slice(end - far_ref.shape[1], end)
        beyond = out_ref.shape[0] - radius
        for p in range(radius):
            far_ref[p] = out_ref[p + core() * beyond, rows]
            near_ref[p] = out_ref[p + (1 - core()) * beyond, rows]
        end -= far_ref.shape[1]


def choose_kernel(window_ref, crossed_ref, out_ref, *edge_refs):
    straight = core() == half()
    for p in range(out_ref.shape[0]):
        out_ref[p] = jnp.where(straight, window_ref[p], crossed_ref[p])
    put_edges(out_ref, edge_refs)


def edge_shapes(shape, radius, chunks):
    planes, _, lanes = shape
    edges = [jax.ShapeDtypeStruct((radius, rows, lanes), F32) for rows in chunks for _ in range(2)]
    return (jax.ShapeDtypeStruct(shape, F32), *edges)


def choose(window, crossed, radius):
    out_shape = edge_shapes(window.shape, radius, window.shape[1:2])
    return call(choose_kernel, out_shape, [VMEM] * 2, "estimate")(window, crossed)


def shift_kernel(offsets_ref, acq_ref, first_ref, second_ref, turned_ref):
    planes, cells_y, cells_z = acq_ref.shape
    near = first_ref.shape[1]
    shift_y, shift_z = offsets_ref[0, 1], offsets_ref[0, 2]
    row = iota((cells_y, cells_z), 0) + shift_y
    col = iota((cells_y, cells_z), 1) + shift_z
    inside = (row >= 0) & (row < cells_y) & (col >= 0) & (col < cells_z)
    turn_y = lax.rem(cells_y - shift_y, cells_y)
    turn_z = lax.rem(cells_z - shift_z, cells_z)

    def body(p, carry):
        x = pltpu.roll(pltpu.roll(acq_ref[p], turn_z, 1), turn_y, 0)
        turned_ref[...] = jnp.where(inside, x, jnp.zeros_like(x))
        for side, out_ref in ((core(), first_ref), (1 - core(), second_ref)):
            for group in range(near // GROUP):
                start = pl.multiple_of(group_row(side, group, cells_y), GROUP)
                out_ref[p, group * GROUP:(group + 1) * GROUP, :] = turned_ref[pl.ds(start, GROUP), :]
        return carry

    lax.fori_loop(0, planes, body, 0)


def shift_and_cut(offsets, acquired, near):
    planes, cells_y, cells_z = acquired.shape
    shape = jax.ShapeDtypeStruct((planes, near, cells_z), F32)
    scratch = [pltpu.VMEM((cells_y, cells_z), F32)]
    return call(shift_kernel, (shape, shape), [SMEM, VMEM], "shift_recorded", scratch)(offsets, acquired)


def gather(ref, row):
    return ref[:, pl.ds(pl.multiple_of(row, 8), 8), :]


def spread_x(hi_ref, lo_ref, index, band_rows, band_lanes, blocks):
    lanes = blocks[0][0].shape[2]
    filled = []
    for parts in blocks:
        count = 8 * sum(part.shape[0] for part in parts)
        missing = (pad_to(count, 128) - count) // 8
        filled += list(parts) + ([jnp.zeros((missing, 8, lanes), F32)] if missing else [])
    high, low = split(jnp.concatenate(filled, axis=0).reshape(-1, lanes))
    band = hi_ref[index, band_rows, band_lanes]
    out = dot(band, high) + (dot(band, low) + dot(lo_ref[index, band_rows, band_lanes], high))
    return out.reshape(-1, 8, lanes)


def near_lanes(planes, radius):
    return pad_to(8 * (planes + radius), 128)


def blur_x_kernel(hi_ref, lo_ref, *refs, far, radius):
    planes_of, before, (first_ref, second_ref) = refs[:2 - far], refs[2 - far:-2], refs[-2:]
    planes, rows, _ = first_ref.shape
    split_at = near_lanes(planes, radius)
    lanes = slice(split_at, None) if far else slice(0, split_at)

    def body(step, carry):
        row = pl.multiple_of(step * 8, 8)
        place = (slice(None), pl.ds(row, 8), slice(None))
        out = spread_x(hi_ref, lo_ref, 0, slice(None), lanes, [[gather(ref, row) for ref in planes_of]])
        out = [out[:planes], out[planes:]]
        if before:
            out = [ref[place] + part for ref, part in zip(before, out)]
        first_ref[place], second_ref[place] = out
        return carry

    lax.fori_loop(0, rows // 8, body, 0)


def blur_x(tables, planes_of, before, planes):
    far, (radius, rows, lanes) = len(planes_of) == 1, planes_of[-1].shape
    shape = jax.ShapeDtypeStruct((planes, rows, lanes), F32)
    kernel = functools.partial(blur_x_kernel, far=far, radius=radius)
    operands = [*tables.x, *planes_of, *before]
    return call(kernel, (shape, shape), [VMEM] * len(operands), "blur_x_far" if far else "blur_x_near")(*operands)


def blur_near(tables, own, near):
    return blur_x(tables, (own, near), (), own.shape[0])


def blur_far(tables, far, parts):
    return blur_x(tables, (far,), parts, parts[0].shape[0])


def spread_y(band, x):
    high, low = split(x)
    return dot(band[:, :3 * x.shape[0]], jnp.concatenate([high, low, high], axis=0))


def spread_z(x, hi_ref, lo_ref, index):
    high, low = split(x)
    return dot(high, hi_ref[index]) + (dot(low, hi_ref[index]) + dot(high, lo_ref[index]))


def blurred_planes(wide_refs, yf_ref, zhi_ref, zlo_ref, order, block):
    wide = [jnp.concatenate([ref[p] for ref in wide_refs], axis=0) for p in block]
    spread = jnp.concatenate([spread_y(yf_ref[order], rows) for rows in wide], axis=0)
    return spread_z(spread, zhi_ref, zlo_ref, order)


def plane_blocks(planes, step=4):
    return [range(start, min(start + step, planes)) for start in range(0, planes, step)]


def blur_yz_kernel(*refs, order):
    wide_refs, (yf_ref, zhi_ref, zlo_ref, out_ref) = refs[:-4], refs[-4:]
    near = yf_ref.shape[1]
    for block in plane_blocks(out_ref.shape[0]):
        blurred = blurred_planes(wide_refs, yf_ref, zhi_ref, zlo_ref, order, block)
        for k, p in enumerate(block):
            out_ref[p] = blurred[k * near:(k + 1) * near]


def blur_yz(wides, tables, order):
    planes, _, lanes = wides[0].shape
    shape = jax.ShapeDtypeStruct((planes, tables.whole[0].shape[1], lanes), F32)
    kernel = functools.partial(blur_yz_kernel, order=order)
    return call(kernel, shape, [VMEM] * (3 + len(wides)), "blur_yz")(*wides, tables.whole[0], *tables.z)


def adjoint_planes(blurred_of, image_of, ya_ref, zhi_ref, zlo_ref, order, out_ref, edge_refs, complete=None):
    planes, rows, _ = out_ref.shape
    for block in plane_blocks(planes):
        blurred = blurred_of(block)
        image = jnp.concatenate([image_of(p) for p in block], axis=0)
        ratio = jnp.where(image >= 0, image / blurred, jnp.ones_like(image))
        near = ratio.shape[0] // len(block)
        ratios = [ratio[k * near:(k + 1) * near] for k in range(len(block))]
        if complete:
            ratios = [complete(p, rows_of) for p, rows_of in zip(block, ratios)]
        spread = jnp.concatenate([spread_y(ya_ref[order], rows_of) for rows_of in ratios], axis=0)
        spread = spread_z(spread, zhi_ref, zlo_ref, 2 + order)
        for k, p in enumerate(block):
            out_ref[p] = spread[k * rows:(k + 1) * rows]
    put_edges(out_ref, edge_refs)


def first_ratio_kernel(
    shift_ref, far_ref, near_ref, own_ref, masks_ref, blurred_ref, ya_ref, zhi_ref, zlo_ref, out_ref, *refs, order, extent_x, cells_y
):
    edge_refs, image_ref, (mine_ref, beyond_ref, semaphores) = refs[:-4], refs[-4], refs[-3:]
    planes, near, cells_z = image_ref.shape
    side = half()
    slab = lax.axis_index("tile") - side + core()
    shift_x, shift_y, shift_z = (shift_ref[order, i] for i in range(3))
    lanes = masks_ref.shape[2]
    pick = iota((near, lanes), 1) == global_row(side, iota((near, lanes), 0), cells_y)
    is_far = (shift_x > 0) == (core() == 1)
    copy = pltpu.make_async_copy(own_ref, mine_ref, semaphores.at[0])
    far_copy = pltpu.make_async_copy(far_ref, beyond_ref, semaphores.at[1])
    near_copy = pltpu.make_async_copy(near_ref, beyond_ref, semaphores.at[1])
    copy.start()
    pl.when(is_far)(far_copy.start)
    pl.when(jnp.logical_not(is_far))(near_copy.start)
    copy.wait()
    far_copy.wait()
    mask = masks_ref[half() if order == 0 else 1 - half()].astype(BF16)
    columns = lax.dot_general(
        pick.astype(F32).astype(BF16), mask, (((1,), (1,)), ((), ())), preferred_element_type=F32
    )
    row = global_row(side, iota((near, cells_z), 0), cells_y) + shift_y
    col = iota((near, cells_z), 1) + shift_z
    inside = (row >= 0) & (row < cells_y) & (col >= 0) & (col < cells_z)

    def fetch(p):
        source = p + shift_x
        x = slab * planes + source
        is_own = (source >= 0) & (source < planes)
        beyond = jnp.clip(jnp.where(source < 0, source + planes, source - planes), 0, planes - 1)
        value = jnp.where(is_own, mine_ref[jnp.clip(source, 0, planes - 1)], beyond_ref[beyond])
        weight = jnp.broadcast_to(columns[:, p:p + 1], (near, cells_z))
        covered = inside & (weight > 0.5) & (x >= 0) & (x < extent_x)
        value = jnp.where(covered, value, jnp.full_like(value, -1.0))
        image_ref[p] = value
        return value

    def blurred_of(block):
        return jnp.concatenate([blurred_ref[p] for p in block], axis=0)

    adjoint_planes(blurred_of, fetch, ya_ref, zhi_ref, zlo_ref, order, out_ref, edge_refs)


def next_ratio_kernel(*refs, inner, count, first_row):
    image_refs, wide_refs, refs = refs[:2], (refs[2:4], refs[4:6]), refs[6:]
    passed_ref, refs = (None, refs) if inner else (refs[0], refs[1:])
    (yf_ref, ya_ref, zhi_ref, zlo_ref), out_refs, (far_ref, near_ref), refs = refs[:4], refs[4:6], refs[6:8], refs[8:]
    planes = out_refs[0].shape[0]
    rows = yf_ref.shape[1]
    for order in range(2):

        def blurred_of(block):
            return blurred_planes(wide_refs[order], yf_ref, zhi_ref, zlo_ref, order, block)

        def image_of(p):
            return image_refs[order][p, first_row:first_row + rows]

        def complete(p, ratio):
            if inner:
                refs[0][order, p] = ratio[rows - count:]
                return ratio
            return jnp.concatenate([passed_ref[order, p], ratio], axis=0)

        edges = (far_ref.at[order], near_ref.at[order])
        adjoint_planes(blurred_of, image_of, ya_ref, zhi_ref, zlo_ref, order, out_refs[order], edges, complete)


def next_ratio(images, wides, passed, y_tables, z_tables, radius, count, first_row):
    planes, _, lanes = images[0].shape
    rows = y_tables[1].shape[1]
    kernel = functools.partial(next_ratio_kernel, inner=passed is None, count=count, first_row=first_row)
    shape = jax.ShapeDtypeStruct
    whole, edge = shape((planes, rows, lanes), F32), shape((2, radius, rows, lanes), F32)
    out_shape = (whole, whole, edge, edge)
    if passed is None:
        out_shape += (shape((2, planes, count, lanes), F32),)
    operands = [*images, *wides[0], *wides[1]] + ([] if passed is None else [passed]) + [*y_tables, *z_tables]
    return call(kernel, out_shape, [VMEM] * len(operands), "ratio")(*operands)


def first_ratio(shifts, blocks, masks, blurred, tables, order, radius, chunks, extent_x, cells_y):
    planes, near, lanes = blurred.shape
    kernel = functools.partial(first_ratio_kernel, order=order, extent_x=extent_x, cells_y=cells_y)
    rows = tables.whole[1].shape[1]
    out_shape = edge_shapes((planes, rows, lanes), radius, chunks) + (jax.ShapeDtypeStruct(blurred.shape, F32),)
    scratch = [
        pltpu.VMEM(blurred.shape, F32), pltpu.VMEM(blurred.shape, F32), pltpu.SemaphoreType.DMA((2,))
    ]
    in_specs = [SMEM] + [pl.BlockSpec(memory_space=pl.ANY)] * 3 + [VMEM] * 5
    return call(kernel, out_shape, in_specs, "image_and_ratio", scratch)(
        shifts, *blocks, masks, blurred, tables.whole[1], *tables.z
    )


def factor_kernel(hi_ref, lo_ref, before_ref, *refs, orders, starts, share):
    out_ref = refs[-1]
    planes, rows, _ = out_ref.shape

    def body(step, carry):
        row = pl.multiple_of(step * 8, 8)
        total = gather(before_ref, starts[0] + row)
        if share:
            total = share * jnp.log(total)
        for index, order in enumerate(orders):
            far_ref, near_ref, own_ref = refs[3 * index:3 * index + 3]
            if len(far_ref.shape) == 4:
                far_ref, near_ref = far_ref.at[order], near_ref.at[order]
            own = gather(own_ref, starts[1] + row)
            blocks = [[own, gather(near_ref, row)], [gather(far_ref, row)]]
            band_rows = slice(order * 8 * planes, (order + 1) * 8 * planes)
            total = total + jnp.log(spread_x(hi_ref, lo_ref, 1, band_rows, slice(None), blocks))
        out_ref[:, pl.ds(row, 8), :] = total
        return carry

    lax.fori_loop(0, rows // 8, body, 0)


def log_factor(tables, before, sides, orders, rows, starts, share):
    kernel = functools.partial(factor_kernel, orders=orders, starts=starts, share=share)
    planes, _, lanes = sides[0][2].shape
    shape = jax.ShapeDtypeStruct((planes, rows, lanes), F32)
    parts = [part for side in sides for part in side]
    return call(kernel, shape, [VMEM] * (3 + len(parts)), "log_factor")(*tables.x, before, *parts)


def update_kernel(*refs, count):
    parts, out_ref, edge_refs = refs[:count], refs[count], refs[count + 1:]
    for p in range(out_ref.shape[0]):
        total = parts[0][p]
        for part in parts[1:]:
            total = total + part[p]
        out_ref[p] = jnp.exp(total)
    put_edges(out_ref, edge_refs)


def update(parts, radius):
    kernel = functools.partial(update_kernel, count=len(parts))
    out_shape = edge_shapes(parts[0].shape, radius, parts[0].shape[1:2])
    return call(kernel, out_shape, [VMEM] * len(parts), "update")(*parts)


def finish_kernel(*refs):
    own, other, out_ref = refs[:(len(refs) - 1) // 2], refs[(len(refs) - 1) // 2:-1], refs[-1]
    straight = core() == half()
    groups = out_ref.shape[1] // GROUP
    for group in range(groups):
        rows = slice(group * GROUP, (group + 1) * GROUP)
        own_total, other_total = own[0][:, rows, :], other[0][:, rows, :]
        for part in own[1:]:
            own_total = own_total + part[:, rows, :]
        for part in other[1:]:
            other_total = other_total + part[:, rows, :]
        start = jnp.where(core() == 0, group, groups - 1 - group) * GROUP
        out_ref[:, pl.ds(pl.multiple_of(start, GROUP), GROUP), :] = jnp.exp(jnp.where(straight, own_total, other_total))


def finish(own_parts, other_parts):
    shape = jax.ShapeDtypeStruct(own_parts[0].shape, F32)
    return call(finish_kernel, shape, [VMEM] * (2 * len(own_parts)), "last_update")(*own_parts, *other_parts)


def join_kernel(*refs, starts):
    sources, out_ref, semaphores = refs[:-2], refs[-2], refs[-1]
    cells_y = out_ref.shape[1]
    copies = []
    for index, source_ref in enumerate(sources):
        rows, start = source_ref.shape[1], starts[index // 2]
        side = core() if index % 2 == 0 else 1 - core()
        place = pl.multiple_of(jnp.where(side == 0, start, cells_y - start - rows), GROUP)
        target = out_ref.at[:, pl.ds(place, rows), :]
        copies.append(pltpu.make_async_copy(source_ref, target, semaphores.at[index]))
    for copy in copies:
        copy.start()
    for copy in copies:
        copy.wait()


def join(pieces, starts, shape):
    anywhere = pl.BlockSpec(memory_space=pl.ANY)
    return pl.pallas_call(
        functools.partial(join_kernel, starts=starts),
        out_shape=jax.ShapeDtypeStruct(shape, F32),
        in_specs=[anywhere] * len(pieces),
        out_specs=anywhere,
        scratch_shapes=[pltpu.SemaphoreType.DMA((len(pieces),))],
        compiler_params=PARAMS,
        name="join_halves",
    )(*pieces)


def shards(acquired, estimate, offsets, view_mask, kern_x, kern_y, kern_z):
    planes, cells_y, cells_z = estimate.shape
    views, slabs = lax.axis_size("view"), lax.axis_size("tile")
    groups = views // 2
    taps_y = kern_y.shape[1]
    radius = kern_x.shape[1] // 2
    own_rows = cells_y // 2
    near = own_rows + pad_to(taps_y // 2, GROUP)
    wide = own_rows + pad_to(2 * (taps_y // 2), GROUP)
    edge_rows = wide - own_rows
    inner_rows = own_rows - edge_rows
    group = lax.axis_index("view") // 2
    straight = core() == half()

    def across(turn, half_of=lambda r: r, core_of=lambda c: c, when=lambda c, r: True):
        return lambda g, c, q, r: ((g + turn) % groups, core_of(c), q, half_of(r)) if when(c, r) else None

    def neighbours(far, near):
        return send(far, to_far), send(near, to_core_partner)

    window, crossed = make_windows(estimate, wide)
    crossed = send(crossed, across(0, lambda r: 1 - r, when=lambda c, r: c == r))

    mine = [jnp.pad(row, ((0, 0), (0, 128 - row.shape[1]))) for row in (kern_x, kern_y, kern_z)]
    mine = after(jnp.concatenate(mine, axis=1), window)
    other = send(mine, to_core_partner)
    taps = kern_x.shape[1], taps_y, kern_z.shape[1]
    tables = make_tables(mine, other, taps, planes, cells_y, cells_z, (own_rows, near, wide))
    offset = after(offsets.astype(F32), tables.whole[0])
    other = send(offset, to_core_partner)
    shifts = jnp.where(straight, jnp.concatenate([offset, other]), jnp.concatenate([other, offset])).astype(jnp.int32)

    mask = view_mask.astype(F32)
    other = send(mask, to_core_partner)
    masks = jnp.where(core() == 0, jnp.concatenate([mask, other]), jnp.concatenate([other, mask]))

    acquired = after(after(acquired, tables.whole[0]), masks)
    first, second = shift_and_cut(offsets, acquired[0], near)

    arrived = send(after(first, tables.whole[0]), lambda g, c, q, r: (g, r, q, c) if c != r else None)
    current, distant, close = choose(after(window, first), crossed, radius)
    second = send(after(second, current), lambda g, c, q, r: (g, r, q, 1 - c))
    distant, close = neighbours(distant, close)
    first = jnp.where(straight, first, arrived)

    masks = jnp.where(straight, masks, send(after(masks, current), to_row_partner))

    blocks = [(*neighbours(block, block), block) for block in (first, second)]
    wide_parts = blur_x(tables, (current, close), blur_x(tables, (distant,), (), planes), planes)
    blurred = [blur_yz([part], tables, order) for order, part in enumerate(wide_parts)]

    row_chunks = [(inner_rows, edge_rows), (0, inner_rows)]
    share = 1.0 / groups
    images, sides = [], []
    for order, chunk_sizes in enumerate(([own_rows], [edge_rows, inner_rows])):
        spread, *edges, image = first_ratio(
            shifts, blocks[order], masks, blurred[order], tables, order, radius, chunk_sizes, planes * slabs, cells_y
        )
        images.append(image)
        sides.append([(*neighbours(*edges[k:k + 2]), spread) for k in range(0, len(edges), 2)])
    total = log_factor(tables, current, sides[0], [0], own_rows, (0, 0), share)
    totals = [
        log_factor(tables, total, [side], [1], rows, (start, start), 0)
        for (start, rows), side in zip(row_chunks, sides[1])
    ]

    for step in range(1, ITERS):
        chunks, before = [], []
        for total in totals:
            parts = [total] + [send(total, across(turn)) for turn in range(1, groups)]
            rows, distant, close = update(parts, radius)
            if total is totals[0]:
                beyond = send(rows, to_row_partner)
            distant = after(distant, chunks[0][0]) if chunks else distant
            distant, close = neighbours(distant, close)
            chunks.append((distant, blur_near(tables, rows, close)))
            before.append(rows)
        rest = planes - radius
        distant, close = neighbours(
            lax.dynamic_slice_in_dim(beyond, core() * rest, radius, 0),
            lax.dynamic_slice_in_dim(beyond, (1 - core()) * rest, radius, 0),
        )
        edge_parts, inner_parts = [blur_far(tables, *chunk) for chunk in chunks]
        halo_parts = blur_near(tables, beyond, close)
        *inner_spreads, distant_inner, close_inner, passed = next_ratio(
            images, list(zip([after(after(part, distant), halo_parts[0]) for part in inner_parts], edge_parts)), None, tables.inner, tables.z, radius, 2 * (near - own_rows), 0
        )
        halo_parts = blur_far(tables, distant, halo_parts)
        inner_side = neighbours(distant_inner, close_inner)
        *edge_spreads, distant, close = next_ratio(
            images, list(zip(edge_parts, halo_parts)), passed, tables.edge, tables.z, radius, 0,
            inner_rows + near - own_rows,
        )
        edge_side = neighbours(distant, close)
        totals = [
            log_factor(tables, rows_of, [(*side, spread) for spread in spreads], [0, 1], rows, (0, 0), share)
            for rows_of, side, spreads, rows in (
                (before[0], edge_side, edge_spreads, edge_rows), (before[1], inner_side, inner_spreads, inner_rows)
            )
        ]

    pieces = []
    for own in totals[::-1]:
        other_parts = [
            send(own, across(turn, lambda r: 1 - r, lambda c: 1 - c, lambda c, r: c != r))
            for turn in reversed(range(groups))
        ]
        own_parts = [own] + [send(own, across(turn, when=lambda c, r: c == r)) for turn in range(1, groups)]
        mine = finish(own_parts, other_parts)
        pieces += [mine, send(mine, to_core_partner)]
    return join(pieces, [start for start, _ in row_chunks[::-1]], estimate.shape)


def solution(mesh):
    in_specs = (
        P("view", "tile", None, None),
        P("tile", None, None),
        P("view", None),
        P("view", "tile", None),
        P("view", None),
        P("view", None),
        P("view", None),
    )
    out_specs = P("tile", None, None)
    return jax.shard_map(shards, mesh=mesh, in_specs=in_specs, out_specs=out_specs, check_vma=False)
```

```python
import functools
import typing

import jax
import jax.numpy as jnp
from jax import lax
from jax.experimental import pallas as pl
from jax.experimental.pallas import tpu as pltpu
from jax.sharding import PartitionSpec as P

ITERS = 2
AXES = ("view", "tile")
F32 = jnp.float32
BF16 = jnp.bfloat16
VMEM = pl.BlockSpec(memory_space=pltpu.VMEM)
SMEM = pl.BlockSpec(memory_space=pltpu.SMEM)
PARAMS = pltpu.CompilerParams(vmem_limit_bytes=12 * 1024 * 1024)
GROUP = 16


def moves(move):
    views, tiles = lax.axis_size("view"), lax.axis_size("tile")
    pairs = []
    for view in range(views):
        for tile in range(tiles):
            target = move(view // 2, view % 2, tile // 2, tile % 2)
            if target is not None:
                g, c, q, r = target
                pairs.append((view * tiles + tile, (2 * g + c) * tiles + 2 * q + r))
    return pairs


def send(array, move):
    return lax.ppermute(array, AXES, moves(move))


def after(array, other):
    return lax.optimization_barrier((array, other))[0]


def to_far(g, c, q, r):
    s = 2 * q + c + (1 if c else -1)
    return (g, s % 2, s // 2, r) if 0 <= s < lax.axis_size("tile") else None


def to_row_partner(g, c, q, r):
    return (g, c, q, 1 - r)


def to_core_partner(g, c, q, r):
    return (g, 1 - c, q, r)


def core():
    return lax.rem(lax.axis_index("view"), 2)


def half():
    return lax.rem(lax.axis_index("tile"), 2)


def split(x):
    high = x.astype(BF16)
    return high, (x - high.astype(F32)).astype(BF16)


def dot(a, b):
    return jnp.dot(a, b, preferred_element_type=F32)


def iota(shape, dim):
    return lax.broadcasted_iota(jnp.int32, shape, dim)


def group_row(half, group, cells_y):
    return group * GROUP + half * (cells_y - GROUP - 2 * group * GROUP)


def global_row(half, local, cells_y):
    group = local // GROUP
    return group_row(half, group, cells_y) + (local - group * GROUP)


def wide_local(place, own, wide):
    group = (place - own) // GROUP
    return own + (wide - own) - GROUP - group * GROUP + (place - own - group * GROUP)


def wide_group(group, own_groups, groups):
    return group if group < own_groups else own_groups + groups - 1 - group


def pad_to(value, unit):
    return -(-value // unit) * unit


def call(kernel, out_shape, in_specs, name, scratch=(), hbm=()):
    if hbm:
        out_shape = tuple(pltpu.HBM(o.shape, o.dtype) if index in hbm else o for index, o in enumerate(out_shape))
    return pl.pallas_call(
        kernel,
        out_shape=out_shape,
        in_specs=in_specs,
        out_specs=(VMEM,) * len(out_shape) if isinstance(out_shape, tuple) else VMEM,
        scratch_shapes=list(scratch),
        compiler_params=PARAMS,
        name=name,
    )


class Tables(typing.NamedTuple):
    whole: tuple
    inner: tuple
    edge: tuple
    z: tuple
    x: tuple


def place(row, count, width, turned, spacing):
    source, target = iota((row.shape[1], width), 0), iota((row.shape[1], width), 1)
    index = count - 1 - source if turned else source
    ones = (target == spacing * index) & (source < count)
    return jnp.dot(row, ones.astype(F32), precision=lax.Precision.HIGHEST, preferred_element_type=F32)


def tables_kernel(mine_ref, other_ref, *refs, blocks, sizes, cells_y, taps):
    y_refs, (zhi_ref, zlo_ref, xhi_ref, xlo_ref) = refs[:-4], refs[-4:]
    taps_x, taps_y, taps_z = taps
    straight = core() == half()
    mine, other = mine_ref[...], other_ref[...]
    both = (jnp.where(straight, mine, other), jnp.where(straight, other, mine))
    radius, radius_x, radius_z = taps_y // 2, taps_x // 2, taps_z // 2
    side = half()
    own, wide = sizes
    for out_ref, adjoint, first_row, first_col, width in zip(y_refs, *zip(*blocks)):
        _, rows, lanes = out_ref.shape
        row = global_row(side, first_row + iota((rows, lanes), 0), cells_y)
        lane = iota((rows, lanes), 1)
        place_of = lane + first_col
        turned = place_of if adjoint else jnp.where(place_of < own, place_of, wide_local(place_of, own, wide))
        col = global_row(side, turned, cells_y)
        delta = (row - col if adjoint else col - row) + radius
        delta = jnp.where(lane < width, delta, -1)
        for order in range(2):
            band = jnp.zeros((rows, lanes), F32)
            values = both[order][:, 128:256]
            for a in range(taps_y):
                band = jnp.where(delta == a, jnp.broadcast_to(values[:, a:a + 1], (rows, lanes)), band)
            high, low = split(band)
            high, low = high.astype(F32), low.astype(F32)
            out_ref[order] = (high + pltpu.roll(high, width, 1) + pltpu.roll(low, 2 * width, 1)).astype(BF16)

    lanes = zhi_ref.shape[2]
    near_z = jnp.abs(iota((lanes, lanes), 1) - iota((lanes, lanes), 0)) <= radius_z
    for index in range(4):
        base = place(both[index % 2][:, 256:384], taps_z, lanes, index < 2, 1)
        base = pltpu.roll(base, lanes - radius_z, 1)
        band = pltpu.roll(jnp.broadcast_to(base, (lanes, lanes)), 0, 1, stride=1, stride_axis=0)
        zhi_ref[index], zlo_ref[index] = split(jnp.where(near_z, band, jnp.zeros_like(band)))

    rows = xhi_ref.shape[1] // 2
    lanes = max(512, 1 << (xhi_ref.shape[2] - 1).bit_length())
    for index in range(4):
        base = place(both[index % 2][:, :128], taps_x, lanes, index >= 2, 8)
        base = jnp.broadcast_to(base, (rows, lanes))
        band = pltpu.roll(base, 0, 1, stride=1, stride_axis=0)
        lane = iota((rows, lanes), 1)
        edge = 8 * radius_x
        far = pad_to(rows + edge, 128)
        next_near = pltpu.roll(band, lanes - edge, 1)
        next_far = pltpu.roll(band, far - rows - edge, 1)
        near_part = jnp.where((lane < rows) | (core() == 0), next_near, pltpu.roll(band, rows, 1))
        far_part = jnp.where(core() == 0, pltpu.roll(band, far, 1), next_far)
        zero = jnp.zeros_like(band)
        band = jnp.where(
            lane < rows + edge, near_part, jnp.where((lane >= far) & (lane < far + edge), far_part, zero)
        )[:, :xhi_ref.shape[2]]
        block = (index // 2, slice(index % 2 * rows, index % 2 * rows + rows))
        xhi_ref[block], xlo_ref[block] = split(band)


def make_tables(mine, other, taps, planes, cells_y, cells_z, sizes):
    own, near, wide = sizes
    inner, beyond = 2 * own - wide, near - own
    radius = taps[0] // 2
    depth = pad_to(8 * (planes + radius), 128) + pad_to(8 * radius, 128)
    blocks = [
        (False, near, 0, 0, wide), (True, own, 0, 0, near),
        (False, inner + beyond, 0, 0, own), (True, inner, 0, 0, inner + beyond),
        (False, near - inner - beyond, inner + beyond, inner, wide - inner),
        (True, own - inner, inner, inner - beyond, near - inner + beyond),
    ]
    kernel = functools.partial(
        tables_kernel, blocks=[block[:1] + block[2:] for block in blocks], sizes=(own, wide), cells_y=cells_y, taps=taps
    )
    shape = jax.ShapeDtypeStruct
    out_shape = tuple(shape((2, block[1], pad_to(3 * block[4], 128)), BF16) for block in blocks) + (
        shape((4, cells_z, cells_z), BF16),
        shape((4, cells_z, cells_z), BF16),
        shape((2, 2 * 8 * planes, depth), BF16),
        shape((2, 2 * 8 * planes, depth), BF16),
    )
    tables = call(kernel, out_shape, [VMEM, VMEM], "band_matrices", hbm=range(1, 6))(mine, other)
    whole, inner_rows, edge_rows = tables[0:2], tables[2:4], tables[4:6]
    return Tables(whole, inner_rows, edge_rows, tables[6:8], tables[8:10])


def window_kernel(estimate_ref, own_ref, other_ref):
    cells_y = estimate_ref.shape[1]
    groups = own_ref.shape[1] // GROUP
    for side, out_ref in ((half(), own_ref), (1 - half(), other_ref)):
        for group in range(groups):
            local = wide_group(group, cells_y // 2 // GROUP, groups)
            start = pl.multiple_of(group_row(side, local, cells_y), GROUP)
            out_ref[:, group * GROUP:(group + 1) * GROUP, :] = estimate_ref[:, pl.ds(start, GROUP), :]


def make_windows(estimate, wide):
    planes, _, cells_z = estimate.shape
    shape = jax.ShapeDtypeStruct((planes, wide, cells_z), F32)
    return call(window_kernel, (shape, shape), [VMEM], "estimate_windows", hbm=(0, 1))(estimate)


def put_edges(out_ref, edge_refs):
    end = out_ref.shape[1]
    for far_ref, near_ref in zip(edge_refs[::2], edge_refs[1::2]):
        radius, rows = far_ref.shape[0], slice(end - far_ref.shape[1], end)
        beyond = out_ref.shape[0] - radius
        for p in range(radius):
            far_ref[p] = out_ref[p + core() * beyond, rows]
            near_ref[p] = out_ref[p + (1 - core()) * beyond, rows]
        end -= far_ref.shape[1]


def choose_kernel(window_ref, crossed_ref, out_ref, *edge_refs):
    straight = core() == half()
    for p in range(out_ref.shape[0]):
        out_ref[p] = jnp.where(straight, window_ref[p], crossed_ref[p])
    put_edges(out_ref, edge_refs)


def edge_shapes(shape, radius, chunks):
    planes, _, lanes = shape
    edges = [jax.ShapeDtypeStruct((radius, rows, lanes), F32) for rows in chunks for _ in range(2)]
    return (jax.ShapeDtypeStruct(shape, F32), *edges)


def choose(window, crossed, radius):
    out_shape = edge_shapes(window.shape, radius, window.shape[1:2])
    return call(choose_kernel, out_shape, [VMEM] * 2, "estimate", hbm=(2,))(
        pltpu.with_memory_space_constraint(window, pltpu.HBM), crossed
    )


def shift_kernel(offsets_ref, acq_ref, first_ref, second_ref, turned_ref):
    planes, cells_y, cells_z = acq_ref.shape
    near = first_ref.shape[1]
    shift_y, shift_z = offsets_ref[0, 1], offsets_ref[0, 2]
    row = iota((cells_y, cells_z), 0) + shift_y
    col = iota((cells_y, cells_z), 1) + shift_z
    inside = (row >= 0) & (row < cells_y) & (col >= 0) & (col < cells_z)
    turn_y = lax.rem(cells_y - shift_y, cells_y)
    turn_z = lax.rem(cells_z - shift_z, cells_z)

    def body(p, carry):
        x = pltpu.roll(pltpu.roll(acq_ref[p], turn_z, 1), turn_y, 0)
        turned_ref[...] = jnp.where(inside, x, jnp.zeros_like(x))
        for side, out_ref in ((core(), first_ref), (1 - core(), second_ref)):
            for group in range(near // GROUP):
                start = pl.multiple_of(group_row(side, group, cells_y), GROUP)
                out_ref[p, group * GROUP:(group + 1) * GROUP, :] = turned_ref[pl.ds(start, GROUP), :]
        return carry

    lax.fori_loop(0, planes, body, 0)


def shift_and_cut(offsets, acquired, near):
    planes, cells_y, cells_z = acquired.shape
    shape = jax.ShapeDtypeStruct((planes, near, cells_z), F32)
    scratch = [pltpu.VMEM((cells_y, cells_z), F32)]
    return call(shift_kernel, (shape, shape), [SMEM, VMEM], "shift_recorded", scratch)(offsets, acquired)


def gather(ref, row):
    return ref[:, pl.ds(pl.multiple_of(row, 8), 8), :]


def spread_x(hi_ref, lo_ref, index, band_rows, band_lanes, blocks):
    lanes = blocks[0][0].shape[2]
    filled = []
    for parts in blocks:
        count = 8 * sum(part.shape[0] for part in parts)
        missing = (pad_to(count, 128) - count) // 8
        filled += list(parts) + ([jnp.zeros((missing, 8, lanes), F32)] if missing else [])
    high, low = split(jnp.concatenate(filled, axis=0).reshape(-1, lanes))
    band = hi_ref[index, band_rows, band_lanes]
    out = dot(band, high) + (dot(band, low) + dot(lo_ref[index, band_rows, band_lanes], high))
    return out.reshape(-1, 8, lanes)


def near_lanes(planes, radius):
    return pad_to(8 * (planes + radius), 128)


def blur_x_kernel(hi_ref, lo_ref, *refs, far, radius):
    planes_of, before, (first_ref, second_ref) = refs[:2 - far], refs[2 - far:-2], refs[-2:]
    planes, rows, _ = first_ref.shape
    split_at = near_lanes(planes, radius)
    lanes = slice(split_at, None) if far else slice(0, split_at)

    def body(step, carry):
        row = pl.multiple_of(step * 8, 8)
        place = (slice(None), pl.ds(row, 8), slice(None))
        out = spread_x(hi_ref, lo_ref, 0, slice(None), lanes, [[gather(ref, row) for ref in planes_of]])
        out = [out[:planes], out[planes:]]
        if before:
            out = [ref[place] + part for ref, part in zip(before, out)]
        first_ref[place], second_ref[place] = out
        return carry

    lax.fori_loop(0, rows // 8, body, 0)


def blur_x(tables, planes_of, before, planes):
    far, (radius, rows, lanes) = len(planes_of) == 1, planes_of[-1].shape
    shape = jax.ShapeDtypeStruct((planes, rows, lanes), F32)
    kernel = functools.partial(blur_x_kernel, far=far, radius=radius)
    operands = [*tables.x, *planes_of, *before]
    return call(kernel, (shape, shape), [VMEM] * len(operands), "blur_x_far" if far else "blur_x_near")(*operands)


def blur_near(tables, own, near):
    return blur_x(tables, (own, near), (), own.shape[0])


def blur_far(tables, far, parts):
    return blur_x(tables, (far,), parts, parts[0].shape[0])


def spread_y(band, x):
    high, low = split(x)
    return dot(band[:, :3 * x.shape[0]], jnp.concatenate([high, low, high], axis=0))


def spread_z(x, hi_ref, lo_ref, index):
    high, low = split(x)
    return dot(high, hi_ref[index]) + (dot(low, hi_ref[index]) + dot(high, lo_ref[index]))


def blurred_planes(wide_refs, yf_ref, zhi_ref, zlo_ref, order, block):
    wide = [jnp.concatenate([ref[p] for ref in wide_refs], axis=0) for p in block]
    spread = jnp.concatenate([spread_y(yf_ref[order], rows) for rows in wide], axis=0)
    return spread_z(spread, zhi_ref, zlo_ref, order)


def plane_blocks(planes, step=4):
    return [range(start, min(start + step, planes)) for start in range(0, planes, step)]


def blur_yz_kernel(*refs, order):
    wide_refs, (yf_ref, zhi_ref, zlo_ref, out_ref) = refs[:-4], refs[-4:]
    near = yf_ref.shape[1]
    for block in plane_blocks(out_ref.shape[0]):
        blurred = blurred_planes(wide_refs, yf_ref, zhi_ref, zlo_ref, order, block)
        for k, p in enumerate(block):
            out_ref[p] = blurred[k * near:(k + 1) * near]


def blur_yz(wides, tables, order):
    planes, _, lanes = wides[0].shape
    shape = jax.ShapeDtypeStruct((planes, tables.whole[0].shape[1], lanes), F32)
    kernel = functools.partial(blur_yz_kernel, order=order)
    return call(kernel, shape, [VMEM] * (3 + len(wides)), "blur_yz")(*wides, tables.whole[0], *tables.z)


def adjoint_planes(blurred_of, image_of, ya_ref, zhi_ref, zlo_ref, order, out_ref, edge_refs, complete=None):
    planes, rows, _ = out_ref.shape
    for block in plane_blocks(planes):
        blurred = blurred_of(block)
        image = jnp.concatenate([image_of(p) for p in block], axis=0)
        ratio = jnp.where(image >= 0, image / blurred, jnp.ones_like(image))
        near = ratio.shape[0] // len(block)
        ratios = [ratio[k * near:(k + 1) * near] for k in range(len(block))]
        if complete:
            ratios = [complete(p, rows_of) for p, rows_of in zip(block, ratios)]
        spread = jnp.concatenate([spread_y(ya_ref[order], rows_of) for rows_of in ratios], axis=0)
        spread = spread_z(spread, zhi_ref, zlo_ref, 2 + order)
        for k, p in enumerate(block):
            out_ref[p] = spread[k * rows:(k + 1) * rows]
    put_edges(out_ref, edge_refs)


def first_ratio_kernel(
    shift_ref, far_ref, near_ref, own_ref, masks_ref, blurred_ref, ya_ref, zhi_ref, zlo_ref, out_ref, *refs, order, extent_x, cells_y
):
    edge_refs, image_ref, (mine_ref, beyond_ref, semaphores) = refs[:-4], refs[-4], refs[-3:]
    planes, near, cells_z = image_ref.shape
    side = half()
    slab = lax.axis_index("tile") - side + core()
    shift_x, shift_y, shift_z = (shift_ref[order, i] for i in range(3))
    lanes = masks_ref.shape[2]
    pick = iota((near, lanes), 1) == global_row(side, iota((near, lanes), 0), cells_y)
    is_far = (shift_x > 0) == (core() == 1)
    copy = pltpu.make_async_copy(own_ref, mine_ref, semaphores.at[0])
    far_copy = pltpu.make_async_copy(far_ref, beyond_ref, semaphores.at[1])
    near_copy = pltpu.make_async_copy(near_ref, beyond_ref, semaphores.at[1])
    copy.start()
    pl.when(is_far)(far_copy.start)
    pl.when(jnp.logical_not(is_far))(near_copy.start)
    copy.wait()
    far_copy.wait()
    mask = masks_ref[half() if order == 0 else 1 - half()].astype(BF16)
    columns = lax.dot_general(
        pick.astype(F32).astype(BF16), mask, (((1,), (1,)), ((), ())), preferred_element_type=F32
    )
    row = global_row(side, iota((near, cells_z), 0), cells_y) + shift_y
    col = iota((near, cells_z), 1) + shift_z
    inside = (row >= 0) & (row < cells_y) & (col >= 0) & (col < cells_z)

    def fetch(p):
        source = p + shift_x
        x = slab * planes + source
        is_own = (source >= 0) & (source < planes)
        beyond = jnp.clip(jnp.where(source < 0, source + planes, source - planes), 0, planes - 1)
        value = jnp.where(is_own, mine_ref[jnp.clip(source, 0, planes - 1)], beyond_ref[beyond])
        weight = jnp.broadcast_to(columns[:, p:p + 1], (near, cells_z))
        covered = inside & (weight > 0.5) & (x >= 0) & (x < extent_x)
        value = jnp.where(covered, value, jnp.full_like(value, -1.0))
        image_ref[p] = value
        return value

    def blurred_of(block):
        return jnp.concatenate([blurred_ref[p] for p in block], axis=0)

    adjoint_planes(blurred_of, fetch, ya_ref, zhi_ref, zlo_ref, order, out_ref, edge_refs)


def next_ratio_kernel(*refs, inner, count, first_row):
    image_refs, wide_refs, refs = refs[:2], (refs[2:4], refs[4:6]), refs[6:]
    passed_ref, refs = (None, refs) if inner else (refs[0], refs[1:])
    (yf_ref, ya_ref, zhi_ref, zlo_ref), out_refs, (far_ref, near_ref), refs = refs[:4], refs[4:6], refs[6:8], refs[8:]
    planes = out_refs[0].shape[0]
    rows = yf_ref.shape[1]
    for order in range(2):

        def blurred_of(block):
            return blurred_planes(wide_refs[order], yf_ref, zhi_ref, zlo_ref, order, block)

        def image_of(p):
            return image_refs[order][p, first_row:first_row + rows]

        def complete(p, ratio):
            if inner:
                refs[0][order, p] = ratio[rows - count:]
                return ratio
            return jnp.concatenate([passed_ref[order, p], ratio], axis=0)

        edges = (far_ref.at[order], near_ref.at[order])
        adjoint_planes(blurred_of, image_of, ya_ref, zhi_ref, zlo_ref, order, out_refs[order], edges, complete)


def next_ratio(images, wides, passed, y_tables, z_tables, radius, count, first_row):
    planes, _, lanes = images[0].shape
    rows = y_tables[1].shape[1]
    kernel = functools.partial(next_ratio_kernel, inner=passed is None, count=count, first_row=first_row)
    shape = jax.ShapeDtypeStruct
    whole, edge = shape((planes, rows, lanes), F32), shape((2, radius, rows, lanes), F32)
    out_shape = (whole, whole, edge, edge)
    if passed is None:
        out_shape += (shape((2, planes, count, lanes), F32),)
    operands = [*images, *wides[0], *wides[1]] + ([] if passed is None else [passed]) + [*y_tables, *z_tables]
    return call(kernel, out_shape, [VMEM] * len(operands), "ratio")(*operands)


def first_ratio(shifts, blocks, masks, blurred, tables, order, radius, chunks, extent_x, cells_y):
    planes, near, lanes = blurred.shape
    kernel = functools.partial(first_ratio_kernel, order=order, extent_x=extent_x, cells_y=cells_y)
    rows = tables.whole[1].shape[1]
    out_shape = edge_shapes((planes, rows, lanes), radius, chunks) + (jax.ShapeDtypeStruct(blurred.shape, F32),)
    scratch = [
        pltpu.VMEM(blurred.shape, F32), pltpu.VMEM(blurred.shape, F32), pltpu.SemaphoreType.DMA((2,))
    ]
    in_specs = [SMEM] + [pl.BlockSpec(memory_space=pl.ANY)] * 3 + [VMEM] * 5
    return call(kernel, out_shape, in_specs, "image_and_ratio", scratch, hbm=(len(out_shape) - 1,))(
        shifts, *blocks, masks, blurred, tables.whole[1], *tables.z
    )


def factor_kernel(hi_ref, lo_ref, before_ref, *refs, orders, starts, share):
    out_ref = refs[-1]
    planes, rows, _ = out_ref.shape

    def body(step, carry):
        row = pl.multiple_of(step * 8, 8)
        total = gather(before_ref, starts[0] + row)
        if share:
            total = share * jnp.log(total)
        for index, order in enumerate(orders):
            far_ref, near_ref, own_ref = refs[3 * index:3 * index + 3]
            if len(far_ref.shape) == 4:
                far_ref, near_ref = far_ref.at[order], near_ref.at[order]
            own = gather(own_ref, starts[1] + row)
            blocks = [[own, gather(near_ref, row)], [gather(far_ref, row)]]
            band_rows = slice(order * 8 * planes, (order + 1) * 8 * planes)
            total = total + jnp.log(spread_x(hi_ref, lo_ref, 1, band_rows, slice(None), blocks))
        out_ref[:, pl.ds(row, 8), :] = total
        return carry

    lax.fori_loop(0, rows // 8, body, 0)


def log_factor(tables, before, sides, orders, rows, starts, share):
    kernel = functools.partial(factor_kernel, orders=orders, starts=starts, share=share)
    planes, _, lanes = sides[0][2].shape
    shape = jax.ShapeDtypeStruct((planes, rows, lanes), F32)
    parts = [part for side in sides for part in side]
    return call(kernel, shape, [VMEM] * (3 + len(parts)), "log_factor")(*tables.x, before, *parts)


def update_kernel(*refs, count):
    parts, out_ref, edge_refs = refs[:count], refs[count], refs[count + 1:]
    for p in range(out_ref.shape[0]):
        total = parts[0][p]
        for part in parts[1:]:
            total = total + part[p]
        out_ref[p] = jnp.exp(total)
    put_edges(out_ref, edge_refs)


def update(parts, radius):
    kernel = functools.partial(update_kernel, count=len(parts))
    out_shape = edge_shapes(parts[0].shape, radius, parts[0].shape[1:2])
    return call(kernel, out_shape, [VMEM] * len(parts), "update")(*parts)


def finish_kernel(*refs):
    own, other, out_ref = refs[:(len(refs) - 1) // 2], refs[(len(refs) - 1) // 2:-1], refs[-1]
    straight = core() == half()
    groups = out_ref.shape[1] // GROUP
    for group in range(groups):
        rows = slice(group * GROUP, (group + 1) * GROUP)
        own_total, other_total = own[0][:, rows, :], other[0][:, rows, :]
        for part in own[1:]:
            own_total = own_total + part[:, rows, :]
        for part in other[1:]:
            other_total = other_total + part[:, rows, :]
        start = jnp.where(core() == 0, group, groups - 1 - group) * GROUP
        out_ref[:, pl.ds(pl.multiple_of(start, GROUP), GROUP), :] = jnp.exp(jnp.where(straight, own_total, other_total))


def finish(own_parts, other_parts):
    shape = jax.ShapeDtypeStruct(own_parts[0].shape, F32)
    return call(finish_kernel, shape, [VMEM] * (2 * len(own_parts)), "last_update")(*own_parts, *other_parts)


def join_kernel(*refs, starts):
    sources, out_ref, semaphores = refs[:-2], refs[-2], refs[-1]
    cells_y = out_ref.shape[1]
    copies = []
    for index, source_ref in enumerate(sources):
        rows, start = source_ref.shape[1], starts[index // 2]
        side = core() if index % 2 == 0 else 1 - core()
        place = pl.multiple_of(jnp.where(side == 0, start, cells_y - start - rows), GROUP)
        target = out_ref.at[:, pl.ds(place, rows), :]
        copies.append(pltpu.make_async_copy(source_ref, target, semaphores.at[index]))
    for copy in copies:
        copy.start()
    for copy in copies:
        copy.wait()


def join(pieces, starts, shape):
    anywhere = pl.BlockSpec(memory_space=pl.ANY)
    return pl.pallas_call(
        functools.partial(join_kernel, starts=starts),
        out_shape=jax.ShapeDtypeStruct(shape, F32),
        in_specs=[anywhere] * len(pieces),
        out_specs=anywhere,
        scratch_shapes=[pltpu.SemaphoreType.DMA((len(pieces),))],
        compiler_params=PARAMS,
        name="join_halves",
    )(*pieces)


def shards(acquired, estimate, offsets, view_mask, kern_x, kern_y, kern_z):
    planes, cells_y, cells_z = estimate.shape
    views, slabs = lax.axis_size("view"), lax.axis_size("tile")
    groups = views // 2
    taps_y = kern_y.shape[1]
    radius = kern_x.shape[1] // 2
    own_rows = cells_y // 2
    near = own_rows + pad_to(taps_y // 2, GROUP)
    wide = own_rows + pad_to(2 * (taps_y // 2), GROUP)
    edge_rows = wide - own_rows
    inner_rows = own_rows - edge_rows
    group = lax.axis_index("view") // 2
    straight = core() == half()

    def across(turn, half_of=lambda r: r, core_of=lambda c: c, when=lambda c, r: True):
        return lambda g, c, q, r: ((g + turn) % groups, core_of(c), q, half_of(r)) if when(c, r) else None

    def neighbours(far, near):
        return send(far, to_far), send(near, to_core_partner)

    window, crossed = make_windows(estimate, wide)
    crossed = send(crossed, across(0, lambda r: 1 - r, when=lambda c, r: c == r))

    mine = [jnp.pad(row, ((0, 0), (0, 128 - row.shape[1]))) for row in (kern_x, kern_y, kern_z)]
    mine = after(jnp.concatenate(mine, axis=1), window)
    other = send(mine, to_core_partner)
    taps = kern_x.shape[1], taps_y, kern_z.shape[1]
    tables = make_tables(mine, other, taps, planes, cells_y, cells_z, (own_rows, near, wide))
    offset = after(offsets.astype(F32), tables.whole[0])
    other = send(offset, to_core_partner)
    shifts = jnp.where(straight, jnp.concatenate([offset, other]), jnp.concatenate([other, offset])).astype(jnp.int32)

    mask = view_mask.astype(F32)
    other = send(mask, to_core_partner)
    masks = jnp.where(core() == 0, jnp.concatenate([mask, other]), jnp.concatenate([other, mask]))

    acquired = after(after(acquired, tables.whole[0]), masks)
    first, second = shift_and_cut(offsets, acquired[0], near)

    arrived = send(after(first, tables.whole[0]), lambda g, c, q, r: (g, r, q, c) if c != r else None)
    current, distant, close = choose(after(window, first), crossed, radius)
    second = send(after(second, current), lambda g, c, q, r: (g, r, q, 1 - c))
    distant, close = neighbours(distant, close)
    first = jnp.where(straight, first, arrived)

    masks = jnp.where(straight, masks, send(after(masks, current), to_row_partner))

    blocks = [(*neighbours(block, block), block) for block in (first, second)]
    wide_parts = blur_x(tables, (current, close), blur_x(tables, (distant,), (), planes), planes)
    blurred = [blur_yz([part], tables, order) for order, part in enumerate(wide_parts)]

    row_chunks = [(inner_rows, edge_rows), (0, inner_rows)]
    share = 1.0 / groups
    images, sides = [], []
    for order, chunk_sizes in enumerate(([own_rows], [edge_rows, inner_rows])):
        spread, *edges, image = first_ratio(
            shifts, blocks[order], masks, blurred[order], tables, order, radius, chunk_sizes, planes * slabs, cells_y
        )
        images.append(image)
        sides.append([(*neighbours(*edges[k:k + 2]), spread) for k in range(0, len(edges), 2)])
    total = log_factor(tables, current, sides[0], [0], own_rows, (0, 0), share)
    totals = [
        log_factor(tables, total, [side], [1], rows, (start, start), 0)
        for (start, rows), side in zip(row_chunks, sides[1])
    ]

    for step in range(1, ITERS):
        chunks, before = [], []
        for total in totals:
            parts = [total] + [send(total, across(turn)) for turn in range(1, groups)]
            rows, distant, close = update(parts, radius)
            if total is totals[0]:
                beyond = send(rows, to_row_partner)
            distant = after(distant, chunks[0][0]) if chunks else distant
            distant, close = neighbours(distant, close)
            chunks.append((distant, blur_near(tables, rows, close)))
            before.append(rows)
        rest = planes - radius
        distant, close = neighbours(
            lax.dynamic_slice_in_dim(beyond, core() * rest, radius, 0),
            lax.dynamic_slice_in_dim(beyond, (1 - core()) * rest, radius, 0),
        )
        edge_parts, inner_parts = [blur_far(tables, *chunk) for chunk in chunks]
        halo_parts = blur_near(tables, beyond, close)
        *inner_spreads, distant_inner, close_inner, passed = next_ratio(
            images, list(zip([after(after(part, distant), halo_parts[0]) for part in inner_parts], edge_parts)), None, tables.inner, tables.z, radius, 2 * (near - own_rows), 0
        )
        halo_parts = blur_far(tables, distant, halo_parts)
        inner_side = neighbours(distant_inner, close_inner)
        *edge_spreads, distant, close = next_ratio(
            images, list(zip(edge_parts, halo_parts)), passed, tables.edge, tables.z, radius, 0,
            inner_rows + near - own_rows,
        )
        edge_side = neighbours(distant, close)
        totals = [
            log_factor(tables, rows_of, [(*side, spread) for spread in spreads], [0, 1], rows, (0, 0), share)
            for rows_of, side, spreads, rows in (
                (before[0], edge_side, edge_spreads, edge_rows), (before[1], inner_side, inner_spreads, inner_rows)
            )
        ]

    pieces = []
    for own in totals[::-1]:
        other_parts = [
            send(own, across(turn, lambda r: 1 - r, lambda c: 1 - c, lambda c, r: c != r))
            for turn in reversed(range(groups))
        ]
        own_parts = [own] + [send(own, across(turn, when=lambda c, r: c == r)) for turn in range(1, groups)]
        mine = finish(own_parts, other_parts)
        pieces += [mine, send(mine, to_core_partner)]
    return join(pieces, [start for start, _ in row_chunks[::-1]], estimate.shape)


def solution(mesh):
    in_specs = (
        P("view", "tile", None, None),
        P("tile", None, None),
        P("view", None),
        P("view", "tile", None),
        P("view", None),
        P("view", None),
        P("view", None),
    )
    out_specs = P("tile", None, None)
    return jax.shard_map(shards, mesh=mesh, in_specs=in_specs, out_specs=out_specs, check_vma=False)
```

```python
import functools
import typing

import jax
import jax.numpy as jnp
from jax import lax
from jax.experimental import pallas as pl
from jax.experimental.pallas import tpu as pltpu
from jax.sharding import PartitionSpec as P

ITERS = 2
AXES = ("view", "tile")
F32 = jnp.float32
BF16 = jnp.bfloat16
VMEM = pl.BlockSpec(memory_space=pltpu.VMEM)
SMEM = pl.BlockSpec(memory_space=pltpu.SMEM)
PARAMS = pltpu.CompilerParams(vmem_limit_bytes=12 * 1024 * 1024)
GROUP = 16


def moves(move):
    views, tiles = lax.axis_size("view"), lax.axis_size("tile")
    pairs = []
    for view in range(views):
        for tile in range(tiles):
            target = move(view // 2, view % 2, tile // 2, tile % 2)
            if target is not None:
                g, c, q, r = target
                pairs.append((view * tiles + tile, (2 * g + c) * tiles + 2 * q + r))
    return pairs


def send(array, move):
    return lax.ppermute(array, AXES, moves(move))


def after(array, other):
    return lax.optimization_barrier((array, other))[0]


def to_far(g, c, q, r):
    s = 2 * q + c + (1 if c else -1)
    return (g, s % 2, s // 2, r) if 0 <= s < lax.axis_size("tile") else None


def to_row_partner(g, c, q, r):
    return (g, c, q, 1 - r)


def to_core_partner(g, c, q, r):
    return (g, 1 - c, q, r)


def core():
    return lax.rem(lax.axis_index("view"), 2)


def half():
    return lax.rem(lax.axis_index("tile"), 2)


def split(x):
    high = x.astype(BF16)
    return high, (x - high.astype(F32)).astype(BF16)


def dot(a, b):
    return jnp.dot(a, b, preferred_element_type=F32)


def iota(shape, dim):
    return lax.broadcasted_iota(jnp.int32, shape, dim)


def group_row(half, group, cells_y):
    return group * GROUP + half * (cells_y - GROUP - 2 * group * GROUP)


def global_row(half, local, cells_y):
    group = local // GROUP
    return group_row(half, group, cells_y) + (local - group * GROUP)


def wide_local(place, own, wide):
    group = (place - own) // GROUP
    return own + (wide - own) - GROUP - group * GROUP + (place - own - group * GROUP)


def wide_group(group, own_groups, groups):
    return group if group < own_groups else own_groups + groups - 1 - group


def pad_to(value, unit):
    return -(-value // unit) * unit


def call(kernel, out_shape, in_specs, name, scratch=(), hbm=()):
    if hbm:
        out_shape = tuple(pltpu.HBM(o.shape, o.dtype) if index in hbm else o for index, o in enumerate(out_shape))
    return pl.pallas_call(
        kernel,
        out_shape=out_shape,
        in_specs=in_specs,
        out_specs=(VMEM,) * len(out_shape) if isinstance(out_shape, tuple) else VMEM,
        scratch_shapes=list(scratch),
        compiler_params=PARAMS,
        name=name,
    )


class Tables(typing.NamedTuple):
    whole: tuple
    inner: tuple
    edge: tuple
    z: tuple
    x: tuple


def place(row, count, width, turned, spacing):
    source, target = iota((row.shape[1], width), 0), iota((row.shape[1], width), 1)
    index = count - 1 - source if turned else source
    ones = (target == spacing * index) & (source < count)
    return jnp.dot(row, ones.astype(F32), precision=lax.Precision.HIGHEST, preferred_element_type=F32)


def tables_kernel(mine_ref, other_ref, *refs, blocks, sizes, cells_y, taps):
    y_refs, (zhi_ref, zlo_ref, xhi_ref, xlo_ref) = refs[:-4], refs[-4:]
    taps_x, taps_y, taps_z = taps
    straight = core() == half()
    mine, other = mine_ref[...], other_ref[...]
    both = (jnp.where(straight, mine, other), jnp.where(straight, other, mine))
    radius, radius_x, radius_z = taps_y // 2, taps_x // 2, taps_z // 2
    side = half()
    own, wide = sizes
    for out_ref, adjoint, first_row, first_col, width in zip(y_refs, *zip(*blocks)):
        _, rows, lanes = out_ref.shape
        row = global_row(side, first_row + iota((rows, lanes), 0), cells_y)
        lane = iota((rows, lanes), 1)
        place_of = lane + first_col
        turned = place_of if adjoint else jnp.where(place_of < own, place_of, wide_local(place_of, own, wide))
        col = global_row(side, turned, cells_y)
        delta = (row - col if adjoint else col - row) + radius
        delta = jnp.where(lane < width, delta, -1)
        for order in range(2):
            band = jnp.zeros((rows, lanes), F32)
            values = both[order][:, 128:256]
            for a in range(taps_y):
                band = jnp.where(delta == a, jnp.broadcast_to(values[:, a:a + 1], (rows, lanes)), band)
            high, low = split(band)
            high, low = high.astype(F32), low.astype(F32)
            out_ref[order] = (high + pltpu.roll(high, width, 1) + pltpu.roll(low, 2 * width, 1)).astype(BF16)

    lanes = zhi_ref.shape[2]
    near_z = jnp.abs(iota((lanes, lanes), 1) - iota((lanes, lanes), 0)) <= radius_z
    for index in range(4):
        base = place(both[index % 2][:, 256:384], taps_z, lanes, index < 2, 1)
        base = pltpu.roll(base, lanes - radius_z, 1)
        band = pltpu.roll(jnp.broadcast_to(base, (lanes, lanes)), 0, 1, stride=1, stride_axis=0)
        zhi_ref[index], zlo_ref[index] = split(jnp.where(near_z, band, jnp.zeros_like(band)))

    rows = xhi_ref.shape[1] // 2
    lanes = max(512, 1 << (xhi_ref.shape[2] - 1).bit_length())
    for index in range(4):
        base = place(both[index % 2][:, :128], taps_x, lanes, index >= 2, 8)
        base = jnp.broadcast_to(base, (rows, lanes))
        band = pltpu.roll(base, 0, 1, stride=1, stride_axis=0)
        lane = iota((rows, lanes), 1)
        edge = 8 * radius_x
        far = pad_to(rows + edge, 128)
        next_near = pltpu.roll(band, lanes - edge, 1)
        next_far = pltpu.roll(band, far - rows - edge, 1)
        near_part = jnp.where((lane < rows) | (core() == 0), next_near, pltpu.roll(band, rows, 1))
        far_part = jnp.where(core() == 0, pltpu.roll(band, far, 1), next_far)
        zero = jnp.zeros_like(band)
        band = jnp.where(
            lane < rows + edge, near_part, jnp.where((lane >= far) & (lane < far + edge), far_part, zero)
        )[:, :xhi_ref.shape[2]]
        block = (index // 2, slice(index % 2 * rows, index % 2 * rows + rows))
        xhi_ref[block], xlo_ref[block] = split(band)


def make_tables(mine, other, taps, planes, cells_y, cells_z, sizes):
    own, near, wide = sizes
    inner, beyond = 2 * own - wide, near - own
    radius = taps[0] // 2
    depth = pad_to(8 * (planes + radius), 128) + pad_to(8 * radius, 128)
    blocks = [
        (False, near, 0, 0, wide), (True, own, 0, 0, near),
        (False, inner + beyond, 0, 0, own), (True, inner, 0, 0, inner + beyond),
        (False, near - inner - beyond, inner + beyond, inner, wide - inner),
        (True, own - inner, inner, inner - beyond, near - inner + beyond),
    ]
    kernel = functools.partial(
        tables_kernel, blocks=[block[:1] + block[2:] for block in blocks], sizes=(own, wide), cells_y=cells_y, taps=taps
    )
    shape = jax.ShapeDtypeStruct
    out_shape = tuple(shape((2, block[1], pad_to(3 * block[4], 128)), BF16) for block in blocks) + (
        shape((4, cells_z, cells_z), BF16),
        shape((4, cells_z, cells_z), BF16),
        shape((2, 2 * 8 * planes, depth), BF16),
        shape((2, 2 * 8 * planes, depth), BF16),
    )
    tables = call(kernel, out_shape, [VMEM, VMEM], "band_matrices")(mine, other)
    whole, inner_rows, edge_rows = tables[0:2], tables[2:4], tables[4:6]
    return Tables(whole, inner_rows, edge_rows, tables[6:8], tables[8:10])


def window_kernel(estimate_ref, own_ref, other_ref):
    cells_y = estimate_ref.shape[1]
    groups = own_ref.shape[1] // GROUP
    for side, out_ref in ((half(), own_ref), (1 - half(), other_ref)):
        for group in range(groups):
            local = wide_group(group, cells_y // 2 // GROUP, groups)
            start = pl.multiple_of(group_row(side, local, cells_y), GROUP)
            out_ref[:, group * GROUP:(group + 1) * GROUP, :] = estimate_ref[:, pl.ds(start, GROUP), :]


def make_windows(estimate, wide):
    planes, _, cells_z = estimate.shape
    shape = jax.ShapeDtypeStruct((planes, wide, cells_z), F32)
    return call(window_kernel, (shape, shape), [VMEM], "estimate_windows")(estimate)


def put_edges(out_ref, edge_refs):
    end = out_ref.shape[1]
    for far_ref, near_ref in zip(edge_refs[::2], edge_refs[1::2]):
        radius, rows = far_ref.shape[0], slice(end - far_ref.shape[1], end)
        beyond = out_ref.shape[0] - radius
        for p in range(radius):
            far_ref[p] = out_ref[p + core() * beyond, rows]
            near_ref[p] = out_ref[p + (1 - core()) * beyond, rows]
        end -= far_ref.shape[1]


def choose_kernel(window_ref, crossed_ref, out_ref, far_ref):
    straight = core() == half()
    for p in range(out_ref.shape[0]):
        out_ref[p] = jnp.where(straight, window_ref[p], crossed_ref[p])
    beyond = core() * (out_ref.shape[0] - far_ref.shape[0])
    for p in range(far_ref.shape[0]):
        far_ref[p] = out_ref[p + beyond]


def edge_shapes(shape, radius, chunks):
    planes, _, lanes = shape
    edges = [jax.ShapeDtypeStruct((radius, rows, lanes), F32) for rows in chunks for _ in range(2)]
    return (jax.ShapeDtypeStruct(shape, F32), *edges)


def choose(window, crossed, radius):
    out_shape = edge_shapes(window.shape, radius, window.shape[1:2])[:2]
    return call(choose_kernel, out_shape, [VMEM] * 2, "estimate")(window, crossed)


def shift_kernel(offsets_ref, acq_ref, first_ref, second_ref, turned_ref):
    planes, cells_y, cells_z = acq_ref.shape
    near = first_ref.shape[1]
    shift_y, shift_z = offsets_ref[0, 1], offsets_ref[0, 2]
    row = iota((cells_y, cells_z), 0) + shift_y
    col = iota((cells_y, cells_z), 1) + shift_z
    inside = (row >= 0) & (row < cells_y) & (col >= 0) & (col < cells_z)
    turn_y = lax.rem(cells_y - shift_y, cells_y)
    turn_z = lax.rem(cells_z - shift_z, cells_z)

    def body(p, carry):
        x = pltpu.roll(pltpu.roll(acq_ref[p], turn_z, 1), turn_y, 0)
        turned_ref[...] = jnp.where(inside, x, jnp.zeros_like(x))
        for side, out_ref in ((core(), first_ref), (1 - core(), second_ref)):
            for group in range(near // GROUP):
                start = pl.multiple_of(group_row(side, group, cells_y), GROUP)
                out_ref[p, group * GROUP:(group + 1) * GROUP, :] = turned_ref[pl.ds(start, GROUP), :]
        return carry

    lax.fori_loop(0, planes, body, 0)


def shift_and_cut(offsets, acquired, near):
    planes, cells_y, cells_z = acquired.shape
    shape = jax.ShapeDtypeStruct((planes, near, cells_z), F32)
    scratch = [pltpu.VMEM((cells_y, cells_z), F32)]
    return call(shift_kernel, (shape, shape), [SMEM, VMEM], "shift_recorded", scratch)(offsets, acquired)


def gather(ref, row):
    return ref[:, pl.ds(pl.multiple_of(row, 8), 8), :]


def spread_x(hi_ref, lo_ref, index, band_rows, band_lanes, blocks):
    lanes = blocks[0][0].shape[2]
    filled = []
    for parts in blocks:
        count = 8 * sum(part.shape[0] for part in parts)
        missing = (pad_to(count, 128) - count) // 8
        filled += list(parts) + ([jnp.zeros((missing, 8, lanes), F32)] if missing else [])
    high, low = split(jnp.concatenate(filled, axis=0).reshape(-1, lanes))
    band = hi_ref[index, band_rows, band_lanes]
    out = dot(band, high) + (dot(band, low) + dot(lo_ref[index, band_rows, band_lanes], high))
    return out.reshape(-1, 8, lanes)


def near_lanes(planes, radius):
    return pad_to(8 * (planes + radius), 128)


def blur_x_kernel(hi_ref, lo_ref, *refs, far, radius):
    planes_of, before, (first_ref, second_ref) = refs[:2 - far], refs[2 - far:-2], refs[-2:]
    planes, rows, _ = first_ref.shape
    split_at = near_lanes(planes, radius)
    lanes = slice(split_at, None) if far else slice(0, split_at)

    def body(step, carry):
        row = pl.multiple_of(step * 8, 8)
        place = (slice(None), pl.ds(row, 8), slice(None))
        out = spread_x(hi_ref, lo_ref, 0, slice(None), lanes, [[gather(ref, row) for ref in planes_of]])
        out = [out[:planes], out[planes:]]
        if before:
            out = [ref[place] + part for ref, part in zip(before, out)]
        first_ref[place], second_ref[place] = out
        return carry

    lax.fori_loop(0, rows // 8, body, 0)


def blur_x(tables, planes_of, before, planes):
    far, (radius, rows, lanes) = len(planes_of) == 1, planes_of[-1].shape
    shape = jax.ShapeDtypeStruct((planes, rows, lanes), F32)
    kernel = functools.partial(blur_x_kernel, far=far, radius=radius)
    operands = [*tables.x, *planes_of, *before]
    return call(kernel, (shape, shape), [VMEM] * len(operands), "blur_x_far" if far else "blur_x_near")(*operands)


def blur_near(tables, own, near):
    return blur_x(tables, (own, near), (), own.shape[0])


def blur_far(tables, far, parts):
    return blur_x(tables, (far,), parts, parts[0].shape[0])


def spread_y(band, x):
    high, low = split(x)
    return dot(band[:, :3 * x.shape[0]], jnp.concatenate([high, low, high], axis=0))


def spread_z(x, hi_ref, lo_ref, index):
    high, low = split(x)
    return dot(high, hi_ref[index]) + (dot(low, hi_ref[index]) + dot(high, lo_ref[index]))


def blurred_planes(wide_refs, yf_ref, zhi_ref, zlo_ref, order, block):
    wide = [jnp.concatenate([ref[p] for ref in wide_refs], axis=0) for p in block]
    spread = jnp.concatenate([spread_y(yf_ref[order], rows) for rows in wide], axis=0)
    return spread_z(spread, zhi_ref, zlo_ref, order)


def plane_blocks(planes, step=4):
    return [range(start, min(start + step, planes)) for start in range(0, planes, step)]


def blur_yz_kernel(*refs, order):
    wide_refs, (yf_ref, zhi_ref, zlo_ref, out_ref) = refs[:-4], refs[-4:]
    near = yf_ref.shape[1]
    for block in plane_blocks(out_ref.shape[0]):
        blurred = blurred_planes(wide_refs, yf_ref, zhi_ref, zlo_ref, order, block)
        for k, p in enumerate(block):
            out_ref[p] = blurred[k * near:(k + 1) * near]


def blur_yz(wides, tables, order):
    planes, _, lanes = wides[0].shape
    shape = jax.ShapeDtypeStruct((planes, tables.whole[0].shape[1], lanes), F32)
    kernel = functools.partial(blur_yz_kernel, order=order)
    return call(kernel, shape, [VMEM] * (3 + len(wides)), "blur_yz")(*wides, tables.whole[0], *tables.z)


def adjoint_planes(blurred_of, image_of, ya_ref, zhi_ref, zlo_ref, order, out_ref, edge_refs, complete=None):
    planes, rows, _ = out_ref.shape
    for block in plane_blocks(planes):
        blurred = blurred_of(block)
        image = jnp.concatenate([image_of(p) for p in block], axis=0)
        ratio = jnp.where(image >= 0, image / blurred, jnp.ones_like(image))
        near = ratio.shape[0] // len(block)
        ratios = [ratio[k * near:(k + 1) * near] for k in range(len(block))]
        if complete:
            ratios = [complete(p, rows_of) for p, rows_of in zip(block, ratios)]
        spread = jnp.concatenate([spread_y(ya_ref[order], rows_of) for rows_of in ratios], axis=0)
        spread = spread_z(spread, zhi_ref, zlo_ref, 2 + order)
        for k, p in enumerate(block):
            out_ref[p] = spread[k * rows:(k + 1) * rows]
    put_edges(out_ref, edge_refs)


def first_ratio_kernel(
    shift_ref, far_ref, near_ref, own_ref, masks_ref, blurred_ref, ya_ref, zhi_ref, zlo_ref, out_ref, *refs, order, extent_x, cells_y
):
    edge_refs, image_ref, (mine_ref, beyond_ref, semaphores) = refs[:-4], refs[-4], refs[-3:]
    planes, near, cells_z = image_ref.shape
    side = half()
    slab = lax.axis_index("tile") - side + core()
    shift_x, shift_y, shift_z = (shift_ref[order, i] for i in range(3))
    lanes = masks_ref.shape[2]
    pick = iota((near, lanes), 1) == global_row(side, iota((near, lanes), 0), cells_y)
    is_far = (shift_x > 0) == (core() == 1)
    copy = pltpu.make_async_copy(own_ref, mine_ref, semaphores.at[0])
    far_copy = pltpu.make_async_copy(far_ref, beyond_ref, semaphores.at[1])
    near_copy = pltpu.make_async_copy(near_ref, beyond_ref, semaphores.at[1])
    copy.start()
    pl.when(is_far)(far_copy.start)
    pl.when(jnp.logical_not(is_far))(near_copy.start)
    copy.wait()
    far_copy.wait()
    mask = masks_ref[half() if order == 0 else 1 - half()].astype(BF16)
    columns = lax.dot_general(
        pick.astype(F32).astype(BF16), mask, (((1,), (1,)), ((), ())), preferred_element_type=F32
    )
    row = global_row(side, iota((near, cells_z), 0), cells_y) + shift_y
    col = iota((near, cells_z), 1) + shift_z
    inside = (row >= 0) & (row < cells_y) & (col >= 0) & (col < cells_z)

    def fetch(p):
        source = p + shift_x
        x = slab * planes + source
        is_own = (source >= 0) & (source < planes)
        beyond = jnp.clip(jnp.where(source < 0, source + planes, source - planes), 0, planes - 1)
        value = jnp.where(is_own, mine_ref[jnp.clip(source, 0, planes - 1)], beyond_ref[beyond])
        weight = jnp.broadcast_to(columns[:, p:p + 1], (near, cells_z))
        covered = inside & (weight > 0.5) & (x >= 0) & (x < extent_x)
        value = jnp.where(covered, value, jnp.full_like(value, -1.0))
        image_ref[p] = value
        return value

    def blurred_of(block):
        return jnp.concatenate([blurred_ref[p] for p in block], axis=0)

    adjoint_planes(blurred_of, fetch, ya_ref, zhi_ref, zlo_ref, order, out_ref, edge_refs)


def next_ratio_kernel(*refs, inner, count, first_row):
    image_refs, wide_refs, refs = refs[:2], (refs[2:4], refs[4:6]), refs[6:]
    passed_ref, refs = (None, refs) if inner else (refs[0], refs[1:])
    (yf_ref, ya_ref, zhi_ref, zlo_ref), out_refs, (far_ref, near_ref), refs = refs[:4], refs[4:6], refs[6:8], refs[8:]
    planes = out_refs[0].shape[0]
    rows = yf_ref.shape[1]
    for order in range(2):

        def blurred_of(block):
            return blurred_planes(wide_refs[order], yf_ref, zhi_ref, zlo_ref, order, block)

        def image_of(p):
            return image_refs[order][p, first_row:first_row + rows]

        def complete(p, ratio):
            if inner:
                refs[0][order, p] = ratio[rows - count:]
                return ratio
            return jnp.concatenate([passed_ref[order, p], ratio], axis=0)

        edges = (far_ref.at[order], near_ref.at[order])
        adjoint_planes(blurred_of, image_of, ya_ref, zhi_ref, zlo_ref, order, out_refs[order], edges, complete)


def next_ratio(images, wides, passed, y_tables, z_tables, radius, count, first_row):
    planes, _, lanes = images[0].shape
    rows = y_tables[1].shape[1]
    kernel = functools.partial(next_ratio_kernel, inner=passed is None, count=count, first_row=first_row)
    shape = jax.ShapeDtypeStruct
    whole, edge = shape((planes, rows, lanes), F32), shape((2, radius, rows, lanes), F32)
    out_shape = (whole, whole, edge, edge)
    if passed is None:
        out_shape += (shape((2, planes, count, lanes), F32),)
    operands = [*images, *wides[0], *wides[1]] + ([] if passed is None else [passed]) + [*y_tables, *z_tables]
    return call(kernel, out_shape, [VMEM] * len(operands), "ratio")(*operands)


def first_ratio(shifts, blocks, masks, blurred, tables, order, radius, chunks, extent_x, cells_y):
    planes, near, lanes = blurred.shape
    kernel = functools.partial(first_ratio_kernel, order=order, extent_x=extent_x, cells_y=cells_y)
    rows = tables.whole[1].shape[1]
    out_shape = edge_shapes((planes, rows, lanes), radius, chunks) + (jax.ShapeDtypeStruct(blurred.shape, F32),)
    scratch = [
        pltpu.VMEM(blurred.shape, F32), pltpu.VMEM(blurred.shape, F32), pltpu.SemaphoreType.DMA((2,))
    ]
    in_specs = [SMEM] + [pl.BlockSpec(memory_space=pl.ANY)] * 3 + [VMEM] * 5
    return call(kernel, out_shape, in_specs, "image_and_ratio", scratch, hbm=(len(out_shape) - 1,))(
        shifts, *blocks, masks, blurred, tables.whole[1], *tables.z
    )


def factor_kernel(hi_ref, lo_ref, before_ref, *refs, orders, starts, share):
    out_ref = refs[-1]
    planes, rows, _ = out_ref.shape

    def body(step, carry):
        row = pl.multiple_of(step * 8, 8)
        total = gather(before_ref, starts[0] + row)
        if share:
            total = share * jnp.log(total)
        for index, order in enumerate(orders):
            far_ref, near_ref, own_ref = refs[3 * index:3 * index + 3]
            if len(far_ref.shape) == 4:
                far_ref, near_ref = far_ref.at[order], near_ref.at[order]
            own = gather(own_ref, starts[1] + row)
            blocks = [[own, gather(near_ref, row)], [gather(far_ref, row)]]
            band_rows = slice(order * 8 * planes, (order + 1) * 8 * planes)
            total = total + jnp.log(spread_x(hi_ref, lo_ref, 1, band_rows, slice(None), blocks))
        out_ref[:, pl.ds(row, 8), :] = total
        return carry

    lax.fori_loop(0, rows // 8, body, 0)


def log_factor(tables, before, sides, orders, rows, starts, share):
    kernel = functools.partial(factor_kernel, orders=orders, starts=starts, share=share)
    planes, _, lanes = sides[0][2].shape
    shape = jax.ShapeDtypeStruct((planes, rows, lanes), F32)
    parts = [part for side in sides for part in side]
    return call(kernel, shape, [VMEM] * (3 + len(parts)), "log_factor")(*tables.x, before, *parts)


def update_kernel(*refs, count):
    parts, out_ref, edge_refs = refs[:count], refs[count], refs[count + 1:]
    for p in range(out_ref.shape[0]):
        total = parts[0][p]
        for part in parts[1:]:
            total = total + part[p]
        out_ref[p] = jnp.exp(total)
    put_edges(out_ref, edge_refs)


def update(parts, radius, hbm):
    kernel = functools.partial(update_kernel, count=len(parts))
    out_shape = edge_shapes(parts[0].shape, radius, parts[0].shape[1:2])
    return call(kernel, out_shape, [VMEM] * len(parts), "update", hbm=hbm)(*parts)


def finish_kernel(*refs):
    own, other, out_ref = refs[:(len(refs) - 1) // 2], refs[(len(refs) - 1) // 2:-1], refs[-1]
    straight = core() == half()
    groups = out_ref.shape[1] // GROUP
    for group in range(groups):
        rows = slice(group * GROUP, (group + 1) * GROUP)
        own_total, other_total = own[0][:, rows, :], other[0][:, rows, :]
        for part in own[1:]:
            own_total = own_total + part[:, rows, :]
        for part in other[1:]:
            other_total = other_total + part[:, rows, :]
        start = jnp.where(core() == 0, group, groups - 1 - group) * GROUP
        out_ref[:, pl.ds(pl.multiple_of(start, GROUP), GROUP), :] = jnp.exp(jnp.where(straight, own_total, other_total))


def finish(own_parts, other_parts):
    shape = jax.ShapeDtypeStruct(own_parts[0].shape, F32)
    return call(finish_kernel, shape, [VMEM] * (2 * len(own_parts)), "last_update")(*own_parts, *other_parts)


def join_kernel(*refs, starts):
    sources, out_ref, semaphores = refs[:-2], refs[-2], refs[-1]
    cells_y = out_ref.shape[1]
    copies = []
    for index, source_ref in enumerate(sources):
        rows, start = source_ref.shape[1], starts[index // 2]
        side = core() if index % 2 == 0 else 1 - core()
        place = pl.multiple_of(jnp.where(side == 0, start, cells_y - start - rows), GROUP)
        target = out_ref.at[:, pl.ds(place, rows), :]
        copies.append(pltpu.make_async_copy(source_ref, target, semaphores.at[index]))
    for copy in copies:
        copy.start()
    for copy in copies:
        copy.wait()


def join(pieces, starts, shape):
    anywhere = pl.BlockSpec(memory_space=pl.ANY)
    return pl.pallas_call(
        functools.partial(join_kernel, starts=starts),
        out_shape=jax.ShapeDtypeStruct(shape, F32),
        in_specs=[anywhere] * len(pieces),
        out_specs=anywhere,
        scratch_shapes=[pltpu.SemaphoreType.DMA((len(pieces),))],
        compiler_params=PARAMS,
        name="join_halves",
    )(*pieces)


def shards(acquired, estimate, offsets, view_mask, kern_x, kern_y, kern_z):
    planes, cells_y, cells_z = estimate.shape
    views, slabs = lax.axis_size("view"), lax.axis_size("tile")
    groups = views // 2
    taps_y = kern_y.shape[1]
    radius = kern_x.shape[1] // 2
    own_rows = cells_y // 2
    near = own_rows + pad_to(taps_y // 2, GROUP)
    wide = own_rows + pad_to(2 * (taps_y // 2), GROUP)
    edge_rows = wide - own_rows
    inner_rows = own_rows - edge_rows
    group = lax.axis_index("view") // 2
    straight = core() == half()

    def across(turn, half_of=lambda r: r, core_of=lambda c: c, when=lambda c, r: True):
        return lambda g, c, q, r: ((g + turn) % groups, core_of(c), q, half_of(r)) if when(c, r) else None

    def neighbours(far, near):
        return send(far, to_far), send(near, to_core_partner)

    window, crossed = make_windows(estimate, wide)
    crossed = send(crossed, across(0, lambda r: 1 - r, when=lambda c, r: c == r))

    mine = [jnp.pad(row, ((0, 0), (0, 128 - row.shape[1]))) for row in (kern_x, kern_y, kern_z)]
    mine = after(jnp.concatenate(mine, axis=1), window)
    other = send(mine, to_core_partner)
    taps = kern_x.shape[1], taps_y, kern_z.shape[1]
    tables = make_tables(mine, other, taps, planes, cells_y, cells_z, (own_rows, near, wide))
    offset = after(offsets.astype(F32), tables.whole[0])
    other = send(offset, to_core_partner)
    shifts = jnp.where(straight, jnp.concatenate([offset, other]), jnp.concatenate([other, offset])).astype(jnp.int32)

    mask = view_mask.astype(F32)
    other = send(mask, to_core_partner)
    masks = jnp.where(core() == 0, jnp.concatenate([mask, other]), jnp.concatenate([other, mask]))

    acquired = after(after(acquired, tables.whole[0]), masks)
    first, second = shift_and_cut(offsets, acquired[0], near)

    arrived = send(after(first, tables.whole[0]), lambda g, c, q, r: (g, r, q, c) if c != r else None)
    current, distant = choose(after(window, first), crossed, radius)
    second = send(after(second, current), lambda g, c, q, r: (g, r, q, 1 - c))
    close = lax.dynamic_slice_in_dim(current, (1 - core()) * (planes - radius), radius, 0)
    distant, close = neighbours(distant, close)
    first = jnp.where(straight, first, arrived)

    masks = jnp.where(straight, masks, send(after(masks, current), to_row_partner))

    blocks = [(*neighbours(block, block), block) for block in (first, second)]
    wide_parts = blur_x(tables, (current, close), blur_x(tables, (distant,), (), planes), planes)
    blurred = [blur_yz([part], tables, order) for order, part in enumerate(wide_parts)]

    row_chunks = [(inner_rows, edge_rows), (0, inner_rows)]
    share = 1.0 / groups
    images, sides = [], []
    for order, chunk_sizes in enumerate(([own_rows], [edge_rows, inner_rows])):
        spread, *edges, image = first_ratio(
            shifts, blocks[order], masks, blurred[order], tables, order, radius, chunk_sizes, planes * slabs, cells_y
        )
        images.append(image)
        sides.append([(*neighbours(*edges[k:k + 2]), spread) for k in range(0, len(edges), 2)])
    total = log_factor(tables, current, sides[0], [0], own_rows, (0, 0), share)
    totals = [
        log_factor(tables, total, [side], [1], rows, (start, start), 0)
        for (start, rows), side in zip(row_chunks, sides[1])
    ]

    for step in range(1, ITERS):
        chunks, before = [], []
        for total in totals:
            parts = [total] + [send(total, across(turn)) for turn in range(1, groups)]
            rows, distant, close = update(parts, radius, () if chunks else (2,))
            if total is totals[0]:
                beyond = send(rows, to_row_partner)
            distant = after(distant, chunks[0][0]) if chunks else distant
            distant, close = neighbours(distant, close)
            chunks.append((distant, blur_near(tables, rows, close)))
            before.append(rows)
        rest = planes - radius
        distant, close = neighbours(
            lax.dynamic_slice_in_dim(beyond, core() * rest, radius, 0),
            lax.dynamic_slice_in_dim(beyond, (1 - core()) * rest, radius, 0),
        )
        edge_parts, inner_parts = [blur_far(tables, *chunk) for chunk in chunks]
        halo_parts = blur_near(tables, beyond, close)
        *inner_spreads, distant_inner, close_inner, passed = next_ratio(
            images, list(zip([after(after(part, distant), halo_parts[0]) for part in inner_parts], edge_parts)), None, tables.inner, tables.z, radius, 2 * (near - own_rows), 0
        )
        halo_parts = blur_far(tables, distant, halo_parts)
        inner_side = neighbours(distant_inner, close_inner)
        *edge_spreads, distant, close = next_ratio(
            images, list(zip(edge_parts, halo_parts)), passed, tables.edge, tables.z, radius, 0,
            inner_rows + near - own_rows,
        )
        edge_side = neighbours(distant, close)
        totals = [
            log_factor(tables, rows_of, [(*side, spread) for spread in spreads], [0, 1], rows, (0, 0), share)
            for rows_of, side, spreads, rows in (
                (before[0], edge_side, edge_spreads, edge_rows), (before[1], inner_side, inner_spreads, inner_rows)
            )
        ]

    pieces = []
    for own in totals[::-1]:
        other_parts = [
            send(own, across(turn, lambda r: 1 - r, lambda c: 1 - c, lambda c, r: c != r))
            for turn in reversed(range(groups))
        ]
        own_parts = [own] + [send(own, across(turn, when=lambda c, r: c == r)) for turn in range(1, groups)]
        mine = finish(own_parts, other_parts)
        pieces += [mine, send(mine, to_core_partner)]
    return join(pieces, [start for start, _ in row_chunks[::-1]], estimate.shape)


def solution(mesh):
    in_specs = (
        P("view", "tile", None, None),
        P("tile", None, None),
        P("view", None),
        P("view", "tile", None),
        P("view", None),
        P("view", None),
        P("view", None),
    )
    out_specs = P("tile", None, None)
    return jax.shard_map(shards, mesh=mesh, in_specs=in_specs, out_specs=out_specs, check_vma=False)
```

```python
import functools
import typing

import jax
import jax.numpy as jnp
from jax import lax
from jax.experimental import pallas as pl
from jax.experimental.pallas import tpu as pltpu
from jax.sharding import PartitionSpec as P

ITERS = 2
AXES = ("view", "tile")
F32 = jnp.float32
BF16 = jnp.bfloat16
VMEM = pl.BlockSpec(memory_space=pltpu.VMEM)
SMEM = pl.BlockSpec(memory_space=pltpu.SMEM)
PARAMS = pltpu.CompilerParams(vmem_limit_bytes=12 * 1024 * 1024)
GROUP = 16


def moves(move):
    views, tiles = lax.axis_size("view"), lax.axis_size("tile")
    pairs = []
    for view in range(views):
        for tile in range(tiles):
            target = move(view // 2, view % 2, tile // 2, tile % 2)
            if target is not None:
                g, c, q, r = target
                pairs.append((view * tiles + tile, (2 * g + c) * tiles + 2 * q + r))
    return pairs


def send(array, move):
    return lax.ppermute(array, AXES, moves(move))


def after(array, other):
    return lax.optimization_barrier((array, other))[0]


def to_far(g, c, q, r):
    s = 2 * q + c + (1 if c else -1)
    return (g, s % 2, s // 2, r) if 0 <= s < lax.axis_size("tile") else None


def to_row_partner(g, c, q, r):
    return (g, c, q, 1 - r)


def to_core_partner(g, c, q, r):
    return (g, 1 - c, q, r)


def core():
    return lax.rem(lax.axis_index("view"), 2)


def half():
    return lax.rem(lax.axis_index("tile"), 2)


def split(x):
    high = x.astype(BF16)
    return high, (x - high.astype(F32)).astype(BF16)


def dot(a, b):
    return jnp.dot(a, b, preferred_element_type=F32)


def iota(shape, dim):
    return lax.broadcasted_iota(jnp.int32, shape, dim)


def group_row(half, group, cells_y):
    return group * GROUP + half * (cells_y - GROUP - 2 * group * GROUP)


def global_row(half, local, cells_y):
    group = local // GROUP
    return group_row(half, group, cells_y) + (local - group * GROUP)


def wide_local(place, own, wide):
    group = (place - own) // GROUP
    return own + (wide - own) - GROUP - group * GROUP + (place - own - group * GROUP)


def wide_group(group, own_groups, groups):
    return group if group < own_groups else own_groups + groups - 1 - group


def pad_to(value, unit):
    return -(-value // unit) * unit


def call(kernel, out_shape, in_specs, name, scratch=(), hbm=()):
    if hbm:
        out_shape = tuple(pltpu.HBM(o.shape, o.dtype) if index in hbm else o for index, o in enumerate(out_shape))
    return pl.pallas_call(
        kernel,
        out_shape=out_shape,
        in_specs=in_specs,
        out_specs=(VMEM,) * len(out_shape) if isinstance(out_shape, tuple) else VMEM,
        scratch_shapes=list(scratch),
        compiler_params=PARAMS,
        name=name,
    )


class Tables(typing.NamedTuple):
    whole: tuple
    inner: tuple
    edge: tuple
    z: tuple
    x: tuple


def place(row, count, width, turned, spacing):
    source, target = iota((row.shape[1], width), 0), iota((row.shape[1], width), 1)
    index = count - 1 - source if turned else source
    ones = (target == spacing * index) & (source < count)
    return jnp.dot(row, ones.astype(F32), precision=lax.Precision.HIGHEST, preferred_element_type=F32)


def tables_kernel(mine_ref, other_ref, *refs, blocks, sizes, cells_y, taps):
    y_refs, (zhi_ref, zlo_ref, xhi_ref, xlo_ref) = refs[:-4], refs[-4:]
    taps_x, taps_y, taps_z = taps
    straight = core() == half()
    mine, other = mine_ref[...], other_ref[...]
    both = (jnp.where(straight, mine, other), jnp.where(straight, other, mine))
    radius, radius_x, radius_z = taps_y // 2, taps_x // 2, taps_z // 2
    side = half()
    own, wide = sizes
    for out_ref, adjoint, first_row, first_col, width in zip(y_refs, *zip(*blocks)):
        _, rows, lanes = out_ref.shape
        row = global_row(side, first_row + iota((rows, lanes), 0), cells_y)
        lane = iota((rows, lanes), 1)
        place_of = lane + first_col
        turned = place_of if adjoint else jnp.where(place_of < own, place_of, wide_local(place_of, own, wide))
        col = global_row(side, turned, cells_y)
        delta = (row - col if adjoint else col - row) + radius
        delta = jnp.where(lane < width, delta, -1)
        for order in range(2):
            band = jnp.zeros((rows, lanes), F32)
            values = both[order][:, 128:256]
            for a in range(taps_y):
                band = jnp.where(delta == a, jnp.broadcast_to(values[:, a:a + 1], (rows, lanes)), band)
            high, low = split(band)
            high, low = high.astype(F32), low.astype(F32)
            out_ref[order] = (high + pltpu.roll(high, width, 1) + pltpu.roll(low, 2 * width, 1)).astype(BF16)

    lanes = zhi_ref.shape[2]
    near_z = jnp.abs(iota((lanes, lanes), 1) - iota((lanes, lanes), 0)) <= radius_z
    for index in range(4):
        base = place(both[index % 2][:, 256:384], taps_z, lanes, index < 2, 1)
        base = pltpu.roll(base, lanes - radius_z, 1)
        band = pltpu.roll(jnp.broadcast_to(base, (lanes, lanes)), 0, 1, stride=1, stride_axis=0)
        zhi_ref[index], zlo_ref[index] = split(jnp.where(near_z, band, jnp.zeros_like(band)))

    rows = xhi_ref.shape[1] // 2
    lanes = max(512, 1 << (xhi_ref.shape[2] - 1).bit_length())
    for index in range(4):
        base = place(both[index % 2][:, :128], taps_x, lanes, index >= 2, 8)
        base = jnp.broadcast_to(base, (rows, lanes))
        band = pltpu.roll(base, 0, 1, stride=1, stride_axis=0)
        lane = iota((rows, lanes), 1)
        edge = 8 * radius_x
        far = pad_to(rows + edge, 128)
        next_near = pltpu.roll(band, lanes - edge, 1)
        next_far = pltpu.roll(band, far - rows - edge, 1)
        near_part = jnp.where((lane < rows) | (core() == 0), next_near, pltpu.roll(band, rows, 1))
        far_part = jnp.where(core() == 0, pltpu.roll(band, far, 1), next_far)
        zero = jnp.zeros_like(band)
        band = jnp.where(
            lane < rows + edge, near_part, jnp.where((lane >= far) & (lane < far + edge), far_part, zero)
        )[:, :xhi_ref.shape[2]]
        block = (index // 2, slice(index % 2 * rows, index % 2 * rows + rows))
        xhi_ref[block], xlo_ref[block] = split(band)


def make_tables(mine, other, taps, planes, cells_y, cells_z, sizes):
    own, near, wide = sizes
    inner, beyond = 2 * own - wide, near - own
    radius = taps[0] // 2
    depth = pad_to(8 * (planes + radius), 128) + pad_to(8 * radius, 128)
    blocks = [
        (False, near, 0, 0, wide), (True, own, 0, 0, near),
        (False, inner + beyond, 0, 0, own), (True, inner, 0, 0, inner + beyond),
        (False, near - inner - beyond, inner + beyond, inner, wide - inner),
        (True, own - inner, inner, inner - beyond, near - inner + beyond),
    ]
    kernel = functools.partial(
        tables_kernel, blocks=[block[:1] + block[2:] for block in blocks], sizes=(own, wide), cells_y=cells_y, taps=taps
    )
    shape = jax.ShapeDtypeStruct
    out_shape = tuple(shape((2, block[1], pad_to(3 * block[4], 128)), BF16) for block in blocks) + (
        shape((4, cells_z, cells_z), BF16),
        shape((4, cells_z, cells_z), BF16),
        shape((2, 2 * 8 * planes, depth), BF16),
        shape((2, 2 * 8 * planes, depth), BF16),
    )
    tables = call(kernel, out_shape, [VMEM, VMEM], "band_matrices")(mine, other)
    whole, inner_rows, edge_rows = tables[0:2], tables[2:4], tables[4:6]
    return Tables(whole, inner_rows, edge_rows, tables[6:8], tables[8:10])


def window_rows(side, groups, cells_y):
    for group in range(groups):
        local = wide_group(group, cells_y // 2 // GROUP, groups)
        start = pl.multiple_of(group_row(side, local, cells_y), GROUP)
        yield slice(group * GROUP, (group + 1) * GROUP), pl.ds(start, GROUP)


def window_kernel(estimate_ref, out_ref):
    for rows, source in window_rows(1 - half(), out_ref.shape[1] // GROUP, estimate_ref.shape[1]):
        out_ref[:, rows, :] = estimate_ref[:, source, :]


def other_window(estimate, wide):
    planes, _, cells_z = estimate.shape
    shape = jax.ShapeDtypeStruct((planes, wide, cells_z), F32)
    return call(window_kernel, shape, [VMEM], "other_window")(estimate)


def put_edges(out_ref, edge_refs):
    end = out_ref.shape[1]
    for far_ref, near_ref in zip(edge_refs[::2], edge_refs[1::2]):
        radius, rows = far_ref.shape[0], slice(end - far_ref.shape[1], end)
        beyond = out_ref.shape[0] - radius
        for p in range(radius):
            far_ref[p] = out_ref[p + core() * beyond, rows]
            near_ref[p] = out_ref[p + (1 - core()) * beyond, rows]
        end -= far_ref.shape[1]


def choose_kernel(estimate_ref, crossed_ref, out_ref, far_ref):
    straight = core() == half()
    for rows, source in window_rows(half(), out_ref.shape[1] // GROUP, estimate_ref.shape[1]):
        out_ref[:, rows, :] = jnp.where(straight, estimate_ref[:, source, :], crossed_ref[:, rows, :])
    beyond = core() * (out_ref.shape[0] - far_ref.shape[0])
    for p in range(far_ref.shape[0]):
        far_ref[p] = out_ref[p + beyond]


def edge_shapes(shape, radius, chunks):
    planes, _, lanes = shape
    edges = [jax.ShapeDtypeStruct((radius, rows, lanes), F32) for rows in chunks for _ in range(2)]
    return (jax.ShapeDtypeStruct(shape, F32), *edges)


def choose(estimate, crossed, radius):
    out_shape = edge_shapes(crossed.shape, radius, crossed.shape[1:2])[:2]
    return call(choose_kernel, out_shape, [VMEM] * 2, "estimate")(estimate, crossed)


def shift_kernel(offsets_ref, acq_ref, first_ref, second_ref, turned_ref):
    planes, cells_y, cells_z = acq_ref.shape
    near = first_ref.shape[1]
    shift_y, shift_z = offsets_ref[0, 1], offsets_ref[0, 2]
    row = iota((cells_y, cells_z), 0) + shift_y
    col = iota((cells_y, cells_z), 1) + shift_z
    inside = (row >= 0) & (row < cells_y) & (col >= 0) & (col < cells_z)
    turn_y = lax.rem(cells_y - shift_y, cells_y)
    turn_z = lax.rem(cells_z - shift_z, cells_z)

    def body(p, carry):
        x = pltpu.roll(pltpu.roll(acq_ref[p], turn_z, 1), turn_y, 0)
        turned_ref[...] = jnp.where(inside, x, jnp.zeros_like(x))
        for side, out_ref in ((core(), first_ref), (1 - core(), second_ref)):
            for group in range(near // GROUP):
                start = pl.multiple_of(group_row(side, group, cells_y), GROUP)
                out_ref[p, group * GROUP:(group + 1) * GROUP, :] = turned_ref[pl.ds(start, GROUP), :]
        return carry

    lax.fori_loop(0, planes, body, 0)


def shift_and_cut(offsets, acquired, near):
    planes, cells_y, cells_z = acquired.shape
    shape = jax.ShapeDtypeStruct((planes, near, cells_z), F32)
    scratch = [pltpu.VMEM((cells_y, cells_z), F32)]
    return call(shift_kernel, (shape, shape), [SMEM, VMEM], "shift_recorded", scratch)(offsets, acquired)


def gather(ref, row):
    return ref[:, pl.ds(pl.multiple_of(row, 8), 8), :]


def spread_x(hi_ref, lo_ref, index, band_rows, band_lanes, blocks):
    lanes = blocks[0][0].shape[2]
    filled = []
    for parts in blocks:
        count = 8 * sum(part.shape[0] for part in parts)
        missing = (pad_to(count, 128) - count) // 8
        filled += list(parts) + ([jnp.zeros((missing, 8, lanes), F32)] if missing else [])
    high, low = split(jnp.concatenate(filled, axis=0).reshape(-1, lanes))
    band = hi_ref[index, band_rows, band_lanes]
    out = dot(band, high) + (dot(band, low) + dot(lo_ref[index, band_rows, band_lanes], high))
    return out.reshape(-1, 8, lanes)


def near_lanes(planes, radius):
    return pad_to(8 * (planes + radius), 128)


def blur_x_kernel(hi_ref, lo_ref, *refs, far, radius):
    planes_of, before, (first_ref, second_ref) = refs[:2 - far], refs[2 - far:-2], refs[-2:]
    planes, rows, _ = first_ref.shape
    split_at = near_lanes(planes, radius)
    lanes = slice(split_at, None) if far else slice(0, split_at)

    def body(step, carry):
        row = pl.multiple_of(step * 8, 8)
        place = (slice(None), pl.ds(row, 8), slice(None))
        out = spread_x(hi_ref, lo_ref, 0, slice(None), lanes, [[gather(ref, row) for ref in planes_of]])
        out = [out[:planes], out[planes:]]
        if before:
            out = [ref[place] + part for ref, part in zip(before, out)]
        first_ref[place], second_ref[place] = out
        return carry

    lax.fori_loop(0, rows // 8, body, 0)


def blur_x(tables, planes_of, before, planes):
    far, (radius, rows, lanes) = len(planes_of) == 1, planes_of[-1].shape
    shape = jax.ShapeDtypeStruct((planes, rows, lanes), F32)
    kernel = functools.partial(blur_x_kernel, far=far, radius=radius)
    operands = [*tables.x, *planes_of, *before]
    return call(kernel, (shape, shape), [VMEM] * len(operands), "blur_x_far" if far else "blur_x_near")(*operands)


def blur_near(tables, own, near):
    return blur_x(tables, (own, near), (), own.shape[0])


def blur_far(tables, far, parts):
    return blur_x(tables, (far,), parts, parts[0].shape[0])


def spread_y(band, x):
    high, low = split(x)
    return dot(band[:, :3 * x.shape[0]], jnp.concatenate([high, low, high], axis=0))


def spread_z(x, hi_ref, lo_ref, index):
    high, low = split(x)
    return dot(high, hi_ref[index]) + (dot(low, hi_ref[index]) + dot(high, lo_ref[index]))


def blurred_planes(wide_refs, yf_ref, zhi_ref, zlo_ref, order, block):
    wide = [jnp.concatenate([ref[p] for ref in wide_refs], axis=0) for p in block]
    spread = jnp.concatenate([spread_y(yf_ref[order], rows) for rows in wide], axis=0)
    return spread_z(spread, zhi_ref, zlo_ref, order)


def plane_blocks(planes, step=4):
    return [range(start, min(start + step, planes)) for start in range(0, planes, step)]


def blur_yz_kernel(*refs, order):
    wide_refs, (yf_ref, zhi_ref, zlo_ref, out_ref) = refs[:-4], refs[-4:]
    near = yf_ref.shape[1]
    for block in plane_blocks(out_ref.shape[0]):
        blurred = blurred_planes(wide_refs, yf_ref, zhi_ref, zlo_ref, order, block)
        for k, p in enumerate(block):
            out_ref[p] = blurred[k * near:(k + 1) * near]


def blur_yz(wides, tables, order):
    planes, _, lanes = wides[0].shape
    shape = jax.ShapeDtypeStruct((planes, tables.whole[0].shape[1], lanes), F32)
    kernel = functools.partial(blur_yz_kernel, order=order)
    return call(kernel, shape, [VMEM] * (3 + len(wides)), "blur_yz")(*wides, tables.whole[0], *tables.z)


def adjoint_planes(blurred_of, image_of, ya_ref, zhi_ref, zlo_ref, order, out_ref, edge_refs, complete=None):
    planes, rows, _ = out_ref.shape
    for block in plane_blocks(planes):
        blurred = blurred_of(block)
        image = jnp.concatenate([image_of(p) for p in block], axis=0)
        ratio = jnp.where(image >= 0, image / blurred, jnp.ones_like(image))
        near = ratio.shape[0] // len(block)
        ratios = [ratio[k * near:(k + 1) * near] for k in range(len(block))]
        if complete:
            ratios = [complete(p, rows_of) for p, rows_of in zip(block, ratios)]
        spread = jnp.concatenate([spread_y(ya_ref[order], rows_of) for rows_of in ratios], axis=0)
        spread = spread_z(spread, zhi_ref, zlo_ref, 2 + order)
        for k, p in enumerate(block):
            out_ref[p] = spread[k * rows:(k + 1) * rows]
    put_edges(out_ref, edge_refs)


def first_ratio_kernel(
    shift_ref, far_ref, near_ref, own_ref, masks_ref, blurred_ref, ya_ref, zhi_ref, zlo_ref, out_ref, *refs, order, extent_x, cells_y
):
    edge_refs, image_ref, (mine_ref, beyond_ref, semaphores) = refs[:-4], refs[-4], refs[-3:]
    planes, near, cells_z = image_ref.shape
    side = half()
    slab = lax.axis_index("tile") - side + core()
    shift_x, shift_y, shift_z = (shift_ref[order, i] for i in range(3))
    lanes = masks_ref.shape[2]
    pick = iota((near, lanes), 1) == global_row(side, iota((near, lanes), 0), cells_y)
    is_far = (shift_x > 0) == (core() == 1)
    copy = pltpu.make_async_copy(own_ref, mine_ref, semaphores.at[0])
    far_copy = pltpu.make_async_copy(far_ref, beyond_ref, semaphores.at[1])
    near_copy = pltpu.make_async_copy(near_ref, beyond_ref, semaphores.at[1])
    copy.start()
    pl.when(is_far)(far_copy.start)
    pl.when(jnp.logical_not(is_far))(near_copy.start)
    copy.wait()
    far_copy.wait()
    mask = masks_ref[half() if order == 0 else 1 - half()].astype(BF16)
    columns = lax.dot_general(
        pick.astype(F32).astype(BF16), mask, (((1,), (1,)), ((), ())), preferred_element_type=F32
    )
    row = global_row(side, iota((near, cells_z), 0), cells_y) + shift_y
    col = iota((near, cells_z), 1) + shift_z
    inside = (row >= 0) & (row < cells_y) & (col >= 0) & (col < cells_z)

    def fetch(p):
        source = p + shift_x
        x = slab * planes + source
        is_own = (source >= 0) & (source < planes)
        beyond = jnp.clip(jnp.where(source < 0, source + planes, source - planes), 0, planes - 1)
        value = jnp.where(is_own, mine_ref[jnp.clip(source, 0, planes - 1)], beyond_ref[beyond])
        weight = jnp.broadcast_to(columns[:, p:p + 1], (near, cells_z))
        covered = inside & (weight > 0.5) & (x >= 0) & (x < extent_x)
        value = jnp.where(covered, value, jnp.full_like(value, -1.0))
        image_ref[p] = value
        return value

    def blurred_of(block):
        return jnp.concatenate([blurred_ref[p] for p in block], axis=0)

    adjoint_planes(blurred_of, fetch, ya_ref, zhi_ref, zlo_ref, order, out_ref, edge_refs)


def next_ratio_kernel(*refs, inner, count, first_row):
    image_refs, wide_refs, refs = refs[:2], (refs[2:4], refs[4:6]), refs[6:]
    passed_ref, refs = (None, refs) if inner else (refs[0], refs[1:])
    (yf_ref, ya_ref, zhi_ref, zlo_ref), out_refs, (far_ref, near_ref), refs = refs[:4], refs[4:6], refs[6:8], refs[8:]
    planes = out_refs[0].shape[0]
    rows = yf_ref.shape[1]
    for order in range(2):

        def blurred_of(block):
            return blurred_planes(wide_refs[order], yf_ref, zhi_ref, zlo_ref, order, block)

        def image_of(p):
            return image_refs[order][p, first_row:first_row + rows]

        def complete(p, ratio):
            if inner:
                refs[0][order, p] = ratio[rows - count:]
                return ratio
            return jnp.concatenate([passed_ref[order, p], ratio], axis=0)

        edges = (far_ref.at[order], near_ref.at[order])
        adjoint_planes(blurred_of, image_of, ya_ref, zhi_ref, zlo_ref, order, out_refs[order], edges, complete)


def next_ratio(images, wides, passed, y_tables, z_tables, radius, count, first_row):
    planes, _, lanes = images[0].shape
    rows = y_tables[1].shape[1]
    kernel = functools.partial(next_ratio_kernel, inner=passed is None, count=count, first_row=first_row)
    shape = jax.ShapeDtypeStruct
    whole, edge = shape((planes, rows, lanes), F32), shape((2, radius, rows, lanes), F32)
    out_shape = (whole, whole, edge, edge)
    if passed is None:
        out_shape += (shape((2, planes, count, lanes), F32),)
    operands = [*images, *wides[0], *wides[1]] + ([] if passed is None else [passed]) + [*y_tables, *z_tables]
    return call(kernel, out_shape, [VMEM] * len(operands), "ratio")(*operands)


def first_ratio(shifts, blocks, masks, blurred, tables, order, radius, chunks, extent_x, cells_y):
    planes, near, lanes = blurred.shape
    kernel = functools.partial(first_ratio_kernel, order=order, extent_x=extent_x, cells_y=cells_y)
    rows = tables.whole[1].shape[1]
    out_shape = edge_shapes((planes, rows, lanes), radius, chunks) + (jax.ShapeDtypeStruct(blurred.shape, F32),)
    scratch = [
        pltpu.VMEM(blurred.shape, F32), pltpu.VMEM(blurred.shape, F32), pltpu.SemaphoreType.DMA((2,))
    ]
    in_specs = [SMEM] + [pl.BlockSpec(memory_space=pl.ANY)] * 3 + [VMEM] * 5
    return call(kernel, out_shape, in_specs, "image_and_ratio", scratch, hbm=(len(out_shape) - 1,))(
        shifts, *blocks, masks, blurred, tables.whole[1], *tables.z
    )


def factor_kernel(hi_ref, lo_ref, before_ref, *refs, orders, starts, share):
    out_ref = refs[-1]
    planes, rows, _ = out_ref.shape

    def body(step, carry):
        row = pl.multiple_of(step * 8, 8)
        total = gather(before_ref, starts[0] + row)
        if share:
            total = share * jnp.log(total)
        for index, order in enumerate(orders):
            far_ref, near_ref, own_ref = refs[3 * index:3 * index + 3]
            if len(far_ref.shape) == 4:
                far_ref, near_ref = far_ref.at[order], near_ref.at[order]
            own = gather(own_ref, starts[1] + row)
            blocks = [[own, gather(near_ref, row)], [gather(far_ref, row)]]
            band_rows = slice(order * 8 * planes, (order + 1) * 8 * planes)
            total = total + jnp.log(spread_x(hi_ref, lo_ref, 1, band_rows, slice(None), blocks))
        out_ref[:, pl.ds(row, 8), :] = total
        return carry

    lax.fori_loop(0, rows // 8, body, 0)


def log_factor(tables, before, sides, orders, rows, starts, share):
    kernel = functools.partial(factor_kernel, orders=orders, starts=starts, share=share)
    planes, _, lanes = sides[0][2].shape
    shape = jax.ShapeDtypeStruct((planes, rows, lanes), F32)
    parts = [part for side in sides for part in side]
    return call(kernel, shape, [VMEM] * (3 + len(parts)), "log_factor")(*tables.x, before, *parts)


def update_kernel(*refs, count):
    parts, out_ref, edge_refs = refs[:count], refs[count], refs[count + 1:]
    for p in range(out_ref.shape[0]):
        total = parts[0][p]
        for part in parts[1:]:
            total = total + part[p]
        out_ref[p] = jnp.exp(total)
    put_edges(out_ref, edge_refs)


def update(parts, radius, hbm):
    kernel = functools.partial(update_kernel, count=len(parts))
    out_shape = edge_shapes(parts[0].shape, radius, parts[0].shape[1:2])
    return call(kernel, out_shape, [VMEM] * len(parts), "update", hbm=hbm)(*parts)


def finish_kernel(*refs):
    own, other, out_ref = refs[:(len(refs) - 1) // 2], refs[(len(refs) - 1) // 2:-1], refs[-1]
    straight = core() == half()
    groups = out_ref.shape[1] // GROUP
    for group in range(groups):
        rows = slice(group * GROUP, (group + 1) * GROUP)
        own_total, other_total = own[0][:, rows, :], other[0][:, rows, :]
        for part in own[1:]:
            own_total = own_total + part[:, rows, :]
        for part in other[1:]:
            other_total = other_total + part[:, rows, :]
        start = jnp.where(core() == 0, group, groups - 1 - group) * GROUP
        out_ref[:, pl.ds(pl.multiple_of(start, GROUP), GROUP), :] = jnp.exp(jnp.where(straight, own_total, other_total))


def finish(own_parts, other_parts):
    shape = jax.ShapeDtypeStruct(own_parts[0].shape, F32)
    return call(finish_kernel, shape, [VMEM] * (2 * len(own_parts)), "last_update")(*own_parts, *other_parts)


def join_kernel(*refs, starts):
    sources, out_ref, semaphores = refs[:-2], refs[-2], refs[-1]
    cells_y = out_ref.shape[1]
    copies = []
    for index, source_ref in enumerate(sources):
        rows, start = source_ref.shape[1], starts[index // 2]
        side = core() if index % 2 == 0 else 1 - core()
        place = pl.multiple_of(jnp.where(side == 0, start, cells_y - start - rows), GROUP)
        target = out_ref.at[:, pl.ds(place, rows), :]
        copies.append(pltpu.make_async_copy(source_ref, target, semaphores.at[index]))
    for copy in copies:
        copy.start()
    for copy in copies:
        copy.wait()


def join(pieces, starts, shape):
    anywhere = pl.BlockSpec(memory_space=pl.ANY)
    return pl.pallas_call(
        functools.partial(join_kernel, starts=starts),
        out_shape=jax.ShapeDtypeStruct(shape, F32),
        in_specs=[anywhere] * len(pieces),
        out_specs=anywhere,
        scratch_shapes=[pltpu.SemaphoreType.DMA((len(pieces),))],
        compiler_params=PARAMS,
        name="join_halves",
    )(*pieces)


def shards(acquired, estimate, offsets, view_mask, kern_x, kern_y, kern_z):
    planes, cells_y, cells_z = estimate.shape
    views, slabs = lax.axis_size("view"), lax.axis_size("tile")
    groups = views // 2
    taps_y = kern_y.shape[1]
    radius = kern_x.shape[1] // 2
    own_rows = cells_y // 2
    near = own_rows + pad_to(taps_y // 2, GROUP)
    wide = own_rows + pad_to(2 * (taps_y // 2), GROUP)
    edge_rows = wide - own_rows
    inner_rows = own_rows - edge_rows
    group = lax.axis_index("view") // 2
    straight = core() == half()

    def across(turn, half_of=lambda r: r, core_of=lambda c: c, when=lambda c, r: True):
        return lambda g, c, q, r: ((g + turn) % groups, core_of(c), q, half_of(r)) if when(c, r) else None

    def neighbours(far, near):
        return send(far, to_far), send(near, to_core_partner)

    crossing = other_window(estimate, wide)
    crossed = send(crossing, across(0, lambda r: 1 - r, when=lambda c, r: c == r))

    mine = [jnp.pad(row, ((0, 0), (0, 128 - row.shape[1]))) for row in (kern_x, kern_y, kern_z)]
    mine = after(jnp.concatenate(mine, axis=1), crossing)
    other = send(mine, to_core_partner)
    taps = kern_x.shape[1], taps_y, kern_z.shape[1]
    tables = make_tables(mine, other, taps, planes, cells_y, cells_z, (own_rows, near, wide))
    offset = after(offsets.astype(F32), tables.whole[0])
    other = send(offset, to_core_partner)
    shifts = jnp.where(straight, jnp.concatenate([offset, other]), jnp.concatenate([other, offset])).astype(jnp.int32)

    mask = view_mask.astype(F32)
    other = send(mask, to_core_partner)
    masks = jnp.where(core() == 0, jnp.concatenate([mask, other]), jnp.concatenate([other, mask]))

    acquired = after(after(acquired, tables.whole[0]), masks)
    first, second = shift_and_cut(offsets, acquired[0], near)

    arrived = send(after(first, tables.whole[0]), lambda g, c, q, r: (g, r, q, c) if c != r else None)
    current, distant = choose(after(estimate, first), crossed, radius)
    second = send(after(second, current), lambda g, c, q, r: (g, r, q, 1 - c))
    close = lax.dynamic_slice_in_dim(current, (1 - core()) * (planes - radius), radius, 0)
    distant, close = neighbours(distant, close)
    first = jnp.where(straight, first, arrived)

    masks = jnp.where(straight, masks, send(after(masks, current), to_row_partner))

    blocks = [(*neighbours(block, block), block) for block in (first, second)]
    wide_parts = blur_x(tables, (current, close), blur_x(tables, (distant,), (), planes), planes)
    blurred = [blur_yz([part], tables, order) for order, part in enumerate(wide_parts)]

    row_chunks = [(inner_rows, edge_rows), (0, inner_rows)]
    share = 1.0 / groups
    images, sides = [], []
    for order, chunk_sizes in enumerate(([own_rows], [edge_rows, inner_rows])):
        spread, *edges, image = first_ratio(
            shifts, blocks[order], masks, blurred[order], tables, order, radius, chunk_sizes, planes * slabs, cells_y
        )
        images.append(image)
        sides.append([(*neighbours(*edges[k:k + 2]), spread) for k in range(0, len(edges), 2)])
    total = log_factor(tables, current, sides[0], [0], own_rows, (0, 0), share)
    totals = [
        log_factor(tables, total, [side], [1], rows, (start, start), 0)
        for (start, rows), side in zip(row_chunks, sides[1])
    ]

    for step in range(1, ITERS):
        chunks, before = [], []
        for total in totals:
            parts = [total] + [send(total, across(turn)) for turn in range(1, groups)]
            rows, distant, close = update(parts, radius, () if chunks else (2,))
            if total is totals[0]:
                beyond = send(rows, to_row_partner)
            distant = after(distant, chunks[0][0]) if chunks else distant
            distant, close = neighbours(distant, close)
            chunks.append((distant, blur_near(tables, rows, close)))
            before.append(rows)
        rest = planes - radius
        distant, close = neighbours(
            lax.dynamic_slice_in_dim(beyond, core() * rest, radius, 0),
            lax.dynamic_slice_in_dim(beyond, (1 - core()) * rest, radius, 0),
        )
        edge_parts, inner_parts = [blur_far(tables, *chunk) for chunk in chunks]
        halo_parts = blur_near(tables, beyond, close)
        *inner_spreads, distant_inner, close_inner, passed = next_ratio(
            images, list(zip([after(after(part, distant), close) for part in inner_parts], edge_parts)), None, tables.inner, tables.z, radius, 2 * (near - own_rows), 0
        )
        halo_parts = blur_far(tables, distant, halo_parts)
        inner_side = neighbours(distant_inner, close_inner)
        *edge_spreads, distant, close = next_ratio(
            images, list(zip(edge_parts, halo_parts)), passed, tables.edge, tables.z, radius, 0,
            inner_rows + near - own_rows,
        )
        edge_side = neighbours(distant, close)
        totals = [
            log_factor(tables, rows_of, [(*side, spread) for spread in spreads], [0, 1], rows, (0, 0), share)
            for rows_of, side, spreads, rows in (
                (before[0], edge_side, edge_spreads, edge_rows), (before[1], inner_side, inner_spreads, inner_rows)
            )
        ]

    pieces = []
    for own in totals[::-1]:
        other_parts = [
            send(own, across(turn, lambda r: 1 - r, lambda c: 1 - c, lambda c, r: c != r))
            for turn in reversed(range(groups))
        ]
        own_parts = [own] + [send(own, across(turn, when=lambda c, r: c == r)) for turn in range(1, groups)]
        mine = finish(own_parts, other_parts)
        pieces += [mine, send(mine, to_core_partner)]
    return join(pieces, [start for start, _ in row_chunks[::-1]], estimate.shape)


def solution(mesh):
    in_specs = (
        P("view", "tile", None, None),
        P("tile", None, None),
        P("view", None),
        P("view", "tile", None),
        P("view", None),
        P("view", None),
        P("view", None),
    )
    out_specs = P("tile", None, None)
    return jax.shard_map(shards, mesh=mesh, in_specs=in_specs, out_specs=out_specs, check_vma=False)
```

```python
import functools
import typing

import jax
import jax.numpy as jnp
from jax import lax
from jax.experimental import pallas as pl
from jax.experimental.pallas import tpu as pltpu
from jax.sharding import PartitionSpec as P

ITERS = 2
AXES = ("view", "tile")
F32 = jnp.float32
BF16 = jnp.bfloat16
VMEM = pl.BlockSpec(memory_space=pltpu.VMEM)
SMEM = pl.BlockSpec(memory_space=pltpu.SMEM)
PARAMS = pltpu.CompilerParams(vmem_limit_bytes=12 * 1024 * 1024)
GROUP = 16


def moves(move):
    views, tiles = lax.axis_size("view"), lax.axis_size("tile")
    pairs = []
    for view in range(views):
        for tile in range(tiles):
            target = move(view // 2, view % 2, tile // 2, tile % 2)
            if target is not None:
                g, c, q, r = target
                pairs.append((view * tiles + tile, (2 * g + c) * tiles + 2 * q + r))
    return pairs


def send(array, move):
    return lax.ppermute(array, AXES, moves(move))


def after(array, other):
    return lax.optimization_barrier((array, other))[0]


def to_far(g, c, q, r):
    s = 2 * q + c + (1 if c else -1)
    return (g, s % 2, s // 2, r) if 0 <= s < lax.axis_size("tile") else None


def to_row_partner(g, c, q, r):
    return (g, c, q, 1 - r)


def to_core_partner(g, c, q, r):
    return (g, 1 - c, q, r)


def core():
    return lax.rem(lax.axis_index("view"), 2)


def half():
    return lax.rem(lax.axis_index("tile"), 2)


def split(x):
    high = x.astype(BF16)
    return high, (x - high.astype(F32)).astype(BF16)


def dot(a, b):
    return jnp.dot(a, b, preferred_element_type=F32)


def iota(shape, dim):
    return lax.broadcasted_iota(jnp.int32, shape, dim)


def group_row(half, group, cells_y):
    return group * GROUP + half * (cells_y - GROUP - 2 * group * GROUP)


def global_row(half, local, cells_y):
    group = local // GROUP
    return group_row(half, group, cells_y) + (local - group * GROUP)


def wide_local(place, own, wide):
    group = (place - own) // GROUP
    return own + (wide - own) - GROUP - group * GROUP + (place - own - group * GROUP)


def wide_group(group, own_groups, groups):
    return group if group < own_groups else own_groups + groups - 1 - group


def pad_to(value, unit):
    return -(-value // unit) * unit


def call(kernel, out_shape, in_specs, name, scratch=(), hbm=()):
    if hbm:
        out_shape = tuple(pltpu.HBM(o.shape, o.dtype) if index in hbm else o for index, o in enumerate(out_shape))
    return pl.pallas_call(
        kernel,
        out_shape=out_shape,
        in_specs=in_specs,
        out_specs=(VMEM,) * len(out_shape) if isinstance(out_shape, tuple) else VMEM,
        scratch_shapes=list(scratch),
        compiler_params=PARAMS,
        name=name,
    )


class Tables(typing.NamedTuple):
    whole: tuple
    inner: tuple
    edge: tuple
    z: tuple
    x: tuple


def place(row, count, width, turned, spacing):
    source, target = iota((row.shape[1], width), 0), iota((row.shape[1], width), 1)
    index = count - 1 - source if turned else source
    ones = (target == spacing * index) & (source < count)
    return jnp.dot(row, ones.astype(F32), precision=lax.Precision.HIGHEST, preferred_element_type=F32)


def tables_kernel(mine_ref, other_ref, *refs, blocks, sizes, cells_y, taps):
    y_refs, (zhi_ref, zlo_ref, xhi_ref, xlo_ref) = refs[:-4], refs[-4:]
    taps_x, taps_y, taps_z = taps
    straight = core() == half()
    mine, other = mine_ref[...], other_ref[...]
    both = (jnp.where(straight, mine, other), jnp.where(straight, other, mine))
    radius, radius_x, radius_z = taps_y // 2, taps_x // 2, taps_z // 2
    side = half()
    own, wide = sizes
    for out_ref, adjoint, first_row, first_col, width in zip(y_refs, *zip(*blocks)):
        _, rows, lanes = out_ref.shape
        row = global_row(side, first_row + iota((rows, lanes), 0), cells_y)
        lane = iota((rows, lanes), 1)
        place_of = lane + first_col
        turned = place_of if adjoint else jnp.where(place_of < own, place_of, wide_local(place_of, own, wide))
        col = global_row(side, turned, cells_y)
        delta = (row - col if adjoint else col - row) + radius
        delta = jnp.where(lane < width, delta, -1)
        for order in range(2):
            band = jnp.zeros((rows, lanes), F32)
            values = both[order][:, 128:256]
            for a in range(taps_y):
                band = jnp.where(delta == a, jnp.broadcast_to(values[:, a:a + 1], (rows, lanes)), band)
            high, low = split(band)
            high, low = high.astype(F32), low.astype(F32)
            out_ref[order] = (high + pltpu.roll(high, width, 1) + pltpu.roll(low, 2 * width, 1)).astype(BF16)

    lanes = zhi_ref.shape[2]
    near_z = jnp.abs(iota((lanes, lanes), 1) - iota((lanes, lanes), 0)) <= radius_z
    for index in range(4):
        base = place(both[index % 2][:, 256:384], taps_z, lanes, index < 2, 1)
        base = pltpu.roll(base, lanes - radius_z, 1)
        band = pltpu.roll(jnp.broadcast_to(base, (lanes, lanes)), 0, 1, stride=1, stride_axis=0)
        zhi_ref[index], zlo_ref[index] = split(jnp.where(near_z, band, jnp.zeros_like(band)))

    rows = xhi_ref.shape[1] // 2
    lanes = max(512, 1 << (xhi_ref.shape[2] - 1).bit_length())
    for index in range(4):
        base = place(both[index % 2][:, :128], taps_x, lanes, index >= 2, 8)
        base = jnp.broadcast_to(base, (rows, lanes))
        band = pltpu.roll(base, 0, 1, stride=1, stride_axis=0)
        lane = iota((rows, lanes), 1)
        edge = 8 * radius_x
        far = pad_to(rows + edge, 128)
        next_near = pltpu.roll(band, lanes - edge, 1)
        next_far = pltpu.roll(band, far - rows - edge, 1)
        near_part = jnp.where((lane < rows) | (core() == 0), next_near, pltpu.roll(band, rows, 1))
        far_part = jnp.where(core() == 0, pltpu.roll(band, far, 1), next_far)
        zero = jnp.zeros_like(band)
        band = jnp.where(
            lane < rows + edge, near_part, jnp.where((lane >= far) & (lane < far + edge), far_part, zero)
        )[:, :xhi_ref.shape[2]]
        block = (index // 2, slice(index % 2 * rows, index % 2 * rows + rows))
        xhi_ref[block], xlo_ref[block] = split(band)


def make_tables(mine, other, taps, planes, cells_y, cells_z, sizes):
    own, near, wide = sizes
    inner, beyond = 2 * own - wide, near - own
    radius = taps[0] // 2
    depth = pad_to(8 * (planes + radius), 128) + pad_to(8 * radius, 128)
    blocks = [
        (False, near, 0, 0, wide), (True, own, 0, 0, near),
        (False, inner + beyond, 0, 0, own), (True, inner, 0, 0, inner + beyond),
        (False, near - inner - beyond, inner + beyond, inner, wide - inner),
        (True, own - inner, inner, inner - beyond, near - inner + beyond),
    ]
    kernel = functools.partial(
        tables_kernel, blocks=[block[:1] + block[2:] for block in blocks], sizes=(own, wide), cells_y=cells_y, taps=taps
    )
    shape = jax.ShapeDtypeStruct
    out_shape = tuple(shape((2, block[1], pad_to(3 * block[4], 128)), BF16) for block in blocks) + (
        shape((4, cells_z, cells_z), BF16),
        shape((4, cells_z, cells_z), BF16),
        shape((2, 2 * 8 * planes, depth), BF16),
        shape((2, 2 * 8 * planes, depth), BF16),
    )
    tables = call(kernel, out_shape, [VMEM, VMEM], "band_matrices")(mine, other)
    whole, inner_rows, edge_rows = tables[0:2], tables[2:4], tables[4:6]
    return Tables(whole, inner_rows, edge_rows, tables[6:8], tables[8:10])


def window_rows(side, groups, cells_y):
    for group in range(groups):
        local = wide_group(group, cells_y // 2 // GROUP, groups)
        start = pl.multiple_of(group_row(side, local, cells_y), GROUP)
        yield slice(group * GROUP, (group + 1) * GROUP), pl.ds(start, GROUP)


def window_kernel(estimate_ref, out_ref):
    for rows, source in window_rows(1 - half(), out_ref.shape[1] // GROUP, estimate_ref.shape[1]):
        out_ref[:, rows, :] = estimate_ref[:, source, :]


def other_window(estimate, wide):
    planes, _, cells_z = estimate.shape
    shape = jax.ShapeDtypeStruct((planes, wide, cells_z), F32)
    return call(window_kernel, shape, [VMEM], "other_window")(estimate)


def put_edges(out_ref, edge_refs):
    end = out_ref.shape[1]
    for far_ref, near_ref in zip(edge_refs[::2], edge_refs[1::2]):
        radius, rows = far_ref.shape[0], slice(end - far_ref.shape[1], end)
        beyond = out_ref.shape[0] - radius
        for p in range(radius):
            far_ref[p] = out_ref[p + core() * beyond, rows]
            near_ref[p] = out_ref[p + (1 - core()) * beyond, rows]
        end -= far_ref.shape[1]


def choose_kernel(estimate_ref, crossed_ref, out_ref, far_ref):
    straight = core() == half()
    for rows, source in window_rows(half(), out_ref.shape[1] // GROUP, estimate_ref.shape[1]):
        out_ref[:, rows, :] = jnp.where(straight, estimate_ref[:, source, :], crossed_ref[:, rows, :])
    beyond = core() * (out_ref.shape[0] - far_ref.shape[0])
    for p in range(far_ref.shape[0]):
        far_ref[p] = out_ref[p + beyond]


def edge_shapes(shape, radius, chunks):
    planes, _, lanes = shape
    edges = [jax.ShapeDtypeStruct((radius, rows, lanes), F32) for rows in chunks for _ in range(2)]
    return (jax.ShapeDtypeStruct(shape, F32), *edges)


def choose(estimate, crossed, radius):
    out_shape = edge_shapes(crossed.shape, radius, crossed.shape[1:2])[:2]
    estimate, crossed = (pltpu.with_memory_space_constraint(array, pltpu.HBM) for array in (estimate, crossed))
    return call(choose_kernel, out_shape, [VMEM] * 2, "estimate")(estimate, crossed)


def shift_kernel(offsets_ref, acq_ref, first_ref, second_ref, turned_ref):
    planes, cells_y, cells_z = acq_ref.shape
    near = first_ref.shape[1]
    shift_y, shift_z = offsets_ref[0, 1], offsets_ref[0, 2]
    row = iota((cells_y, cells_z), 0) + shift_y
    col = iota((cells_y, cells_z), 1) + shift_z
    inside = (row >= 0) & (row < cells_y) & (col >= 0) & (col < cells_z)
    turn_y = lax.rem(cells_y - shift_y, cells_y)
    turn_z = lax.rem(cells_z - shift_z, cells_z)

    def body(p, carry):
        x = pltpu.roll(pltpu.roll(acq_ref[p], turn_z, 1), turn_y, 0)
        turned_ref[...] = jnp.where(inside, x, jnp.zeros_like(x))
        for side, out_ref in ((core(), first_ref), (1 - core(), second_ref)):
            for group in range(near // GROUP):
                start = pl.multiple_of(group_row(side, group, cells_y), GROUP)
                out_ref[p, group * GROUP:(group + 1) * GROUP, :] = turned_ref[pl.ds(start, GROUP), :]
        return carry

    lax.fori_loop(0, planes, body, 0)


def shift_and_cut(offsets, acquired, near):
    planes, cells_y, cells_z = acquired.shape
    shape = jax.ShapeDtypeStruct((planes, near, cells_z), F32)
    scratch = [pltpu.VMEM((cells_y, cells_z), F32)]
    return call(shift_kernel, (shape, shape), [SMEM, VMEM], "shift_recorded", scratch)(offsets, acquired)


def gather(ref, row):
    return ref[:, pl.ds(pl.multiple_of(row, 8), 8), :]


def spread_x(hi_ref, lo_ref, index, band_rows, band_lanes, blocks):
    lanes = blocks[0][0].shape[2]
    filled = []
    for parts in blocks:
        count = 8 * sum(part.shape[0] for part in parts)
        missing = (pad_to(count, 128) - count) // 8
        filled += list(parts) + ([jnp.zeros((missing, 8, lanes), F32)] if missing else [])
    high, low = split(jnp.concatenate(filled, axis=0).reshape(-1, lanes))
    band = hi_ref[index, band_rows, band_lanes]
    out = dot(band, high) + (dot(band, low) + dot(lo_ref[index, band_rows, band_lanes], high))
    return out.reshape(-1, 8, lanes)


def near_lanes(planes, radius):
    return pad_to(8 * (planes + radius), 128)


def blur_x_kernel(hi_ref, lo_ref, *refs, far, radius):
    planes_of, before, (first_ref, second_ref) = refs[:2 - far], refs[2 - far:-2], refs[-2:]
    planes, rows, _ = first_ref.shape
    split_at = near_lanes(planes, radius)
    lanes = slice(split_at, None) if far else slice(0, split_at)

    def body(step, carry):
        row = pl.multiple_of(step * 8, 8)
        place = (slice(None), pl.ds(row, 8), slice(None))
        out = spread_x(hi_ref, lo_ref, 0, slice(None), lanes, [[gather(ref, row) for ref in planes_of]])
        out = [out[:planes], out[planes:]]
        if before:
            out = [ref[place] + part for ref, part in zip(before, out)]
        first_ref[place], second_ref[place] = out
        return carry

    lax.fori_loop(0, rows // 8, body, 0)


def blur_x(tables, planes_of, before, planes):
    far, (radius, rows, lanes) = len(planes_of) == 1, planes_of[-1].shape
    shape = jax.ShapeDtypeStruct((planes, rows, lanes), F32)
    kernel = functools.partial(blur_x_kernel, far=far, radius=radius)
    operands = [*tables.x, *planes_of, *before]
    return call(kernel, (shape, shape), [VMEM] * len(operands), "blur_x_far" if far else "blur_x_near")(*operands)


def blur_near(tables, own, near):
    return blur_x(tables, (own, near), (), own.shape[0])


def blur_far(tables, far, parts):
    return blur_x(tables, (far,), parts, parts[0].shape[0])


def spread_y(band, x):
    high, low = split(x)
    return dot(band[:, :3 * x.shape[0]], jnp.concatenate([high, low, high], axis=0))


def spread_z(x, hi_ref, lo_ref, index):
    high, low = split(x)
    return dot(high, hi_ref[index]) + (dot(low, hi_ref[index]) + dot(high, lo_ref[index]))


def blurred_planes(wide_refs, yf_ref, zhi_ref, zlo_ref, order, block):
    wide = [jnp.concatenate([ref[p] for ref in wide_refs], axis=0) for p in block]
    spread = jnp.concatenate([spread_y(yf_ref[order], rows) for rows in wide], axis=0)
    return spread_z(spread, zhi_ref, zlo_ref, order)


def plane_blocks(planes, step=4):
    return [range(start, min(start + step, planes)) for start in range(0, planes, step)]


def blur_yz_kernel(*refs, order):
    wide_refs, (yf_ref, zhi_ref, zlo_ref, out_ref) = refs[:-4], refs[-4:]
    near = yf_ref.shape[1]
    for block in plane_blocks(out_ref.shape[0]):
        blurred = blurred_planes(wide_refs, yf_ref, zhi_ref, zlo_ref, order, block)
        for k, p in enumerate(block):
            out_ref[p] = blurred[k * near:(k + 1) * near]


def blur_yz(wides, tables, order):
    planes, _, lanes = wides[0].shape
    shape = jax.ShapeDtypeStruct((planes, tables.whole[0].shape[1], lanes), F32)
    kernel = functools.partial(blur_yz_kernel, order=order)
    return call(kernel, shape, [VMEM] * (3 + len(wides)), "blur_yz")(*wides, tables.whole[0], *tables.z)


def adjoint_planes(blurred_of, image_of, ya_ref, zhi_ref, zlo_ref, order, out_ref, edge_refs, complete=None):
    planes, rows, _ = out_ref.shape
    for block in plane_blocks(planes):
        blurred = blurred_of(block)
        image = jnp.concatenate([image_of(p) for p in block], axis=0)
        ratio = jnp.where(image >= 0, image / blurred, jnp.ones_like(image))
        near = ratio.shape[0] // len(block)
        ratios = [ratio[k * near:(k + 1) * near] for k in range(len(block))]
        if complete:
            ratios = [complete(p, rows_of) for p, rows_of in zip(block, ratios)]
        spread = jnp.concatenate([spread_y(ya_ref[order], rows_of) for rows_of in ratios], axis=0)
        spread = spread_z(spread, zhi_ref, zlo_ref, 2 + order)
        for k, p in enumerate(block):
            out_ref[p] = spread[k * rows:(k + 1) * rows]
    put_edges(out_ref, edge_refs)


def first_ratio_kernel(
    shift_ref, far_ref, near_ref, own_ref, masks_ref, blurred_ref, ya_ref, zhi_ref, zlo_ref, out_ref, *refs, order, extent_x, cells_y
):
    edge_refs, image_ref, (mine_ref, beyond_ref, semaphores) = refs[:-4], refs[-4], refs[-3:]
    planes, near, cells_z = image_ref.shape
    side = half()
    slab = lax.axis_index("tile") - side + core()
    shift_x, shift_y, shift_z = (shift_ref[order, i] for i in range(3))
    lanes = masks_ref.shape[2]
    pick = iota((near, lanes), 1) == global_row(side, iota((near, lanes), 0), cells_y)
    is_far = (shift_x > 0) == (core() == 1)
    copy = pltpu.make_async_copy(own_ref, mine_ref, semaphores.at[0])
    far_copy = pltpu.make_async_copy(far_ref, beyond_ref, semaphores.at[1])
    near_copy = pltpu.make_async_copy(near_ref, beyond_ref, semaphores.at[1])
    copy.start()
    pl.when(is_far)(far_copy.start)
    pl.when(jnp.logical_not(is_far))(near_copy.start)
    copy.wait()
    far_copy.wait()
    mask = masks_ref[half() if order == 0 else 1 - half()].astype(BF16)
    columns = lax.dot_general(
        pick.astype(F32).astype(BF16), mask, (((1,), (1,)), ((), ())), preferred_element_type=F32
    )
    row = global_row(side, iota((near, cells_z), 0), cells_y) + shift_y
    col = iota((near, cells_z), 1) + shift_z
    inside = (row >= 0) & (row < cells_y) & (col >= 0) & (col < cells_z)

    def fetch(p):
        source = p + shift_x
        x = slab * planes + source
        is_own = (source >= 0) & (source < planes)
        beyond = jnp.clip(jnp.where(source < 0, source + planes, source - planes), 0, planes - 1)
        value = jnp.where(is_own, mine_ref[jnp.clip(source, 0, planes - 1)], beyond_ref[beyond])
        weight = jnp.broadcast_to(columns[:, p:p + 1], (near, cells_z))
        covered = inside & (weight > 0.5) & (x >= 0) & (x < extent_x)
        value = jnp.where(covered, value, jnp.full_like(value, -1.0))
        image_ref[p] = value
        return value

    def blurred_of(block):
        return jnp.concatenate([blurred_ref[p] for p in block], axis=0)

    adjoint_planes(blurred_of, fetch, ya_ref, zhi_ref, zlo_ref, order, out_ref, edge_refs)


def next_ratio_kernel(*refs, inner, count, first_row):
    image_refs, wide_refs, refs = refs[:2], (refs[2:4], refs[4:6]), refs[6:]
    passed_ref, refs = (None, refs) if inner else (refs[0], refs[1:])
    (yf_ref, ya_ref, zhi_ref, zlo_ref), out_refs, (far_ref, near_ref), refs = refs[:4], refs[4:6], refs[6:8], refs[8:]
    planes = out_refs[0].shape[0]
    rows = yf_ref.shape[1]
    for order in range(2):

        def blurred_of(block):
            return blurred_planes(wide_refs[order], yf_ref, zhi_ref, zlo_ref, order, block)

        def image_of(p):
            return image_refs[order][p, first_row:first_row + rows]

        def complete(p, ratio):
            if inner:
                refs[0][order, p] = ratio[rows - count:]
                return ratio
            return jnp.concatenate([passed_ref[order, p], ratio], axis=0)

        edges = (far_ref.at[order], near_ref.at[order])
        adjoint_planes(blurred_of, image_of, ya_ref, zhi_ref, zlo_ref, order, out_refs[order], edges, complete)


def next_ratio(images, wides, passed, y_tables, z_tables, radius, count, first_row):
    planes, _, lanes = images[0].shape
    rows = y_tables[1].shape[1]
    kernel = functools.partial(next_ratio_kernel, inner=passed is None, count=count, first_row=first_row)
    shape = jax.ShapeDtypeStruct
    whole, edge = shape((planes, rows, lanes), F32), shape((2, radius, rows, lanes), F32)
    out_shape = (whole, whole, edge, edge)
    if passed is None:
        out_shape += (shape((2, planes, count, lanes), F32),)
    operands = [*images, *wides[0], *wides[1]] + ([] if passed is None else [passed]) + [*y_tables, *z_tables]
    return call(kernel, out_shape, [VMEM] * len(operands), "ratio")(*operands)


def first_ratio(shifts, blocks, masks, blurred, tables, order, radius, chunks, extent_x, cells_y):
    planes, near, lanes = blurred.shape
    kernel = functools.partial(first_ratio_kernel, order=order, extent_x=extent_x, cells_y=cells_y)
    rows = tables.whole[1].shape[1]
    out_shape = edge_shapes((planes, rows, lanes), radius, chunks) + (jax.ShapeDtypeStruct(blurred.shape, F32),)
    scratch = [
        pltpu.VMEM(blurred.shape, F32), pltpu.VMEM(blurred.shape, F32), pltpu.SemaphoreType.DMA((2,))
    ]
    in_specs = [SMEM] + [pl.BlockSpec(memory_space=pl.ANY)] * 3 + [VMEM] * 5
    return call(kernel, out_shape, in_specs, "image_and_ratio", scratch, hbm=(len(out_shape) - 1,))(
        shifts, *blocks, masks, blurred, tables.whole[1], *tables.z
    )


def factor_kernel(hi_ref, lo_ref, before_ref, *refs, orders, starts, share):
    out_ref = refs[-1]
    planes, rows, _ = out_ref.shape

    def body(step, carry):
        row = pl.multiple_of(step * 8, 8)
        total = gather(before_ref, starts[0] + row)
        if share:
            total = share * jnp.log(total)
        for index, order in enumerate(orders):
            far_ref, near_ref, own_ref = refs[3 * index:3 * index + 3]
            if len(far_ref.shape) == 4:
                far_ref, near_ref = far_ref.at[order], near_ref.at[order]
            own = gather(own_ref, starts[1] + row)
            blocks = [[own, gather(near_ref, row)], [gather(far_ref, row)]]
            band_rows = slice(order * 8 * planes, (order + 1) * 8 * planes)
            total = total + jnp.log(spread_x(hi_ref, lo_ref, 1, band_rows, slice(None), blocks))
        out_ref[:, pl.ds(row, 8), :] = total
        return carry

    lax.fori_loop(0, rows // 8, body, 0)


def log_factor(tables, before, sides, orders, rows, starts, share):
    kernel = functools.partial(factor_kernel, orders=orders, starts=starts, share=share)
    planes, _, lanes = sides[0][2].shape
    shape = jax.ShapeDtypeStruct((planes, rows, lanes), F32)
    parts = [part for side in sides for part in side]
    return call(kernel, shape, [VMEM] * (3 + len(parts)), "log_factor")(*tables.x, before, *parts)


def update_kernel(*refs, count):
    parts, out_ref, edge_refs = refs[:count], refs[count], refs[count + 1:]
    for p in range(out_ref.shape[0]):
        total = parts[0][p]
        for part in parts[1:]:
            total = total + part[p]
        out_ref[p] = jnp.exp(total)
    put_edges(out_ref, edge_refs)


def update(parts, radius, hbm):
    kernel = functools.partial(update_kernel, count=len(parts))
    out_shape = edge_shapes(parts[0].shape, radius, parts[0].shape[1:2])
    return call(kernel, out_shape, [VMEM] * len(parts), "update", hbm=hbm)(*parts)


def finish_kernel(*refs):
    own, other, out_ref = refs[:(len(refs) - 1) // 2], refs[(len(refs) - 1) // 2:-1], refs[-1]
    straight = core() == half()
    groups = out_ref.shape[1] // GROUP
    for group in range(groups):
        rows = slice(group * GROUP, (group + 1) * GROUP)
        own_total, other_total = own[0][:, rows, :], other[0][:, rows, :]
        for part in own[1:]:
            own_total = own_total + part[:, rows, :]
        for part in other[1:]:
            other_total = other_total + part[:, rows, :]
        start = jnp.where(core() == 0, group, groups - 1 - group) * GROUP
        out_ref[:, pl.ds(pl.multiple_of(start, GROUP), GROUP), :] = jnp.exp(jnp.where(straight, own_total, other_total))


def finish(own_parts, other_parts):
    shape = jax.ShapeDtypeStruct(own_parts[0].shape, F32)
    return call(finish_kernel, shape, [VMEM] * (2 * len(own_parts)), "last_update")(*own_parts, *other_parts)


def join_kernel(*refs, starts):
    sources, out_ref, semaphores = refs[:-2], refs[-2], refs[-1]
    cells_y = out_ref.shape[1]
    copies = []
    for index, source_ref in enumerate(sources):
        rows, start = source_ref.shape[1], starts[index // 2]
        side = core() if index % 2 == 0 else 1 - core()
        place = pl.multiple_of(jnp.where(side == 0, start, cells_y - start - rows), GROUP)
        target = out_ref.at[:, pl.ds(place, rows), :]
        copies.append(pltpu.make_async_copy(source_ref, target, semaphores.at[index]))
    for copy in copies:
        copy.start()
    for copy in copies:
        copy.wait()


def join(pieces, starts, shape):
    anywhere = pl.BlockSpec(memory_space=pl.ANY)
    return pl.pallas_call(
        functools.partial(join_kernel, starts=starts),
        out_shape=jax.ShapeDtypeStruct(shape, F32),
        in_specs=[anywhere] * len(pieces),
        out_specs=anywhere,
        scratch_shapes=[pltpu.SemaphoreType.DMA((len(pieces),))],
        compiler_params=PARAMS,
        name="join_halves",
    )(*pieces)


def shards(acquired, estimate, offsets, view_mask, kern_x, kern_y, kern_z):
    planes, cells_y, cells_z = estimate.shape
    views, slabs = lax.axis_size("view"), lax.axis_size("tile")
    groups = views // 2
    taps_y = kern_y.shape[1]
    radius = kern_x.shape[1] // 2
    own_rows = cells_y // 2
    near = own_rows + pad_to(taps_y // 2, GROUP)
    wide = own_rows + pad_to(2 * (taps_y // 2), GROUP)
    edge_rows = wide - own_rows
    inner_rows = own_rows - edge_rows
    group = lax.axis_index("view") // 2
    straight = core() == half()

    def across(turn, half_of=lambda r: r, core_of=lambda c: c, when=lambda c, r: True):
        return lambda g, c, q, r: ((g + turn) % groups, core_of(c), q, half_of(r)) if when(c, r) else None

    def neighbours(far, near):
        return send(far, to_far), send(near, to_core_partner)

    crossing = other_window(estimate, wide)
    crossed = send(crossing, across(0, lambda r: 1 - r, when=lambda c, r: c == r))

    mine = [jnp.pad(row, ((0, 0), (0, 128 - row.shape[1]))) for row in (kern_x, kern_y, kern_z)]
    mine = after(jnp.concatenate(mine, axis=1), crossing)
    other = send(mine, to_core_partner)
    taps = kern_x.shape[1], taps_y, kern_z.shape[1]
    tables = make_tables(mine, other, taps, planes, cells_y, cells_z, (own_rows, near, wide))
    offset = after(offsets.astype(F32), tables.whole[0])
    other = send(offset, to_core_partner)
    shifts = jnp.where(straight, jnp.concatenate([offset, other]), jnp.concatenate([other, offset])).astype(jnp.int32)

    mask = view_mask.astype(F32)
    other = send(mask, to_core_partner)
    masks = jnp.where(core() == 0, jnp.concatenate([mask, other]), jnp.concatenate([other, mask]))

    acquired = after(after(acquired, tables.whole[0]), masks)
    first, second = shift_and_cut(offsets, acquired[0], near)

    arrived = send(after(first, tables.whole[0]), lambda g, c, q, r: (g, r, q, c) if c != r else None)
    current, distant = choose(after(estimate, first), crossed, radius)
    second = send(after(second, current), lambda g, c, q, r: (g, r, q, 1 - c))
    close = lax.dynamic_slice_in_dim(current, (1 - core()) * (planes - radius), radius, 0)
    distant, close = neighbours(distant, close)
    first = jnp.where(straight, first, arrived)

    masks = jnp.where(straight, masks, send(after(masks, current), to_row_partner))

    blocks = [(*neighbours(block, block), block) for block in (first, second)]
    wide_parts = blur_x(tables, (current, close), blur_x(tables, (distant,), (), planes), planes)
    blurred = [blur_yz([part], tables, order) for order, part in enumerate(wide_parts)]

    row_chunks = [(inner_rows, edge_rows), (0, inner_rows)]
    share = 1.0 / groups
    images, sides = [], []
    for order, chunk_sizes in enumerate(([own_rows], [edge_rows, inner_rows])):
        spread, *edges, image = first_ratio(
            shifts, blocks[order], masks, blurred[order], tables, order, radius, chunk_sizes, planes * slabs, cells_y
        )
        images.append(image)
        sides.append([(*neighbours(*edges[k:k + 2]), spread) for k in range(0, len(edges), 2)])
    total = log_factor(tables, current, sides[0], [0], own_rows, (0, 0), share)
    totals = [
        log_factor(tables, total, [side], [1], rows, (start, start), 0)
        for (start, rows), side in zip(row_chunks, sides[1])
    ]

    for step in range(1, ITERS):
        chunks, before = [], []
        for total in totals:
            parts = [total] + [send(total, across(turn)) for turn in range(1, groups)]
            rows, distant, close = update(parts, radius, () if chunks else (2,))
            if total is totals[0]:
                beyond = send(rows, to_row_partner)
            distant = after(distant, chunks[0][0]) if chunks else distant
            distant, close = neighbours(distant, close)
            chunks.append((distant, blur_near(tables, rows, close)))
            before.append(rows)
        rest = planes - radius
        distant, close = neighbours(
            lax.dynamic_slice_in_dim(beyond, core() * rest, radius, 0),
            lax.dynamic_slice_in_dim(beyond, (1 - core()) * rest, radius, 0),
        )
        edge_parts, inner_parts = [blur_far(tables, *chunk) for chunk in chunks]
        halo_parts = blur_near(tables, beyond, close)
        *inner_spreads, distant_inner, close_inner, passed = next_ratio(
            images, list(zip([after(after(part, distant), close) for part in inner_parts], edge_parts)), None, tables.inner, tables.z, radius, 2 * (near - own_rows), 0
        )
        halo_parts = blur_far(tables, distant, halo_parts)
        inner_side = neighbours(distant_inner, close_inner)
        *edge_spreads, distant, close = next_ratio(
            images, list(zip(edge_parts, halo_parts)), passed, tables.edge, tables.z, radius, 0,
            inner_rows + near - own_rows,
        )
        edge_side = neighbours(distant, close)
        totals = [
            log_factor(tables, rows_of, [(*side, spread) for spread in spreads], [0, 1], rows, (0, 0), share)
            for rows_of, side, spreads, rows in (
                (before[0], edge_side, edge_spreads, edge_rows), (before[1], inner_side, inner_spreads, inner_rows)
            )
        ]

    pieces = []
    for own in totals[::-1]:
        other_parts = [
            send(own, across(turn, lambda r: 1 - r, lambda c: 1 - c, lambda c, r: c != r))
            for turn in reversed(range(groups))
        ]
        own_parts = [own] + [send(own, across(turn, when=lambda c, r: c == r)) for turn in range(1, groups)]
        mine = finish(own_parts, other_parts)
        pieces += [mine, send(mine, to_core_partner)]
    return join(pieces, [start for start, _ in row_chunks[::-1]], estimate.shape)


def solution(mesh):
    in_specs = (
        P("view", "tile", None, None),
        P("tile", None, None),
        P("view", None),
        P("view", "tile", None),
        P("view", None),
        P("view", None),
        P("view", None),
    )
    out_specs = P("tile", None, None)
    return jax.shard_map(shards, mesh=mesh, in_specs=in_specs, out_specs=out_specs, check_vma=False)
```

```python
import functools
import typing

import jax
import jax.numpy as jnp
from jax import lax
from jax.experimental import pallas as pl
from jax.experimental.pallas import tpu as pltpu
from jax.sharding import PartitionSpec as P

ITERS = 2
AXES = ("view", "tile")
F32 = jnp.float32
BF16 = jnp.bfloat16
VMEM = pl.BlockSpec(memory_space=pltpu.VMEM)
SMEM = pl.BlockSpec(memory_space=pltpu.SMEM)
PARAMS = pltpu.CompilerParams(vmem_limit_bytes=12 * 1024 * 1024)
GROUP = 16


def moves(move):
    views, tiles = lax.axis_size("view"), lax.axis_size("tile")
    pairs = []
    for view in range(views):
        for tile in range(tiles):
            target = move(view // 2, view % 2, tile // 2, tile % 2)
            if target is not None:
                g, c, q, r = target
                pairs.append((view * tiles + tile, (2 * g + c) * tiles + 2 * q + r))
    return pairs


def send(array, move):
    return lax.ppermute(array, AXES, moves(move))


def after(array, other):
    return lax.optimization_barrier((array, other))[0]


def to_far(g, c, q, r):
    s = 2 * q + c + (1 if c else -1)
    return (g, s % 2, s // 2, r) if 0 <= s < lax.axis_size("tile") else None


def to_row_partner(g, c, q, r):
    return (g, c, q, 1 - r)


def to_core_partner(g, c, q, r):
    return (g, 1 - c, q, r)


def core():
    return lax.rem(lax.axis_index("view"), 2)


def half():
    return lax.rem(lax.axis_index("tile"), 2)


def split(x):
    high = x.astype(BF16)
    return high, (x - high.astype(F32)).astype(BF16)


def dot(a, b):
    return jnp.dot(a, b, preferred_element_type=F32)


def iota(shape, dim):
    return lax.broadcasted_iota(jnp.int32, shape, dim)


def group_row(half, group, cells_y):
    return group * GROUP + half * (cells_y - GROUP - 2 * group * GROUP)


def global_row(half, local, cells_y):
    group = local // GROUP
    return group_row(half, group, cells_y) + (local - group * GROUP)


def wide_local(place, own, wide):
    group = (place - own) // GROUP
    return own + (wide - own) - GROUP - group * GROUP + (place - own - group * GROUP)


def wide_group(group, own_groups, groups):
    return group if group < own_groups else own_groups + groups - 1 - group


def pad_to(value, unit):
    return -(-value // unit) * unit


def call(kernel, out_shape, in_specs, name, scratch=(), hbm=()):
    if hbm:
        out_shape = tuple(pltpu.HBM(o.shape, o.dtype) if index in hbm else o for index, o in enumerate(out_shape))
    return pl.pallas_call(
        kernel,
        out_shape=out_shape,
        in_specs=in_specs,
        out_specs=(VMEM,) * len(out_shape) if isinstance(out_shape, tuple) else VMEM,
        scratch_shapes=list(scratch),
        compiler_params=PARAMS,
        name=name,
    )


class Tables(typing.NamedTuple):
    whole: tuple
    inner: tuple
    edge: tuple
    z: tuple
    x: tuple


def place(row, count, width, turned, spacing):
    source, target = iota((row.shape[1], width), 0), iota((row.shape[1], width), 1)
    index = count - 1 - source if turned else source
    ones = (target == spacing * index) & (source < count)
    return jnp.dot(row, ones.astype(F32), precision=lax.Precision.HIGHEST, preferred_element_type=F32)


def tables_kernel(mine_ref, other_ref, *refs, blocks, sizes, cells_y, taps):
    y_refs, (zhi_ref, zlo_ref, xhi_ref, xlo_ref) = refs[:-4], refs[-4:]
    taps_x, taps_y, taps_z = taps
    straight = core() == half()
    mine, other = mine_ref[...], other_ref[...]
    both = (jnp.where(straight, mine, other), jnp.where(straight, other, mine))
    radius, radius_x, radius_z = taps_y // 2, taps_x // 2, taps_z // 2
    side = half()
    own, wide = sizes
    for out_ref, adjoint, first_row, first_col, width in zip(y_refs, *zip(*blocks)):
        _, rows, lanes = out_ref.shape
        row = global_row(side, first_row + iota((rows, lanes), 0), cells_y)
        lane = iota((rows, lanes), 1)
        place_of = lane + first_col
        turned = place_of if adjoint else jnp.where(place_of < own, place_of, wide_local(place_of, own, wide))
        col = global_row(side, turned, cells_y)
        delta = (row - col if adjoint else col - row) + radius
        delta = jnp.where(lane < width, delta, -1)
        for order in range(2):
            band = jnp.zeros((rows, lanes), F32)
            values = both[order][:, 128:256]
            for a in range(taps_y):
                band = jnp.where(delta == a, jnp.broadcast_to(values[:, a:a + 1], (rows, lanes)), band)
            high, low = split(band)
            high, low = high.astype(F32), low.astype(F32)
            out_ref[order] = (high + pltpu.roll(high, width, 1) + pltpu.roll(low, 2 * width, 1)).astype(BF16)

    lanes = zhi_ref.shape[2]
    near_z = jnp.abs(iota((lanes, lanes), 1) - iota((lanes, lanes), 0)) <= radius_z
    for index in range(4):
        base = place(both[index % 2][:, 256:384], taps_z, lanes, index < 2, 1)
        base = pltpu.roll(base, lanes - radius_z, 1)
        band = pltpu.roll(jnp.broadcast_to(base, (lanes, lanes)), 0, 1, stride=1, stride_axis=0)
        zhi_ref[index], zlo_ref[index] = split(jnp.where(near_z, band, jnp.zeros_like(band)))

    rows = xhi_ref.shape[1] // 2
    lanes = max(512, 1 << (xhi_ref.shape[2] - 1).bit_length())
    for index in range(4):
        base = place(both[index % 2][:, :128], taps_x, lanes, index >= 2, 8)
        base = jnp.broadcast_to(base, (rows, lanes))
        band = pltpu.roll(base, 0, 1, stride=1, stride_axis=0)
        lane = iota((rows, lanes), 1)
        edge = 8 * radius_x
        far = pad_to(rows + edge, 128)
        next_near = pltpu.roll(band, lanes - edge, 1)
        next_far = pltpu.roll(band, far - rows - edge, 1)
        near_part = jnp.where((lane < rows) | (core() == 0), next_near, pltpu.roll(band, rows, 1))
        far_part = jnp.where(core() == 0, pltpu.roll(band, far, 1), next_far)
        zero = jnp.zeros_like(band)
        band = jnp.where(
            lane < rows + edge, near_part, jnp.where((lane >= far) & (lane < far + edge), far_part, zero)
        )[:, :xhi_ref.shape[2]]
        block = (index // 2, slice(index % 2 * rows, index % 2 * rows + rows))
        xhi_ref[block], xlo_ref[block] = split(band)


def make_tables(mine, other, taps, planes, cells_y, cells_z, sizes):
    own, near, wide = sizes
    inner, beyond = 2 * own - wide, near - own
    radius = taps[0] // 2
    depth = pad_to(8 * (planes + radius), 128) + pad_to(8 * radius, 128)
    blocks = [
        (False, near, 0, 0, wide), (True, own, 0, 0, near),
        (False, inner + beyond, 0, 0, own), (True, inner, 0, 0, inner + beyond),
        (False, near - inner - beyond, inner + beyond, inner, wide - inner),
        (True, own - inner, inner, inner - beyond, near - inner + beyond),
    ]
    kernel = functools.partial(
        tables_kernel, blocks=[block[:1] + block[2:] for block in blocks], sizes=(own, wide), cells_y=cells_y, taps=taps
    )
    shape = jax.ShapeDtypeStruct
    out_shape = tuple(shape((2, block[1], pad_to(3 * block[4], 128)), BF16) for block in blocks) + (
        shape((4, cells_z, cells_z), BF16),
        shape((4, cells_z, cells_z), BF16),
        shape((2, 2 * 8 * planes, depth), BF16),
        shape((2, 2 * 8 * planes, depth), BF16),
    )
    tables = call(kernel, out_shape, [VMEM, VMEM], "band_matrices")(mine, other)
    whole, inner_rows, edge_rows = tables[0:2], tables[2:4], tables[4:6]
    return Tables(whole, inner_rows, edge_rows, tables[6:8], tables[8:10])


def window_rows(side, groups, cells_y):
    for group in range(groups):
        local = wide_group(group, cells_y // 2 // GROUP, groups)
        start = pl.multiple_of(group_row(side, local, cells_y), GROUP)
        yield slice(group * GROUP, (group + 1) * GROUP), pl.ds(start, GROUP)


def window_kernel(estimate_ref, out_ref):
    for rows, source in window_rows(1 - half(), out_ref.shape[1] // GROUP, estimate_ref.shape[1]):
        out_ref[:, rows, :] = estimate_ref[:, source, :]


def other_window(estimate, wide):
    planes, _, cells_z = estimate.shape
    shape = jax.ShapeDtypeStruct((planes, wide, cells_z), F32)
    return call(window_kernel, shape, [VMEM], "other_window")(estimate)


def put_edges(out_ref, edge_refs):
    end = out_ref.shape[1]
    for far_ref, near_ref in zip(edge_refs[::2], edge_refs[1::2]):
        radius, rows = far_ref.shape[0], slice(end - far_ref.shape[1], end)
        beyond = out_ref.shape[0] - radius
        for p in range(radius):
            far_ref[p] = out_ref[p + core() * beyond, rows]
            near_ref[p] = out_ref[p + (1 - core()) * beyond, rows]
        end -= far_ref.shape[1]


def choose_kernel(estimate_ref, crossed_ref, out_ref, far_ref):
    straight = core() == half()
    for rows, source in window_rows(half(), out_ref.shape[1] // GROUP, estimate_ref.shape[1]):
        out_ref[:, rows, :] = jnp.where(straight, estimate_ref[:, source, :], crossed_ref[:, rows, :])
    beyond = core() * (out_ref.shape[0] - far_ref.shape[0])
    for p in range(far_ref.shape[0]):
        far_ref[p] = out_ref[p + beyond]


def edge_shapes(shape, radius, chunks):
    planes, _, lanes = shape
    edges = [jax.ShapeDtypeStruct((radius, rows, lanes), F32) for rows in chunks for _ in range(2)]
    return (jax.ShapeDtypeStruct(shape, F32), *edges)


def choose(estimate, crossed, radius):
    out_shape = edge_shapes(crossed.shape, radius, crossed.shape[1:2])[:2]
    estimate, crossed = (pltpu.with_memory_space_constraint(array, pltpu.HBM) for array in (estimate, crossed))
    return call(choose_kernel, out_shape, [VMEM] * 2, "estimate")(estimate, crossed)


def shift_kernel(offsets_ref, acq_ref, first_ref, second_ref, turned_ref):
    planes, cells_y, cells_z = acq_ref.shape
    near = first_ref.shape[1]
    shift_y, shift_z = offsets_ref[0, 1], offsets_ref[0, 2]
    row = iota((cells_y, cells_z), 0) + shift_y
    col = iota((cells_y, cells_z), 1) + shift_z
    inside = (row >= 0) & (row < cells_y) & (col >= 0) & (col < cells_z)
    turn_y = lax.rem(cells_y - shift_y, cells_y)
    turn_z = lax.rem(cells_z - shift_z, cells_z)

    def body(p, carry):
        x = pltpu.roll(pltpu.roll(acq_ref[p], turn_z, 1), turn_y, 0)
        turned_ref[...] = jnp.where(inside, x, jnp.zeros_like(x))
        for side, out_ref in ((core(), first_ref), (1 - core(), second_ref)):
            for group in range(near // GROUP):
                start = pl.multiple_of(group_row(side, group, cells_y), GROUP)
                out_ref[p, group * GROUP:(group + 1) * GROUP, :] = turned_ref[pl.ds(start, GROUP), :]
        return carry

    lax.fori_loop(0, planes, body, 0)


def shift_and_cut(offsets, acquired, near):
    planes, cells_y, cells_z = acquired.shape
    shape = jax.ShapeDtypeStruct((planes, near, cells_z), F32)
    scratch = [pltpu.VMEM((cells_y, cells_z), F32)]
    return call(shift_kernel, (shape, shape), [SMEM, VMEM], "shift_recorded", scratch)(offsets, acquired)


def gather(ref, row):
    return ref[:, pl.ds(pl.multiple_of(row, 8), 8), :]


def spread_x(hi_ref, lo_ref, index, band_rows, band_lanes, blocks):
    lanes = blocks[0][0].shape[2]
    filled = []
    for parts in blocks:
        count = 8 * sum(part.shape[0] for part in parts)
        missing = (pad_to(count, 128) - count) // 8
        filled += list(parts) + ([jnp.zeros((missing, 8, lanes), F32)] if missing else [])
    high, low = split(jnp.concatenate(filled, axis=0).reshape(-1, lanes))
    band = hi_ref[index, band_rows, band_lanes]
    out = dot(band, high) + (dot(band, low) + dot(lo_ref[index, band_rows, band_lanes], high))
    return out.reshape(-1, 8, lanes)


def near_lanes(planes, radius):
    return pad_to(8 * (planes + radius), 128)


def blur_x_kernel(hi_ref, lo_ref, *refs, far, radius):
    planes_of, before, (first_ref, second_ref) = refs[:2 - far], refs[2 - far:-2], refs[-2:]
    planes, rows, _ = first_ref.shape
    split_at = near_lanes(planes, radius)
    lanes = slice(split_at, None) if far else slice(0, split_at)

    def body(step, carry):
        row = pl.multiple_of(step * 8, 8)
        place = (slice(None), pl.ds(row, 8), slice(None))
        out = spread_x(hi_ref, lo_ref, 0, slice(None), lanes, [[gather(ref, row) for ref in planes_of]])
        out = [out[:planes], out[planes:]]
        if before:
            out = [ref[place] + part for ref, part in zip(before, out)]
        first_ref[place], second_ref[place] = out
        return carry

    lax.fori_loop(0, rows // 8, body, 0)


def blur_x(tables, planes_of, before, planes):
    far, (radius, rows, lanes) = len(planes_of) == 1, planes_of[-1].shape
    shape = jax.ShapeDtypeStruct((planes, rows, lanes), F32)
    kernel = functools.partial(blur_x_kernel, far=far, radius=radius)
    operands = [*tables.x, *planes_of, *before]
    return call(kernel, (shape, shape), [VMEM] * len(operands), "blur_x_far" if far else "blur_x_near")(*operands)


def blur_near(tables, own, near):
    return blur_x(tables, (own, near), (), own.shape[0])


def blur_far(tables, far, parts):
    return blur_x(tables, (far,), parts, parts[0].shape[0])


def spread_y(band, x):
    high, low = split(x)
    return dot(band[:, :3 * x.shape[0]], jnp.concatenate([high, low, high], axis=0))


def spread_z(x, hi_ref, lo_ref, index):
    high, low = split(x)
    return dot(high, hi_ref[index]) + (dot(low, hi_ref[index]) + dot(high, lo_ref[index]))


def blurred_planes(wide_refs, yf_ref, zhi_ref, zlo_ref, order, block):
    wide = [jnp.concatenate([ref[p] for ref in wide_refs], axis=0) for p in block]
    spread = jnp.concatenate([spread_y(yf_ref[order], rows) for rows in wide], axis=0)
    return spread_z(spread, zhi_ref, zlo_ref, order)


def plane_blocks(planes, step=4):
    return [range(start, min(start + step, planes)) for start in range(0, planes, step)]


def blur_yz_kernel(*refs, order):
    wide_refs, (yf_ref, zhi_ref, zlo_ref, out_ref) = refs[:-4], refs[-4:]
    near = yf_ref.shape[1]
    for block in plane_blocks(out_ref.shape[0]):
        blurred = blurred_planes(wide_refs, yf_ref, zhi_ref, zlo_ref, order, block)
        for k, p in enumerate(block):
            out_ref[p] = blurred[k * near:(k + 1) * near]


def blur_yz(wides, tables, order):
    planes, _, lanes = wides[0].shape
    shape = jax.ShapeDtypeStruct((planes, tables.whole[0].shape[1], lanes), F32)
    kernel = functools.partial(blur_yz_kernel, order=order)
    return call(kernel, shape, [VMEM] * (3 + len(wides)), "blur_yz")(*wides, tables.whole[0], *tables.z)


def adjoint_planes(blurred_of, image_of, ya_ref, zhi_ref, zlo_ref, order, out_ref, edge_refs, complete=None):
    planes, rows, _ = out_ref.shape
    for block in plane_blocks(planes):
        blurred = blurred_of(block)
        image = jnp.concatenate([image_of(p) for p in block], axis=0)
        ratio = jnp.where(image >= 0, image / blurred, jnp.ones_like(image))
        near = ratio.shape[0] // len(block)
        ratios = [ratio[k * near:(k + 1) * near] for k in range(len(block))]
        if complete:
            ratios = [complete(p, rows_of) for p, rows_of in zip(block, ratios)]
        spread = jnp.concatenate([spread_y(ya_ref[order], rows_of) for rows_of in ratios], axis=0)
        spread = spread_z(spread, zhi_ref, zlo_ref, 2 + order)
        for k, p in enumerate(block):
            out_ref[p] = spread[k * rows:(k + 1) * rows]
    put_edges(out_ref, edge_refs)


def first_ratio_kernel(
    shift_ref, far_ref, near_ref, own_ref, masks_ref, blurred_ref, ya_ref, zhi_ref, zlo_ref, out_ref, *refs, order, extent_x, cells_y
):
    edge_refs, image_ref, (mine_ref, beyond_ref, semaphores) = refs[:-4], refs[-4], refs[-3:]
    planes, near, cells_z = image_ref.shape
    side = half()
    slab = lax.axis_index("tile") - side + core()
    shift_x, shift_y, shift_z = (shift_ref[order, i] for i in range(3))
    lanes = masks_ref.shape[2]
    pick = iota((near, lanes), 1) == global_row(side, iota((near, lanes), 0), cells_y)
    is_far = (shift_x > 0) == (core() == 1)
    copy = pltpu.make_async_copy(own_ref, mine_ref, semaphores.at[0])
    far_copy = pltpu.make_async_copy(far_ref, beyond_ref, semaphores.at[1])
    near_copy = pltpu.make_async_copy(near_ref, beyond_ref, semaphores.at[1])
    copy.start()
    pl.when(is_far)(far_copy.start)
    pl.when(jnp.logical_not(is_far))(near_copy.start)
    copy.wait()
    far_copy.wait()
    mask = masks_ref[half() if order == 0 else 1 - half()].astype(BF16)
    columns = lax.dot_general(
        pick.astype(F32).astype(BF16), mask, (((1,), (1,)), ((), ())), preferred_element_type=F32
    )
    row = global_row(side, iota((near, cells_z), 0), cells_y) + shift_y
    col = iota((near, cells_z), 1) + shift_z
    inside = (row >= 0) & (row < cells_y) & (col >= 0) & (col < cells_z)

    def fetch(p):
        source = p + shift_x
        x = slab * planes + source
        is_own = (source >= 0) & (source < planes)
        beyond = jnp.clip(jnp.where(source < 0, source + planes, source - planes), 0, planes - 1)
        value = jnp.where(is_own, mine_ref[jnp.clip(source, 0, planes - 1)], beyond_ref[beyond])
        weight = jnp.broadcast_to(columns[:, p:p + 1], (near, cells_z))
        covered = inside & (weight > 0.5) & (x >= 0) & (x < extent_x)
        value = jnp.where(covered, value, jnp.full_like(value, -1.0))
        image_ref[p] = value
        return value

    def blurred_of(block):
        return jnp.concatenate([blurred_ref[p] for p in block], axis=0)

    adjoint_planes(blurred_of, fetch, ya_ref, zhi_ref, zlo_ref, order, out_ref, edge_refs)


def next_ratio_kernel(*refs, inner, count, first_row):
    image_refs, wide_refs, refs = refs[:2], (refs[2:4], refs[4:6]), refs[6:]
    passed_ref, refs = (None, refs) if inner else (refs[0], refs[1:])
    (yf_ref, ya_ref, zhi_ref, zlo_ref), out_refs, (far_ref, near_ref), refs = refs[:4], refs[4:6], refs[6:8], refs[8:]
    planes = out_refs[0].shape[0]
    rows = yf_ref.shape[1]
    for order in range(2):

        def blurred_of(block):
            return blurred_planes(wide_refs[order], yf_ref, zhi_ref, zlo_ref, order, block)

        def image_of(p):
            return image_refs[order][p, first_row:first_row + rows]

        def complete(p, ratio):
            if inner:
                refs[0][order, p] = ratio[rows - count:]
                return ratio
            return jnp.concatenate([passed_ref[order, p], ratio], axis=0)

        edges = (far_ref.at[order], near_ref.at[order])
        adjoint_planes(blurred_of, image_of, ya_ref, zhi_ref, zlo_ref, order, out_refs[order], edges, complete)


def next_ratio(images, wides, passed, y_tables, z_tables, radius, count, first_row):
    planes, _, lanes = images[0].shape
    rows = y_tables[1].shape[1]
    kernel = functools.partial(next_ratio_kernel, inner=passed is None, count=count, first_row=first_row)
    shape = jax.ShapeDtypeStruct
    whole, edge = shape((planes, rows, lanes), F32), shape((2, radius, rows, lanes), F32)
    out_shape = (whole, whole, edge, edge)
    if passed is None:
        out_shape += (shape((2, planes, count, lanes), F32),)
    operands = [*images, *wides[0], *wides[1]] + ([] if passed is None else [passed]) + [*y_tables, *z_tables]
    return call(kernel, out_shape, [VMEM] * len(operands), "ratio")(*operands)


def first_ratio(shifts, blocks, masks, blurred, tables, order, radius, chunks, extent_x, cells_y):
    planes, near, lanes = blurred.shape
    kernel = functools.partial(first_ratio_kernel, order=order, extent_x=extent_x, cells_y=cells_y)
    rows = tables.whole[1].shape[1]
    out_shape = edge_shapes((planes, rows, lanes), radius, chunks) + (jax.ShapeDtypeStruct(blurred.shape, F32),)
    scratch = [
        pltpu.VMEM(blurred.shape, F32), pltpu.VMEM(blurred.shape, F32), pltpu.SemaphoreType.DMA((2,))
    ]
    in_specs = [SMEM] + [pl.BlockSpec(memory_space=pl.ANY)] * 3 + [VMEM] * 5
    return call(kernel, out_shape, in_specs, "image_and_ratio", scratch, hbm=(len(out_shape) - 1,))(
        shifts, *blocks, masks, blurred, tables.whole[1], *tables.z
    )


def factor_kernel(hi_ref, lo_ref, before_ref, *refs, orders, starts, share):
    out_ref = refs[-1]
    planes, rows, _ = out_ref.shape

    def body(step, carry):
        row = pl.multiple_of(step * 8, 8)
        total = gather(before_ref, starts[0] + row)
        if share:
            total = share * jnp.log(total)
        for index, order in enumerate(orders):
            far_ref, near_ref, own_ref = refs[3 * index:3 * index + 3]
            if len(far_ref.shape) == 4:
                far_ref, near_ref = far_ref.at[order], near_ref.at[order]
            own = gather(own_ref, starts[1] + row)
            blocks = [[own, gather(near_ref, row)], [gather(far_ref, row)]]
            band_rows = slice(order * 8 * planes, (order + 1) * 8 * planes)
            total = total + jnp.log(spread_x(hi_ref, lo_ref, 1, band_rows, slice(None), blocks))
        out_ref[:, pl.ds(row, 8), :] = total
        return carry

    lax.fori_loop(0, rows // 8, body, 0)


def log_factor(tables, before, sides, orders, rows, starts, share):
    kernel = functools.partial(factor_kernel, orders=orders, starts=starts, share=share)
    planes, _, lanes = sides[0][2].shape
    shape = jax.ShapeDtypeStruct((planes, rows, lanes), F32)
    parts = [part for side in sides for part in side]
    return call(kernel, shape, [VMEM] * (3 + len(parts)), "log_factor")(*tables.x, before, *parts)


def update_kernel(*refs, count):
    parts, out_ref, edge_refs = refs[:count], refs[count], refs[count + 1:]
    for p in range(out_ref.shape[0]):
        total = parts[0][p]
        for part in parts[1:]:
            total = total + part[p]
        out_ref[p] = jnp.exp(total)
    put_edges(out_ref, edge_refs)


def update(parts, radius, hbm):
    kernel = functools.partial(update_kernel, count=len(parts))
    out_shape = edge_shapes(parts[0].shape, radius, parts[0].shape[1:2])
    return call(kernel, out_shape, [VMEM] * len(parts), "update", hbm=hbm)(*parts)


def finish_kernel(*refs):
    own, other, out_ref = refs[:(len(refs) - 1) // 2], refs[(len(refs) - 1) // 2:-1], refs[-1]
    straight = core() == half()
    groups = out_ref.shape[1] // GROUP
    for group in range(groups):
        rows = slice(group * GROUP, (group + 1) * GROUP)
        own_total, other_total = own[0][:, rows, :], other[0][:, rows, :]
        for part in own[1:]:
            own_total = own_total + part[:, rows, :]
        for part in other[1:]:
            other_total = other_total + part[:, rows, :]
        start = jnp.where(core() == 0, group, groups - 1 - group) * GROUP
        out_ref[:, pl.ds(pl.multiple_of(start, GROUP), GROUP), :] = jnp.exp(jnp.where(straight, own_total, other_total))


def finish(own_parts, other_parts):
    shape = jax.ShapeDtypeStruct(own_parts[0].shape, F32)
    return call(finish_kernel, shape, [VMEM] * (2 * len(own_parts)), "last_update")(*own_parts, *other_parts)


def join_kernel(*refs, starts):
    sources, out_ref, semaphores = refs[:-2], refs[-2], refs[-1]
    cells_y = out_ref.shape[1]
    copies = []
    for index, source_ref in enumerate(sources):
        rows, start = source_ref.shape[1], starts[index // 2]
        side = core() if index % 2 == 0 else 1 - core()
        place = pl.multiple_of(jnp.where(side == 0, start, cells_y - start - rows), GROUP)
        target = out_ref.at[:, pl.ds(place, rows), :]
        copies.append(pltpu.make_async_copy(source_ref, target, semaphores.at[index]))
    for copy in copies:
        copy.start()
    for copy in copies:
        copy.wait()


def join(pieces, starts, shape):
    anywhere = pl.BlockSpec(memory_space=pl.ANY)
    return pl.pallas_call(
        functools.partial(join_kernel, starts=starts),
        out_shape=jax.ShapeDtypeStruct(shape, F32),
        in_specs=[anywhere] * len(pieces),
        out_specs=anywhere,
        scratch_shapes=[pltpu.SemaphoreType.DMA((len(pieces),))],
        compiler_params=PARAMS,
        name="join_halves",
    )(*pieces)


def shards(acquired, estimate, offsets, view_mask, kern_x, kern_y, kern_z):
    planes, cells_y, cells_z = estimate.shape
    views, slabs = lax.axis_size("view"), lax.axis_size("tile")
    groups = views // 2
    taps_y = kern_y.shape[1]
    radius = kern_x.shape[1] // 2
    own_rows = cells_y // 2
    near = own_rows + pad_to(taps_y // 2, GROUP)
    wide = own_rows + pad_to(2 * (taps_y // 2), GROUP)
    edge_rows = wide - own_rows
    inner_rows = own_rows - edge_rows
    group = lax.axis_index("view") // 2
    straight = core() == half()

    def across(turn, half_of=lambda r: r, core_of=lambda c: c, when=lambda c, r: True):
        return lambda g, c, q, r: ((g + turn) % groups, core_of(c), q, half_of(r)) if when(c, r) else None

    def neighbours(far, near):
        return send(far, to_far), send(near, to_core_partner)

    crossing = other_window(estimate, wide)
    crossed = send(crossing, across(0, lambda r: 1 - r, when=lambda c, r: c == r))

    mine = [jnp.pad(row, ((0, 0), (0, 128 - row.shape[1]))) for row in (kern_x, kern_y, kern_z)]
    mine = after(jnp.concatenate(mine, axis=1), crossing)
    other = send(mine, to_core_partner)
    taps = kern_x.shape[1], taps_y, kern_z.shape[1]
    tables = make_tables(mine, other, taps, planes, cells_y, cells_z, (own_rows, near, wide))
    offset = after(offsets.astype(F32), tables.whole[0])
    other = send(offset, to_core_partner)
    shifts = jnp.where(straight, jnp.concatenate([offset, other]), jnp.concatenate([other, offset])).astype(jnp.int32)

    mask = view_mask.astype(F32)
    other = send(mask, to_core_partner)
    masks = jnp.where(core() == 0, jnp.concatenate([mask, other]), jnp.concatenate([other, mask]))

    acquired = after(after(acquired, tables.whole[0]), masks)
    first, second = shift_and_cut(offsets, acquired[0], near)

    arrived = send(after(first, tables.whole[0]), lambda g, c, q, r: (g, r, q, c) if c != r else None)
    current, distant = choose(after(estimate, first), crossed, radius)
    second = send(after(second, current), lambda g, c, q, r: (g, r, q, 1 - c))
    close = lax.dynamic_slice_in_dim(current, (1 - core()) * (planes - radius), radius, 0)
    distant, close = neighbours(distant, close)
    first = jnp.where(straight, first, arrived)

    masks = jnp.where(straight, masks, send(after(masks, second), to_row_partner))

    blocks = [(*neighbours(block, block), block) for block in (first, second)]
    wide_parts = blur_x(tables, (current, close), blur_x(tables, (distant,), (), planes), planes)
    blurred = [blur_yz([part], tables, order) for order, part in enumerate(wide_parts)]

    row_chunks = [(inner_rows, edge_rows), (0, inner_rows)]
    share = 1.0 / groups
    images, sides = [], []
    for order, chunk_sizes in enumerate(([own_rows], [edge_rows, inner_rows])):
        spread, *edges, image = first_ratio(
            shifts, blocks[order], masks, blurred[order], tables, order, radius, chunk_sizes, planes * slabs, cells_y
        )
        images.append(image)
        sides.append([(*neighbours(*edges[k:k + 2]), spread) for k in range(0, len(edges), 2)])
    total = log_factor(tables, current, sides[0], [0], own_rows, (0, 0), share)
    totals = [
        log_factor(tables, total, [side], [1], rows, (start, start), 0)
        for (start, rows), side in zip(row_chunks, sides[1])
    ]

    for step in range(1, ITERS):
        chunks, before = [], []
        for total in totals:
            parts = [total] + [send(total, across(turn)) for turn in range(1, groups)]
            rows, distant, close = update(parts, radius, () if chunks else (2,))
            if total is totals[0]:
                beyond = send(rows, to_row_partner)
            distant = after(distant, chunks[0][0]) if chunks else distant
            distant, close = neighbours(distant, close)
            chunks.append((distant, blur_near(tables, rows, close)))
            before.append(rows)
        rest = planes - radius
        distant, close = neighbours(
            lax.dynamic_slice_in_dim(beyond, core() * rest, radius, 0),
            lax.dynamic_slice_in_dim(beyond, (1 - core()) * rest, radius, 0),
        )
        edge_parts, inner_parts = [blur_far(tables, *chunk) for chunk in chunks]
        halo_parts = blur_near(tables, beyond, close)
        *inner_spreads, distant_inner, close_inner, passed = next_ratio(
            images, list(zip([after(after(part, distant), close) for part in inner_parts], edge_parts)), None, tables.inner, tables.z, radius, 2 * (near - own_rows), 0
        )
        halo_parts = blur_far(tables, distant, halo_parts)
        inner_side = neighbours(distant_inner, close_inner)
        *edge_spreads, distant, close = next_ratio(
            images, list(zip(edge_parts, halo_parts)), passed, tables.edge, tables.z, radius, 0,
            inner_rows + near - own_rows,
        )
        edge_side = neighbours(distant, close)
        totals = [
            log_factor(tables, rows_of, [(*side, spread) for spread in spreads], [0, 1], rows, (0, 0), share)
            for rows_of, side, spreads, rows in (
                (before[0], edge_side, edge_spreads, edge_rows), (before[1], inner_side, inner_spreads, inner_rows)
            )
        ]

    pieces = []
    for own in totals[::-1]:
        other_parts = [
            send(own, across(turn, lambda r: 1 - r, lambda c: 1 - c, lambda c, r: c != r))
            for turn in reversed(range(groups))
        ]
        own_parts = [own] + [send(own, across(turn, when=lambda c, r: c == r)) for turn in range(1, groups)]
        mine = finish(own_parts, other_parts)
        pieces += [mine, send(mine, to_core_partner)]
    return join(pieces, [start for start, _ in row_chunks[::-1]], estimate.shape)


def solution(mesh):
    in_specs = (
        P("view", "tile", None, None),
        P("tile", None, None),
        P("view", None),
        P("view", "tile", None),
        P("view", None),
        P("view", None),
        P("view", None),
    )
    out_specs = P("tile", None, None)
    return jax.shard_map(shards, mesh=mesh, in_specs=in_specs, out_specs=out_specs, check_vma=False)
```
